32 devices in a mesh: dp: 16 (over z, y, core), mp: 2 (over x).
Axes of the slice: x: 2, y: 2, z: 4, core: 2. Of those that a mesh axis runs over, the one named last changes fastest.
Arguments:
- tokens: bfloat16 [40960, 1024], P(('dp', 'mp')), may hold values from -6 to 6
- ln1_gain: float32 [1024], replicated, may hold values from 0.5 to 1.5
- ln1_bias: float32 [1024], replicated, may hold values from -1 to 1
- w_qkv: bfloat16 [1024, 3, 1024], P(None, None, 'mp'), may hold values from -0.1875 to 0.1875
- qv_bias: float32 [2, 1024], P(None, 'mp'), may hold values from -1.5 to 1.5
- w_out: bfloat16 [1024, 1024], P('mp'), may hold values from -0.1875 to 0.1875
- out_bias: float32 [1024], replicated, may hold values from -1.5 to 1.5
- ln2_gain: float32 [1024], replicated, may hold values from 0.5 to 1.5
- ln2_bias: float32 [1024], replicated, may hold values from -1 to 1
- ln3_gain: float32 [1024], replicated, may hold values from 0.5 to 1.5
- ln3_bias: float32 [1024], replicated, may hold values from -1 to 1
- w_up: bfloat16 [1024, 4096], P(None, 'mp'), may hold values from -0.1875 to 0.1875
- up_bias: float32 [4096], P('mp'), may hold values from -1.5 to 1.5
- w_down: bfloat16 [4096, 1024], P('mp'), may hold values from -0.09375 to 0.09375
- down_bias: float32 [1024], replicated, may hold values from -1.5 to 1.5
- ln4_gain: float32 [1024], replicated, may hold values from 0.5 to 1.5
- ln4_bias: float32 [1024], replicated, may hold values from -1 to 1
- row_grid: int32 [16, 8], P('dp'), may hold values from 0 to 48, as said below
- pad_mask: int32 [40960], P('dp'), may hold values from 0 to 1, as said below
- cotangent: bfloat16 [40960, 1024], P(('dp', 'mp')), may hold values from -6 to 6
Outputs:
- layer_out: bfloat16 [40960, 1024], P(('dp', 'mp'))
- grad_in: float32 [40960, 1024], P(('dp', 'mp'))
- g_ln1_gain: float32 [1024], replicated
- g_ln1_bias: float32 [1024], replicated
- g_w_qkv: float32 [1024, 3, 1024], P(None, None, 'mp')
- g_qv_bias: float32 [2, 1024], P(None, 'mp')
- g_w_out: float32 [1024, 1024], P('mp')
- g_out_bias: float32 [1024], replicated
- g_ln2_gain: float32 [1024], replicated
- g_ln2_bias: float32 [1024], replicated
- g_ln3_gain: float32 [1024], replicated
- g_ln3_bias: float32 [1024], replicated
- g_w_up: float32 [1024, 4096], P(None, 'mp')
- g_up_bias: float32 [4096], P('mp')
- g_w_down: float32 [4096, 1024], P('mp')
- g_down_bias: float32 [1024], replicated
- g_ln4_gain: float32 [1024], replicated
- g_ln4_bias: float32 [1024], replicated
The draws below stay inside these ranges and needn't reach their ends.
Inputs may be any that keep to these rules, and one draw needn't show every extreme that they name: `row_grid`: in each group all nonzero entries are the same side, 16, 32 or 48; the first 2560 // (64 + side^2) slots of a group hold it and the rest are 0; some group has side 3 * 16. `pad_mask`: in each row the first few text tokens (at least one, fewer than 64) and all image tokens are 1, the rest of its text tokens 0; slots after a group's last row are 0.
All inputs are finite; a program needn't handle non-finite values.
Results may differ from the reference program's by a relative error of at most 0.022.
Values may be sent and summed in bfloat16 or wider, within the bound.
No kernel may reach another device: no remote copies, remote signals or barrier semaphores. Data moves between devices by JAX's collectives and lax.ppermute only.
A program may use at most 320 MiB of HBM per device.

```python
import jax
import jax.numpy as jnp
from jax import lax

D = 1024
HEADS = 16
HDIM = 64
FF = 4096
TEXT = 64
GRID = 16
GTOK = 2560
QBLK = 512
SLOTS = 8
TOKENS = 40960


def group_sides(key):
    groups = TOKENS // GTOK
    pick_key = jax.random.fold_in(key, 11)
    levels = jax.random.randint(jax.random.fold_in(pick_key, 1), (groups,), 1, 4)
    widest = jax.random.randint(jax.random.fold_in(pick_key, 2), (), 0, groups)
    levels = jnp.where(jnp.arange(groups) == widest, 3, levels)
    side_len = levels * GRID
    counts = GTOK // (TEXT + side_len * side_len)
    slot_ids = jnp.arange(SLOTS)
    return jnp.where(slot_ids[None, :] < counts[:, None], side_len[:, None], 0).astype(jnp.int32)


def draw_row_grid(key, part):
    return group_sides(key)


def draw_pad_mask(key, part):
    grid_rows = group_sides(key)
    groups = grid_rows.shape[0]
    lengths = jnp.where(grid_rows > 0, TEXT + grid_rows * grid_rows, 0).astype(jnp.int32)
    row_ends = jnp.cumsum(lengths, axis=1).astype(jnp.int32)
    row_starts = row_ends - lengths
    live_rows = jnp.sum((grid_rows > 0).astype(jnp.int32), axis=1)
    text_lens = jax.random.randint(jax.random.fold_in(key, 23), grid_rows.shape, TEXT // 4, TEXT)
    position = jnp.arange(GTOK, dtype=jnp.int32)
    seg_of = jnp.sum((position[None, :, None] >= row_ends[:, None, :]).astype(jnp.int32), axis=2)
    inside = seg_of < live_rows[:, None]
    seg_clip = jnp.clip(seg_of, 0, SLOTS - 1)
    start_of = jnp.take_along_axis(row_starts, seg_clip, axis=1)
    text_of = jnp.take_along_axis(text_lens, seg_clip, axis=1)
    offset = position[None, :] - start_of
    keep_flags = inside & ((offset >= TEXT) | (offset < text_of))
    return keep_flags.astype(jnp.int32).reshape(groups * GTOK)


def steps_of(key, dims, split, least, high):
    gain = 1.0
    for dim, shards_of in split:
        steps = jax.random.uniform(jax.random.fold_in(jax.random.fold_in(key, 6), dim), (shards_of,), jnp.float32, least / len(split), high / len(split))
        gain = gain * jnp.repeat(jnp.exp(steps), dims[dim] // shards_of).reshape((-1,) + (1,) * (len(dims) - 1 - dim))
    return gain


def normal_values(key, dims, deviation, limit, shards=(), held_as=jnp.bfloat16):
    gain = steps_of(key, dims, shards, -0.22, 0.18) if shards else 1.0
    array = jax.random.normal(key, dims, jnp.float32) * deviation * gain
    return jnp.minimum(jnp.maximum(array, -limit), limit).astype(held_as)


def setup_inputs(seed: int = 0) -> dict:
    streams_of = jax.random.split(jax.random.key(seed), 21)
    tokens = normal_values(streams_of[0], (TOKENS, D), 1.0, 6.0, ((0, 32),))
    ln1_gain = jnp.clip(1.0 + 0.1 * jax.random.normal(streams_of[1], (D,), jnp.float32), 0.5, 1.5)
    ln1_bias = normal_values(streams_of[2], (D,), 0.2, 1.0, (), jnp.float32)
    w_qkv = normal_values(streams_of[3], (D, 3, D), D ** -0.5, 0.1875, ((2, 2),))
    qv_bias = normal_values(streams_of[4], (2, D), 0.3, 1.5, ((1, 2),), jnp.float32)
    w_out = normal_values(streams_of[5], (D, D), D ** -0.5, 0.1875, ((0, 2),))
    out_bias = normal_values(streams_of[6], (D,), 0.3, 1.5, (), jnp.float32)
    ln2_gain = jnp.clip(1.0 + 0.1 * jax.random.normal(streams_of[7], (D,), jnp.float32), 0.5, 1.5)
    ln2_bias = normal_values(streams_of[8], (D,), 0.2, 1.0, (), jnp.float32)
    ln3_gain = jnp.clip(1.0 + 0.1 * jax.random.normal(streams_of[9], (D,), jnp.float32), 0.5, 1.5)
    ln3_bias = normal_values(streams_of[10], (D,), 0.2, 1.0, (), jnp.float32)
    w_up = normal_values(streams_of[11], (D, FF), D ** -0.5, 0.1875, ((1, 2),))
    up_bias = normal_values(streams_of[12], (FF,), 0.3, 1.5, ((0, 2),), jnp.float32)
    w_down = normal_values(streams_of[13], (FF, D), FF ** -0.5, 0.09375, ((0, 2),))
    down_bias = normal_values(streams_of[14], (D,), 0.3, 1.5, (), jnp.float32)
    ln4_gain = jnp.clip(1.0 + 0.1 * jax.random.normal(streams_of[15], (D,), jnp.float32), 0.5, 1.5)
    ln4_bias = normal_values(streams_of[16], (D,), 0.2, 1.0, (), jnp.float32)
    row_grid = draw_row_grid(jax.random.fold_in(streams_of[20], 71), 0)
    pad_mask = draw_pad_mask(jax.random.fold_in(streams_of[20], 71), 0)
    cotangent = normal_values(streams_of[19], (TOKENS, D), 1.0, 6.0, ((0, 32),))
    return dict(tokens=tokens, ln1_gain=ln1_gain, ln1_bias=ln1_bias, w_qkv=w_qkv, qv_bias=qv_bias, w_out=w_out, out_bias=out_bias, ln2_gain=ln2_gain, ln2_bias=ln2_bias, ln3_gain=ln3_gain, ln3_bias=ln3_bias, w_up=w_up, up_bias=up_bias, w_down=w_down, down_bias=down_bias, ln4_gain=ln4_gain, ln4_bias=ln4_bias, row_grid=row_grid, pad_mask=pad_mask, cotangent=cotangent)


@jax.custom_vjp
def low(v):
    return lax.optimization_barrier(v.astype(jnp.bfloat16)).astype(jnp.float32)

@jax.custom_vjp
def low_back(v):
    return v

def low_keep(v):
    return (low(v), None)

def low_pass(kept, grad):
    return (grad,)

def back_keep(v):
    return (v, None)

def back_low(kept, grad):
    return (low(grad),)
low.defvjp(low_keep, low_pass)
low_back.defvjp(back_keep, back_low)
highest = lax.Precision.HIGHEST
epsilon = 1e-05
masked_score = -1e+30

def layer_norm(values, ln_gain, ln_bias):
    centred = values - lax.optimization_barrier(jnp.mean(values, -1, keepdims=True))
    inv_std = lax.rsqrt(lax.optimization_barrier(jnp.mean(centred * centred, -1, keepdims=True)) + epsilon)
    return centred * inv_std * ln_gain + ln_bias

def segment_ids(grid_row):
    position = jnp.arange(GTOK, dtype=jnp.int32)
    lengths = jnp.where(grid_row > 0, TEXT + grid_row * grid_row, 0).astype(jnp.int32)
    row_ends = jnp.cumsum(lengths).astype(jnp.int32)
    return lax.optimization_barrier(jnp.sum((position[:, None] >= row_ends[None, :]).astype(jnp.int32), axis=1)).astype(jnp.int32)

def permitted(seg_all, keep_all, row_start, row_count):
    key_pos = jnp.arange(seg_all.shape[0], dtype=jnp.int32)
    row_pos = row_start + jnp.arange(row_count, dtype=jnp.int32)
    seg_rows = lax.dynamic_slice_in_dim(seg_all, row_start, row_count, 0)
    same_row = seg_rows[:, None] == seg_all[None, :]
    causal = key_pos[None, :] <= row_pos[:, None]
    visible = (keep_all[None, :] == 1) | (key_pos[None, :] == row_pos[:, None])
    return same_row & causal & visible

def attention(query, keys_all, values_all, seg_all, keep_all):
    head_scale = HDIM ** (-0.5)

    def score_block(block_idx):
        row_start = block_idx * QBLK
        query_blk = lax.dynamic_slice_in_dim(query, row_start, QBLK, 0)
        raw_scores = low_back(jnp.einsum('qhd,khd->hqk', query_blk, keys_all, precision=highest))
        scores = jnp.where(permitted(seg_all, keep_all, row_start, QBLK)[None], raw_scores * head_scale, masked_score)
        row_top = lax.optimization_barrier(jnp.max(scores, -1, keepdims=True))
        exp_scores = jnp.exp(scores - row_top)
        probs = low(exp_scores / lax.optimization_barrier(jnp.sum(exp_scores, -1, keepdims=True)))
        return jnp.einsum('hqk,khd->qhd', probs, values_all, precision=highest)
    context = lax.map(jax.checkpoint(score_block), jnp.arange(GTOK // QBLK, dtype=jnp.int32))
    return context.reshape(GTOK, HEADS * HDIM)

def group_layer(resid_in, grid_row, keep_row, weights):
    ln1_gain, ln1_bias, w_qkv, qv_bias, w_out, out_bias, ln2_gain, ln2_bias, ln3_gain, ln3_bias, w_up, up_bias, w_down, down_bias, ln4_gain, ln4_bias = weights
    seg_all = segment_ids(grid_row)
    attn_input = low(layer_norm(resid_in, ln1_gain, ln1_bias))
    qkv_raw = jnp.dot(attn_input, w_qkv.reshape(D, 3 * D), precision=highest).reshape(GTOK, 3, D)
    query = low(low_back(qkv_raw[:, 0] + qv_bias[0])).reshape(GTOK, HEADS, HDIM)
    keys_all = low(low_back(qkv_raw[:, 1])).reshape(GTOK, HEADS, HDIM)
    values_all = low(low_back(qkv_raw[:, 2] + qv_bias[1])).reshape(GTOK, HEADS, HDIM)
    context = low(low_back(attention(query, keys_all, values_all, seg_all, keep_row)))
    branch_z = low_back(jnp.dot(context, w_out, precision=highest) + out_bias)
    resid_mid = resid_in + layer_norm(branch_z, ln2_gain, ln2_bias)
    ffn_input = low(layer_norm(resid_mid, ln3_gain, ln3_bias))
    hidden_pre = low_back(jnp.dot(ffn_input, w_up, precision=highest) + up_bias)
    hidden_act = low(jax.nn.gelu(hidden_pre, approximate=True))
    branch_f = low_back(jnp.dot(hidden_act, w_down, precision=highest) + down_bias)
    return resid_mid + layer_norm(branch_f, ln4_gain, ln4_bias)

def reference(tokens, ln1_gain, ln1_bias, w_qkv, qv_bias, w_out, out_bias, ln2_gain, ln2_bias, ln3_gain, ln3_bias, w_up, up_bias, w_down, down_bias, ln4_gain, ln4_bias, row_grid, pad_mask, cotangent):
    weights = jax.tree.map(lambda element: element.astype(jnp.float32), (ln1_gain, ln1_bias, w_qkv, qv_bias, w_out, out_bias, ln2_gain, ln2_bias, ln3_gain, ln3_bias, w_up, up_bias, w_down, down_bias, ln4_gain, ln4_bias))
    groups = tokens.shape[0] // GTOK
    keep_groups = pad_mask.reshape(groups, GTOK)

    def forward(resid_all, layer_weights):
        stacked = resid_all.reshape(groups, GTOK, D)

        def one_group(items):
            return jax.checkpoint(group_layer)(items[0], items[1], items[2], layer_weights)
        outputs = lax.map(one_group, (stacked, row_grid, keep_groups))
        return outputs.reshape(groups * GTOK, D)
    layer_result, pullback = jax.vjp(forward, tokens.astype(jnp.float32), weights)
    grad_input, grad_weights = pullback(cotangent.astype(jnp.float32))
    g_ln1_gain, g_ln1_bias, g_w_qkv, g_qv_bias, g_w_out, g_out_bias, g_ln2_gain, g_ln2_bias, g_ln3_gain, g_ln3_bias, g_w_up, g_up_bias, g_w_down, g_down_bias, g_ln4_gain, g_ln4_bias = grad_weights
    return (layer_result.astype(jnp.bfloat16), grad_input, g_ln1_gain, g_ln1_bias, g_w_qkv, g_qv_bias, g_w_out, g_out_bias, g_ln2_gain, g_ln2_bias, g_ln3_gain, g_ln3_bias, g_w_up, g_up_bias, g_w_down, g_down_bias, g_ln4_gain, g_ln4_bias)
```

```python
import functools

import jax
import jax.numpy as jnp
from jax import lax
from jax.experimental import pallas as pl
from jax.experimental.pallas import tpu as pltpu
from jax.sharding import PartitionSpec as P

HDIM = 64
TEXT = 64


epsilon = 1e-05
masked_score = -1e30


def norm_parts(values, ln_gain, ln_bias):
    centred = values - jnp.mean(values, -1, keepdims=True)
    inv_std = lax.rsqrt(jnp.mean(centred * centred, -1, keepdims=True) + epsilon)
    normed = centred * inv_std
    return (normed * ln_gain + ln_bias, normed, inv_std)


def norm_back(upstream, normed, inv_std, ln_gain):
    scaled = upstream * ln_gain
    return inv_std * (
        scaled
        - jnp.mean(scaled, -1, keepdims=True)
        - normed * jnp.mean(scaled * normed, -1, keepdims=True)
    )


def gelu_tanh(values):
    return jax.nn.gelu(values, approximate=True)


def contract_rows(left, right):
    return lax.dot_general(
        left, right, (((0,), (0,)), ((), ())), preferred_element_type=jnp.float32
    )


def contract_cols(left, right):
    return lax.dot_general(
        left, right, (((1,), (1,)), ((), ())), preferred_element_type=jnp.float32
    )


BQ=256; BK=256
F32=jnp.float32; BF16=jnp.bfloat16

def dot(a,b):
    return jnp.dot(a,b,preferred_element_type=F32)

def row_tables(grid_row, tokens):
    side=jnp.max(grid_row)
    length=TEXT+side*side
    rows=tokens//length
    used=rows*length
    position=jnp.arange(tokens,dtype=jnp.int32)
    seg=jnp.minimum(position//length,rows)
    blocks=tokens//BQ
    first=jnp.arange(blocks,dtype=jnp.int32)*BQ
    last=first+BQ-1
    start=jnp.where(first<used,(first//length)*length,first)
    low=start//BK
    diag=first//BK
    row_start=(last//length)*length
    clean=jnp.where(last<used,(row_start+TEXT+BK-1)//BK,diag)
    clean=jnp.clip(clean,low,diag)
    return seg,jnp.stack([low,clean,diag]).astype(jnp.int32)

def allowed(kseg_ref,qseg_ref,i,j):
    qs=qseg_ref[:,pl.ds(pl.multiple_of(i*BQ,BQ),BQ)]
    ks=kseg_ref[pl.ds(pl.multiple_of(j*BK,BK),BK),:]
    ik=j*BK+lax.broadcasted_iota(jnp.int32,(BK,BQ),0)
    iq=i*BQ+lax.broadcasted_iota(jnp.int32,(BK,BQ),1)
    return ((ks==qs)&(ik<=iq))|(ik==iq)

def sweep(tab_ref,i,step,carry):
    low,clean,diag=tab_ref[0,i],tab_ref[1,i],tab_ref[2,i]
    carry=lax.fori_loop(low,clean,functools.partial(step,True),carry)
    carry=lax.fori_loop(clean,diag,functools.partial(step,False),carry)
    return lax.fori_loop(diag,diag+BQ//BK if BQ>BK else diag+1,functools.partial(step,True),carry)

def forward_kernel(tab_ref,kseg_ref,qseg_ref,q_ref,k_ref,v_ref,o_ref,lse_ref,kx,vx):
    tokens=q_ref.shape[1]
    lane=lax.broadcasted_iota(jnp.int32,(BK,128),1)
    def prepare(c,_):
        at=pl.ds(pl.multiple_of(c*BK,BK),BK)
        kt=k_ref[:,at].astype(F32).T
        kx[0,at,:]=jnp.where(lane<HDIM,kt,0.0).astype(BF16)
        kx[1,at,:]=jnp.where(lane<HDIM,0.0,kt).astype(BF16)
        return 0
    lax.fori_loop(0,tokens//BK,prepare,0)
    for h in range(2):
        vx[h,:HDIM,:]=v_ref[h*HDIM:(h+1)*HDIM,:]
        vx[h,HDIM:,:]=jnp.ones((16,tokens),BF16)
    def block(i,_):
        cols=pl.ds(pl.multiple_of(i*BQ,BQ),BQ)
        qb=q_ref[:,cols]
        def step(masked,j,carry):
            at=pl.ds(pl.multiple_of(j*BK,BK),BK)
            if masked: ok=allowed(kseg_ref,qseg_ref,i,j)
            out=[]
            for h in range(2):
                top,acc=carry[h]
                s=dot(kx[h,at,:],qb)
                if masked: s=jnp.where(ok,s,masked_score)
                new=jnp.maximum(top,jnp.max(s,axis=0,keepdims=True))
                p=jnp.exp(s-new).astype(BF16)
                acc=acc*jnp.exp(top-new)+dot(vx[h,:,at],p)
                out.append((new,acc))
            return tuple(out)
        init=tuple((jnp.full((1,BQ),masked_score,F32),jnp.zeros((HDIM+16,BQ),F32)) for _ in range(2))
        res=sweep(tab_ref,i,step,init)
        for h in range(2):
            top,acc=res[h]
            total=acc[HDIM:HDIM+1,:]
            o_ref[h*HDIM:(h+1)*HDIM,cols]=(acc[:HDIM,:]/total).astype(BF16)
            lse_ref[0,h:h+1,cols]=top+jnp.log(total)
        return 0
    lax.fori_loop(0,tokens//BQ,block,0)

def parts3(x):
    hi=x.astype(BF16); r=x-hi.astype(F32)
    mid=r.astype(BF16); lo=(r-mid.astype(F32)).astype(BF16)
    return hi,mid,lo

def backward_kernel(tab_ref,kseg_ref,qseg_ref,q_ref,k_ref,v_ref,o_ref,do_ref,lse_ref,out_ref,
                    kx,vx,qx,dox,qt,dot_,dk,dv):
    tokens=q_ref.shape[1]
    lane=lax.broadcasted_iota(jnp.int32,(BK,128),1)
    sub=lax.broadcasted_iota(jnp.int32,(HDIM,BK),0)
    one0=jnp.where((lane>=HDIM)&(lane<HDIM+3),1.0,0.0)
    one1=jnp.where(lane<3,1.0,0.0)
    def extra(x):
        hi,mid,lo=(e.astype(F32) for e in parts3(x))
        z=jnp.where(sub==0,hi,jnp.where(sub==1,mid,jnp.where(sub==2,lo,0.0)))
        return z.astype(BF16)
    def prepare(c,_):
        at=pl.ds(pl.multiple_of(c*BK,BK),BK)
        kt=k_ref[:,at].astype(F32).T
        kx[0,at,:]=jnp.where(lane<HDIM,kt,one0).astype(BF16)
        kx[1,at,:]=jnp.where(lane<HDIM,one1,kt).astype(BF16)
        vt=v_ref[:,at].astype(F32).T
        vx[0,at,:]=jnp.where(lane<HDIM,vt,one0).astype(BF16)
        vx[1,at,:]=jnp.where(lane<HDIM,one1,vt).astype(BF16)
        q=q_ref[:,at]
        qtt=q.astype(F32).T
        qt[0,at,:]=jnp.where(lane<HDIM,qtt,0.0).astype(BF16)
        qt[1,at,:]=jnp.where(lane<HDIM,0.0,qtt).astype(BF16)
        do=do_ref[:,at]
        dof=do.astype(F32)
        dtt=dof.T
        dot_[0,at,:]=jnp.where(lane<HDIM,dtt,0.0).astype(BF16)
        dot_[1,at,:]=jnp.where(lane<HDIM,0.0,dtt).astype(BF16)
        prod=dof*o_ref[:,at].astype(F32)
        d0=jnp.sum(prod[:HDIM],axis=0,keepdims=True)
        d1=jnp.sum(prod[HDIM:],axis=0,keepdims=True)
        qx[0,:HDIM,at]=q[:HDIM]
        qx[0,HDIM:,at]=extra(-lse_ref[0,0:1,at])
        qx[1,HDIM:,at]=q[HDIM:]
        qx[1,:HDIM,at]=extra(-lse_ref[0,1:2,at])
        dox[0,:HDIM,at]=do[:HDIM]
        dox[0,HDIM:,at]=extra(-d0)
        dox[1,HDIM:,at]=do[HDIM:]
        dox[1,:HDIM,at]=extra(-d1)
        dk[at,:]=jnp.zeros((BK,128),F32)
        dv[at,:]=jnp.zeros((BK,128),F32)
        return 0
    lax.fori_loop(0,tokens//BK,prepare,0)
    def block(i,_):
        cols=pl.ds(pl.multiple_of(i*BQ,BQ),BQ)
        def step(masked,j,carry):
            at=pl.ds(pl.multiple_of(j*BK,BK),BK)
            if masked: ok=allowed(kseg_ref,qseg_ref,i,j)
            new=[]; dvs=dv[at,:]; dks=dk[at,:]
            for h in range(2):
                s=dot(kx[h,at,:],qx[h,:,cols])
                if masked: s=jnp.where(ok,s,masked_score)
                p=jnp.exp(s)
                dp=dot(vx[h,at,:],dox[h,:,cols])
                ds=(p*dp).astype(BF16)
                dvs=dvs+dot(p.astype(BF16),dot_[h,cols,:])
                dks=dks+dot(ds,qt[h,cols,:])
                new.append(carry[h]+dot(k_ref[h*HDIM:(h+1)*HDIM,at],ds))
            dv[at,:]=dvs
            dk[at,:]=dks
            return tuple(new)
        init=tuple(jnp.zeros((HDIM,BQ),F32) for _ in range(2))
        res=sweep(tab_ref,i,step,init)
        for h in range(2):
            out_ref[0,h*HDIM:(h+1)*HDIM,cols]=(res[h]*(HDIM**-0.5)).astype(BF16)
        return 0
    lax.fori_loop(0,tokens//BQ,block,0)
    def finish(c,_):
        at=pl.ds(pl.multiple_of(c*BK,BK),BK)
        out_ref[1,:,at]=dk[at,:].T.astype(BF16)
        out_ref[2,:,at]=dv[at,:].T.astype(BF16)
        return 0
    lax.fori_loop(0,tokens//BK,finish,0)

PAIR=2*HDIM
def specs(tokens,heads):
    pairs=heads//2
    seg_specs=[pl.BlockSpec((tokens,1),lambda g,t:(0,0)),pl.BlockSpec((1,tokens),lambda g,t:(0,0))]
    def part(c): return pl.BlockSpec((PAIR,tokens),lambda g,t,c=c:(c*pairs+g,0))
    return pairs,seg_specs,part

def attend_forward(qkv,seg,keep,tables):
    tokens=qkv.shape[1]; heads=qkv.shape[0]//(3*HDIM)
    pairs,seg_specs,part=specs(tokens,heads)
    kseg=jnp.where(keep==1,seg,-1)[:,None]
    return pl.pallas_call(forward_kernel,
        grid_spec=pltpu.PrefetchScalarGridSpec(num_scalar_prefetch=1,grid=(pairs,),
            in_specs=seg_specs+[part(0),part(1),part(2)],
            out_specs=[part(0),pl.BlockSpec((1,2,tokens),lambda g,t:(g,0,0))],
            scratch_shapes=[pltpu.VMEM((2,tokens,128),BF16),pltpu.VMEM((2,HDIM+16,tokens),BF16)]),
        out_shape=[jax.ShapeDtypeStruct((heads*HDIM,tokens),BF16),jax.ShapeDtypeStruct((pairs,2,tokens),F32)],
        compiler_params=pltpu.CompilerParams(vmem_limit_bytes=48*2**20),
        name="attend_forward",
    )(tables,kseg,seg[None,:],qkv,qkv,qkv)

def attend_backward(qkv,context,grad_ctx,lse,seg,keep,tables):
    tokens=qkv.shape[1]; heads=qkv.shape[0]//(3*HDIM)
    pairs,seg_specs,part=specs(tokens,heads)
    kseg=jnp.where(keep==1,seg,-1)[:,None]
    out=pl.pallas_call(backward_kernel,
        grid_spec=pltpu.PrefetchScalarGridSpec(num_scalar_prefetch=1,grid=(pairs,),
            in_specs=seg_specs+[part(0),part(1),part(2),part(0),part(0),pl.BlockSpec((1,2,tokens),lambda g,t:(g,0,0))],
            out_specs=pl.BlockSpec((3,PAIR,tokens),lambda g,t:(0,g,0)),
            scratch_shapes=[pltpu.VMEM((2,tokens,128),BF16),pltpu.VMEM((2,tokens,128),BF16),
                pltpu.VMEM((2,128,tokens),BF16),pltpu.VMEM((2,128,tokens),BF16),
                pltpu.VMEM((2,tokens,128),BF16),pltpu.VMEM((2,tokens,128),BF16),
                pltpu.VMEM((tokens,128),F32),pltpu.VMEM((tokens,128),F32)]),
        out_shape=jax.ShapeDtypeStruct((3,heads*HDIM,tokens),BF16),
        compiler_params=pltpu.CompilerParams(vmem_limit_bytes=48*2**20),
        name="attend_backward",
    )(tables,kseg,seg[None,:],qkv,qkv,qkv,context,grad_ctx,lse)
    return out.reshape(3*heads*HDIM,tokens)


def body(
    tokens,
    ln1_gain,
    ln1_bias,
    w_qkv,
    qv_bias,
    w_out,
    out_bias,
    ln2_gain,
    ln2_bias,
    ln3_gain,
    ln3_bias,
    w_up,
    up_bias,
    w_down,
    down_bias,
    ln4_gain,
    ln4_bias,
    row_grid,
    pad_mask,
    cotangent,
):
    model_dim = tokens.shape[1]
    group_rows = pad_mask.shape[0]
    local_width = w_qkv.shape[2]
    seg_all, tables = row_tables(row_grid[0], group_rows)
    flat_qkv = w_qkv.reshape(model_dim, 3 * local_width)
    resid_in = tokens.astype(jnp.float32)
    norm1_out, normed1, inv1 = norm_parts(resid_in, ln1_gain, ln1_bias)
    attn_full = lax.all_gather(norm1_out.astype(jnp.bfloat16), "mp", axis=0, tiled=True)
    qkv_raw = lax.dot_general(
        flat_qkv, attn_full, (((0,), (1,)), ((), ())), preferred_element_type=jnp.float32
    ).reshape(3, local_width, group_rows)
    query = (qkv_raw[0] + qv_bias[0][:, None]).astype(jnp.bfloat16) * HDIM ** (-0.5)
    values_all = (qkv_raw[2] + qv_bias[1][:, None]).astype(jnp.bfloat16)
    qkv = jnp.concatenate([query, qkv_raw[1].astype(jnp.bfloat16), values_all], 0)
    context, log_total = attend_forward(qkv, seg_all, pad_mask, tables)
    proj_sum = lax.psum_scatter(
        contract_rows(context, w_out).astype(jnp.bfloat16),
        "mp",
        scatter_dimension=0,
        tiled=True,
    ).astype(jnp.float32)
    branch_z = proj_sum + out_bias
    norm2_out, normed2, inv2 = norm_parts(branch_z, ln2_gain, ln2_bias)
    resid_mid = resid_in + norm2_out
    norm3_out, normed3, inv3 = norm_parts(resid_mid, ln3_gain, ln3_bias)
    ffn_full = lax.all_gather(norm3_out.astype(jnp.bfloat16), "mp", axis=0, tiled=True)
    hidden_pre = jnp.dot(ffn_full, w_up, preferred_element_type=jnp.float32) + up_bias
    hidden_act = gelu_tanh(hidden_pre).astype(jnp.bfloat16)
    branch_f = (
        lax.psum_scatter(
            jnp.dot(hidden_act, w_down, preferred_element_type=jnp.float32).astype(jnp.bfloat16),
            "mp",
            scatter_dimension=0,
            tiled=True,
        ).astype(jnp.float32)
        + down_bias
    )
    norm4_out, normed4, inv4 = norm_parts(branch_f, ln4_gain, ln4_bias)
    layer_out = (resid_mid + norm4_out).astype(jnp.bfloat16)
    upstream = cotangent.astype(jnp.float32)
    grad_f = norm_back(upstream, normed4, inv4, ln4_gain).astype(jnp.bfloat16)
    grad_f_full = lax.all_gather(grad_f, "mp", axis=0, tiled=True)
    g_w_down = contract_rows(hidden_act, grad_f_full)
    grad_act = contract_cols(grad_f_full, w_down)
    grad_pre = jax.vjp(gelu_tanh, hidden_pre)[1](grad_act)[0].astype(jnp.bfloat16)
    g_up_bias = jnp.sum(grad_pre.astype(jnp.float32), 0)
    g_w_up = contract_rows(ffn_full, grad_pre)
    grad_a3 = lax.psum_scatter(
        contract_cols(grad_pre, w_up).astype(jnp.bfloat16), "mp", scatter_dimension=0, tiled=True
    ).astype(jnp.float32)
    grad_mid = upstream + norm_back(grad_a3, normed3, inv3, ln3_gain)
    grad_z = norm_back(grad_mid, normed2, inv2, ln2_gain).astype(jnp.bfloat16)
    grad_z_full = lax.all_gather(grad_z, "mp", axis=0, tiled=True)
    g_w_out = jnp.dot(context, grad_z_full, preferred_element_type=jnp.float32)
    grad_ctx = contract_cols(w_out, grad_z_full).astype(jnp.bfloat16)
    grad_qkv = attend_backward(
        qkv, context, grad_ctx, log_total, seg_all, pad_mask, tables
    )
    sums = jnp.sum(grad_qkv.astype(jnp.float32).reshape(3, local_width, group_rows), 2)
    g_qv_bias = jnp.stack([sums[0], sums[2]], 0)
    g_w_qkv = lax.dot_general(
        attn_full, grad_qkv, (((0,), (1,)), ((), ())), preferred_element_type=jnp.float32
    ).reshape(model_dim, 3, local_width)
    grad_a1 = lax.psum_scatter(
        lax.dot_general(
            grad_qkv, flat_qkv, (((0,), (1,)), ((), ())), preferred_element_type=jnp.float32
        ).astype(jnp.bfloat16),
        "mp",
        scatter_dimension=0,
        tiled=True,
    ).astype(jnp.float32)
    grad_input = grad_mid + norm_back(grad_a1, normed1, inv1, ln1_gain)
    norm_terms = jnp.stack(
        [
            jnp.sum(grad_a1 * normed1, 0),
            jnp.sum(grad_a1, 0),
            jnp.sum(grad_z.astype(jnp.float32), 0),
            jnp.sum(grad_mid * normed2, 0),
            jnp.sum(grad_mid, 0),
            jnp.sum(grad_a3 * normed3, 0),
            jnp.sum(grad_a3, 0),
            jnp.sum(grad_f.astype(jnp.float32), 0),
            jnp.sum(upstream * normed4, 0),
            jnp.sum(upstream, 0),
        ],
        0,
    )
    weight_grads = (
        lax.psum(g_w_qkv.astype(jnp.bfloat16), "dp").astype(jnp.float32),
        lax.psum(g_qv_bias.astype(jnp.bfloat16), "dp").astype(jnp.float32),
        lax.psum(g_w_out.astype(jnp.bfloat16), "dp").astype(jnp.float32),
        lax.psum(g_w_up.astype(jnp.bfloat16), "dp").astype(jnp.float32),
        lax.psum(g_up_bias.astype(jnp.bfloat16), "dp").astype(jnp.float32),
        lax.psum(g_w_down.astype(jnp.bfloat16), "dp").astype(jnp.float32),
    )
    norm_grads = lax.psum(norm_terms, ("dp", "mp"))
    return (
        layer_out,
        grad_input,
        norm_grads[0],
        norm_grads[1],
        weight_grads[0],
        weight_grads[1],
        weight_grads[2],
        norm_grads[2],
        norm_grads[3],
        norm_grads[4],
        norm_grads[5],
        norm_grads[6],
        weight_grads[3],
        weight_grads[4],
        weight_grads[5],
        norm_grads[7],
        norm_grads[8],
        norm_grads[9],
    )


def solution(mesh):
    in_specs = (
        P(("dp", "mp"), None),
        P(),
        P(),
        P(None, None, "mp"),
        P(None, "mp"),
        P("mp", None),
        P(),
        P(),
        P(),
        P(),
        P(),
        P(None, "mp"),
        P("mp"),
        P("mp", None),
        P(),
        P(),
        P(),
        P("dp", None),
        P("dp"),
        P(("dp", "mp"), None),
    )
    out_specs = (
        P(("dp", "mp"), None),
        P(("dp", "mp"), None),
        P(),
        P(),
        P(None, None, "mp"),
        P(None, "mp"),
        P("mp", None),
        P(),
        P(),
        P(),
        P(),
        P(),
        P(None, "mp"),
        P("mp"),
        P("mp", None),
        P(),
        P(),
        P(),
    )
    return jax.shard_map(body, mesh=mesh, in_specs=in_specs, out_specs=out_specs, check_vma=False)
```

```python
import functools

import jax
import jax.numpy as jnp
from jax import lax
from jax.experimental import pallas as pl
from jax.experimental.pallas import tpu as pltpu
from jax.sharding import PartitionSpec as P

HDIM = 64
TEXT = 64


epsilon = 1e-05
masked_score = -1e30


def norm_parts(values, ln_gain, ln_bias):
    centred = values - jnp.mean(values, -1, keepdims=True)
    inv_std = lax.rsqrt(jnp.mean(centred * centred, -1, keepdims=True) + epsilon)
    normed = centred * inv_std
    return (normed * ln_gain + ln_bias, normed, inv_std)


def norm_back(upstream, normed, inv_std, ln_gain):
    scaled = upstream * ln_gain
    return inv_std * (
        scaled
        - jnp.mean(scaled, -1, keepdims=True)
        - normed * jnp.mean(scaled * normed, -1, keepdims=True)
    )


def contract_rows(left, right):
    return lax.dot_general(
        left, right, (((0,), (0,)), ((), ())), preferred_element_type=jnp.float32
    )


def contract_cols(left, right):
    return lax.dot_general(
        left, right, (((1,), (1,)), ((), ())), preferred_element_type=jnp.float32
    )


BQ = 256
BK = 256
PAIR = 2 * HDIM
F32 = jnp.float32
BF16 = jnp.bfloat16


def matmul(left, right):
    return jnp.dot(left, right, preferred_element_type=F32)


def row_tables(grid_row, tokens, turn):
    side = jnp.max(grid_row)
    length = TEXT + side * side
    rows = tokens // length
    used = rows * length
    position = jnp.arange(tokens, dtype=jnp.int32)
    seg = jnp.minimum(position // length, rows)
    blocks = tokens // BQ
    first = jnp.arange(blocks, dtype=jnp.int32) * BQ
    last = first + BQ - 1
    start = jnp.where(first < used, (first // length) * length, first)
    low = start // BK
    diag = first // BK
    row_start = (last // length) * length
    clean = jnp.where(last < used, (row_start + TEXT + BK - 1) // BK, diag)
    clean = jnp.clip(clean, low, diag)
    turns = jnp.full((blocks,), turn, jnp.int32)
    return seg, jnp.stack([low, clean, diag, turns]).astype(jnp.int32)


def allowed(kseg_ref, qseg_ref, i, j):
    qs = qseg_ref[:, pl.ds(pl.multiple_of(i * BQ, BQ), BQ)]
    ks = kseg_ref[pl.ds(pl.multiple_of(j * BK, BK), BK), :]
    ik = j * BK + lax.broadcasted_iota(jnp.int32, (BK, BQ), 0)
    iq = i * BQ + lax.broadcasted_iota(jnp.int32, (BK, BQ), 1)
    return ((ks == qs) & (ik <= iq)) | (ik == iq)


def sweep(tab_ref, i, step, carry):
    low, clean, diag = tab_ref[0, i], tab_ref[1, i], tab_ref[2, i]
    carry = lax.fori_loop(low, clean, functools.partial(step, True), carry)
    carry = lax.fori_loop(clean, diag, functools.partial(step, False), carry)
    return step(True, diag, carry)


def each_block(tab_ref, parts, width, work):
    blocks = width // BQ
    count = blocks * parts
    for part in range(parts):

        def one(c, _, part=part):
            whole = lax.rem(tab_ref[3, 0] + part * blocks + c, count)
            work(
                part,
                pl.ds(pl.multiple_of(c * BQ, BQ), BQ),
                pl.ds(pl.multiple_of(whole * BQ, BQ), BQ),
            )
            return 0

        lax.fori_loop(0, blocks, one, 0)


def forward_kernel(parts, tab_ref, kseg_ref, qseg_ref, *refs):
    q_refs, k_refs, v_refs, o_refs = (refs[n * parts : (n + 1) * parts] for n in range(4))
    lse_ref, kx, vx, qx, ox = refs[4 * parts :]
    tokens = qx.shape[1]
    width = tokens // parts
    lane = lax.broadcasted_iota(jnp.int32, (BK, 128), 1)

    def prepare(part, here, there):
        kt = k_refs[part][:, here].astype(F32).T
        kx[0, there, :] = jnp.where(lane < HDIM, kt, 0.0).astype(BF16)
        kx[1, there, :] = jnp.where(lane < HDIM, 0.0, kt).astype(BF16)
        qx[:, there] = q_refs[part][:, here]
        for h in range(2):
            vx[h, :HDIM, there] = v_refs[part][h * HDIM : (h + 1) * HDIM, here]
            vx[h, HDIM:, there] = jnp.ones((16, BQ), BF16)

    each_block(tab_ref, parts, width, prepare)

    def block(i, _):
        cols = pl.ds(pl.multiple_of(i * BQ, BQ), BQ)
        qb = qx[:, cols]

        def step(masked, j, carry):
            at = pl.ds(pl.multiple_of(j * BK, BK), BK)
            if masked:
                ok = allowed(kseg_ref, qseg_ref, i, j)
            out = []
            for h in range(2):
                top, acc = carry[h]
                s = matmul(kx[h, at, :], qb)
                if masked:
                    s = jnp.where(ok, s, masked_score)
                new = jnp.maximum(top, jnp.max(s, axis=0, keepdims=True))
                p = jnp.exp(s - new).astype(BF16)
                acc = acc * jnp.exp(top - new) + matmul(vx[h, :, at], p)
                out.append((new, acc))
            return tuple(out)

        init = tuple(
            (jnp.full((1, BQ), masked_score, F32), jnp.zeros((HDIM + 16, BQ), F32))
            for _ in range(2)
        )
        res = sweep(tab_ref, i, step, init)
        for h in range(2):
            top, acc = res[h]
            total = acc[HDIM : HDIM + 1, :]
            ox[h * HDIM : (h + 1) * HDIM, cols] = (acc[:HDIM, :] / total).astype(BF16)
            lse_ref[0, h : h + 1, cols] = top + jnp.log(total)
        return 0

    lax.fori_loop(0, tokens // BQ, block, 0)

    def finish(part, here, there):
        o_refs[part][:, here] = ox[:, there]

    each_block(tab_ref, parts, width, finish)


def three_parts(x):
    high = x.astype(BF16)
    rest = x - high.astype(F32)
    middle = rest.astype(BF16)
    return high, middle, (rest - middle.astype(F32)).astype(BF16)


def backward_kernel(parts, tab_ref, kseg_ref, qseg_ref, *refs):
    q_refs, k_refs, v_refs, o_refs, do_refs = (
        refs[n * parts : (n + 1) * parts] for n in range(5)
    )
    lse_ref = refs[5 * parts]
    out_refs = refs[5 * parts + 1 : 6 * parts + 1]
    kx, vx, kt, qx, dox, qt, dot, dq, dk, dv = refs[6 * parts + 1 :]
    tokens = kt.shape[1]
    width = tokens // parts
    lane = lax.broadcasted_iota(jnp.int32, (BK, 128), 1)
    sub = lax.broadcasted_iota(jnp.int32, (HDIM, BK), 0)
    one0 = jnp.where((lane >= HDIM) & (lane < HDIM + 3), 1.0, 0.0)
    one1 = jnp.where(lane < 3, 1.0, 0.0)

    def extra(x):
        high, middle, low = (e.astype(F32) for e in three_parts(x))
        rows = jnp.where(
            sub == 0, high, jnp.where(sub == 1, middle, jnp.where(sub == 2, low, 0.0))
        )
        return rows.astype(BF16)

    def prepare(part, here, there):
        k = k_refs[part][:, here]
        kt[:, there] = k
        turned = k.astype(F32).T
        kx[0, there, :] = jnp.where(lane < HDIM, turned, one0).astype(BF16)
        kx[1, there, :] = jnp.where(lane < HDIM, one1, turned).astype(BF16)
        turned = v_refs[part][:, here].astype(F32).T
        vx[0, there, :] = jnp.where(lane < HDIM, turned, one0).astype(BF16)
        vx[1, there, :] = jnp.where(lane < HDIM, one1, turned).astype(BF16)
        q = q_refs[part][:, here]
        turned = q.astype(F32).T
        qt[0, there, :] = jnp.where(lane < HDIM, turned, 0.0).astype(BF16)
        qt[1, there, :] = jnp.where(lane < HDIM, 0.0, turned).astype(BF16)
        do = do_refs[part][:, here]
        wide = do.astype(F32)
        turned = wide.T
        dot[0, there, :] = jnp.where(lane < HDIM, turned, 0.0).astype(BF16)
        dot[1, there, :] = jnp.where(lane < HDIM, 0.0, turned).astype(BF16)
        prod = wide * o_refs[part][:, here].astype(F32)
        inner0 = jnp.sum(prod[:HDIM], axis=0, keepdims=True)
        inner1 = jnp.sum(prod[HDIM:], axis=0, keepdims=True)
        qx[0, :HDIM, there] = q[:HDIM]
        qx[0, HDIM:, there] = extra(-lse_ref[0, 0:1, there])
        qx[1, HDIM:, there] = q[HDIM:]
        qx[1, :HDIM, there] = extra(-lse_ref[0, 1:2, there])
        dox[0, :HDIM, there] = do[:HDIM]
        dox[0, HDIM:, there] = extra(-inner0)
        dox[1, HDIM:, there] = do[HDIM:]
        dox[1, :HDIM, there] = extra(-inner1)
        dk[there, :] = jnp.zeros((BK, 128), F32)
        dv[there, :] = jnp.zeros((BK, 128), F32)

    each_block(tab_ref, parts, width, prepare)

    def block(i, _):
        cols = pl.ds(pl.multiple_of(i * BQ, BQ), BQ)

        def step(masked, j, carry):
            at = pl.ds(pl.multiple_of(j * BK, BK), BK)
            if masked:
                ok = allowed(kseg_ref, qseg_ref, i, j)
            new = []
            dvs = dv[at, :]
            dks = dk[at, :]
            for h in range(2):
                s = matmul(kx[h, at, :], qx[h, :, cols])
                if masked:
                    s = jnp.where(ok, s, masked_score)
                p = jnp.exp(s)
                dp = matmul(vx[h, at, :], dox[h, :, cols])
                ds = (p * dp).astype(BF16)
                dvs = dvs + matmul(p.astype(BF16), dot[h, cols, :])
                dks = dks + matmul(ds, qt[h, cols, :])
                new.append(carry[h] + matmul(kt[h * HDIM : (h + 1) * HDIM, at], ds))
            dv[at, :] = dvs
            dk[at, :] = dks
            return tuple(new)

        init = tuple(jnp.zeros((HDIM, BQ), F32) for _ in range(2))
        res = sweep(tab_ref, i, step, init)
        for h in range(2):
            dq[h * HDIM : (h + 1) * HDIM, cols] = (res[h] * (HDIM**-0.5)).astype(BF16)
        return 0

    lax.fori_loop(0, tokens // BQ, block, 0)

    def finish(part, here, there):
        out_refs[part][0, :, here] = dq[:, there]
        out_refs[part][1, :, here] = dk[there, :].T.astype(BF16)
        out_refs[part][2, :, here] = dv[there, :].T.astype(BF16)

    each_block(tab_ref, parts, width, finish)


def rows_of(pairs, which):
    return lambda g, t: (which * pairs + g, 0)


def attend_specs(qkv_parts):
    parts = len(qkv_parts)
    width = qkv_parts[0].shape[1]
    tokens = parts * width
    heads = qkv_parts[0].shape[0] // (3 * HDIM)
    pairs = heads // 2
    seg_specs = [
        pl.BlockSpec((tokens, 1), lambda g, t: (0, 0)),
        pl.BlockSpec((1, tokens), lambda g, t: (0, 0)),
    ]
    per_part = [[pl.BlockSpec((PAIR, width), rows_of(pairs, c))] * parts for c in range(3)]
    lse_spec = pl.BlockSpec((1, 2, tokens), lambda g, t: (g, 0, 0))
    return parts, width, tokens, heads, pairs, seg_specs, per_part, lse_spec


def attend_forward(qkv_parts, seg, keep, tables):
    parts, width, tokens, heads, pairs, seg_specs, per_part, lse_spec = attend_specs(qkv_parts)
    kseg = jnp.where(keep == 1, seg, -1)[:, None]
    *context, log_total = pl.pallas_call(
        functools.partial(forward_kernel, parts),
        grid_spec=pltpu.PrefetchScalarGridSpec(
            num_scalar_prefetch=1,
            grid=(pairs,),
            in_specs=seg_specs + per_part[0] + per_part[1] + per_part[2],
            out_specs=per_part[0] + [lse_spec],
            scratch_shapes=[
                pltpu.VMEM((2, tokens, 128), BF16),
                pltpu.VMEM((2, HDIM + 16, tokens), BF16),
                pltpu.VMEM((PAIR, tokens), BF16),
                pltpu.VMEM((PAIR, tokens), BF16),
            ],
        ),
        out_shape=[jax.ShapeDtypeStruct((heads * HDIM, width), BF16)] * parts
        + [jax.ShapeDtypeStruct((pairs, 2, tokens), F32)],
        compiler_params=pltpu.CompilerParams(vmem_limit_bytes=40 * 2**20),
        cost_estimate=pl.CostEstimate(
            flops=3000 * tokens * tokens * heads, bytes_accessed=2**23, transcendentals=0
        ),
        name="attend_forward",
    )(tables, kseg, seg[None, :], *qkv_parts, *qkv_parts, *qkv_parts)
    return context, log_total


def attend_backward(qkv_parts, context, grad_ctx, lse, seg, keep, tables):
    parts, width, tokens, heads, pairs, seg_specs, per_part, lse_spec = attend_specs(qkv_parts)
    kseg = jnp.where(keep == 1, seg, -1)[:, None]
    out = pl.pallas_call(
        functools.partial(backward_kernel, parts),
        grid_spec=pltpu.PrefetchScalarGridSpec(
            num_scalar_prefetch=1,
            grid=(pairs,),
            in_specs=seg_specs
            + per_part[0]
            + per_part[1]
            + per_part[2]
            + per_part[0]
            + per_part[0]
            + [lse_spec],
            out_specs=[pl.BlockSpec((3, PAIR, width), lambda g, t: (0, g, 0))] * parts,
            scratch_shapes=[
                pltpu.VMEM((2, tokens, 128), BF16),
                pltpu.VMEM((2, tokens, 128), BF16),
                pltpu.VMEM((PAIR, tokens), BF16),
                pltpu.VMEM((2, 128, tokens), BF16),
                pltpu.VMEM((2, 128, tokens), BF16),
                pltpu.VMEM((2, tokens, 128), BF16),
                pltpu.VMEM((2, tokens, 128), BF16),
                pltpu.VMEM((PAIR, tokens), BF16),
                pltpu.VMEM((tokens, 128), F32),
                pltpu.VMEM((tokens, 128), F32),
            ],
        ),
        out_shape=[jax.ShapeDtypeStruct((3, heads * HDIM, width), BF16)] * parts,
        compiler_params=pltpu.CompilerParams(vmem_limit_bytes=48 * 2**20),
        cost_estimate=pl.CostEstimate(
            flops=3000 * tokens * tokens * heads, bytes_accessed=2**24, transcendentals=0
        ),
        name="attend_backward",
    )(
        tables,
        kseg,
        seg[None, :],
        *qkv_parts,
        *qkv_parts,
        *qkv_parts,
        *context,
        *grad_ctx,
        lse,
    )
    return [part.reshape(3 * heads * HDIM, width) for part in out]


def gelu_and_slope(u):
    root = 0.7978845608028654
    square = u * u
    t = jnp.tanh(root * u * (1.0 + 0.044715 * square))
    half = 0.5 * (1.0 + t)
    slope = half + 0.5 * u * (1.0 - t * t) * (root * (1.0 + 0.134145 * square))
    return u * half, slope


def after(value, *others):
    return lax.optimization_barrier((value, *others))[0]


class Layout:
    def __init__(self, mesh):
        self.dp, self.n = mesh.shape["dp"], mesh.shape["mp"]
        self.pairs = self.dp // 2
        self.axes = ("dp", "mp")

    def device(self, pair, core, m):
        return (2 * pair + core) * self.n + m

    def at_rank(self, pair, group, rank):
        return self.device(pair, rank % 2, group * (self.n // 2) + rank // 2)

    def each(self):
        for pair in range(self.pairs):
            for group in range(2):
                for rank in range(self.n):
                    yield pair, group, rank

    def moved(self, value, moves):
        there = lax.ppermute(value, self.axes, [(a, b) for a, b in moves if a != b])
        core, m = lax.axis_index("dp") % 2, lax.axis_index("mp")
        stays = (m // (self.n // 2) == core) & ((m % (self.n // 2)) * 2 + core == m)
        return jnp.where(stays, value, there)

    def regroup(self, value):
        moves = [(self.device(p, g, r), self.at_rank(p, g, r)) for p, g, r in self.each()]
        return self.moved(value, moves)

    def give_back(self, value):
        moves = [(self.at_rank(p, g, r), self.device(p, g, r)) for p, g, r in self.each()]
        return self.moved(value, moves)

    def to_rank(self, value, ahead):
        moves = [
            (self.at_rank(p, g, r), self.at_rank(p, g, (r + ahead) % self.n))
            for p, g, r in self.each()
        ]
        return lax.ppermute(value, self.axes, moves)

    def rank(self):
        core = lax.axis_index("dp") % 2
        return (lax.axis_index("mp") % (self.n // 2)) * 2 + core

    def gather(self, mine):
        return [mine] + [self.to_rank(mine, self.n - k) for k in range(1, self.n)]

    def scatter_sum(self, shares):
        total = shares[0].astype(jnp.float32)
        for k in range(1, self.n):
            total = total + self.to_rank(shares[k].astype(jnp.bfloat16), k).astype(jnp.float32)
        return total

    def sum_all(self, value):
        devices = self.dp * self.n
        step = 1
        while step < devices:
            value = value + lax.ppermute(value, self.axes, [(i, i ^ step) for i in range(devices)])
            step *= 2
        return value

    def weight_sum(self, grad, turn):
        order = [(i + turn) % self.dp for i in range(self.dp)]
        grad = self.give_back(grad.astype(jnp.bfloat16))
        return lax.psum(grad, "dp", axis_index_groups=[order]).astype(jnp.float32)


def for_kernel(columns, rank):
    width = columns[0].shape[1]
    if width % BQ == 0:
        return columns, rank * (width // BQ)
    return [jnp.roll(jnp.concatenate(columns, 1), rank * width, 1)], 0


def from_kernel(columns, rank, shares):
    if len(columns) == shares:
        return columns
    width = columns[0].shape[1] // shares
    return jnp.split(jnp.roll(columns[0], -rank * width, 1), shares, 1)


def cols_by_cols(left, right):
    return lax.dot_general(
        left, right, (((0,), (1,)), ((), ())), preferred_element_type=jnp.float32
    )


def total(terms):
    return functools.reduce(jnp.add, terms)


def body(
    layout,
    tokens,
    ln1_gain,
    ln1_bias,
    w_qkv,
    qv_bias,
    w_out,
    out_bias,
    ln2_gain,
    ln2_bias,
    ln3_gain,
    ln3_bias,
    w_up,
    up_bias,
    w_down,
    down_bias,
    ln4_gain,
    ln4_bias,
    row_grid,
    pad_mask,
    cotangent,
):
    f32, bf16 = jnp.float32, jnp.bfloat16
    model_dim = tokens.shape[1]
    group_rows = pad_mask.shape[0]
    width = w_qkv.shape[2]
    units = w_up.shape[1]
    shares = layout.n
    rank = layout.rank()

    small = jnp.concatenate(
        [
            qv_bias.reshape(-1),
            up_bias,
            pad_mask.astype(f32),
            row_grid[0].astype(f32),
        ]
    )
    small = layout.regroup(small)
    qv_bias = small[: 2 * width].reshape(2, width)
    up_bias = small[2 * width : 2 * width + units]
    keep = small[2 * width + units : 2 * width + units + group_rows].astype(jnp.int32)
    grid_row = small[2 * width + units + group_rows :].astype(jnp.int32)
    tokens = layout.regroup(tokens)
    w_qkv = w_qkv.reshape(model_dim, 3 * width)
    w_qkv = layout.regroup(w_qkv)
    w_out = layout.regroup(after(w_out, w_qkv))
    w_up = layout.regroup(after(w_up, w_qkv))
    w_down = layout.regroup(after(w_down, w_qkv))
    cotangent = layout.regroup(after(cotangent, w_qkv))

    resid_in = tokens.astype(f32)
    norm1_out, normed1, inv1 = norm_parts(resid_in, ln1_gain, ln1_bias)
    a1 = layout.gather(norm1_out.astype(bf16))
    zeros = jnp.zeros((width,), f32)
    qkv_bias = jnp.concatenate([qv_bias[0], zeros, qv_bias[1]])[:, None]
    qkv_scale = jnp.concatenate([zeros + HDIM ** (-0.5), zeros + 1.0, zeros + 1.0])[:, None]
    qkv = [((cols_by_cols(w_qkv, x) + qkv_bias) * qkv_scale).astype(bf16) for x in a1]
    qkv, turn = for_kernel(qkv, rank)
    seg, tables = row_tables(grid_row, group_rows, turn)
    context_in, log_total = attend_forward(qkv, seg, keep, tables)
    context = from_kernel(context_in, rank, shares)
    branch_z = layout.scatter_sum([contract_rows(x, w_out) for x in context]) + out_bias
    norm2_out, normed2, inv2 = norm_parts(branch_z, ln2_gain, ln2_bias)
    resid_mid = resid_in + norm2_out
    norm3_out, normed3, inv3 = norm_parts(resid_mid, ln3_gain, ln3_bias)
    a3 = layout.gather(norm3_out.astype(bf16))
    hidden, slope = [], []
    for x in a3:
        act, der = gelu_and_slope(matmul(x, w_up) + up_bias)
        hidden.append(act.astype(bf16))
        slope.append(der.astype(bf16))
    branch_f = layout.scatter_sum([matmul(x, w_down) for x in hidden]) + down_bias
    norm4_out, normed4, inv4 = norm_parts(branch_f, ln4_gain, ln4_bias)
    layer_out = layout.give_back((resid_mid + norm4_out).astype(bf16))

    upstream = cotangent.astype(f32)
    grad_f = norm_back(upstream, normed4, inv4, ln4_gain).astype(bf16)
    grad_f_all = layout.gather(grad_f)
    grad_pre = [
        (contract_cols(g, w_down) * s.astype(f32)).astype(bf16)
        for g, s in zip(grad_f_all, slope)
    ]
    grad_a3 = layout.scatter_sum([contract_cols(g, w_up) for g in grad_pre])
    g_w_down = layout.weight_sum(total([contract_rows(x, g) for x, g in zip(hidden, grad_f_all)]), 0)
    g_w_up = layout.weight_sum(total([contract_rows(x, g) for x, g in zip(a3, grad_pre)]), 0)
    g_up_bias = total([jnp.sum(g.astype(f32), 0) for g in grad_pre])
    grad_mid = upstream + norm_back(grad_a3, normed3, inv3, ln3_gain)
    grad_z = norm_back(grad_mid, normed2, inv2, ln2_gain).astype(bf16)
    grad_z_all = layout.gather(grad_z)
    grad_ctx = [contract_cols(w_out, g).astype(bf16) for g in grad_z_all]
    g_w_out = layout.weight_sum(total([matmul(x, g) for x, g in zip(context, grad_z_all)]), 1)
    grad_ctx, _ = for_kernel(grad_ctx, rank)
    grad_qkv = attend_backward(qkv, context_in, grad_ctx, log_total, seg, keep, tables)
    grad_qkv = from_kernel(grad_qkv, rank, shares)
    grad_a1 = layout.scatter_sum([cols_by_cols(g, w_qkv) for g in grad_qkv])
    g_w_qkv = layout.weight_sum(
        total([contract_cols(x.T, g) for x, g in zip(a1, grad_qkv)]), 2
    ).reshape(model_dim, 3, width)
    grad_input = grad_mid + norm_back(grad_a1, normed1, inv1, ln1_gain)
    grad_input = layout.give_back(grad_input.astype(bf16)).astype(f32)

    early = jnp.stack(
        [
            jnp.sum(grad_z.astype(f32), 0),
            jnp.sum(grad_mid * normed2, 0),
            jnp.sum(grad_mid, 0),
            jnp.sum(grad_a3 * normed3, 0),
            jnp.sum(grad_a3, 0),
            jnp.sum(grad_f.astype(f32), 0),
            jnp.sum(upstream * normed4, 0),
            jnp.sum(upstream, 0),
        ],
        0,
    )
    all_units = lax.dynamic_update_slice(jnp.zeros((units * shares,), f32), g_up_bias, (rank * units,))
    early = layout.sum_all(jnp.concatenate([early.reshape(-1), all_units]))
    all_units = early[8 * model_dim :]
    early = early[: 8 * model_dim].reshape(8, model_dim)
    sums = total([jnp.sum(g.astype(f32), 1) for g in grad_qkv]).reshape(3, width)
    all_width = lax.dynamic_update_slice(
        jnp.zeros((2, width * shares), f32), jnp.stack([sums[0], sums[2]], 0), (0, rank * width)
    )
    late = layout.sum_all(
        jnp.concatenate(
            [jnp.sum(grad_a1 * normed1, 0), jnp.sum(grad_a1, 0), all_width.reshape(-1)]
        )
    )
    all_width = late[2 * model_dim :].reshape(2, width * shares)
    m = lax.axis_index("mp")
    g_qv_bias = lax.dynamic_slice(all_width, (0, m * width), (2, width))
    g_up_bias = lax.dynamic_slice(all_units, (m * units,), (units,))
    return (
        layer_out,
        grad_input,
        late[:model_dim],
        late[model_dim : 2 * model_dim],
        g_w_qkv,
        g_qv_bias,
        g_w_out,
        early[0],
        early[1],
        early[2],
        early[3],
        early[4],
        g_w_up,
        g_up_bias,
        g_w_down,
        early[5],
        early[6],
        early[7],
    )


def solution(mesh):
    in_specs = (
        P(("dp", "mp"), None),
        P(),
        P(),
        P(None, None, "mp"),
        P(None, "mp"),
        P("mp", None),
        P(),
        P(),
        P(),
        P(),
        P(),
        P(None, "mp"),
        P("mp"),
        P("mp", None),
        P(),
        P(),
        P(),
        P("dp", None),
        P("dp"),
        P(("dp", "mp"), None),
    )
    out_specs = (
        P(("dp", "mp"), None),
        P(("dp", "mp"), None),
        P(),
        P(),
        P(None, None, "mp"),
        P(None, "mp"),
        P("mp", None),
        P(),
        P(),
        P(),
        P(),
        P(),
        P(None, "mp"),
        P("mp"),
        P("mp", None),
        P(),
        P(),
        P(),
    )
    return jax.shard_map(functools.partial(body, Layout(mesh)), mesh=mesh, in_specs=in_specs, out_specs=out_specs, check_vma=False)
```

```python
import functools

import jax
import jax.numpy as jnp
from jax import lax
from jax.experimental import pallas as pl
from jax.experimental.pallas import tpu as pltpu
from jax.sharding import PartitionSpec as P

HDIM = 64
TEXT = 64


epsilon = 1e-05
masked_score = -1e30


def norm_parts(values, ln_gain, ln_bias):
    centred = values - jnp.mean(values, -1, keepdims=True)
    inv_std = lax.rsqrt(jnp.mean(centred * centred, -1, keepdims=True) + epsilon)
    normed = centred * inv_std
    return (normed * ln_gain + ln_bias, normed, inv_std)


def norm_back(upstream, normed, inv_std, ln_gain):
    scaled = upstream * ln_gain
    return inv_std * (
        scaled
        - jnp.mean(scaled, -1, keepdims=True)
        - normed * jnp.mean(scaled * normed, -1, keepdims=True)
    )


def contract_rows(left, right):
    return lax.dot_general(
        left, right, (((0,), (0,)), ((), ())), preferred_element_type=jnp.float32
    )


def contract_cols(left, right):
    return lax.dot_general(
        left, right, (((1,), (1,)), ((), ())), preferred_element_type=jnp.float32
    )


BQ = 256
BK = 256
MOST = 4
PAIR = 2 * HDIM
F32 = jnp.float32
BF16 = jnp.bfloat16


def matmul(left, right):
    return jnp.dot(left, right, preferred_element_type=F32)


def row_tables(grid_row, tokens, turn):
    side = jnp.max(grid_row)
    length = TEXT + side * side
    rows = tokens // length
    used = rows * length
    position = jnp.arange(tokens, dtype=jnp.int32)
    seg = jnp.minimum(position // length, rows)
    blocks = tokens // BQ
    first = jnp.arange(blocks, dtype=jnp.int32) * BQ
    start = jnp.where(first < used, (first // length) * length, first)
    low = start // BK
    diag = first // BK
    turns = jnp.full((blocks,), turn, jnp.int32)
    return seg, jnp.stack([low, diag, turns]).astype(jnp.int32)


def allowed(kseg_ref, qseg_ref, i, j, blocks):
    qs = qseg_ref[:, pl.ds(pl.multiple_of(i * BQ, BQ), BQ)]
    ks = kseg_ref[pl.ds(pl.multiple_of(j * BK, BK), blocks * BK), :]
    ik = j * BK + lax.broadcasted_iota(jnp.int32, (blocks * BK, BQ), 0)
    iq = i * BQ + lax.broadcasted_iota(jnp.int32, (blocks * BK, BQ), 1)
    return ((ks == qs) & (ik <= iq)) | (ik == iq)


def sweep(tab_ref, i, step, carry):
    return several(tab_ref[0, i], tab_ref[1, i] + 1, step, carry)


def several(first, stop, step, carry, most=MOST):
    while most > 1:
        turns = (stop - first) // most

        def turn(n, carry, first=first, most=most):
            return step(most, first + most * n, carry)

        carry = lax.fori_loop(0, turns, turn, carry)
        first, most = first + most * turns, most // 2
    return lax.fori_loop(first, stop, functools.partial(step, 1), carry)


def each_block(tab_ref, parts, width, work):
    blocks = width // BQ
    count = blocks * parts
    for part in range(parts):

        def one(c, _, part=part):
            whole = lax.rem(tab_ref[2, 0] + part * blocks + c, count)
            work(
                part,
                pl.ds(pl.multiple_of(c * BQ, BQ), BQ),
                pl.ds(pl.multiple_of(whole * BQ, BQ), BQ),
            )
            return 0

        lax.fori_loop(0, blocks, one, 0)


def forward_kernel(parts, tab_ref, kseg_ref, qseg_ref, *refs):
    qkv_refs = refs[:parts]
    *o_refs, ot_ref, lse_ref, kx, vx, qx, scores = refs[-6 - parts :]
    tokens = qx.shape[1]
    width = tokens // parts
    lane = lax.broadcasted_iota(jnp.int32, (BK, 128), 1)
    zero = jnp.zeros((BK, 128), BF16)

    def prepare(part, here, there):
        k = qkv_refs[part][here, PAIR : 2 * PAIR]
        kx[0, there, :] = jnp.where(lane < HDIM, k, zero)
        kx[1, there, :] = jnp.where(lane < HDIM, zero, k)
        qx[:, there] = qkv_refs[part][here, :PAIR].astype(F32).T.astype(BF16)
        v = qkv_refs[part][here, 2 * PAIR :].astype(F32).T.astype(BF16)
        for h in range(2):
            vx[h, :HDIM, there] = v[h * HDIM : (h + 1) * HDIM]
            vx[h, HDIM:, there] = jnp.ones((16, BQ), BF16)

    each_block(tab_ref, parts, width, prepare)

    def block(i, _):
        cols = pl.ds(pl.multiple_of(i * BQ, BQ), BQ)
        qb = qx[:, cols]

        def score(blocks, j, tops):
            at = pl.ds(pl.multiple_of(j * BK, BK), blocks * BK)
            ok = allowed(kseg_ref, qseg_ref, i, j, blocks)
            out = []
            for h in range(2):
                s = matmul(kx[h, at, :], qb)
                s = jnp.where(ok, s, masked_score)
                scores[h, at, :] = s
                out.append(jnp.maximum(tops[h], jnp.max(s.reshape(blocks * BK // 8, 8, BQ), axis=0)))
            return tuple(out)

        tops = sweep(tab_ref, i, score, (jnp.full((8, BQ), masked_score, F32),) * 2)
        tops = [jnp.max(top, axis=0, keepdims=True) for top in tops]

        def weigh(blocks, j, accs):
            at = pl.ds(pl.multiple_of(j * BK, BK), blocks * BK)
            out = []
            for h in range(2):
                p = jnp.exp(scores[h, at, :] - tops[h]).astype(BF16)
                out.append(accs[h] + matmul(vx[h, :, at], p))
            return tuple(out)

        accs = sweep(tab_ref, i, weigh, (jnp.zeros((HDIM + 16, BQ), F32),) * 2)
        for h in range(2):
            total = accs[h][HDIM : HDIM + 1, :]
            ot_ref[h * HDIM : (h + 1) * HDIM, cols] = (accs[h][:HDIM, :] / total).astype(BF16)
            lse_ref[0, h : h + 1, cols] = tops[h] + jnp.log(total)
        return 0

    lax.fori_loop(0, tokens // BQ, block, 0)

    def finish(part, here, there):
        o_refs[part][here, :] = ot_ref[:, there].astype(F32).T.astype(BF16)

    each_block(tab_ref, parts, width, finish)


def three_parts(x):
    high = x.astype(BF16)
    rest = x - high.astype(F32)
    middle = rest.astype(BF16)
    return high, middle, (rest - middle.astype(F32)).astype(BF16)


def backward_kernel(parts, tab_ref, kseg_ref, qseg_ref, *refs):
    qkv_refs, do_refs = refs[:parts], refs[parts : 2 * parts]
    ot_ref, lse_ref = refs[2 * parts : 2 * parts + 2]
    out_refs = refs[2 * parts + 2 : 3 * parts + 2]
    kx, vx, kt, qx, dox, qt, dot, dq, dk, dv = refs[3 * parts + 2 :]
    tokens = kt.shape[1]
    width = tokens // parts
    lane = lax.broadcasted_iota(jnp.int32, (BK, 128), 1)
    sub = lax.broadcasted_iota(jnp.int32, (HDIM, BK), 0)
    one0 = jnp.where((lane >= HDIM) & (lane < HDIM + 3), 1.0, 0.0).astype(BF16)
    one1 = jnp.where(lane < 3, 1.0, 0.0).astype(BF16)
    zero = jnp.zeros((BK, 128), BF16)

    def extra(x):
        high, middle, low = (e.astype(F32) for e in three_parts(x))
        rows = jnp.where(
            sub == 0, high, jnp.where(sub == 1, middle, jnp.where(sub == 2, low, 0.0))
        )
        return rows.astype(BF16)

    def prepare(part, here, there):
        k = qkv_refs[part][here, PAIR : 2 * PAIR]
        kt[:, there] = k.astype(F32).T.astype(BF16)
        kx[0, there, :] = jnp.where(lane < HDIM, k, one0)
        kx[1, there, :] = jnp.where(lane < HDIM, one1, k)
        v = qkv_refs[part][here, 2 * PAIR :]
        vx[0, there, :] = jnp.where(lane < HDIM, v, one0)
        vx[1, there, :] = jnp.where(lane < HDIM, one1, v)
        q = qkv_refs[part][here, :PAIR]
        qt[0, there, :] = jnp.where(lane < HDIM, q, zero)
        qt[1, there, :] = jnp.where(lane < HDIM, zero, q)
        do = do_refs[part][here, :]
        dot[0, there, :] = jnp.where(lane < HDIM, do, zero)
        dot[1, there, :] = jnp.where(lane < HDIM, zero, do)
        turned = do.astype(F32).T
        prod = turned * ot_ref[:, there].astype(F32)
        inner0 = jnp.sum(prod[:HDIM], axis=0, keepdims=True)
        inner1 = jnp.sum(prod[HDIM:], axis=0, keepdims=True)
        turned = turned.astype(BF16)
        dox[0, :HDIM, there] = turned[:HDIM]
        dox[0, HDIM:, there] = extra(-inner0)
        dox[1, HDIM:, there] = turned[HDIM:]
        dox[1, :HDIM, there] = extra(-inner1)
        turned = q.astype(F32).T.astype(BF16)
        qx[0, :HDIM, there] = turned[:HDIM]
        qx[0, HDIM:, there] = extra(-lse_ref[0, 0:1, there])
        qx[1, HDIM:, there] = turned[HDIM:]
        qx[1, :HDIM, there] = extra(-lse_ref[0, 1:2, there])
        dk[there, :] = jnp.zeros((BK, 128), F32)
        dv[there, :] = jnp.zeros((BK, 128), F32)

    each_block(tab_ref, parts, width, prepare)

    def block(i, _):
        cols = pl.ds(pl.multiple_of(i * BQ, BQ), BQ)

        def step(blocks, j, carry):
            at = pl.ds(pl.multiple_of(j * BK, BK), blocks * BK)
            ok = allowed(kseg_ref, qseg_ref, i, j, blocks)
            new = []
            dvs = dv[at, :]
            dks = dk[at, :]
            for h in range(2):
                s = matmul(kx[h, at, :], qx[h, :, cols])
                s = jnp.where(ok, s, masked_score)
                p = jnp.exp(s)
                dp = matmul(vx[h, at, :], dox[h, :, cols])
                ds = (p * dp).astype(BF16)
                dvs = dvs + matmul(p.astype(BF16), dot[h, cols, :])
                dks = dks + matmul(ds, qt[h, cols, :])
                new.append(carry[h] + matmul(kt[h * HDIM : (h + 1) * HDIM, at], ds))
            dv[at, :] = dvs
            dk[at, :] = dks
            return tuple(new)

        init = tuple(jnp.zeros((HDIM, BQ), F32) for _ in range(2))
        res = sweep(tab_ref, i, step, init)
        for h in range(2):
            dq[h * HDIM : (h + 1) * HDIM, cols] = res[h] * (HDIM**-0.5)
        return 0

    lax.fori_loop(0, tokens // BQ, block, 0)

    def finish(part, here, there):
        out_refs[part][here, :PAIR] = dq[:, there].T.astype(BF16)
        out_refs[part][here, PAIR : 2 * PAIR] = dk[there, :].astype(BF16)
        out_refs[part][here, 2 * PAIR :] = dv[there, :].astype(BF16)

    each_block(tab_ref, parts, width, finish)


def lanes_of(first, step):
    return lambda g, t: (0, first + step * g)


def attend_specs(qkv_parts, chunk):
    parts = len(qkv_parts)
    width = qkv_parts[0].shape[0]
    tokens = parts * width
    every = qkv_parts[0].shape[1] // (3 * PAIR)
    pairs = every // chunk[1]
    first = pairs * chunk[0]
    seg_specs = [
        pl.BlockSpec((tokens, 1), lambda g, t: (0, 0)),
        pl.BlockSpec((1, tokens), lambda g, t: (0, 0)),
    ]
    qkv_specs = [pl.BlockSpec((width, 3 * PAIR), lanes_of(first, 1))] * parts
    o_specs = [pl.BlockSpec((width, PAIR), lanes_of(first, 1))] * parts
    ot_spec = pl.BlockSpec((PAIR, tokens), lambda g, t: (first + g, 0))
    lse_spec = pl.BlockSpec((1, 2, tokens), lambda g, t: (first + g, 0, 0))
    return parts, width, tokens, every, pairs, seg_specs, qkv_specs, o_specs, ot_spec, lse_spec


def attend_forward(qkv_parts, seg, keep, tables, chunk, begun=()):
    parts, width, tokens, every, pairs, seg_specs, qkv_specs, o_specs, ot_spec, lse_spec = (
        attend_specs(qkv_parts, chunk)
    )
    kseg = jnp.where(keep == 1, seg, -1)[:, None]
    return pl.pallas_call(
        functools.partial(forward_kernel, parts),
        grid_spec=pltpu.PrefetchScalarGridSpec(
            num_scalar_prefetch=1,
            grid=(pairs,),
            in_specs=seg_specs + qkv_specs + [pl.BlockSpec(memory_space=pl.ANY)] * len(begun),
            out_specs=o_specs + [ot_spec, lse_spec],
            scratch_shapes=[
                pltpu.VMEM((2, tokens, 128), BF16),
                pltpu.VMEM((2, HDIM + 16, tokens), BF16),
                pltpu.VMEM((PAIR, tokens), BF16),
                pltpu.VMEM((2, tokens, BQ), F32),
            ],
        ),
        out_shape=[jax.ShapeDtypeStruct((width, every * PAIR), BF16)] * parts
        + [
            jax.ShapeDtypeStruct((every * PAIR, tokens), BF16),
            jax.ShapeDtypeStruct((every, 2, tokens), F32),
        ],
        compiler_params=pltpu.CompilerParams(vmem_limit_bytes=40 * 2**20),
        cost_estimate=pl.CostEstimate(
            flops=3000 * tokens * tokens * pairs, bytes_accessed=2**23, transcendentals=0
        ),
        input_output_aliases={3 + parts + n: n for n in range(len(begun))},
        name="attend_forward",
    )(tables, kseg, seg[None, :], *qkv_parts, *begun)


def attend_backward(qkv_parts, turned, grad_ctx, lse, seg, keep, tables, chunk):
    parts, width, tokens, every, pairs, seg_specs, qkv_specs, o_specs, ot_spec, lse_spec = (
        attend_specs(qkv_parts, chunk)
    )
    kseg = jnp.where(keep == 1, seg, -1)[:, None]
    return pl.pallas_call(
        functools.partial(backward_kernel, parts),
        grid_spec=pltpu.PrefetchScalarGridSpec(
            num_scalar_prefetch=1,
            grid=(pairs,),
            in_specs=seg_specs + qkv_specs + o_specs + [ot_spec, lse_spec],
            out_specs=[pl.BlockSpec((width, 3 * PAIR), lanes_of(0, 1))] * parts,
            scratch_shapes=[
                pltpu.VMEM((2, tokens, 128), BF16),
                pltpu.VMEM((2, tokens, 128), BF16),
                pltpu.VMEM((PAIR, tokens), BF16),
                pltpu.VMEM((2, 128, tokens), BF16),
                pltpu.VMEM((2, 128, tokens), BF16),
                pltpu.VMEM((2, tokens, 128), BF16),
                pltpu.VMEM((2, tokens, 128), BF16),
                pltpu.VMEM((PAIR, tokens), F32),
                pltpu.VMEM((tokens, 128), F32),
                pltpu.VMEM((tokens, 128), F32),
            ],
        ),
        out_shape=[jax.ShapeDtypeStruct((width, pairs * 3 * PAIR), BF16)] * parts,
        compiler_params=pltpu.CompilerParams(vmem_limit_bytes=48 * 2**20),
        cost_estimate=pl.CostEstimate(
            flops=4000 * tokens * tokens * pairs, bytes_accessed=2**24, transcendentals=0
        ),
        name="attend_backward",
    )(tables, kseg, seg[None, :], *qkv_parts, *grad_ctx, turned, lse)


def gelu_and_slope(u):
    root = 0.7978845608028654
    square = u * u
    t = jnp.tanh(root * u * (1.0 + 0.044715 * square))
    half = 0.5 * (1.0 + t)
    slope = half + 0.5 * u * (1.0 - t * t) * (root * (1.0 + 0.134145 * square))
    return u * half, slope


def after(value, *others):
    return lax.optimization_barrier((value, *others))[0]


class Layout:
    def __init__(self, mesh):
        self.dp, self.n = mesh.shape["dp"], mesh.shape["mp"]
        self.pairs = self.dp // 2
        self.axes = ("dp", "mp")

    def device(self, pair, core, m):
        return (2 * pair + core) * self.n + m

    def at_rank(self, pair, group, rank):
        return self.device(pair, rank % 2, group * (self.n // 2) + rank // 2)

    def each(self):
        for pair in range(self.pairs):
            for group in range(2):
                for rank in range(self.n):
                    yield pair, group, rank

    def stays(self):
        core, m = lax.axis_index("dp") % 2, lax.axis_index("mp")
        return (m // (self.n // 2) == core) & (self.rank() == m)

    def send(self, value, back=False):
        moves = [(self.device(p, g, r), self.at_rank(p, g, r)) for p, g, r in self.each()]
        return lax.ppermute(
            value, self.axes, [(b, a) if back else (a, b) for a, b in moves if a != b]
        )

    def regroup(self, value):
        return jnp.where(self.stays(), value, self.send(value))

    def give_back(self, value):
        return jnp.where(self.stays(), value, self.send(value, True))

    def partner(self, value, bit, only=lambda p, g, r: True):
        def other(p, c):
            return (p, 1 - c) if bit < 0 else (p ^ (1 << bit), c)

        moves = [
            (self.device(*other(p, c), m), self.device(p, c, m))
            for p, c, m in self.each()
            if only(p, c, m)
        ]
        return lax.ppermute(value, self.axes, moves)

    def side(self, bit):
        dp = lax.axis_index("dp")
        return dp % 2 if bit < 0 else (dp // 2 >> bit) % 2

    def joined(self, mine, theirs, bit):
        high = self.side(bit) == 1
        return jnp.concatenate(
            [jnp.where(high, theirs, mine), jnp.where(high, mine, theirs)], 0
        )

    def regroup_spread(self, value):
        bits = (1, 0)
        rows = value.shape[0] // 4
        part = 2 * self.side(0) + self.side(1)
        got = self.send(lax.dynamic_slice_in_dim(value, part * rows, rows, 0))
        for bit in bits:
            got = self.joined(got, self.partner(got, bit, self.moving), bit)
        return jnp.where(self.stays(), value, got)

    def moving(self, pair, core, m):
        return self.at_rank(pair, core, m) != self.device(pair, core, m)

    def to_rank(self, value, ahead):
        moves = [
            (self.at_rank(p, g, r), self.at_rank(p, g, (r + ahead) % self.n))
            for p, g, r in self.each()
        ]
        return lax.ppermute(value, self.axes, moves)

    def rank(self):
        core = lax.axis_index("dp") % 2
        return (lax.axis_index("mp") % (self.n // 2)) * 2 + core

    def gather(self, mine):
        return [mine] + [self.to_rank(mine, self.n - k) for k in range(1, self.n)]

    def scatter_sum(self, shares):
        total = shares[0].astype(jnp.float32)
        for k in range(1, self.n):
            total = total + self.to_rank(shares[k].astype(jnp.bfloat16), k).astype(jnp.float32)
        return total

    def sum_all(self, value):
        devices = self.dp * self.n
        steps = [1 << k for k in range(devices.bit_length() - 1)]
        within = self.n.bit_length() - 1
        for step in steps[within:] + steps[:within]:
            value = value + lax.ppermute(value, self.axes, [(i, i ^ step) for i in range(devices)])
        return value

    def weight_sum(self, grad):
        grad = self.give_back(grad.astype(jnp.bfloat16))
        return lax.psum(grad, "dp").astype(jnp.float32)

    def weight_sum_by_halves(self, grad):
        value = self.give_back(grad.astype(jnp.bfloat16))
        bits = [-1, *range(self.pairs.bit_length() - 1)]
        for bit in bits:
            half, high = value.shape[0] // 2, self.side(bit)
            sent = lax.dynamic_slice_in_dim(value, (1 - high) * half, half, 0)
            kept = lax.dynamic_slice_in_dim(value, high * half, half, 0)
            got = self.partner(sent, bit)
            value = (kept.astype(jnp.float32) + got.astype(jnp.float32)).astype(jnp.bfloat16)
        for bit in bits[::-1]:
            value = self.joined(value, self.partner(value, bit), bit)
        return value.astype(jnp.float32)


def for_kernel(shares, rank):
    width = shares[0].shape[0]
    if width % BQ == 0:
        return shares, rank * (width // BQ)
    return [jnp.roll(jnp.concatenate(shares, 0), rank * width, 0)], 0


def from_kernel(arrays, rank, shares):
    if len(arrays) == shares:
        return arrays
    width = arrays[0].shape[0] // shares
    return jnp.split(jnp.roll(arrays[0], -rank * width, 0), shares, 0)


def by_pairs(weight, pairs):
    return (
        weight.reshape(-1, 3, pairs, PAIR).transpose(0, 2, 1, 3).reshape(-1, 3 * pairs * PAIR)
    )


def total(terms):
    return functools.reduce(jnp.add, terms)


def body(
    layout,
    tokens,
    ln1_gain,
    ln1_bias,
    w_qkv,
    qv_bias,
    w_out,
    out_bias,
    ln2_gain,
    ln2_bias,
    ln3_gain,
    ln3_bias,
    w_up,
    up_bias,
    w_down,
    down_bias,
    ln4_gain,
    ln4_bias,
    row_grid,
    pad_mask,
    cotangent,
):
    f32, bf16 = jnp.float32, jnp.bfloat16
    model_dim = tokens.shape[1]
    group_rows = pad_mask.shape[0]
    width = w_qkv.shape[2]
    units = w_up.shape[1]
    shares = layout.n
    rank = layout.rank()

    small = jnp.concatenate(
        [
            qv_bias.reshape(-1),
            up_bias,
            pad_mask.astype(f32),
            row_grid[0].astype(f32),
        ]
    )
    small = layout.regroup(small)
    qv_bias = small[: 2 * width].reshape(2, width)
    up_bias = small[2 * width : 2 * width + units]
    keep = small[2 * width + units : 2 * width + units + group_rows].astype(jnp.int32)
    grid_row = small[2 * width + units + group_rows :].astype(jnp.int32)
    pairs = width // PAIR
    chunks = 2 if pairs % 2 == 0 else 1
    tokens = layout.regroup(tokens)
    w_qkv = by_pairs(layout.regroup_spread(w_qkv), pairs)
    w_out_far = layout.send(after(w_out, tokens))
    w_up_far = layout.send(after(w_up, tokens))
    w_down = layout.regroup(after(w_down, w_up_far))
    cotangent = layout.regroup(after(cotangent, w_up_far))

    resid_in = tokens.astype(f32)
    norm1_out, normed1, inv1 = norm_parts(resid_in, ln1_gain, ln1_bias)
    a1 = layout.gather(norm1_out.astype(bf16))
    zeros = jnp.zeros((width,), f32)
    qkv_bias = by_pairs(jnp.concatenate([qv_bias[0], zeros, qv_bias[1]]), pairs)
    qkv_scale = by_pairs(
        jnp.concatenate([zeros + HDIM ** (-0.5), zeros + 1.0, zeros + 1.0]), pairs
    )
    qkv = [((matmul(x, w_qkv) + qkv_bias) * qkv_scale).astype(bf16) for x in a1]
    qkv, turn = for_kernel(qkv, rank)
    seg, tables = row_tables(grid_row, group_rows, turn)
    begun = ()
    for chunk in range(chunks):
        if chunk == chunks - 1:
            tables, w_out_far, w_up_far = lax.optimization_barrier((tables, w_out_far, w_up_far))
        begun = attend_forward(qkv, seg, keep, tables, (chunk, chunks), begun)
    *context, context_turned, log_total = begun
    context = from_kernel(context, rank, shares)
    w_out = jnp.where(layout.stays(), w_out, w_out_far)
    w_up = jnp.where(layout.stays(), w_up, w_up_far)
    branch_z = layout.scatter_sum([matmul(x, w_out) for x in context]) + out_bias
    norm2_out, normed2, inv2 = norm_parts(branch_z, ln2_gain, ln2_bias)
    resid_mid = resid_in + norm2_out
    norm3_out, normed3, inv3 = norm_parts(resid_mid, ln3_gain, ln3_bias)
    a3 = layout.gather(norm3_out.astype(bf16))
    hidden, slope = [], []
    for x in a3:
        act, der = gelu_and_slope(matmul(x, w_up) + up_bias)
        hidden.append(act.astype(bf16))
        slope.append(der.astype(bf16))
    branch_f = layout.scatter_sum([matmul(x, w_down) for x in hidden]) + down_bias
    norm4_out, normed4, inv4 = norm_parts(branch_f, ln4_gain, ln4_bias)
    layer_out = layout.give_back((resid_mid + norm4_out).astype(bf16))

    upstream = cotangent.astype(f32)
    grad_f = norm_back(upstream, normed4, inv4, ln4_gain).astype(bf16)
    grad_f_all = layout.gather(grad_f)
    grad_pre = [
        (contract_cols(g, w_down) * s.astype(f32)).astype(bf16)
        for g, s in zip(grad_f_all, slope)
    ]
    grad_a3 = layout.scatter_sum([contract_cols(g, w_up) for g in grad_pre])
    g_w_down = layout.weight_sum(total([contract_rows(x, g) for x, g in zip(hidden, grad_f_all)]))
    g_w_up = layout.weight_sum(total([contract_rows(x, g) for x, g in zip(a3, grad_pre)]))
    g_up_bias = total([jnp.sum(g.astype(f32), 0) for g in grad_pre])
    grad_mid = upstream + norm_back(grad_a3, normed3, inv3, ln3_gain)
    grad_z = norm_back(grad_mid, normed2, inv2, ln2_gain).astype(bf16)
    grad_z_all = layout.gather(grad_z)
    grad_ctx = [contract_cols(g, w_out).astype(bf16) for g in grad_z_all]
    g_w_out = layout.weight_sum(total([contract_rows(x, g) for x, g in zip(context, grad_z_all)]))
    grad_ctx, _ = for_kernel(grad_ctx, rank)
    grad_a1, g_w_qkv, sums = [], [], []
    for chunk in range(chunks):
        grad_qkv = attend_backward(
            qkv, context_turned, grad_ctx, log_total, seg, keep, tables, (chunk, chunks)
        )
        grad_qkv = from_kernel(grad_qkv, rank, shares)
        columns = grad_qkv[0].shape[1]
        w_part = w_qkv[:, chunk * columns : (chunk + 1) * columns]
        grad_a1.append([contract_cols(g, w_part) for g in grad_qkv])
        sums.append(total([jnp.sum(g.astype(f32), 0) for g in grad_qkv]))
        g_w_qkv.append(
            layout.weight_sum_by_halves(total([contract_rows(x, g) for x, g in zip(a1, grad_qkv)]))
        )
    g_w_qkv = (
        jnp.concatenate(g_w_qkv, 1)
        .reshape(model_dim, pairs, 3, PAIR)
        .transpose(0, 2, 1, 3)
        .reshape(model_dim, 3, width)
    )
    sums = jnp.concatenate(sums).reshape(pairs, 3, PAIR).transpose(1, 0, 2).reshape(3, width)
    grad_a1 = layout.scatter_sum([total(terms) for terms in zip(*grad_a1)])
    grad_input = grad_mid + norm_back(grad_a1, normed1, inv1, ln1_gain)
    grad_input = layout.give_back(grad_input.astype(bf16)).astype(f32)

    norm_terms = jnp.stack(
        [
            jnp.sum(grad_a1 * normed1, 0),
            jnp.sum(grad_a1, 0),
            jnp.sum(grad_z.astype(f32), 0),
            jnp.sum(grad_mid * normed2, 0),
            jnp.sum(grad_mid, 0),
            jnp.sum(grad_a3 * normed3, 0),
            jnp.sum(grad_a3, 0),
            jnp.sum(grad_f.astype(f32), 0),
            jnp.sum(upstream * normed4, 0),
            jnp.sum(upstream, 0),
        ],
        0,
    )
    all_units = lax.dynamic_update_slice(jnp.zeros((units * shares,), f32), g_up_bias, (rank * units,))
    all_width = lax.dynamic_update_slice(
        jnp.zeros((2, width * shares), f32), jnp.stack([sums[0], sums[2]], 0), (0, rank * width)
    )
    small = layout.sum_all(
        jnp.concatenate([norm_terms.reshape(-1), all_width.reshape(-1), all_units])
    )
    norm_terms = small[: 10 * model_dim].reshape(10, model_dim)
    all_width = small[10 * model_dim : 12 * model_dim].reshape(2, width * shares)
    all_units = small[12 * model_dim :]
    m = lax.axis_index("mp")
    g_qv_bias = lax.dynamic_slice(all_width, (0, m * width), (2, width))
    g_up_bias = lax.dynamic_slice(all_units, (m * units,), (units,))
    return (
        layer_out,
        grad_input,
        norm_terms[0],
        norm_terms[1],
        g_w_qkv,
        g_qv_bias,
        g_w_out,
        norm_terms[2],
        norm_terms[3],
        norm_terms[4],
        norm_terms[5],
        norm_terms[6],
        g_w_up,
        g_up_bias,
        g_w_down,
        norm_terms[7],
        norm_terms[8],
        norm_terms[9],
    )


def solution(mesh):
    in_specs = (
        P(("dp", "mp"), None),
        P(),
        P(),
        P(None, None, "mp"),
        P(None, "mp"),
        P("mp", None),
        P(),
        P(),
        P(),
        P(),
        P(),
        P(None, "mp"),
        P("mp"),
        P("mp", None),
        P(),
        P(),
        P(),
        P("dp", None),
        P("dp"),
        P(("dp", "mp"), None),
    )
    out_specs = (
        P(("dp", "mp"), None),
        P(("dp", "mp"), None),
        P(),
        P(),
        P(None, None, "mp"),
        P(None, "mp"),
        P("mp", None),
        P(),
        P(),
        P(),
        P(),
        P(),
        P(None, "mp"),
        P("mp"),
        P("mp", None),
        P(),
        P(),
        P(),
    )
    return jax.shard_map(functools.partial(body, Layout(mesh)), mesh=mesh, in_specs=in_specs, out_specs=out_specs, check_vma=False)
```

```python
import functools

import jax
import jax.numpy as jnp
from jax import lax
from jax.experimental import pallas as pl
from jax.experimental.pallas import tpu as pltpu
from jax.sharding import PartitionSpec as P

HDIM = 64
TEXT = 64


epsilon = 1e-05
masked_score = -1e30


def norm_parts(values, ln_gain, ln_bias):
    centred = values - jnp.mean(values, -1, keepdims=True)
    inv_std = lax.rsqrt(jnp.mean(centred * centred, -1, keepdims=True) + epsilon)
    normed = centred * inv_std
    return (normed * ln_gain + ln_bias, normed, inv_std)


def norm_back(upstream, normed, inv_std, ln_gain):
    scaled = upstream * ln_gain
    return inv_std * (
        scaled
        - jnp.mean(scaled, -1, keepdims=True)
        - normed * jnp.mean(scaled * normed, -1, keepdims=True)
    )


def contract_rows(left, right):
    return lax.dot_general(
        left, right, (((0,), (0,)), ((), ())), preferred_element_type=jnp.float32
    )


def contract_cols(left, right):
    return lax.dot_general(
        left, right, (((1,), (1,)), ((), ())), preferred_element_type=jnp.float32
    )


BQ = 256
BK = 256
MOST = 4
FEED = 1024
FEED_ROWS = 640
PAIR = 2 * HDIM
F32 = jnp.float32
BF16 = jnp.bfloat16


def matmul(left, right):
    return jnp.dot(left, right, preferred_element_type=F32)


def row_tables(grid_row, tokens, turn):
    side = jnp.max(grid_row)
    length = TEXT + side * side
    rows = tokens // length
    used = rows * length
    position = jnp.arange(tokens, dtype=jnp.int32)
    seg = jnp.minimum(position // length, rows)
    blocks = tokens // BQ
    first = jnp.arange(blocks, dtype=jnp.int32) * BQ
    start = jnp.where(first < used, (first // length) * length, first)
    low = start // BK
    diag = first // BK
    turns = jnp.full((blocks,), turn, jnp.int32)
    return seg, jnp.stack([low, diag, turns]).astype(jnp.int32)


def allowed(kseg_ref, qseg_ref, i, j, blocks):
    qs = qseg_ref[:, pl.ds(pl.multiple_of(i * BQ, BQ), BQ)]
    ks = kseg_ref[pl.ds(pl.multiple_of(j * BK, BK), blocks * BK), :]
    ik = j * BK + lax.broadcasted_iota(jnp.int32, (blocks * BK, BQ), 0)
    iq = i * BQ + lax.broadcasted_iota(jnp.int32, (blocks * BK, BQ), 1)
    return ((ks == qs) & (ik <= iq)) | (ik == iq)


def sweep(tab_ref, i, step, carry):
    return several(tab_ref[0, i], tab_ref[1, i] + 1, step, carry)


def several(first, stop, step, carry, most=MOST):
    while most > 1:
        turns = (stop - first) // most

        def turn(n, carry, first=first, most=most):
            return step(most, first + most * n, carry)

        carry = lax.fori_loop(0, turns, turn, carry)
        first, most = first + most * turns, most // 2
    return lax.fori_loop(first, stop, functools.partial(step, 1), carry)


def each_block(tab_ref, parts, width, work):
    blocks = width // BQ
    count = blocks * parts
    for part in range(parts):

        def one(c, _, part=part):
            whole = lax.rem(tab_ref[2, 0] + part * blocks + c, count)
            work(
                part,
                pl.ds(pl.multiple_of(c * BQ, BQ), BQ),
                pl.ds(pl.multiple_of(whole * BQ, BQ), BQ),
            )
            return 0

        lax.fori_loop(0, blocks, one, 0)


def forward_kernel(parts, tab_ref, kseg_ref, qseg_ref, *refs):
    qkv_refs = refs[:parts]
    *o_refs, ot_ref, lse_ref, kx, vx, qx, scores = refs[-6 - parts :]
    tokens = qx.shape[1]
    width = tokens // parts
    lane = lax.broadcasted_iota(jnp.int32, (BK, 128), 1)
    zero = jnp.zeros((BK, 128), BF16)

    def prepare(part, here, there):
        k = qkv_refs[part][here, PAIR : 2 * PAIR]
        kx[0, there, :] = jnp.where(lane < HDIM, k, zero)
        kx[1, there, :] = jnp.where(lane < HDIM, zero, k)
        qx[:, there] = qkv_refs[part][here, :PAIR].astype(F32).T.astype(BF16)
        v = qkv_refs[part][here, 2 * PAIR :].astype(F32).T.astype(BF16)
        for h in range(2):
            vx[h, :HDIM, there] = v[h * HDIM : (h + 1) * HDIM]
            vx[h, HDIM:, there] = jnp.ones((16, BQ), BF16)

    each_block(tab_ref, parts, width, prepare)

    def block(i, _):
        cols = pl.ds(pl.multiple_of(i * BQ, BQ), BQ)
        qb = qx[:, cols]

        def score(blocks, j, tops):
            at = pl.ds(pl.multiple_of(j * BK, BK), blocks * BK)
            ok = allowed(kseg_ref, qseg_ref, i, j, blocks)
            out = []
            for h in range(2):
                s = matmul(kx[h, at, :], qb)
                s = jnp.where(ok, s, masked_score)
                scores[h, at, :] = s
                out.append(jnp.maximum(tops[h], jnp.max(s.reshape(blocks * BK // 8, 8, BQ), axis=0)))
            return tuple(out)

        tops = sweep(tab_ref, i, score, (jnp.full((8, BQ), masked_score, F32),) * 2)
        tops = [jnp.max(top, axis=0, keepdims=True) for top in tops]

        def weigh(blocks, j, accs):
            at = pl.ds(pl.multiple_of(j * BK, BK), blocks * BK)
            out = []
            for h in range(2):
                p = jnp.exp(scores[h, at, :] - tops[h]).astype(BF16)
                out.append(accs[h] + matmul(vx[h, :, at], p))
            return tuple(out)

        accs = sweep(tab_ref, i, weigh, (jnp.zeros((HDIM + 16, BQ), F32),) * 2)
        for h in range(2):
            total = accs[h][HDIM : HDIM + 1, :]
            ot_ref[h * HDIM : (h + 1) * HDIM, cols] = (accs[h][:HDIM, :] / total).astype(BF16)
            lse_ref[0, h : h + 1, cols] = tops[h] + jnp.log(total)
        return 0

    lax.fori_loop(0, tokens // BQ, block, 0)

    def finish(part, here, there):
        o_refs[part][here, :] = ot_ref[:, there].astype(F32).T.astype(BF16)

    each_block(tab_ref, parts, width, finish)


def three_parts(x):
    high = x.astype(BF16)
    rest = x - high.astype(F32)
    middle = rest.astype(BF16)
    return high, middle, (rest - middle.astype(F32)).astype(BF16)


def backward_kernel(parts, tab_ref, kseg_ref, qseg_ref, *refs):
    qkv_refs, do_refs = refs[:parts], refs[parts : 2 * parts]
    ot_ref, lse_ref = refs[2 * parts : 2 * parts + 2]
    out_refs = refs[2 * parts + 2 : 3 * parts + 2]
    kx, vx, kt, qx, dox, qt, dot, dq, dk, dv = refs[3 * parts + 2 :]
    tokens = kt.shape[1]
    width = tokens // parts
    lane = lax.broadcasted_iota(jnp.int32, (BK, 128), 1)
    sub = lax.broadcasted_iota(jnp.int32, (HDIM, BK), 0)
    one0 = jnp.where((lane >= HDIM) & (lane < HDIM + 3), 1.0, 0.0).astype(BF16)
    one1 = jnp.where(lane < 3, 1.0, 0.0).astype(BF16)
    zero = jnp.zeros((BK, 128), BF16)

    def extra(x):
        high, middle, low = (e.astype(F32) for e in three_parts(x))
        rows = jnp.where(
            sub == 0, high, jnp.where(sub == 1, middle, jnp.where(sub == 2, low, 0.0))
        )
        return rows.astype(BF16)

    def prepare(part, here, there):
        k = qkv_refs[part][here, PAIR : 2 * PAIR]
        kt[:, there] = k.astype(F32).T.astype(BF16)
        kx[0, there, :] = jnp.where(lane < HDIM, k, one0)
        kx[1, there, :] = jnp.where(lane < HDIM, one1, k)
        v = qkv_refs[part][here, 2 * PAIR :]
        vx[0, there, :] = jnp.where(lane < HDIM, v, one0)
        vx[1, there, :] = jnp.where(lane < HDIM, one1, v)
        q = qkv_refs[part][here, :PAIR]
        qt[0, there, :] = jnp.where(lane < HDIM, q, zero)
        qt[1, there, :] = jnp.where(lane < HDIM, zero, q)
        do = do_refs[part][here, :]
        dot[0, there, :] = jnp.where(lane < HDIM, do, zero)
        dot[1, there, :] = jnp.where(lane < HDIM, zero, do)
        turned = do.astype(F32).T
        prod = turned * ot_ref[:, there].astype(F32)
        inner0 = jnp.sum(prod[:HDIM], axis=0, keepdims=True)
        inner1 = jnp.sum(prod[HDIM:], axis=0, keepdims=True)
        turned = turned.astype(BF16)
        dox[0, :HDIM, there] = turned[:HDIM]
        dox[0, HDIM:, there] = extra(-inner0)
        dox[1, HDIM:, there] = turned[HDIM:]
        dox[1, :HDIM, there] = extra(-inner1)
        turned = q.astype(F32).T.astype(BF16)
        qx[0, :HDIM, there] = turned[:HDIM]
        qx[0, HDIM:, there] = extra(-lse_ref[0, 0:1, there])
        qx[1, HDIM:, there] = turned[HDIM:]
        qx[1, :HDIM, there] = extra(-lse_ref[0, 1:2, there])
        dk[there, :] = jnp.zeros((BK, 128), F32)
        dv[there, :] = jnp.zeros((BK, 128), F32)

    each_block(tab_ref, parts, width, prepare)

    def block(i, _):
        cols = pl.ds(pl.multiple_of(i * BQ, BQ), BQ)

        def step(blocks, j, carry):
            at = pl.ds(pl.multiple_of(j * BK, BK), blocks * BK)
            ok = allowed(kseg_ref, qseg_ref, i, j, blocks)
            new = []
            dvs = dv[at, :]
            dks = dk[at, :]
            for h in range(2):
                s = matmul(kx[h, at, :], qx[h, :, cols])
                s = jnp.where(ok, s, masked_score)
                p = jnp.exp(s)
                dp = matmul(vx[h, at, :], dox[h, :, cols])
                ds = (p * dp).astype(BF16)
                dvs = dvs + matmul(p.astype(BF16), dot[h, cols, :])
                dks = dks + matmul(ds, qt[h, cols, :])
                new.append(carry[h] + matmul(kt[h * HDIM : (h + 1) * HDIM, at], ds))
            dv[at, :] = dvs
            dk[at, :] = dks
            return tuple(new)

        init = tuple(jnp.zeros((HDIM, BQ), F32) for _ in range(2))
        res = sweep(tab_ref, i, step, init)
        for h in range(2):
            dq[h * HDIM : (h + 1) * HDIM, cols] = res[h] * (HDIM**-0.5)
        return 0

    lax.fori_loop(0, tokens // BQ, block, 0)

    def finish(part, here, there):
        out_refs[part][here, :PAIR] = dq[:, there].T.astype(BF16)
        out_refs[part][here, PAIR : 2 * PAIR] = dk[there, :].astype(BF16)
        out_refs[part][here, 2 * PAIR :] = dv[there, :].astype(BF16)

    each_block(tab_ref, parts, width, finish)


def lanes_of(first, step):
    return lambda g, t: (0, first + step * g)


def attend_specs(qkv_parts, chunk):
    parts = len(qkv_parts)
    width = qkv_parts[0].shape[0]
    tokens = parts * width
    every = qkv_parts[0].shape[1] // (3 * PAIR)
    pairs = every // chunk[1]
    first = pairs * chunk[0]
    seg_specs = [
        pl.BlockSpec((tokens, 1), lambda g, t: (0, 0)),
        pl.BlockSpec((1, tokens), lambda g, t: (0, 0)),
    ]
    qkv_specs = [pl.BlockSpec((width, 3 * PAIR), lanes_of(first, 1))] * parts
    o_specs = [pl.BlockSpec((width, PAIR), lanes_of(first, 1))] * parts
    ot_spec = pl.BlockSpec((PAIR, tokens), lambda g, t: (first + g, 0))
    lse_spec = pl.BlockSpec((1, 2, tokens), lambda g, t: (first + g, 0, 0))
    return parts, width, tokens, every, pairs, seg_specs, qkv_specs, o_specs, ot_spec, lse_spec


def attend_forward(qkv_parts, seg, keep, tables, chunk, begun=()):
    parts, width, tokens, every, pairs, seg_specs, qkv_specs, o_specs, ot_spec, lse_spec = (
        attend_specs(qkv_parts, chunk)
    )
    kseg = jnp.where(keep == 1, seg, -1)[:, None]
    return pl.pallas_call(
        functools.partial(forward_kernel, parts),
        grid_spec=pltpu.PrefetchScalarGridSpec(
            num_scalar_prefetch=1,
            grid=(pairs,),
            in_specs=seg_specs + qkv_specs + [pl.BlockSpec(memory_space=pl.ANY)] * len(begun),
            out_specs=o_specs + [ot_spec, lse_spec],
            scratch_shapes=[
                pltpu.VMEM((2, tokens, 128), BF16),
                pltpu.VMEM((2, HDIM + 16, tokens), BF16),
                pltpu.VMEM((PAIR, tokens), BF16),
                pltpu.VMEM((2, tokens, BQ), F32),
            ],
        ),
        out_shape=[jax.ShapeDtypeStruct((width, every * PAIR), BF16)] * parts
        + [
            jax.ShapeDtypeStruct((every * PAIR, tokens), BF16),
            jax.ShapeDtypeStruct((every, 2, tokens), F32),
        ],
        compiler_params=pltpu.CompilerParams(vmem_limit_bytes=40 * 2**20),
        cost_estimate=pl.CostEstimate(
            flops=3000 * tokens * tokens * pairs, bytes_accessed=2**23, transcendentals=0
        ),
        input_output_aliases={3 + parts + n: n for n in range(len(begun))},
        name="attend_forward",
    )(tables, kseg, seg[None, :], *qkv_parts, *begun)


def attend_backward(qkv_parts, turned, grad_ctx, lse, seg, keep, tables, chunk, work):
    parts, width, tokens, every, pairs, seg_specs, qkv_specs, o_specs, ot_spec, lse_spec = (
        attend_specs(qkv_parts, chunk)
    )
    kseg = jnp.where(keep == 1, seg, -1)[:, None]
    return pl.pallas_call(
        functools.partial(backward_kernel, parts),
        grid_spec=pltpu.PrefetchScalarGridSpec(
            num_scalar_prefetch=1,
            grid=(pairs,),
            in_specs=seg_specs + qkv_specs + o_specs + [ot_spec, lse_spec],
            out_specs=[pl.BlockSpec((width, 3 * PAIR), lanes_of(0, 1))] * parts,
            scratch_shapes=[
                pltpu.VMEM((2, tokens, 128), BF16),
                pltpu.VMEM((2, tokens, 128), BF16),
                pltpu.VMEM((PAIR, tokens), BF16),
                pltpu.VMEM((2, 128, tokens), BF16),
                pltpu.VMEM((2, 128, tokens), BF16),
                pltpu.VMEM((2, tokens, 128), BF16),
                pltpu.VMEM((2, tokens, 128), BF16),
                pltpu.VMEM((PAIR, tokens), F32),
                pltpu.VMEM((tokens, 128), F32),
                pltpu.VMEM((tokens, 128), F32),
            ],
        ),
        out_shape=[jax.ShapeDtypeStruct((width, pairs * 3 * PAIR), BF16)] * parts,
        compiler_params=pltpu.CompilerParams(vmem_limit_bytes=48 * 2**20),
        cost_estimate=pl.CostEstimate(
            flops=work * tokens * tokens * pairs, bytes_accessed=2**10, transcendentals=0
        ),
        name="attend_backward",
    )(tables, kseg, seg[None, :], *qkv_parts, *grad_ctx, turned, lse)


def row_block(width):
    return FEED_ROWS if width % FEED_ROWS == 0 else width


def gelu_and_slope(u):
    root = 0.7978845608028654
    square = u * u
    t = jnp.tanh(u * (root + (root * 0.044715) * square))
    half = 0.5 * t + 0.5
    slope = half + (0.5 * u) * (1.0 - t * t) * (root + (root * 0.134145) * square)
    return u * half, slope


def feed_kernel(step, x_ref, up_ref, bias_ref, down_ref, *refs):
    x_all, hidden_all, slope_all, out_ref = refs[-4:]
    x = x_ref[...]
    x_all[...] = x
    units = up_ref.shape[1]
    total = None
    for first in range(0, units, step):
        at = slice(first, first + step)
        act, slope = gelu_and_slope(matmul(x, up_ref[:, at]) + bias_ref[:, at])
        act = act.astype(BF16)
        hidden_all[:, at] = act
        slope_all[:, at] = slope.astype(BF16)
        term = matmul(act, down_ref[at, :])
        total = term if total is None else total + term
    out_ref[...] = total.astype(BF16)


def feed_forward(part, parts, x, up, bias, down, begun):
    width, model = x.shape
    units = up.shape[1]
    rows = row_block(width)
    steps = width // rows
    own = lambda k: (k, 0)
    whole = lambda k: (part * steps + k, 0)
    fixed = lambda k: (0, 0)
    once = pl.Buffered(1)
    every = parts * width
    return pl.pallas_call(
        functools.partial(feed_kernel, min(units, FEED)),
        grid=(steps,),
        in_specs=[
            pl.BlockSpec((rows, model), own),
            pl.BlockSpec((model, units), fixed, pipeline_mode=once),
            pl.BlockSpec((1, units), fixed, pipeline_mode=once),
            pl.BlockSpec((units, model), fixed, pipeline_mode=once),
        ]
        + [pl.BlockSpec(memory_space=pl.ANY)] * len(begun),
        out_specs=[
            pl.BlockSpec((rows, model), whole),
            pl.BlockSpec((rows, units), whole),
            pl.BlockSpec((rows, units), whole),
            pl.BlockSpec((rows, model), own),
        ],
        out_shape=[
            jax.ShapeDtypeStruct((every, model), BF16),
            jax.ShapeDtypeStruct((every, units), BF16),
            jax.ShapeDtypeStruct((every, units), BF16),
            jax.ShapeDtypeStruct((width, model), BF16),
        ],
        input_output_aliases={4 + n: n for n in range(len(begun))},
        compiler_params=pltpu.CompilerParams(vmem_limit_bytes=48 * 2**20),
        cost_estimate=pl.CostEstimate(
            flops=6 * width * model * units, bytes_accessed=2**24, transcendentals=0
        ),
        name="feed_forward",
    )(x, up, bias[None, :], down, *begun)


def feed_back_kernel(step, g_ref, slope_ref, down_ref, up_ref, *refs):
    pre_all, sums_ref, out_ref = refs[-3:]
    g = g_ref[...]
    units = up_ref.shape[1]

    @pl.when(pl.program_id(0) == 0)
    def _():
        sums_ref[...] = jnp.zeros_like(sums_ref)

    total = None
    for first in range(0, units, step):
        at = slice(first, first + step)
        pre = contract_cols(g, down_ref[at, :]) * slope_ref[:, at].astype(F32)
        pre = pre.astype(BF16)
        pre_all[:, at] = pre
        sums_ref[:, at] += jnp.sum(pre.astype(F32), axis=0, keepdims=True)
        term = contract_cols(pre, up_ref[:, at])
        total = term if total is None else total + term
    out_ref[...] = total.astype(BF16)


def feed_back(part, parts, g, slope_all, up, down, begun):
    width, model = g.shape
    units = up.shape[1]
    rows = row_block(width)
    steps = width // rows
    own = lambda k: (k, 0)
    whole = lambda k: (part * steps + k, 0)
    fixed = lambda k: (0, 0)
    once = pl.Buffered(1)
    every = parts * width
    return pl.pallas_call(
        functools.partial(feed_back_kernel, min(units, FEED)),
        grid=(steps,),
        in_specs=[
            pl.BlockSpec((rows, model), own),
            pl.BlockSpec((rows, units), whole),
            pl.BlockSpec((units, model), fixed, pipeline_mode=once),
            pl.BlockSpec((model, units), fixed, pipeline_mode=once),
        ]
        + [pl.BlockSpec(memory_space=pl.ANY)] * len(begun),
        out_specs=[
            pl.BlockSpec((rows, units), whole),
            pl.BlockSpec((1, units), fixed),
            pl.BlockSpec((rows, model), own),
        ],
        out_shape=[
            jax.ShapeDtypeStruct((every, units), BF16),
            jax.ShapeDtypeStruct((1, units), F32),
            jax.ShapeDtypeStruct((width, model), BF16),
        ],
        input_output_aliases={4 + n: n for n in range(len(begun))},
        compiler_params=pltpu.CompilerParams(vmem_limit_bytes=48 * 2**20),
        cost_estimate=pl.CostEstimate(
            flops=6 * width * model * units, bytes_accessed=2**24, transcendentals=0
        ),
        name="feed_back",
    )(g, slope_all, down, up, *begun)


def after(value, *others):
    return lax.optimization_barrier((value, *others))[0]


class Layout:
    def __init__(self, mesh):
        self.dp, self.n = mesh.shape["dp"], mesh.shape["mp"]
        self.pairs = self.dp // 2
        self.axes = ("dp", "mp")

    def device(self, pair, core, m):
        return (2 * pair + core) * self.n + m

    def at_rank(self, pair, group, rank):
        return self.device(pair, rank % 2, group * (self.n // 2) + rank // 2)

    def each(self):
        for pair in range(self.pairs):
            for group in range(2):
                for rank in range(self.n):
                    yield pair, group, rank

    def stays(self):
        core, m = lax.axis_index("dp") % 2, lax.axis_index("mp")
        return (m // (self.n // 2) == core) & (self.rank() == m)

    def send(self, value, back=False):
        moves = [(self.device(p, g, r), self.at_rank(p, g, r)) for p, g, r in self.each()]
        return lax.ppermute(
            value, self.axes, [(b, a) if back else (a, b) for a, b in moves if a != b]
        )

    def regroup(self, value):
        return jnp.where(self.stays(), value, self.send(value))

    def give_back(self, value):
        return jnp.where(self.stays(), value, self.send(value, True))

    def partner(self, value, bit, only=lambda p, g, r: True):
        def other(p, c):
            return (p, 1 - c) if bit < 0 else (p ^ (1 << bit), c)

        moves = [
            (self.device(*other(p, c), m), self.device(p, c, m))
            for p, c, m in self.each()
            if only(p, c, m)
        ]
        return lax.ppermute(value, self.axes, moves)

    def side(self, bit):
        dp = lax.axis_index("dp")
        return dp % 2 if bit < 0 else (dp // 2 >> bit) % 2

    def joined(self, mine, theirs, bit):
        high = self.side(bit) == 1
        return jnp.concatenate(
            [jnp.where(high, theirs, mine), jnp.where(high, mine, theirs)], 0
        )

    def regroup_first(self, weight, tokens):
        rows = weight.shape[0] // 4
        part = 2 * self.side(0) + self.side(1)
        quarter = lax.dynamic_slice_in_dim(weight, part * rows, rows, 0)
        got = self.send(quarter)
        tokens = self.regroup(after(tokens, got))
        for bit in (1, 0):
            got = self.joined(got, self.partner(got, bit, self.moving), bit)
        return jnp.where(self.stays(), weight, got), tokens

    def moving(self, pair, core, m):
        return self.at_rank(pair, core, m) != self.device(pair, core, m)

    def to_rank(self, value, ahead):
        moves = [
            (self.at_rank(p, g, r), self.at_rank(p, g, (r + ahead) % self.n))
            for p, g, r in self.each()
        ]
        return lax.ppermute(value, self.axes, moves)

    def rank(self):
        core = lax.axis_index("dp") % 2
        return (lax.axis_index("mp") % (self.n // 2)) * 2 + core

    def gather(self, mine):
        return [mine] + [self.to_rank(mine, self.n - k) for k in range(1, self.n)]

    def scatter_sum(self, shares):
        total = shares[0].astype(jnp.float32)
        for k in range(1, self.n):
            total = total + self.to_rank(shares[k].astype(jnp.bfloat16), k).astype(jnp.float32)
        return total

    def sum_all(self, value):
        devices = self.dp * self.n
        steps = [1 << k for k in range(devices.bit_length() - 1)]
        within = self.n.bit_length() - 1
        for step in steps[within:] + steps[:within]:
            value = value + lax.ppermute(value, self.axes, [(i, i ^ step) for i in range(devices)])
        return value

    def sum_dp(self, value, turn):
        order = [(i + turn) % self.dp for i in range(self.dp)]
        return lax.psum(value, "dp", axis_index_groups=[order])

    def weight_sum_by_halves(self, grad):
        value = self.give_back(grad)
        bits = [-1, *range(self.pairs.bit_length() - 1)]
        for bit in bits:
            half, high = value.shape[0] // 2, self.side(bit)
            sent = lax.dynamic_slice_in_dim(value, (1 - high) * half, half, 0)
            kept = lax.dynamic_slice_in_dim(value, high * half, half, 0)
            got = self.partner(sent, bit)
            value = (kept.astype(jnp.float32) + got.astype(jnp.float32)).astype(jnp.bfloat16)
        for bit in bits[::-1]:
            value = self.joined(value, self.partner(value, bit), bit)
        return value.astype(jnp.float32)


def for_kernel(shares, rank):
    width = shares[0].shape[0]
    if width % BQ == 0:
        return shares, rank * (width // BQ)
    return [jnp.roll(jnp.concatenate(shares, 0), rank * width, 0)], 0


def from_kernel(arrays, rank, shares):
    if len(arrays) == shares:
        return arrays
    width = arrays[0].shape[0] // shares
    return jnp.split(jnp.roll(arrays[0], -rank * width, 0), shares, 0)


def by_pairs(weight, pairs):
    return (
        weight.reshape(-1, 3, pairs, PAIR).transpose(0, 2, 1, 3).reshape(-1, 3 * pairs * PAIR)
    )


def total(terms):
    return functools.reduce(jnp.add, terms)


def body(
    layout,
    tokens,
    ln1_gain,
    ln1_bias,
    w_qkv,
    qv_bias,
    w_out,
    out_bias,
    ln2_gain,
    ln2_bias,
    ln3_gain,
    ln3_bias,
    w_up,
    up_bias,
    w_down,
    down_bias,
    ln4_gain,
    ln4_bias,
    row_grid,
    pad_mask,
    cotangent,
):
    f32, bf16 = jnp.float32, jnp.bfloat16
    model_dim = tokens.shape[1]
    group_rows = pad_mask.shape[0]
    width = w_qkv.shape[2]
    units = w_up.shape[1]
    shares = layout.n
    rank = layout.rank()

    small = jnp.concatenate(
        [
            qv_bias.reshape(-1),
            up_bias,
            pad_mask.astype(f32),
            row_grid[0].astype(f32),
        ]
    )
    small = layout.regroup(small)
    qv_bias = small[: 2 * width].reshape(2, width)
    up_bias = small[2 * width : 2 * width + units]
    keep = small[2 * width + units : 2 * width + units + group_rows].astype(jnp.int32)
    grid_row = small[2 * width + units + group_rows :].astype(jnp.int32)
    pairs = width // PAIR
    chunks = 2 if pairs % 2 == 0 else 1
    pairs = width // PAIR
    chunks = 2 if pairs % 2 == 0 else 1
    w_qkv, tokens = layout.regroup_first(w_qkv, tokens)
    w_qkv = by_pairs(w_qkv, pairs)
    half = units // 2
    w_out_far = layout.send(after(w_out, tokens))
    w_up_far = layout.send(after(w_up, tokens))
    w_top_far = layout.send(after(w_down[:half], tokens))
    w_low_far = layout.send(after(w_down[half:], w_up_far))
    cotangent = layout.regroup(after(cotangent, w_top_far))

    resid_in = tokens.astype(f32)
    norm1_out, normed1, inv1 = norm_parts(resid_in, ln1_gain, ln1_bias)
    a1 = layout.gather(norm1_out.astype(bf16))
    zeros = jnp.zeros((width,), f32)
    qkv_bias = by_pairs(jnp.concatenate([qv_bias[0], zeros, qv_bias[1]]), pairs)
    qkv_scale = by_pairs(
        jnp.concatenate([zeros + HDIM ** (-0.5), zeros + 1.0, zeros + 1.0]), pairs
    )
    qkv = [((matmul(x, w_qkv) + qkv_bias) * qkv_scale).astype(bf16) for x in a1]
    qkv, turn = for_kernel(qkv, rank)
    seg, tables = row_tables(grid_row, group_rows, turn)
    begun = ()
    for pair in range(pairs):
        if pair and pair == pairs // 2:
            tables, w_out_far, w_up_far = lax.optimization_barrier((tables, w_out_far, w_up_far))
        if pair and pair == pairs - 1:
            tables, w_top_far = lax.optimization_barrier((tables, w_top_far))
        begun = attend_forward(qkv, seg, keep, tables, (pair, pairs), begun)
    *context, context_turned, log_total = begun
    context = from_kernel(context, rank, shares)
    stays = layout.stays()
    w_out = jnp.where(stays, w_out, w_out_far)
    w_up = jnp.where(stays, w_up, w_up_far)
    w_down = jnp.where(stays, w_down, jnp.concatenate([w_top_far, w_low_far], 0))
    branch_z = layout.scatter_sum([matmul(x, w_out) for x in context]) + out_bias
    norm2_out, normed2, inv2 = norm_parts(branch_z, ln2_gain, ln2_bias)
    resid_mid = resid_in + norm2_out
    norm3_out, normed3, inv3 = norm_parts(resid_mid, ln3_gain, ln3_bias)
    a3 = layout.gather(norm3_out.astype(bf16))
    begun, shares_f = (), []
    for part, x in enumerate(a3):
        *begun, share = feed_forward(part, shares, x, w_up, up_bias, w_down, begun)
        shares_f.append(share)
    a3_all, hidden, slope = begun
    branch_f = layout.scatter_sum(shares_f) + down_bias
    norm4_out, normed4, inv4 = norm_parts(branch_f, ln4_gain, ln4_bias)
    layer_out = (resid_mid + norm4_out).astype(bf16)

    upstream = cotangent.astype(f32)
    grad_f = norm_back(upstream, normed4, inv4, ln4_gain).astype(bf16)
    grad_f_all = layout.gather(grad_f)
    g_w_down = contract_rows(hidden, jnp.concatenate(grad_f_all, 0)).astype(bf16)
    begun, shares_a3, g_up_bias = (), [], []
    for part, g in enumerate(grad_f_all):
        if part:
            g, g_w_down = lax.optimization_barrier((g, g_w_down))
        *begun, unit_sums, share = feed_back(part, shares, g, slope, w_up, w_down, begun)
        shares_a3.append(share)
        g_up_bias.append(unit_sums[0])
    [grad_pre] = begun
    g_w_down_far = layout.send(g_w_down, True)
    grad_a3 = layout.scatter_sum(shares_a3)
    g_up_bias = total(g_up_bias)
    g_w_up = contract_rows(a3_all, grad_pre).astype(bf16)
    g_w_up_far = layout.send(after(g_w_up, g_w_down_far), True)
    grad_mid = upstream + norm_back(grad_a3, normed3, inv3, ln3_gain)
    grad_z = norm_back(grad_mid, normed2, inv2, ln2_gain).astype(bf16)
    grad_z_all = layout.gather(grad_z)
    grad_ctx = [contract_cols(g, w_out).astype(bf16) for g in grad_z_all]
    g_w_out = total([contract_rows(x, g) for x, g in zip(context, grad_z_all)]).astype(bf16)
    g_w_out_far = layout.send(g_w_out, True)
    layer_out = layout.give_back(after(layer_out, g_w_out_far))
    grad_ctx, _ = for_kernel(grad_ctx, rank)
    g_w_down = jnp.where(stays, g_w_down, g_w_down_far)
    tables, g_w_down = lax.optimization_barrier((tables, g_w_down))
    g_w_down = layout.sum_dp(g_w_down, 1).astype(f32)
    grad_a1, g_w_qkv, sums = [], [], []
    for chunk in range(chunks):
        grad_qkv = attend_backward(
            qkv, context_turned, grad_ctx, log_total, seg, keep, tables, (chunk, chunks), 4000 * (chunk == 0)
        )
        grad_qkv = from_kernel(grad_qkv, rank, shares)
        columns = grad_qkv[0].shape[1]
        w_part = w_qkv[:, chunk * columns : (chunk + 1) * columns]
        grad_a1.append([contract_cols(g, w_part) for g in grad_qkv])
        sums.append(total([jnp.sum(g.astype(f32), 0) for g in grad_qkv]))
        g_part = total([contract_rows(x, g) for x, g in zip(a1, grad_qkv)]).astype(bf16)
        if chunk == 0:
            g_w_up_far, g_w_out_far, g_part = lax.optimization_barrier(
                (g_w_up_far, g_w_out_far, g_part)
            )
            g_w_up = jnp.where(stays, g_w_up, g_w_up_far)
            g_w_out = jnp.where(stays, g_w_out, g_w_out_far)
            tables, g_w_up, g_w_out, g_part = lax.optimization_barrier(
                (tables, g_w_up, g_w_out, g_part)
            )
            g_w_up = layout.sum_dp(g_w_up, 0).astype(f32)
            g_w_out = layout.sum_dp(g_w_out, 0).astype(f32)
        g_w_qkv.append(layout.weight_sum_by_halves(g_part))
    g_w_qkv = (
        jnp.concatenate(g_w_qkv, 1)
        .reshape(model_dim, pairs, 3, PAIR)
        .transpose(0, 2, 1, 3)
        .reshape(model_dim, 3, width)
    )
    sums = jnp.concatenate(sums).reshape(pairs, 3, PAIR).transpose(1, 0, 2).reshape(3, width)
    grad_a1 = layout.scatter_sum([total(terms) for terms in zip(*grad_a1)])
    grad_input = grad_mid + norm_back(grad_a1, normed1, inv1, ln1_gain)
    grad_input = layout.give_back(grad_input.astype(bf16)).astype(f32)

    norm_terms = jnp.stack(
        [
            jnp.sum(grad_a1 * normed1, 0),
            jnp.sum(grad_a1, 0),
            jnp.sum(grad_z.astype(f32), 0),
            jnp.sum(grad_mid * normed2, 0),
            jnp.sum(grad_mid, 0),
            jnp.sum(grad_a3 * normed3, 0),
            jnp.sum(grad_a3, 0),
            jnp.sum(grad_f.astype(f32), 0),
            jnp.sum(upstream * normed4, 0),
            jnp.sum(upstream, 0),
        ],
        0,
    )
    all_units = lax.dynamic_update_slice(jnp.zeros((units * shares,), f32), g_up_bias, (rank * units,))
    all_width = lax.dynamic_update_slice(
        jnp.zeros((2, width * shares), f32), jnp.stack([sums[0], sums[2]], 0), (0, rank * width)
    )
    small = layout.sum_all(
        jnp.concatenate([norm_terms.reshape(-1), all_width.reshape(-1), all_units])
    )
    norm_terms = small[: 10 * model_dim].reshape(10, model_dim)
    all_width = small[10 * model_dim : 12 * model_dim].reshape(2, width * shares)
    all_units = small[12 * model_dim :]
    m = lax.axis_index("mp")
    g_qv_bias = lax.dynamic_slice(all_width, (0, m * width), (2, width))
    g_up_bias = lax.dynamic_slice(all_units, (m * units,), (units,))
    return (
        layer_out,
        grad_input,
        norm_terms[0],
        norm_terms[1],
        g_w_qkv,
        g_qv_bias,
        g_w_out,
        norm_terms[2],
        norm_terms[3],
        norm_terms[4],
        norm_terms[5],
        norm_terms[6],
        g_w_up,
        g_up_bias,
        g_w_down,
        norm_terms[7],
        norm_terms[8],
        norm_terms[9],
    )


def solution(mesh):
    in_specs = (
        P(("dp", "mp"), None),
        P(),
        P(),
        P(None, None, "mp"),
        P(None, "mp"),
        P("mp", None),
        P(),
        P(),
        P(),
        P(),
        P(),
        P(None, "mp"),
        P("mp"),
        P("mp", None),
        P(),
        P(),
        P(),
        P("dp", None),
        P("dp"),
        P(("dp", "mp"), None),
    )
    out_specs = (
        P(("dp", "mp"), None),
        P(("dp", "mp"), None),
        P(),
        P(),
        P(None, None, "mp"),
        P(None, "mp"),
        P("mp", None),
        P(),
        P(),
        P(),
        P(),
        P(),
        P(None, "mp"),
        P("mp"),
        P("mp", None),
        P(),
        P(),
        P(),
    )
    return jax.shard_map(functools.partial(body, Layout(mesh)), mesh=mesh, in_specs=in_specs, out_specs=out_specs, check_vma=False)
```

```python
import functools

import jax
import jax.numpy as jnp
from jax import lax
from jax.experimental import pallas as pl
from jax.experimental.pallas import tpu as pltpu
from jax.sharding import PartitionSpec as P

HDIM = 64
TEXT = 64


epsilon = 1e-05
masked_score = -1e30


def norm_parts(values, ln_gain, ln_bias):
    centred = values - jnp.mean(values, -1, keepdims=True)
    inv_std = lax.rsqrt(jnp.mean(centred * centred, -1, keepdims=True) + epsilon)
    normed = centred * inv_std
    return (normed * ln_gain + ln_bias, normed, inv_std)


def norm_back(upstream, normed, inv_std, ln_gain):
    scaled = upstream * ln_gain
    return inv_std * (
        scaled
        - jnp.mean(scaled, -1, keepdims=True)
        - normed * jnp.mean(scaled * normed, -1, keepdims=True)
    )


def contract_rows(left, right):
    return lax.dot_general(
        left, right, (((0,), (0,)), ((), ())), preferred_element_type=jnp.float32
    )


def contract_cols(left, right):
    return lax.dot_general(
        left, right, (((1,), (1,)), ((), ())), preferred_element_type=jnp.float32
    )


BQ = 256
BK = 256
MOST = 4
FEED = 1024
FEED_ROWS = 640
PAIR = 2 * HDIM
F32 = jnp.float32
BF16 = jnp.bfloat16


def matmul(left, right):
    return jnp.dot(left, right, preferred_element_type=F32)


def row_tables(grid_row, tokens, turn):
    side = jnp.max(grid_row)
    length = TEXT + side * side
    rows = tokens // length
    used = rows * length
    position = jnp.arange(tokens, dtype=jnp.int32)
    seg = jnp.minimum(position // length, rows)
    blocks = tokens // BQ
    first = jnp.arange(blocks, dtype=jnp.int32) * BQ
    start = jnp.where(first < used, (first // length) * length, first)
    low = start // BK
    diag = first // BK
    turns = jnp.full((blocks,), turn, jnp.int32)
    return seg, jnp.stack([low, diag, turns]).astype(jnp.int32)


def allowed(kseg_ref, qseg_ref, i, j, blocks):
    qs = qseg_ref[:, pl.ds(pl.multiple_of(i * BQ, BQ), BQ)]
    ks = kseg_ref[pl.ds(pl.multiple_of(j * BK, BK), blocks * BK), :]
    ik = j * BK + lax.broadcasted_iota(jnp.int32, (blocks * BK, BQ), 0)
    iq = i * BQ + lax.broadcasted_iota(jnp.int32, (blocks * BK, BQ), 1)
    return ((ks == qs) & (ik <= iq)) | (ik == iq)


def sweep(tab_ref, i, step, carry):
    return several(tab_ref[0, i], tab_ref[1, i] + 1, step, carry)


def several(first, stop, step, carry, most=MOST):
    while most > 1:
        turns = (stop - first) // most

        def turn(n, carry, first=first, most=most):
            return step(most, first + most * n, carry)

        carry = lax.fori_loop(0, turns, turn, carry)
        first, most = first + most * turns, most // 2
    return lax.fori_loop(first, stop, functools.partial(step, 1), carry)


def each_block(tab_ref, parts, width, work):
    blocks = width // BQ
    count = blocks * parts
    for part in range(parts):

        def one(c, _, part=part):
            whole = lax.rem(tab_ref[2, 0] + part * blocks + c, count)
            work(
                part,
                pl.ds(pl.multiple_of(c * BQ, BQ), BQ),
                pl.ds(pl.multiple_of(whole * BQ, BQ), BQ),
            )
            return 0

        lax.fori_loop(0, blocks, one, 0)


def forward_kernel(parts, tab_ref, kseg_ref, qseg_ref, *refs):
    qkv_refs = refs[:parts]
    *o_refs, ot_ref, lse_ref, kx, vx, qx, scores = refs[-6 - parts :]
    tokens = qx.shape[1]
    width = tokens // parts
    lane = lax.broadcasted_iota(jnp.int32, (BK, 128), 1)
    zero = jnp.zeros((BK, 128), BF16)

    def prepare(part, here, there):
        k = qkv_refs[part][here, PAIR : 2 * PAIR]
        kx[0, there, :] = jnp.where(lane < HDIM, k, zero)
        kx[1, there, :] = jnp.where(lane < HDIM, zero, k)
        qx[:, there] = qkv_refs[part][here, :PAIR].astype(F32).T.astype(BF16)
        v = qkv_refs[part][here, 2 * PAIR :].astype(F32).T.astype(BF16)
        for h in range(2):
            vx[h, :HDIM, there] = v[h * HDIM : (h + 1) * HDIM]
            vx[h, HDIM:, there] = jnp.ones((16, BQ), BF16)

    each_block(tab_ref, parts, width, prepare)

    def block(i, _):
        cols = pl.ds(pl.multiple_of(i * BQ, BQ), BQ)
        qb = qx[:, cols]

        def score(blocks, j, tops):
            at = pl.ds(pl.multiple_of(j * BK, BK), blocks * BK)
            ok = allowed(kseg_ref, qseg_ref, i, j, blocks)
            out = []
            for h in range(2):
                s = matmul(kx[h, at, :], qb)
                s = jnp.where(ok, s, masked_score)
                scores[h, at, :] = s
                out.append(jnp.maximum(tops[h], jnp.max(s.reshape(blocks * BK // 8, 8, BQ), axis=0)))
            return tuple(out)

        tops = sweep(tab_ref, i, score, (jnp.full((8, BQ), masked_score, F32),) * 2)
        tops = [jnp.max(top, axis=0, keepdims=True) for top in tops]

        def weigh(blocks, j, accs):
            at = pl.ds(pl.multiple_of(j * BK, BK), blocks * BK)
            out = []
            for h in range(2):
                p = jnp.exp(scores[h, at, :] - tops[h]).astype(BF16)
                out.append(accs[h] + matmul(vx[h, :, at], p))
            return tuple(out)

        accs = sweep(tab_ref, i, weigh, (jnp.zeros((HDIM + 16, BQ), F32),) * 2)
        for h in range(2):
            total = accs[h][HDIM : HDIM + 1, :]
            ot_ref[h * HDIM : (h + 1) * HDIM, cols] = (accs[h][:HDIM, :] / total).astype(BF16)
            lse_ref[0, h : h + 1, cols] = tops[h] + jnp.log(total)
        return 0

    lax.fori_loop(0, tokens // BQ, block, 0)

    def finish(part, here, there):
        o_refs[part][here, :] = ot_ref[:, there].astype(F32).T.astype(BF16)

    each_block(tab_ref, parts, width, finish)


def three_parts(x):
    high = x.astype(BF16)
    rest = x - high.astype(F32)
    middle = rest.astype(BF16)
    return high, middle, (rest - middle.astype(F32)).astype(BF16)


def backward_kernel(parts, tab_ref, kseg_ref, qseg_ref, *refs):
    qkv_refs, do_refs = refs[:parts], refs[parts : 2 * parts]
    ot_ref, lse_ref = refs[2 * parts : 2 * parts + 2]
    *out_refs, kx, vx, kt, qx, dox, qt, dot, dq, dk, dv = refs[-10 - parts :]
    tokens = kt.shape[1]
    width = tokens // parts
    lane = lax.broadcasted_iota(jnp.int32, (BK, 128), 1)
    sub = lax.broadcasted_iota(jnp.int32, (HDIM, BK), 0)
    one0 = jnp.where((lane >= HDIM) & (lane < HDIM + 3), 1.0, 0.0).astype(BF16)
    one1 = jnp.where(lane < 3, 1.0, 0.0).astype(BF16)
    zero = jnp.zeros((BK, 128), BF16)

    def extra(x):
        high, middle, low = (e.astype(F32) for e in three_parts(x))
        rows = jnp.where(
            sub == 0, high, jnp.where(sub == 1, middle, jnp.where(sub == 2, low, 0.0))
        )
        return rows.astype(BF16)

    def prepare(part, here, there):
        k = qkv_refs[part][here, PAIR : 2 * PAIR]
        kt[:, there] = k.astype(F32).T.astype(BF16)
        kx[0, there, :] = jnp.where(lane < HDIM, k, one0)
        kx[1, there, :] = jnp.where(lane < HDIM, one1, k)
        v = qkv_refs[part][here, 2 * PAIR :]
        vx[0, there, :] = jnp.where(lane < HDIM, v, one0)
        vx[1, there, :] = jnp.where(lane < HDIM, one1, v)
        q = qkv_refs[part][here, :PAIR]
        qt[0, there, :] = jnp.where(lane < HDIM, q, zero)
        qt[1, there, :] = jnp.where(lane < HDIM, zero, q)
        do = do_refs[part][here, :]
        dot[0, there, :] = jnp.where(lane < HDIM, do, zero)
        dot[1, there, :] = jnp.where(lane < HDIM, zero, do)
        turned = do.astype(F32).T
        prod = turned * ot_ref[:, there].astype(F32)
        inner0 = jnp.sum(prod[:HDIM], axis=0, keepdims=True)
        inner1 = jnp.sum(prod[HDIM:], axis=0, keepdims=True)
        turned = turned.astype(BF16)
        dox[0, :HDIM, there] = turned[:HDIM]
        dox[0, HDIM:, there] = extra(-inner0)
        dox[1, HDIM:, there] = turned[HDIM:]
        dox[1, :HDIM, there] = extra(-inner1)
        turned = q.astype(F32).T.astype(BF16)
        qx[0, :HDIM, there] = turned[:HDIM]
        qx[0, HDIM:, there] = extra(-lse_ref[0, 0:1, there])
        qx[1, HDIM:, there] = turned[HDIM:]
        qx[1, :HDIM, there] = extra(-lse_ref[0, 1:2, there])
        dk[there, :] = jnp.zeros((BK, 128), F32)
        dv[there, :] = jnp.zeros((BK, 128), F32)

    each_block(tab_ref, parts, width, prepare)

    def block(i, _):
        cols = pl.ds(pl.multiple_of(i * BQ, BQ), BQ)

        def step(blocks, j, carry):
            at = pl.ds(pl.multiple_of(j * BK, BK), blocks * BK)
            ok = allowed(kseg_ref, qseg_ref, i, j, blocks)
            new = []
            dvs = dv[at, :]
            dks = dk[at, :]
            for h in range(2):
                s = matmul(kx[h, at, :], qx[h, :, cols])
                s = jnp.where(ok, s, masked_score)
                p = jnp.exp(s)
                dp = matmul(vx[h, at, :], dox[h, :, cols])
                ds = (p * dp).astype(BF16)
                dvs = dvs + matmul(p.astype(BF16), dot[h, cols, :])
                dks = dks + matmul(ds, qt[h, cols, :])
                new.append(carry[h] + matmul(kt[h * HDIM : (h + 1) * HDIM, at], ds))
            dv[at, :] = dvs
            dk[at, :] = dks
            return tuple(new)

        init = tuple(jnp.zeros((HDIM, BQ), F32) for _ in range(2))
        res = sweep(tab_ref, i, step, init)
        for h in range(2):
            dq[h * HDIM : (h + 1) * HDIM, cols] = res[h] * (HDIM**-0.5)
        return 0

    lax.fori_loop(0, tokens // BQ, block, 0)

    def finish(part, here, there):
        out_refs[part][here, :PAIR] = dq[:, there].T.astype(BF16)
        out_refs[part][here, PAIR : 2 * PAIR] = dk[there, :].astype(BF16)
        out_refs[part][here, 2 * PAIR :] = dv[there, :].astype(BF16)

    each_block(tab_ref, parts, width, finish)


def lanes_of(first, step):
    return lambda g, t: (0, first + step * g)


def attend_specs(qkv_parts, chunk):
    parts = len(qkv_parts)
    width = qkv_parts[0].shape[0]
    tokens = parts * width
    every = qkv_parts[0].shape[1] // (3 * PAIR)
    pairs = every // chunk[1]
    first = pairs * chunk[0]
    seg_specs = [
        pl.BlockSpec((tokens, 1), lambda g, t: (0, 0)),
        pl.BlockSpec((1, tokens), lambda g, t: (0, 0)),
    ]
    qkv_specs = [pl.BlockSpec((width, 3 * PAIR), lanes_of(first, 1))] * parts
    o_specs = [pl.BlockSpec((width, PAIR), lanes_of(first, 1))] * parts
    ot_spec = pl.BlockSpec((PAIR, tokens), lambda g, t: (first + g, 0))
    lse_spec = pl.BlockSpec((1, 2, tokens), lambda g, t: (first + g, 0, 0))
    return parts, width, tokens, every, pairs, seg_specs, qkv_specs, o_specs, ot_spec, lse_spec


def attend_forward(qkv_parts, seg, keep, tables, chunk, begun=()):
    parts, width, tokens, every, pairs, seg_specs, qkv_specs, o_specs, ot_spec, lse_spec = (
        attend_specs(qkv_parts, chunk)
    )
    kseg = jnp.where(keep == 1, seg, -1)[:, None]
    return pl.pallas_call(
        functools.partial(forward_kernel, parts),
        grid_spec=pltpu.PrefetchScalarGridSpec(
            num_scalar_prefetch=1,
            grid=(pairs,),
            in_specs=seg_specs + qkv_specs + [pl.BlockSpec(memory_space=pl.ANY)] * len(begun),
            out_specs=o_specs + [ot_spec, lse_spec],
            scratch_shapes=[
                pltpu.VMEM((2, tokens, 128), BF16),
                pltpu.VMEM((2, HDIM + 16, tokens), BF16),
                pltpu.VMEM((PAIR, tokens), BF16),
                pltpu.VMEM((2, tokens, BQ), F32),
            ],
        ),
        out_shape=[jax.ShapeDtypeStruct((width, every * PAIR), BF16)] * parts
        + [
            jax.ShapeDtypeStruct((every * PAIR, tokens), BF16),
            jax.ShapeDtypeStruct((every, 2, tokens), F32),
        ],
        compiler_params=pltpu.CompilerParams(vmem_limit_bytes=40 * 2**20),
        cost_estimate=pl.CostEstimate(
            flops=3000 * tokens * tokens * pairs, bytes_accessed=2**23, transcendentals=0
        ),
        input_output_aliases={3 + parts + n: n for n in range(len(begun))},
        name="attend_forward",
    )(tables, kseg, seg[None, :], *qkv_parts, *begun)


def attend_backward(qkv_parts, turned, grad_ctx, lse, seg, keep, tables, chunk, place, begun=()):
    parts, width, tokens, every, pairs, seg_specs, qkv_specs, o_specs, ot_spec, lse_spec = (
        attend_specs(qkv_parts, chunk)
    )
    kseg = jnp.where(keep == 1, seg, -1)[:, None]
    result = pl.BlockSpec((width, 3 * PAIR), lanes_of(place[0] * pairs, 1))
    return pl.pallas_call(
        functools.partial(backward_kernel, parts),
        grid_spec=pltpu.PrefetchScalarGridSpec(
            num_scalar_prefetch=1,
            grid=(pairs,),
            in_specs=seg_specs
            + qkv_specs
            + o_specs
            + [ot_spec, lse_spec]
            + [pl.BlockSpec(memory_space=pl.ANY)] * len(begun),
            out_specs=[result] * parts,
            scratch_shapes=[
                pltpu.VMEM((2, tokens, 128), BF16),
                pltpu.VMEM((2, tokens, 128), BF16),
                pltpu.VMEM((PAIR, tokens), BF16),
                pltpu.VMEM((2, 128, tokens), BF16),
                pltpu.VMEM((2, 128, tokens), BF16),
                pltpu.VMEM((2, tokens, 128), BF16),
                pltpu.VMEM((2, tokens, 128), BF16),
                pltpu.VMEM((PAIR, tokens), F32),
                pltpu.VMEM((tokens, 128), F32),
                pltpu.VMEM((tokens, 128), F32),
            ],
        ),
        out_shape=[jax.ShapeDtypeStruct((width, place[1] * pairs * 3 * PAIR), BF16)] * parts,
        input_output_aliases={5 + 2 * parts + n: n for n in range(len(begun))},
        compiler_params=pltpu.CompilerParams(vmem_limit_bytes=48 * 2**20),
        cost_estimate=pl.CostEstimate(
            flops=(4000 if chunk[0] < chunk[1] - 1 else 0) * tokens * tokens * pairs,
            bytes_accessed=2**10,
            transcendentals=0,
        ),
        name="attend_backward",
    )(tables, kseg, seg[None, :], *qkv_parts, *grad_ctx, turned, lse, *begun)


def row_block(width):
    return FEED_ROWS if width % FEED_ROWS == 0 else width


def gelu_and_slope(u):
    root = 0.7978845608028654
    square = u * u
    t = jnp.tanh(u * (root + (root * 0.044715) * square))
    half = 0.5 * t + 0.5
    slope = half + (0.5 * u) * (1.0 - t * t) * (root + (root * 0.134145) * square)
    return u * half, slope


def feed_kernel(step, x_ref, up_ref, bias_ref, down_ref, *refs):
    x_all, hidden_all, slope_all, out_ref = refs[-4:]
    x = x_ref[...]
    x_all[...] = x
    units = up_ref.shape[1]
    total = None
    for first in range(0, units, step):
        at = slice(first, first + step)
        act, slope = gelu_and_slope(matmul(x, up_ref[:, at]) + bias_ref[:, at])
        act = act.astype(BF16)
        hidden_all[:, at] = act
        slope_all[:, at] = slope.astype(BF16)
        term = matmul(act, down_ref[at, :])
        total = term if total is None else total + term
    out_ref[...] = total.astype(BF16)


def feed_forward(part, parts, x, up, bias, down, begun):
    width, model = x.shape
    units = up.shape[1]
    rows = row_block(width)
    steps = width // rows
    own = lambda k: (k, 0)
    whole = lambda k: (part * steps + k, 0)
    fixed = lambda k: (0, 0)
    once = pl.Buffered(1)
    every = parts * width
    return pl.pallas_call(
        functools.partial(feed_kernel, min(units, FEED)),
        grid=(steps,),
        in_specs=[
            pl.BlockSpec((rows, model), own),
            pl.BlockSpec((model, units), fixed, pipeline_mode=once),
            pl.BlockSpec((1, units), fixed, pipeline_mode=once),
            pl.BlockSpec((units, model), fixed, pipeline_mode=once),
        ]
        + [pl.BlockSpec(memory_space=pl.ANY)] * len(begun),
        out_specs=[
            pl.BlockSpec((rows, model), whole),
            pl.BlockSpec((rows, units), whole),
            pl.BlockSpec((rows, units), whole),
            pl.BlockSpec((rows, model), own),
        ],
        out_shape=[
            jax.ShapeDtypeStruct((every, model), BF16),
            jax.ShapeDtypeStruct((every, units), BF16),
            jax.ShapeDtypeStruct((every, units), BF16),
            jax.ShapeDtypeStruct((width, model), BF16),
        ],
        input_output_aliases={4 + n: n for n in range(len(begun))},
        compiler_params=pltpu.CompilerParams(vmem_limit_bytes=48 * 2**20),
        cost_estimate=pl.CostEstimate(
            flops=6 * width * model * units, bytes_accessed=2**24, transcendentals=0
        ),
        name="feed_forward",
    )(x, up, bias[None, :], down, *begun)


def feed_back_kernel(step, g_ref, slope_ref, down_ref, up_ref, *refs):
    pre_all, sums_ref, out_ref = refs[-3:]
    g = g_ref[...]
    units = up_ref.shape[1]

    @pl.when(pl.program_id(0) == 0)
    def _():
        sums_ref[...] = jnp.zeros_like(sums_ref)

    total = None
    for first in range(0, units, step):
        at = slice(first, first + step)
        pre = contract_cols(g, down_ref[at, :]) * slope_ref[:, at].astype(F32)
        pre = pre.astype(BF16)
        pre_all[:, at] = pre
        sums_ref[:, at] += jnp.sum(pre.astype(F32), axis=0, keepdims=True)
        term = contract_cols(pre, up_ref[:, at])
        total = term if total is None else total + term
    out_ref[...] = total.astype(BF16)


def feed_back(part, parts, g, slope_all, up, down, begun):
    width, model = g.shape
    units = up.shape[1]
    rows = row_block(width)
    steps = width // rows
    own = lambda k: (k, 0)
    whole = lambda k: (part * steps + k, 0)
    fixed = lambda k: (0, 0)
    once = pl.Buffered(1)
    every = parts * width
    return pl.pallas_call(
        functools.partial(feed_back_kernel, min(units, FEED)),
        grid=(steps,),
        in_specs=[
            pl.BlockSpec((rows, model), own),
            pl.BlockSpec((rows, units), whole),
            pl.BlockSpec((units, model), fixed, pipeline_mode=once),
            pl.BlockSpec((model, units), fixed, pipeline_mode=once),
        ]
        + [pl.BlockSpec(memory_space=pl.ANY)] * len(begun),
        out_specs=[
            pl.BlockSpec((rows, units), whole),
            pl.BlockSpec((1, units), fixed),
            pl.BlockSpec((rows, model), own),
        ],
        out_shape=[
            jax.ShapeDtypeStruct((every, units), BF16),
            jax.ShapeDtypeStruct((1, units), F32),
            jax.ShapeDtypeStruct((width, model), BF16),
        ],
        input_output_aliases={4 + n: n for n in range(len(begun))},
        compiler_params=pltpu.CompilerParams(vmem_limit_bytes=48 * 2**20),
        cost_estimate=pl.CostEstimate(
            flops=6 * width * model * units, bytes_accessed=2**24, transcendentals=0
        ),
        name="feed_back",
    )(g, slope_all, down, up, *begun)


def after(value, *others):
    return lax.optimization_barrier((value, *others))[0]


class Layout:
    def __init__(self, mesh):
        self.dp, self.n = mesh.shape["dp"], mesh.shape["mp"]
        self.pairs = self.dp // 2
        self.axes = ("dp", "mp")

    def device(self, pair, core, m):
        return (2 * pair + core) * self.n + m

    def at_rank(self, pair, group, rank):
        return self.device(pair, rank % 2, group * (self.n // 2) + rank // 2)

    def each(self):
        for pair in range(self.pairs):
            for group in range(2):
                for rank in range(self.n):
                    yield pair, group, rank

    def stays(self):
        core, m = lax.axis_index("dp") % 2, lax.axis_index("mp")
        return (m // (self.n // 2) == core) & (self.rank() == m)

    def send(self, value, back=False):
        moves = [(self.device(p, g, r), self.at_rank(p, g, r)) for p, g, r in self.each()]
        return lax.ppermute(
            value, self.axes, [(b, a) if back else (a, b) for a, b in moves if a != b]
        )

    def regroup(self, value):
        return jnp.where(self.stays(), value, self.send(value))

    def give_back(self, value):
        return jnp.where(self.stays(), value, self.send(value, True))

    def partner(self, value, bit, only=lambda p, g, r: True):
        def other(p, c):
            return (p, 1 - c) if bit < 0 else (p ^ (1 << bit), c)

        moves = [
            (self.device(*other(p, c), m), self.device(p, c, m))
            for p, c, m in self.each()
            if only(p, c, m)
        ]
        return lax.ppermute(value, self.axes, moves)

    def side(self, bit):
        dp = lax.axis_index("dp")
        return dp % 2 if bit < 0 else (dp // 2 >> bit) % 2

    def joined(self, mine, theirs, bit):
        high = self.side(bit) == 1
        return jnp.concatenate(
            [jnp.where(high, theirs, mine), jnp.where(high, mine, theirs)], 0
        )

    def regroup_first(self, weight, small, tokens):
        rows = weight.shape[0] // 4
        part = 2 * self.side(0) + self.side(1)
        quarter = lax.dynamic_slice_in_dim(weight, part * rows, rows, 0)
        got = self.send(quarter)
        small = self.regroup(after(small, got))
        tokens = self.regroup(after(tokens, got, small))
        for bit in (1, 0):
            got = self.joined(got, self.partner(got, bit, self.moving), bit)
        return jnp.where(self.stays(), weight, got), small, tokens

    def moving(self, pair, core, m):
        return self.at_rank(pair, core, m) != self.device(pair, core, m)

    def to_rank(self, value, ahead):
        moves = [
            (self.at_rank(p, g, r), self.at_rank(p, g, (r + ahead) % self.n))
            for p, g, r in self.each()
        ]
        return lax.ppermute(value, self.axes, moves)

    def rank(self):
        core = lax.axis_index("dp") % 2
        return (lax.axis_index("mp") % (self.n // 2)) * 2 + core

    def gather(self, mine):
        return [mine] + [self.to_rank(mine, self.n - k) for k in range(1, self.n)]

    def scatter_sum(self, shares):
        total = shares[0].astype(jnp.float32)
        for k in range(1, self.n):
            total = total + self.to_rank(shares[k].astype(jnp.bfloat16), k).astype(jnp.float32)
        return total

    def sum_all(self, value):
        devices = self.dp * self.n
        steps = [1 << k for k in range(devices.bit_length() - 1)]
        within = self.n.bit_length() - 1
        for step in steps[within:] + steps[:within]:
            value = value + lax.ppermute(value, self.axes, [(i, i ^ step) for i in range(devices)])
        return value

    def sum_dp(self, value, turn):
        order = [(i + turn) % self.dp for i in range(self.dp)]
        return lax.psum(value, "dp", axis_index_groups=[order])

    def halved(self, value, bit):
        half, high = value.shape[0] // 2, self.side(bit)
        sent = lax.dynamic_slice_in_dim(value, (1 - high) * half, half, 0)
        kept = lax.dynamic_slice_in_dim(value, high * half, half, 0)
        got = self.partner(sent, bit)
        return (kept.astype(jnp.float32) + got.astype(jnp.float32)).astype(jnp.bfloat16)

    def bits(self):
        return list(range(self.pairs.bit_length() - 1))

    def sum_rest(self, value, bits):
        for bit in bits:
            value = self.halved(value, bit)
        for bit in [*self.bits()[::-1], -1]:
            value = self.joined(value, self.partner(value, bit), bit)
        return value


def for_kernel(shares, rank):
    width = shares[0].shape[0]
    if width % BQ == 0:
        return shares, rank * (width // BQ)
    return [jnp.roll(jnp.concatenate(shares, 0), rank * width, 0)], 0


def from_kernel(arrays, rank, shares):
    if len(arrays) == shares:
        return arrays
    width = arrays[0].shape[0] // shares
    return jnp.split(jnp.roll(arrays[0], -rank * width, 0), shares, 0)


def by_pairs(weight, pairs):
    return (
        weight.reshape(-1, 3, pairs, PAIR).transpose(0, 2, 1, 3).reshape(-1, 3 * pairs * PAIR)
    )


def total(terms):
    return functools.reduce(jnp.add, terms)


def body(
    layout,
    tokens,
    ln1_gain,
    ln1_bias,
    w_qkv,
    qv_bias,
    w_out,
    out_bias,
    ln2_gain,
    ln2_bias,
    ln3_gain,
    ln3_bias,
    w_up,
    up_bias,
    w_down,
    down_bias,
    ln4_gain,
    ln4_bias,
    row_grid,
    pad_mask,
    cotangent,
):
    f32, bf16 = jnp.float32, jnp.bfloat16
    model_dim = tokens.shape[1]
    group_rows = pad_mask.shape[0]
    width = w_qkv.shape[2]
    units = w_up.shape[1]
    shares = layout.n
    rank = layout.rank()

    small = jnp.concatenate(
        [
            qv_bias.reshape(-1),
            up_bias,
            pad_mask.astype(f32),
            row_grid[0].astype(f32),
        ]
    )
    pairs = width // PAIR
    chunks = 2 if pairs % 2 == 0 else 1
    w_qkv, small, tokens = layout.regroup_first(w_qkv, small, tokens)
    qv_bias = small[: 2 * width].reshape(2, width)
    up_bias = small[2 * width : 2 * width + units]
    keep = small[2 * width + units : 2 * width + units + group_rows].astype(jnp.int32)
    grid_row = small[2 * width + units + group_rows :].astype(jnp.int32)
    w_qkv = by_pairs(w_qkv, pairs)
    half = units // 2
    w_out_far = layout.send(after(w_out, tokens))
    w_up_far = layout.send(after(w_up, w_out_far))
    w_top_far = layout.send(after(w_down[:half], w_up_far))
    w_low_far = layout.send(after(w_down[half:], w_top_far))
    cotangent = layout.regroup(after(cotangent, w_low_far))

    resid_in = tokens.astype(f32)
    norm1_out, normed1, inv1 = norm_parts(resid_in, ln1_gain, ln1_bias)
    a1 = layout.gather(norm1_out.astype(bf16))
    zeros = jnp.zeros((width,), f32)
    qkv_bias = by_pairs(jnp.concatenate([qv_bias[0], zeros, qv_bias[1]]), pairs)
    qkv_scale = by_pairs(
        jnp.concatenate([zeros + HDIM ** (-0.5), zeros + 1.0, zeros + 1.0]), pairs
    )
    qkv = [((matmul(x, w_qkv) + qkv_bias) * qkv_scale).astype(bf16) for x in a1]
    qkv, turn = for_kernel(qkv, rank)
    seg, tables = row_tables(grid_row, group_rows, turn)
    begun = ()
    for pair in range(pairs):
        if pair and pair == pairs // 2:
            tables, w_out_far, w_up_far = lax.optimization_barrier((tables, w_out_far, w_up_far))
        if pair and pair == pairs - 1:
            tables, w_top_far = lax.optimization_barrier((tables, w_top_far))
        begun = attend_forward(qkv, seg, keep, tables, (pair, pairs), begun)
    *context, context_turned, log_total = begun
    context = from_kernel(context, rank, shares)
    stays = layout.stays()
    w_out = jnp.where(stays, w_out, w_out_far)
    w_up = jnp.where(stays, w_up, w_up_far)
    w_down = jnp.where(stays, w_down, jnp.concatenate([w_top_far, w_low_far], 0))
    branch_z = layout.scatter_sum([matmul(x, w_out) for x in context]) + out_bias
    norm2_out, normed2, inv2 = norm_parts(branch_z, ln2_gain, ln2_bias)
    resid_mid = resid_in + norm2_out
    norm3_out, normed3, inv3 = norm_parts(resid_mid, ln3_gain, ln3_bias)
    a3 = layout.gather(norm3_out.astype(bf16))
    begun, shares_f = (), []
    for part, x in enumerate(a3):
        if part == shares - 1:
            x, cotangent = lax.optimization_barrier((x, cotangent))
        *begun, share = feed_forward(part, shares, x, w_up, up_bias, w_down, begun)
        shares_f.append(share)
    a3_all, hidden, slope = begun
    branch_f = layout.scatter_sum(shares_f) + down_bias
    norm4_out, normed4, inv4 = norm_parts(branch_f, ln4_gain, ln4_bias)
    layer_out = (resid_mid + norm4_out).astype(bf16)

    upstream = cotangent.astype(f32)
    grad_f = norm_back(upstream, normed4, inv4, ln4_gain).astype(bf16)
    grad_f_all = layout.gather(grad_f)
    g_w_down = contract_rows(hidden, jnp.concatenate(grad_f_all, 0)).astype(bf16)
    begun, shares_a3, g_up_bias = (), [], []
    for part, g in enumerate(grad_f_all):
        if part:
            g, g_w_down = lax.optimization_barrier((g, g_w_down))
        *begun, unit_sums, share = feed_back(part, shares, g, slope, w_up, w_down, begun)
        shares_a3.append(share)
        g_up_bias.append(unit_sums[0])
    [grad_pre] = begun
    g_w_down_far = layout.send(g_w_down, True)
    grad_a3 = layout.scatter_sum(shares_a3)
    g_up_bias = total(g_up_bias)
    g_w_up = contract_rows(a3_all, grad_pre).astype(bf16)
    g_w_up_far = layout.send(after(g_w_up, g_w_down_far), True)
    grad_mid = upstream + norm_back(grad_a3, normed3, inv3, ln3_gain)
    grad_z = norm_back(grad_mid, normed2, inv2, ln2_gain).astype(bf16)
    grad_z_all = layout.gather(grad_z)
    grad_ctx = [contract_cols(g, w_out).astype(bf16) for g in grad_z_all]
    g_w_out = total([contract_rows(x, g) for x, g in zip(context, grad_z_all)]).astype(bf16)
    g_w_out_far = layout.send(g_w_out, True)
    layer_out = layout.give_back(after(layer_out, g_w_out_far))
    grad_ctx, _ = for_kernel(grad_ctx, rank)
    g_w_down = jnp.where(stays, g_w_down, g_w_down_far)
    g_w_down = layout.halved(g_w_down, -1)
    tables, g_w_down = lax.optimization_barrier((tables, g_w_down))
    bits = layout.bits()
    grad_a1, g_w_qkv, sums, done = [], [], [], []
    each = pairs // chunks
    for chunk in range(chunks):
        grad_qkv = ()
        for slot in range(each):
            pair = chunk * each + slot
            if pair and bits:
                g_w_down = layout.halved(g_w_down, bits.pop(0))
                tables, g_w_down = lax.optimization_barrier((tables, g_w_down))
            if pair and pair == pairs - 1:
                tables, g_w_qkv[0] = lax.optimization_barrier((tables, g_w_qkv[0]))
            grad_qkv = attend_backward(
                qkv,
                context_turned,
                grad_ctx,
                log_total,
                seg,
                keep,
                tables,
                (pair, pairs),
                (slot, each),
                grad_qkv,
            )
        grad_qkv = from_kernel(grad_qkv, rank, shares)
        done.append(grad_qkv)
        g_part = total([contract_rows(x, g) for x, g in zip(a1, grad_qkv)]).astype(bf16)
        if chunk == 0:
            g_w_up_far, g_w_out_far, g_part = lax.optimization_barrier(
                (g_w_up_far, g_w_out_far, g_part)
            )
            g_w_up = jnp.where(stays, g_w_up, g_w_up_far)
            g_w_out = jnp.where(stays, g_w_out, g_w_out_far)
            tables, g_w_up, g_w_out, g_part = lax.optimization_barrier(
                (tables, g_w_up, g_w_out, g_part)
            )
            g_w_up = layout.sum_dp(g_w_up, 0)
            g_w_out = layout.sum_dp(g_w_out, 0)
        g_w_qkv.append(layout.halved(layout.give_back(g_part), -1))
    done = lax.optimization_barrier(done)
    g_w_down = layout.sum_rest(g_w_down, bits)
    for chunk, grad_qkv in enumerate(done):
        columns = grad_qkv[0].shape[1]
        w_part = w_qkv[:, chunk * columns : (chunk + 1) * columns]
        grad_a1.append([contract_cols(g, w_part) for g in grad_qkv])
        sums.append(total([jnp.sum(g.astype(f32), 0) for g in grad_qkv]))
    g_w_qkv = jnp.concatenate([layout.sum_rest(g, layout.bits()) for g in g_w_qkv], 1).astype(f32)
    g_w_qkv = (
        g_w_qkv.reshape(model_dim, pairs, 3, PAIR)
        .transpose(0, 2, 1, 3)
        .reshape(model_dim, 3, width)
    )
    sums = jnp.concatenate(sums).reshape(pairs, 3, PAIR).transpose(1, 0, 2).reshape(3, width)
    grad_a1 = layout.scatter_sum([total(terms) for terms in zip(*grad_a1)])
    grad_input = grad_mid + norm_back(grad_a1, normed1, inv1, ln1_gain)
    grad_input = layout.give_back(grad_input.astype(bf16)).astype(f32)

    norm_terms = jnp.stack(
        [
            jnp.sum(grad_a1 * normed1, 0),
            jnp.sum(grad_a1, 0),
            jnp.sum(grad_z.astype(f32), 0),
            jnp.sum(grad_mid * normed2, 0),
            jnp.sum(grad_mid, 0),
            jnp.sum(grad_a3 * normed3, 0),
            jnp.sum(grad_a3, 0),
            jnp.sum(grad_f.astype(f32), 0),
            jnp.sum(upstream * normed4, 0),
            jnp.sum(upstream, 0),
        ],
        0,
    )
    all_units = lax.dynamic_update_slice(jnp.zeros((units * shares,), f32), g_up_bias, (rank * units,))
    all_width = lax.dynamic_update_slice(
        jnp.zeros((2, width * shares), f32), jnp.stack([sums[0], sums[2]], 0), (0, rank * width)
    )
    small = layout.sum_all(
        jnp.concatenate([norm_terms.reshape(-1), all_width.reshape(-1), all_units])
    )
    norm_terms = small[: 10 * model_dim].reshape(10, model_dim)
    all_width = small[10 * model_dim : 12 * model_dim].reshape(2, width * shares)
    all_units = small[12 * model_dim :]
    m = lax.axis_index("mp")
    g_qv_bias = lax.dynamic_slice(all_width, (0, m * width), (2, width))
    g_up_bias = lax.dynamic_slice(all_units, (m * units,), (units,))
    g_w_up, g_w_out, g_w_qkv, grad_input, g_qv_bias = lax.optimization_barrier(
        (g_w_up, g_w_out, g_w_qkv, grad_input, g_qv_bias)
    )
    return (
        layer_out,
        grad_input,
        norm_terms[0],
        norm_terms[1],
        g_w_qkv,
        g_qv_bias,
        g_w_out.astype(f32),
        norm_terms[2],
        norm_terms[3],
        norm_terms[4],
        norm_terms[5],
        norm_terms[6],
        g_w_up.astype(f32),
        g_up_bias,
        g_w_down.astype(f32),
        norm_terms[7],
        norm_terms[8],
        norm_terms[9],
    )


def solution(mesh):
    in_specs = (
        P(("dp", "mp"), None),
        P(),
        P(),
        P(None, None, "mp"),
        P(None, "mp"),
        P("mp", None),
        P(),
        P(),
        P(),
        P(),
        P(),
        P(None, "mp"),
        P("mp"),
        P("mp", None),
        P(),
        P(),
        P(),
        P("dp", None),
        P("dp"),
        P(("dp", "mp"), None),
    )
    out_specs = (
        P(("dp", "mp"), None),
        P(("dp", "mp"), None),
        P(),
        P(),
        P(None, None, "mp"),
        P(None, "mp"),
        P("mp", None),
        P(),
        P(),
        P(),
        P(),
        P(),
        P(None, "mp"),
        P("mp"),
        P("mp", None),
        P(),
        P(),
        P(),
    )
    return jax.shard_map(functools.partial(body, Layout(mesh)), mesh=mesh, in_specs=in_specs, out_specs=out_specs, check_vma=False)
```

```python
import functools

import jax
import jax.numpy as jnp
from jax import lax
from jax.experimental import pallas as pl
from jax.experimental.pallas import tpu as pltpu
from jax.sharding import PartitionSpec as P

HDIM = 64
TEXT = 64


epsilon = 1e-05
masked_score = -1e30


def norm_parts(values, ln_gain, ln_bias):
    centred = values - jnp.mean(values, -1, keepdims=True)
    inv_std = lax.rsqrt(jnp.mean(centred * centred, -1, keepdims=True) + epsilon)
    normed = centred * inv_std
    return (normed * ln_gain + ln_bias, normed, inv_std)


def norm_back(upstream, normed, inv_std, ln_gain):
    scaled = upstream * ln_gain
    return inv_std * (
        scaled
        - jnp.mean(scaled, -1, keepdims=True)
        - normed * jnp.mean(scaled * normed, -1, keepdims=True)
    )


def contract_rows(left, right):
    return lax.dot_general(
        left, right, (((0,), (0,)), ((), ())), preferred_element_type=jnp.float32
    )


def contract_cols(left, right):
    return lax.dot_general(
        left, right, (((1,), (1,)), ((), ())), preferred_element_type=jnp.float32
    )


BQ = 256
BK = 256
MOST = 4
FEED = 1024
FEED_ROWS = 640
PAIR = 2 * HDIM
F32 = jnp.float32
BF16 = jnp.bfloat16


def matmul(left, right):
    return jnp.dot(left, right, preferred_element_type=F32)


def row_tables(grid_row, tokens, turn):
    side = jnp.max(grid_row)
    length = TEXT + side * side
    rows = tokens // length
    used = rows * length
    position = jnp.arange(tokens, dtype=jnp.int32)
    seg = jnp.minimum(position // length, rows)
    blocks = tokens // BQ
    first = jnp.arange(blocks, dtype=jnp.int32) * BQ
    start = jnp.where(first < used, (first // length) * length, first)
    low = start // BK
    diag = first // BK
    turns = jnp.full((blocks,), turn, jnp.int32)
    return seg, jnp.stack([low, diag, turns]).astype(jnp.int32)


def allowed(kseg_ref, qseg_ref, i, j, blocks):
    qs = qseg_ref[:, pl.ds(pl.multiple_of(i * BQ, BQ), BQ)]
    ks = kseg_ref[pl.ds(pl.multiple_of(j * BK, BK), blocks * BK), :]
    ik = j * BK + lax.broadcasted_iota(jnp.int32, (blocks * BK, BQ), 0)
    iq = i * BQ + lax.broadcasted_iota(jnp.int32, (blocks * BK, BQ), 1)
    return ((ks == qs) & (ik <= iq)) | (ik == iq)


def sweep(tab_ref, i, step, carry):
    return several(tab_ref[0, i], tab_ref[1, i] + 1, step, carry)


def several(first, stop, step, carry, most=MOST):
    while most > 1:
        turns = (stop - first) // most

        def turn(n, carry, first=first, most=most):
            return step(most, first + most * n, carry)

        carry = lax.fori_loop(0, turns, turn, carry)
        first, most = first + most * turns, most // 2
    return lax.fori_loop(first, stop, functools.partial(step, 1), carry)


def each_block(tab_ref, parts, width, work):
    blocks = width // BQ
    count = blocks * parts
    for part in range(parts):

        def one(c, _, part=part):
            whole = lax.rem(tab_ref[2, 0] + part * blocks + c, count)
            work(
                part,
                pl.ds(pl.multiple_of(c * BQ, BQ), BQ),
                pl.ds(pl.multiple_of(whole * BQ, BQ), BQ),
            )
            return 0

        lax.fori_loop(0, blocks, one, 0)


def forward_kernel(parts, tab_ref, kseg_ref, qseg_ref, *refs):
    qkv_refs = refs[:parts]
    *o_refs, ot_ref, lse_ref, kx, vx, qx, scores = refs[-6 - parts :]
    tokens = qx.shape[1]
    width = tokens // parts
    lane = lax.broadcasted_iota(jnp.int32, (BK, 128), 1)
    zero = jnp.zeros((BK, 128), BF16)

    def prepare(part, here, there):
        k = qkv_refs[part][here, PAIR : 2 * PAIR]
        kx[0, there, :] = jnp.where(lane < HDIM, k, zero)
        kx[1, there, :] = jnp.where(lane < HDIM, zero, k)
        qx[:, there] = qkv_refs[part][here, :PAIR].astype(F32).T.astype(BF16)
        v = qkv_refs[part][here, 2 * PAIR :].astype(F32).T.astype(BF16)
        for h in range(2):
            vx[h, :HDIM, there] = v[h * HDIM : (h + 1) * HDIM]
            vx[h, HDIM:, there] = jnp.ones((16, BQ), BF16)

    each_block(tab_ref, parts, width, prepare)

    def block(i, _):
        cols = pl.ds(pl.multiple_of(i * BQ, BQ), BQ)
        qb = qx[:, cols]

        def score(blocks, j, tops):
            at = pl.ds(pl.multiple_of(j * BK, BK), blocks * BK)
            ok = allowed(kseg_ref, qseg_ref, i, j, blocks)
            out = []
            for h in range(2):
                s = matmul(kx[h, at, :], qb)
                s = jnp.where(ok, s, masked_score)
                scores[h, at, :] = s
                out.append(jnp.maximum(tops[h], jnp.max(s.reshape(blocks * BK // 8, 8, BQ), axis=0)))
            return tuple(out)

        tops = sweep(tab_ref, i, score, (jnp.full((8, BQ), masked_score, F32),) * 2)
        tops = [jnp.max(top, axis=0, keepdims=True) for top in tops]

        def weigh(blocks, j, accs):
            at = pl.ds(pl.multiple_of(j * BK, BK), blocks * BK)
            out = []
            for h in range(2):
                p = jnp.exp(scores[h, at, :] - tops[h]).astype(BF16)
                out.append(accs[h] + matmul(vx[h, :, at], p))
            return tuple(out)

        accs = sweep(tab_ref, i, weigh, (jnp.zeros((HDIM + 16, BQ), F32),) * 2)
        for h in range(2):
            total = accs[h][HDIM : HDIM + 1, :]
            ot_ref[h * HDIM : (h + 1) * HDIM, cols] = (accs[h][:HDIM, :] / total).astype(BF16)
            lse_ref[0, h : h + 1, cols] = tops[h] + jnp.log(total)
        return 0

    lax.fori_loop(0, tokens // BQ, block, 0)

    def finish(part, here, there):
        o_refs[part][here, :] = ot_ref[:, there].astype(F32).T.astype(BF16)

    each_block(tab_ref, parts, width, finish)


def three_parts(x):
    high = x.astype(BF16)
    rest = x - high.astype(F32)
    middle = rest.astype(BF16)
    return high, middle, (rest - middle.astype(F32)).astype(BF16)


def backward_kernel(parts, tab_ref, kseg_ref, qseg_ref, *refs):
    qkv_refs, do_refs = refs[:parts], refs[parts : 2 * parts]
    ot_ref, lse_ref = refs[2 * parts : 2 * parts + 2]
    *out_refs, kx, vx, kt, qx, dox, qt, dot, dq, dk, dv = refs[-10 - parts :]
    tokens = kt.shape[1]
    width = tokens // parts
    lane = lax.broadcasted_iota(jnp.int32, (BK, 128), 1)
    sub = lax.broadcasted_iota(jnp.int32, (HDIM, BK), 0)
    one0 = jnp.where((lane >= HDIM) & (lane < HDIM + 3), 1.0, 0.0).astype(BF16)
    one1 = jnp.where(lane < 3, 1.0, 0.0).astype(BF16)
    zero = jnp.zeros((BK, 128), BF16)

    def extra(x):
        high, middle, low = (e.astype(F32) for e in three_parts(x))
        rows = jnp.where(
            sub == 0, high, jnp.where(sub == 1, middle, jnp.where(sub == 2, low, 0.0))
        )
        return rows.astype(BF16)

    def prepare(part, here, there):
        k = qkv_refs[part][here, PAIR : 2 * PAIR]
        kt[:, there] = k.astype(F32).T.astype(BF16)
        kx[0, there, :] = jnp.where(lane < HDIM, k, one0)
        kx[1, there, :] = jnp.where(lane < HDIM, one1, k)
        v = qkv_refs[part][here, 2 * PAIR :]
        vx[0, there, :] = jnp.where(lane < HDIM, v, one0)
        vx[1, there, :] = jnp.where(lane < HDIM, one1, v)
        q = qkv_refs[part][here, :PAIR]
        qt[0, there, :] = jnp.where(lane < HDIM, q, zero)
        qt[1, there, :] = jnp.where(lane < HDIM, zero, q)
        do = do_refs[part][here, :]
        dot[0, there, :] = jnp.where(lane < HDIM, do, zero)
        dot[1, there, :] = jnp.where(lane < HDIM, zero, do)
        turned = do.astype(F32).T
        prod = turned * ot_ref[:, there].astype(F32)
        inner0 = jnp.sum(prod[:HDIM], axis=0, keepdims=True)
        inner1 = jnp.sum(prod[HDIM:], axis=0, keepdims=True)
        turned = turned.astype(BF16)
        dox[0, :HDIM, there] = turned[:HDIM]
        dox[0, HDIM:, there] = extra(-inner0)
        dox[1, HDIM:, there] = turned[HDIM:]
        dox[1, :HDIM, there] = extra(-inner1)
        turned = q.astype(F32).T.astype(BF16)
        qx[0, :HDIM, there] = turned[:HDIM]
        qx[0, HDIM:, there] = extra(-lse_ref[0, 0:1, there])
        qx[1, HDIM:, there] = turned[HDIM:]
        qx[1, :HDIM, there] = extra(-lse_ref[0, 1:2, there])
        dk[there, :] = jnp.zeros((BK, 128), F32)
        dv[there, :] = jnp.zeros((BK, 128), F32)

    each_block(tab_ref, parts, width, prepare)

    def block(i, _):
        cols = pl.ds(pl.multiple_of(i * BQ, BQ), BQ)

        def step(blocks, j, carry):
            at = pl.ds(pl.multiple_of(j * BK, BK), blocks * BK)
            ok = allowed(kseg_ref, qseg_ref, i, j, blocks)
            new = []
            dvs = dv[at, :]
            dks = dk[at, :]
            for h in range(2):
                s = matmul(kx[h, at, :], qx[h, :, cols])
                s = jnp.where(ok, s, masked_score)
                p = jnp.exp(s)
                dp = matmul(vx[h, at, :], dox[h, :, cols])
                ds = (p * dp).astype(BF16)
                dvs = dvs + matmul(p.astype(BF16), dot[h, cols, :])
                dks = dks + matmul(ds, qt[h, cols, :])
                new.append(carry[h] + matmul(kt[h * HDIM : (h + 1) * HDIM, at], ds))
            dv[at, :] = dvs
            dk[at, :] = dks
            return tuple(new)

        init = tuple(jnp.zeros((HDIM, BQ), F32) for _ in range(2))
        res = sweep(tab_ref, i, step, init)
        for h in range(2):
            dq[h * HDIM : (h + 1) * HDIM, cols] = res[h] * (HDIM**-0.5)
        return 0

    lax.fori_loop(0, tokens // BQ, block, 0)

    def finish(part, here, there):
        out_refs[part][here, :PAIR] = dq[:, there].T.astype(BF16)
        out_refs[part][here, PAIR : 2 * PAIR] = dk[there, :].astype(BF16)
        out_refs[part][here, 2 * PAIR :] = dv[there, :].astype(BF16)

    each_block(tab_ref, parts, width, finish)


def lanes_of(first, step):
    return lambda g, t: (0, first + step * g)


def attend_specs(qkv_parts, chunk):
    parts = len(qkv_parts)
    width = qkv_parts[0].shape[0]
    tokens = parts * width
    every = qkv_parts[0].shape[1] // (3 * PAIR)
    pairs = every // chunk[1]
    first = pairs * chunk[0]
    seg_specs = [
        pl.BlockSpec((tokens, 1), lambda g, t: (0, 0)),
        pl.BlockSpec((1, tokens), lambda g, t: (0, 0)),
    ]
    qkv_specs = [pl.BlockSpec((width, 3 * PAIR), lanes_of(first, 1))] * parts
    o_specs = [pl.BlockSpec((width, PAIR), lanes_of(first, 1))] * parts
    ot_spec = pl.BlockSpec((PAIR, tokens), lambda g, t: (first + g, 0))
    lse_spec = pl.BlockSpec((1, 2, tokens), lambda g, t: (first + g, 0, 0))
    return parts, width, tokens, every, pairs, seg_specs, qkv_specs, o_specs, ot_spec, lse_spec


def attend_forward(qkv_parts, seg, keep, tables, chunk, begun=()):
    parts, width, tokens, every, pairs, seg_specs, qkv_specs, o_specs, ot_spec, lse_spec = (
        attend_specs(qkv_parts, chunk)
    )
    kseg = jnp.where(keep == 1, seg, -1)[:, None]
    return pl.pallas_call(
        functools.partial(forward_kernel, parts),
        grid_spec=pltpu.PrefetchScalarGridSpec(
            num_scalar_prefetch=1,
            grid=(pairs,),
            in_specs=seg_specs + qkv_specs + [pl.BlockSpec(memory_space=pl.ANY)] * len(begun),
            out_specs=o_specs + [ot_spec, lse_spec],
            scratch_shapes=[
                pltpu.VMEM((2, tokens, 128), BF16),
                pltpu.VMEM((2, HDIM + 16, tokens), BF16),
                pltpu.VMEM((PAIR, tokens), BF16),
                pltpu.VMEM((2, tokens, BQ), F32),
            ],
        ),
        out_shape=[jax.ShapeDtypeStruct((width, every * PAIR), BF16)] * parts
        + [
            jax.ShapeDtypeStruct((every * PAIR, tokens), BF16),
            jax.ShapeDtypeStruct((every, 2, tokens), F32),
        ],
        compiler_params=pltpu.CompilerParams(vmem_limit_bytes=40 * 2**20),
        cost_estimate=pl.CostEstimate(
            flops=3000 * tokens * tokens * pairs, bytes_accessed=2**23, transcendentals=0
        ),
        input_output_aliases={3 + parts + n: n for n in range(len(begun))},
        name="attend_forward",
    )(tables, kseg, seg[None, :], *qkv_parts, *begun)


def attend_backward(qkv_parts, turned, grad_ctx, lse, seg, keep, tables, chunk, place, begun=()):
    parts, width, tokens, every, pairs, seg_specs, qkv_specs, o_specs, ot_spec, lse_spec = (
        attend_specs(qkv_parts, chunk)
    )
    kseg = jnp.where(keep == 1, seg, -1)[:, None]
    result = pl.BlockSpec((width, 3 * PAIR), lanes_of(place[0] * pairs, 1))
    return pl.pallas_call(
        functools.partial(backward_kernel, parts),
        grid_spec=pltpu.PrefetchScalarGridSpec(
            num_scalar_prefetch=1,
            grid=(pairs,),
            in_specs=seg_specs
            + qkv_specs
            + o_specs
            + [ot_spec, lse_spec]
            + [pl.BlockSpec(memory_space=pl.ANY)] * len(begun),
            out_specs=[result] * parts,
            scratch_shapes=[
                pltpu.VMEM((2, tokens, 128), BF16),
                pltpu.VMEM((2, tokens, 128), BF16),
                pltpu.VMEM((PAIR, tokens), BF16),
                pltpu.VMEM((2, 128, tokens), BF16),
                pltpu.VMEM((2, 128, tokens), BF16),
                pltpu.VMEM((2, tokens, 128), BF16),
                pltpu.VMEM((2, tokens, 128), BF16),
                pltpu.VMEM((PAIR, tokens), F32),
                pltpu.VMEM((tokens, 128), F32),
                pltpu.VMEM((tokens, 128), F32),
            ],
        ),
        out_shape=[jax.ShapeDtypeStruct((width, place[1] * pairs * 3 * PAIR), BF16)] * parts,
        input_output_aliases={5 + 2 * parts + n: n for n in range(len(begun))},
        compiler_params=pltpu.CompilerParams(vmem_limit_bytes=48 * 2**20),
        cost_estimate=pl.CostEstimate(
            flops=2**10,
            bytes_accessed=2**10,
            transcendentals=0,
        ),
        name="attend_backward",
    )(tables, kseg, seg[None, :], *qkv_parts, *grad_ctx, turned, lse, *begun)


def row_block(width):
    return FEED_ROWS if width % FEED_ROWS == 0 else width


def gelu_and_slope(u):
    root = 0.7978845608028654
    square = u * u
    t = jnp.tanh(u * (root + (root * 0.044715) * square))
    half = 0.5 * t + 0.5
    slope = half + (0.5 * u) * (1.0 - t * t) * (root + (root * 0.134145) * square)
    return u * half, slope


def feed_kernel(step, x_ref, up_ref, bias_ref, down_ref, *refs):
    x_all, hidden_all, slope_all, out_ref = refs[-4:]
    x = x_ref[...]
    x_all[...] = x
    units = up_ref.shape[1]
    total = None
    for first in range(0, units, step):
        at = slice(first, first + step)
        act, slope = gelu_and_slope(matmul(x, up_ref[:, at]) + bias_ref[:, at])
        act = act.astype(BF16)
        hidden_all[:, at] = act
        slope_all[:, at] = slope.astype(BF16)
        term = matmul(act, down_ref[at, :])
        total = term if total is None else total + term
    out_ref[...] = total.astype(BF16)


def feed_forward(part, parts, x, up, bias, down, begun):
    width, model = x.shape
    units = up.shape[1]
    rows = row_block(width)
    steps = width // rows
    own = lambda k: (k, 0)
    whole = lambda k: (part * steps + k, 0)
    fixed = lambda k: (0, 0)
    once = pl.Buffered(1)
    every = parts * width
    return pl.pallas_call(
        functools.partial(feed_kernel, min(units, FEED)),
        grid=(steps,),
        in_specs=[
            pl.BlockSpec((rows, model), own),
            pl.BlockSpec((model, units), fixed, pipeline_mode=once),
            pl.BlockSpec((1, units), fixed, pipeline_mode=once),
            pl.BlockSpec((units, model), fixed, pipeline_mode=once),
        ]
        + [pl.BlockSpec(memory_space=pl.ANY)] * len(begun),
        out_specs=[
            pl.BlockSpec((rows, model), whole),
            pl.BlockSpec((rows, units), whole),
            pl.BlockSpec((rows, units), whole),
            pl.BlockSpec((rows, model), own),
        ],
        out_shape=[
            jax.ShapeDtypeStruct((every, model), BF16),
            jax.ShapeDtypeStruct((every, units), BF16),
            jax.ShapeDtypeStruct((every, units), BF16),
            jax.ShapeDtypeStruct((width, model), BF16),
        ],
        input_output_aliases={4 + n: n for n in range(len(begun))},
        compiler_params=pltpu.CompilerParams(vmem_limit_bytes=48 * 2**20),
        cost_estimate=pl.CostEstimate(
            flops=6 * width * model * units, bytes_accessed=2**24, transcendentals=0
        ),
        name="feed_forward",
    )(x, up, bias[None, :], down, *begun)


def feed_back_kernel(step, g_ref, slope_ref, down_ref, up_ref, *refs):
    pre_all, sums_ref, out_ref = refs[-3:]
    g = g_ref[...]
    units = up_ref.shape[1]

    @pl.when(pl.program_id(0) == 0)
    def _():
        sums_ref[...] = jnp.zeros_like(sums_ref)

    total = None
    for first in range(0, units, step):
        at = slice(first, first + step)
        pre = contract_cols(g, down_ref[at, :]) * slope_ref[:, at].astype(F32)
        pre = pre.astype(BF16)
        pre_all[:, at] = pre
        sums_ref[:, at] += jnp.sum(pre.astype(F32), axis=0, keepdims=True)
        term = contract_cols(pre, up_ref[:, at])
        total = term if total is None else total + term
    out_ref[...] = total.astype(BF16)


def feed_back(part, parts, g, slope_all, up, down, begun):
    width, model = g.shape
    units = up.shape[1]
    rows = row_block(width)
    steps = width // rows
    own = lambda k: (k, 0)
    whole = lambda k: (part * steps + k, 0)
    fixed = lambda k: (0, 0)
    once = pl.Buffered(1)
    every = parts * width
    return pl.pallas_call(
        functools.partial(feed_back_kernel, min(units, FEED)),
        grid=(steps,),
        in_specs=[
            pl.BlockSpec((rows, model), own),
            pl.BlockSpec((rows, units), whole),
            pl.BlockSpec((units, model), fixed, pipeline_mode=once),
            pl.BlockSpec((model, units), fixed, pipeline_mode=once),
        ]
        + [pl.BlockSpec(memory_space=pl.ANY)] * len(begun),
        out_specs=[
            pl.BlockSpec((rows, units), whole),
            pl.BlockSpec((1, units), fixed),
            pl.BlockSpec((rows, model), own),
        ],
        out_shape=[
            jax.ShapeDtypeStruct((every, units), BF16),
            jax.ShapeDtypeStruct((1, units), F32),
            jax.ShapeDtypeStruct((width, model), BF16),
        ],
        input_output_aliases={4 + n: n for n in range(len(begun))},
        compiler_params=pltpu.CompilerParams(vmem_limit_bytes=48 * 2**20),
        cost_estimate=pl.CostEstimate(
            flops=2**10, bytes_accessed=2**10, transcendentals=0
        ),
        name="feed_back",
    )(g, slope_all, down, up, *begun)


def after(value, *others):
    return lax.optimization_barrier((value, *others))[0]


class Layout:
    def __init__(self, mesh):
        self.dp, self.n = mesh.shape["dp"], mesh.shape["mp"]
        self.pairs = self.dp // 2
        self.axes = ("dp", "mp")

    def device(self, pair, core, m):
        return (2 * pair + core) * self.n + m

    def at_rank(self, pair, group, rank):
        return self.device(pair, rank % 2, group * (self.n // 2) + rank // 2)

    def each(self):
        for pair in range(self.pairs):
            for group in range(2):
                for rank in range(self.n):
                    yield pair, group, rank

    def stays(self):
        core, m = lax.axis_index("dp") % 2, lax.axis_index("mp")
        return (m // (self.n // 2) == core) & (self.rank() == m)

    def send(self, value, back=False):
        moves = [(self.device(p, g, r), self.at_rank(p, g, r)) for p, g, r in self.each()]
        return lax.ppermute(
            value, self.axes, [(b, a) if back else (a, b) for a, b in moves if a != b]
        )

    def regroup(self, value):
        return jnp.where(self.stays(), value, self.send(value))

    def give_back(self, value):
        return jnp.where(self.stays(), value, self.send(value, True))

    def partner(self, value, bit, only=lambda p, g, r: True):
        def other(p, c):
            return (p, 1 - c) if bit < 0 else (p ^ (1 << bit), c)

        moves = [
            (self.device(*other(p, c), m), self.device(p, c, m))
            for p, c, m in self.each()
            if only(p, c, m)
        ]
        return lax.ppermute(value, self.axes, moves)

    def side(self, bit):
        dp = lax.axis_index("dp")
        return dp % 2 if bit < 0 else (dp // 2 >> bit) % 2

    def joined(self, mine, theirs, bit):
        high = self.side(bit) == 1
        return jnp.concatenate(
            [jnp.where(high, theirs, mine), jnp.where(high, mine, theirs)], 0
        )

    def regroup_first(self, weight, small, tokens):
        rows = weight.shape[0] // 4
        part = 2 * self.side(0) + self.side(1)
        quarter = lax.dynamic_slice_in_dim(weight, part * rows, rows, 0)
        got = self.send(quarter)
        small = self.regroup(after(small, got))
        tokens = self.regroup(after(tokens, got, small))
        for bit in (1, 0):
            got = self.joined(got, self.partner(got, bit, self.moving), bit)
        return jnp.where(self.stays(), weight, got), small, tokens

    def moving(self, pair, core, m):
        return self.at_rank(pair, core, m) != self.device(pair, core, m)

    def to_rank(self, value, ahead):
        moves = [
            (self.at_rank(p, g, r), self.at_rank(p, g, (r + ahead) % self.n))
            for p, g, r in self.each()
        ]
        return lax.ppermute(value, self.axes, moves)

    def rank(self):
        core = lax.axis_index("dp") % 2
        return (lax.axis_index("mp") % (self.n // 2)) * 2 + core

    def gather(self, mine):
        return [mine] + [self.to_rank(mine, self.n - k) for k in range(1, self.n)]

    def scatter_sum(self, shares):
        total = shares[0].astype(jnp.float32)
        for k in range(1, self.n):
            total = total + self.to_rank(shares[k].astype(jnp.bfloat16), k).astype(jnp.float32)
        return total

    def sum_all(self, value):
        devices = self.dp * self.n
        steps = [1 << k for k in range(devices.bit_length() - 1)]
        within = self.n.bit_length() - 1
        for step in steps[within:] + steps[:within]:
            value = value + lax.ppermute(value, self.axes, [(i, i ^ step) for i in range(devices)])
        return value

    def sum_dp(self, value, turn):
        order = [(i + turn) % self.dp for i in range(self.dp)]
        return lax.psum(value, "dp", axis_index_groups=[order])

    def halved(self, value, bit):
        half, high = value.shape[0] // 2, self.side(bit)
        sent = lax.dynamic_slice_in_dim(value, (1 - high) * half, half, 0)
        kept = lax.dynamic_slice_in_dim(value, high * half, half, 0)
        got = self.partner(sent, bit)
        return (kept.astype(jnp.float32) + got.astype(jnp.float32)).astype(jnp.bfloat16)

    def bits(self):
        return list(range(self.pairs.bit_length() - 1))

    def sum_rest(self, value):
        for bit in self.bits():
            value = self.halved(value, bit)
        for bit in self.bits()[::-1]:
            value = self.joined(value, self.partner(value, bit), bit)
        return value


def for_kernel(shares, rank):
    width = shares[0].shape[0]
    if width % BQ == 0:
        return shares, rank * (width // BQ)
    return [jnp.roll(jnp.concatenate(shares, 0), rank * width, 0)], 0


def from_kernel(arrays, rank, shares):
    if len(arrays) == shares:
        return arrays
    width = arrays[0].shape[0] // shares
    return jnp.split(jnp.roll(arrays[0], -rank * width, 0), shares, 0)


def by_pairs(weight, pairs):
    return (
        weight.reshape(-1, 3, pairs, PAIR).transpose(0, 2, 1, 3).reshape(-1, 3 * pairs * PAIR)
    )


def total(terms):
    return functools.reduce(jnp.add, terms)


def body(
    layout,
    tokens,
    ln1_gain,
    ln1_bias,
    w_qkv,
    qv_bias,
    w_out,
    out_bias,
    ln2_gain,
    ln2_bias,
    ln3_gain,
    ln3_bias,
    w_up,
    up_bias,
    w_down,
    down_bias,
    ln4_gain,
    ln4_bias,
    row_grid,
    pad_mask,
    cotangent,
):
    f32, bf16 = jnp.float32, jnp.bfloat16
    model_dim = tokens.shape[1]
    group_rows = pad_mask.shape[0]
    width = w_qkv.shape[2]
    units = w_up.shape[1]
    shares = layout.n
    rank = layout.rank()

    small = jnp.concatenate(
        [
            qv_bias.reshape(-1),
            up_bias,
            pad_mask.astype(f32),
            row_grid[0].astype(f32),
        ]
    )
    pairs = width // PAIR
    chunks = 2 if pairs % 2 == 0 else 1
    w_qkv, small, tokens = layout.regroup_first(w_qkv, small, tokens)
    qv_bias = small[: 2 * width].reshape(2, width)
    up_bias = small[2 * width : 2 * width + units]
    keep = small[2 * width + units : 2 * width + units + group_rows].astype(jnp.int32)
    grid_row = small[2 * width + units + group_rows :].astype(jnp.int32)
    w_qkv = by_pairs(w_qkv, pairs)
    half = units // 2
    w_out_far = layout.send(after(w_out, tokens))
    w_up_far = layout.send(after(w_up, w_out_far))
    w_top_far = layout.send(after(w_down[:half], w_up_far))
    w_low_far = layout.send(after(w_down[half:], w_top_far))
    cotangent = layout.regroup(after(cotangent, w_low_far))

    resid_in = tokens.astype(f32)
    norm1_out, normed1, inv1 = norm_parts(resid_in, ln1_gain, ln1_bias)
    a1 = layout.gather(norm1_out.astype(bf16))
    zeros = jnp.zeros((width,), f32)
    qkv_bias = by_pairs(jnp.concatenate([qv_bias[0], zeros, qv_bias[1]]), pairs)
    qkv_scale = by_pairs(
        jnp.concatenate([zeros + HDIM ** (-0.5), zeros + 1.0, zeros + 1.0]), pairs
    )
    qkv = [((matmul(x, w_qkv) + qkv_bias) * qkv_scale).astype(bf16) for x in a1]
    qkv, turn = for_kernel(qkv, rank)
    seg, tables = row_tables(grid_row, group_rows, turn)
    begun = ()
    for pair in range(pairs):
        if pair and pair == pairs // 2:
            tables, w_out_far, w_up_far = lax.optimization_barrier((tables, w_out_far, w_up_far))
        if pair and pair == pairs - 1:
            tables, w_top_far = lax.optimization_barrier((tables, w_top_far))
        begun = attend_forward(qkv, seg, keep, tables, (pair, pairs), begun)
    *context, context_turned, log_total = begun
    *context, w_low_far = lax.optimization_barrier((*context, w_low_far))
    context = from_kernel(context, rank, shares)
    stays = layout.stays()
    w_out = jnp.where(stays, w_out, w_out_far)
    w_up = jnp.where(stays, w_up, w_up_far)
    w_down = jnp.where(stays, w_down, jnp.concatenate([w_top_far, w_low_far], 0))
    branch_z = layout.scatter_sum([matmul(x, w_out) for x in context]) + out_bias
    norm2_out, normed2, inv2 = norm_parts(branch_z, ln2_gain, ln2_bias)
    resid_mid = resid_in + norm2_out
    norm3_out, normed3, inv3 = norm_parts(resid_mid, ln3_gain, ln3_bias)
    a3 = layout.gather(norm3_out.astype(bf16))
    begun, shares_f = (), []
    for part, x in enumerate(a3):
        if part == shares - 1:
            x, cotangent = lax.optimization_barrier((x, cotangent))
        *begun, share = feed_forward(part, shares, x, w_up, up_bias, w_down, begun)
        shares_f.append(share)
    a3_all, hidden, slope = begun
    branch_f = layout.scatter_sum(shares_f) + down_bias
    norm4_out, normed4, inv4 = norm_parts(branch_f, ln4_gain, ln4_bias)
    layer_out = (resid_mid + norm4_out).astype(bf16)

    upstream = cotangent.astype(f32)
    grad_f = norm_back(upstream, normed4, inv4, ln4_gain).astype(bf16)
    grad_f_all = layout.gather(grad_f)
    g_w_down = contract_rows(hidden, jnp.concatenate(grad_f_all, 0)).astype(bf16)
    begun, shares_a3, g_up_bias = (), [], []
    for part, g in enumerate(grad_f_all):
        if part:
            g, g_w_down = lax.optimization_barrier((g, g_w_down))
        *begun, unit_sums, share = feed_back(part, shares, g, slope, w_up, w_down, begun)
        shares_a3.append(share)
        g_up_bias.append(unit_sums[0])
    [grad_pre] = begun
    g_w_down_far = layout.send(g_w_down, True)
    grad_a3 = layout.scatter_sum(shares_a3)
    g_up_bias = total(g_up_bias)
    g_w_up = contract_rows(a3_all, grad_pre).astype(bf16)
    g_w_up_far = layout.send(after(g_w_up, g_w_down_far), True)
    grad_mid = upstream + norm_back(grad_a3, normed3, inv3, ln3_gain)
    grad_z = norm_back(grad_mid, normed2, inv2, ln2_gain).astype(bf16)
    grad_z_all = layout.gather(grad_z)
    grad_ctx = [contract_cols(g, w_out).astype(bf16) for g in grad_z_all]
    g_w_out = total([contract_rows(x, g) for x, g in zip(context, grad_z_all)]).astype(bf16)
    g_w_out_far = layout.send(after(g_w_out, g_w_up_far), True)
    g_w_down_far, g_w_up, *grad_ctx = lax.optimization_barrier((g_w_down_far, g_w_up, *grad_ctx))
    grad_ctx, _ = for_kernel(grad_ctx, rank)
    g_w_down = jnp.where(stays, g_w_down, g_w_down_far)
    tables, g_w_down = lax.optimization_barrier((tables, g_w_down))
    g_w_down = layout.sum_dp(g_w_down, 1)
    grad_a1, g_w_qkv, sums, done = [], [], [], []
    each = pairs // chunks
    for chunk in range(chunks):
        calls = 1 if chunk == 0 else each
        grad_qkv = ()
        for call in range(calls):
            grad_qkv = attend_backward(
                qkv,
                context_turned,
                grad_ctx,
                log_total,
                seg,
                keep,
                tables,
                (chunk * calls + call, chunks * calls),
                (call, calls),
                grad_qkv,
            )
            if chunk and call < calls - 1:
                tables, g_w_qkv[0], *grad_qkv = lax.optimization_barrier(
                    (tables, g_w_qkv[0], *grad_qkv)
                )
        grad_qkv = from_kernel(grad_qkv, rank, shares)
        done.append(grad_qkv)
        g_part = total([contract_rows(x, g) for x, g in zip(a1, grad_qkv)]).astype(bf16)
        if chunk == 0:
            g_w_up_far, g_w_out_far, g_part = lax.optimization_barrier(
                (g_w_up_far, g_w_out_far, g_part)
            )
            g_w_up = jnp.where(stays, g_w_up, g_w_up_far)
            g_w_out = jnp.where(stays, g_w_out, g_w_out_far)
            tables, g_w_down, g_w_up, g_w_out, g_part = lax.optimization_barrier(
                (tables, g_w_down, g_w_up, g_w_out, g_part)
            )
            g_w_up = layout.sum_dp(g_w_up, 0)
            g_w_out = layout.sum_dp(g_w_out, 0)
        g_w_qkv.append(layout.halved(layout.give_back(g_part), -1))
    layer_out = layout.give_back(after(layer_out, g_w_qkv[0]))
    done = lax.optimization_barrier(done)
    for chunk, grad_qkv in enumerate(done):
        columns = grad_qkv[0].shape[1]
        w_part = w_qkv[:, chunk * columns : (chunk + 1) * columns]
        grad_a1.append([contract_cols(g, w_part) for g in grad_qkv])
        sums.append(total([jnp.sum(g.astype(f32), 0) for g in grad_qkv]))
    g_w_qkv = [layout.sum_rest(g) for g in g_w_qkv]
    g_w_up, g_w_out, *g_w_qkv = lax.optimization_barrier((g_w_up, g_w_out, *g_w_qkv))
    g_w_qkv = [layout.joined(g, layout.partner(g, -1), -1) for g in g_w_qkv]
    g_w_qkv = jnp.concatenate(g_w_qkv, 1).astype(f32)
    g_w_qkv = (
        g_w_qkv.reshape(model_dim, pairs, 3, PAIR)
        .transpose(0, 2, 1, 3)
        .reshape(model_dim, 3, width)
    )
    sums = jnp.concatenate(sums).reshape(pairs, 3, PAIR).transpose(1, 0, 2).reshape(3, width)
    grad_a1 = layout.scatter_sum([total(terms) for terms in zip(*grad_a1)])
    grad_input = grad_mid + norm_back(grad_a1, normed1, inv1, ln1_gain)
    grad_input = layout.give_back(grad_input.astype(bf16)).astype(f32)

    norm_terms = jnp.stack(
        [
            jnp.sum(grad_a1 * normed1, 0),
            jnp.sum(grad_a1, 0),
            jnp.sum(grad_z.astype(f32), 0),
            jnp.sum(grad_mid * normed2, 0),
            jnp.sum(grad_mid, 0),
            jnp.sum(grad_a3 * normed3, 0),
            jnp.sum(grad_a3, 0),
            jnp.sum(grad_f.astype(f32), 0),
            jnp.sum(upstream * normed4, 0),
            jnp.sum(upstream, 0),
        ],
        0,
    )
    all_units = lax.dynamic_update_slice(jnp.zeros((units * shares,), f32), g_up_bias, (rank * units,))
    all_width = lax.dynamic_update_slice(
        jnp.zeros((2, width * shares), f32), jnp.stack([sums[0], sums[2]], 0), (0, rank * width)
    )
    small = layout.sum_all(
        jnp.concatenate([norm_terms.reshape(-1), all_width.reshape(-1), all_units])
    )
    norm_terms = small[: 10 * model_dim].reshape(10, model_dim)
    all_width = small[10 * model_dim : 12 * model_dim].reshape(2, width * shares)
    all_units = small[12 * model_dim :]
    m = lax.axis_index("mp")
    g_qv_bias = lax.dynamic_slice(all_width, (0, m * width), (2, width))
    g_up_bias = lax.dynamic_slice(all_units, (m * units,), (units,))
    return (
        layer_out,
        grad_input,
        norm_terms[0],
        norm_terms[1],
        g_w_qkv,
        g_qv_bias,
        g_w_out.astype(f32),
        norm_terms[2],
        norm_terms[3],
        norm_terms[4],
        norm_terms[5],
        norm_terms[6],
        g_w_up.astype(f32),
        g_up_bias,
        g_w_down.astype(f32),
        norm_terms[7],
        norm_terms[8],
        norm_terms[9],
    )


def solution(mesh):
    in_specs = (
        P(("dp", "mp"), None),
        P(),
        P(),
        P(None, None, "mp"),
        P(None, "mp"),
        P("mp", None),
        P(),
        P(),
        P(),
        P(),
        P(),
        P(None, "mp"),
        P("mp"),
        P("mp", None),
        P(),
        P(),
        P(),
        P("dp", None),
        P("dp"),
        P(("dp", "mp"), None),
    )
    out_specs = (
        P(("dp", "mp"), None),
        P(("dp", "mp"), None),
        P(),
        P(),
        P(None, None, "mp"),
        P(None, "mp"),
        P("mp", None),
        P(),
        P(),
        P(),
        P(),
        P(),
        P(None, "mp"),
        P("mp"),
        P("mp", None),
        P(),
        P(),
        P(),
    )
    return jax.shard_map(functools.partial(body, Layout(mesh)), mesh=mesh, in_specs=in_specs, out_specs=out_specs, check_vma=False)
```

```python
import functools

import jax
import jax.numpy as jnp
from jax import lax
from jax.experimental import pallas as pl
from jax.experimental.pallas import tpu as pltpu
from jax.sharding import PartitionSpec as P

HDIM = 64
TEXT = 64


epsilon = 1e-05
masked_score = -1e30


def norm_parts(values, ln_gain, ln_bias):
    centred = values - jnp.mean(values, -1, keepdims=True)
    inv_std = lax.rsqrt(jnp.mean(centred * centred, -1, keepdims=True) + epsilon)
    normed = centred * inv_std
    return (normed * ln_gain + ln_bias, normed, inv_std)


def norm_back(upstream, normed, inv_std, ln_gain):
    scaled = upstream * ln_gain
    return inv_std * (
        scaled
        - jnp.mean(scaled, -1, keepdims=True)
        - normed * jnp.mean(scaled * normed, -1, keepdims=True)
    )


def contract_rows(left, right):
    return lax.dot_general(
        left, right, (((0,), (0,)), ((), ())), preferred_element_type=jnp.float32
    )


def contract_cols(left, right):
    return lax.dot_general(
        left, right, (((1,), (1,)), ((), ())), preferred_element_type=jnp.float32
    )


BQ = 256
BK = 256
MOST = 4
FEED = 1024
FEED_ROWS = 640
PAIR = 2 * HDIM
F32 = jnp.float32
BF16 = jnp.bfloat16


def matmul(left, right):
    return jnp.dot(left, right, preferred_element_type=F32)


def row_tables(grid_row, tokens, turn):
    side = jnp.max(grid_row)
    length = TEXT + side * side
    rows = tokens // length
    used = rows * length
    position = jnp.arange(tokens, dtype=jnp.int32)
    seg = jnp.minimum(position // length, rows)
    blocks = tokens // BQ
    first = jnp.arange(blocks, dtype=jnp.int32) * BQ
    start = jnp.where(first < used, (first // length) * length, first)
    low = start // BK
    diag = first // BK
    turns = jnp.full((blocks,), turn, jnp.int32)
    return seg, jnp.stack([low, diag, turns]).astype(jnp.int32)


def allowed(kseg_ref, qseg_ref, i, j, blocks):
    qs = qseg_ref[:, pl.ds(pl.multiple_of(i * BQ, BQ), BQ)]
    ks = kseg_ref[pl.ds(pl.multiple_of(j * BK, BK), blocks * BK), :]
    ik = j * BK + lax.broadcasted_iota(jnp.int32, (blocks * BK, BQ), 0)
    iq = i * BQ + lax.broadcasted_iota(jnp.int32, (blocks * BK, BQ), 1)
    return ((ks == qs) & (ik <= iq)) | (ik == iq)


def sweep(tab_ref, i, step, carry):
    return several(tab_ref[0, i], tab_ref[1, i] + 1, step, carry)


def several(first, stop, step, carry, most=MOST):
    while most > 1:
        turns = (stop - first) // most

        def turn(n, carry, first=first, most=most):
            return step(most, first + most * n, carry)

        carry = lax.fori_loop(0, turns, turn, carry)
        first, most = first + most * turns, most // 2
    return lax.fori_loop(first, stop, functools.partial(step, 1), carry)


def each_block(tab_ref, parts, width, work):
    blocks = width // BQ
    count = blocks * parts
    for part in range(parts):

        def one(c, _, part=part):
            whole = lax.rem(tab_ref[2, 0] + part * blocks + c, count)
            work(
                part,
                pl.ds(pl.multiple_of(c * BQ, BQ), BQ),
                pl.ds(pl.multiple_of(whole * BQ, BQ), BQ),
            )
            return 0

        lax.fori_loop(0, blocks, one, 0)


def forward_kernel(parts, tab_ref, kseg_ref, qseg_ref, *refs):
    qkv_refs = refs[:parts]
    *o_refs, ot_ref, lse_ref, kx, vx, qx, scores = refs[-6 - parts :]
    tokens = qx.shape[1]
    width = tokens // parts
    lane = lax.broadcasted_iota(jnp.int32, (BK, 128), 1)
    zero = jnp.zeros((BK, 128), BF16)

    def prepare(part, here, there):
        k = qkv_refs[part][here, PAIR : 2 * PAIR]
        kx[0, there, :] = jnp.where(lane < HDIM, k, zero)
        kx[1, there, :] = jnp.where(lane < HDIM, zero, k)
        qx[:, there] = qkv_refs[part][here, :PAIR].astype(F32).T.astype(BF16)
        v = qkv_refs[part][here, 2 * PAIR :].astype(F32).T.astype(BF16)
        for h in range(2):
            vx[h, :HDIM, there] = v[h * HDIM : (h + 1) * HDIM]
            vx[h, HDIM:, there] = jnp.ones((16, BQ), BF16)

    each_block(tab_ref, parts, width, prepare)

    def block(i, _):
        cols = pl.ds(pl.multiple_of(i * BQ, BQ), BQ)
        qb = qx[:, cols]

        def score(blocks, j, tops):
            at = pl.ds(pl.multiple_of(j * BK, BK), blocks * BK)
            ok = allowed(kseg_ref, qseg_ref, i, j, blocks)
            out = []
            for h in range(2):
                s = matmul(kx[h, at, :], qb)
                s = jnp.where(ok, s, masked_score)
                scores[h, at, :] = s
                out.append(jnp.maximum(tops[h], jnp.max(s.reshape(blocks * BK // 8, 8, BQ), axis=0)))
            return tuple(out)

        tops = sweep(tab_ref, i, score, (jnp.full((8, BQ), masked_score, F32),) * 2)
        tops = [jnp.max(top, axis=0, keepdims=True) for top in tops]

        def weigh(blocks, j, accs):
            at = pl.ds(pl.multiple_of(j * BK, BK), blocks * BK)
            out = []
            for h in range(2):
                p = jnp.exp(scores[h, at, :] - tops[h]).astype(BF16)
                out.append(accs[h] + matmul(vx[h, :, at], p))
            return tuple(out)

        accs = sweep(tab_ref, i, weigh, (jnp.zeros((HDIM + 16, BQ), F32),) * 2)
        for h in range(2):
            total = accs[h][HDIM : HDIM + 1, :]
            ot_ref[h * HDIM : (h + 1) * HDIM, cols] = (accs[h][:HDIM, :] / total).astype(BF16)
            lse_ref[0, h : h + 1, cols] = tops[h] + jnp.log(total)
        return 0

    lax.fori_loop(0, tokens // BQ, block, 0)

    def finish(part, here, there):
        o_refs[part][here, :] = ot_ref[:, there].astype(F32).T.astype(BF16)

    each_block(tab_ref, parts, width, finish)


def three_parts(x):
    high = x.astype(BF16)
    rest = x - high.astype(F32)
    middle = rest.astype(BF16)
    return high, middle, (rest - middle.astype(F32)).astype(BF16)


def backward_kernel(parts, tab_ref, kseg_ref, qseg_ref, *refs):
    qkv_refs, do_refs = refs[:parts], refs[parts : 2 * parts]
    ot_ref, lse_ref = refs[2 * parts : 2 * parts + 2]
    *out_refs, kx, vx, kt, qx, dox, qt, dot, dq, dk, dv = refs[-10 - parts :]
    tokens = kt.shape[1]
    width = tokens // parts
    lane = lax.broadcasted_iota(jnp.int32, (BK, 128), 1)
    sub = lax.broadcasted_iota(jnp.int32, (HDIM, BK), 0)
    one0 = jnp.where((lane >= HDIM) & (lane < HDIM + 3), 1.0, 0.0).astype(BF16)
    one1 = jnp.where(lane < 3, 1.0, 0.0).astype(BF16)
    zero = jnp.zeros((BK, 128), BF16)

    def extra(x):
        high, middle, low = (e.astype(F32) for e in three_parts(x))
        rows = jnp.where(
            sub == 0, high, jnp.where(sub == 1, middle, jnp.where(sub == 2, low, 0.0))
        )
        return rows.astype(BF16)

    def prepare(part, here, there):
        k = qkv_refs[part][here, PAIR : 2 * PAIR]
        kt[:, there] = k.astype(F32).T.astype(BF16)
        kx[0, there, :] = jnp.where(lane < HDIM, k, one0)
        kx[1, there, :] = jnp.where(lane < HDIM, one1, k)
        v = qkv_refs[part][here, 2 * PAIR :]
        vx[0, there, :] = jnp.where(lane < HDIM, v, one0)
        vx[1, there, :] = jnp.where(lane < HDIM, one1, v)
        q = qkv_refs[part][here, :PAIR]
        qt[0, there, :] = jnp.where(lane < HDIM, q, zero)
        qt[1, there, :] = jnp.where(lane < HDIM, zero, q)
        do = do_refs[part][here, :]
        dot[0, there, :] = jnp.where(lane < HDIM, do, zero)
        dot[1, there, :] = jnp.where(lane < HDIM, zero, do)
        turned = do.astype(F32).T
        prod = turned * ot_ref[:, there].astype(F32)
        inner0 = jnp.sum(prod[:HDIM], axis=0, keepdims=True)
        inner1 = jnp.sum(prod[HDIM:], axis=0, keepdims=True)
        turned = turned.astype(BF16)
        dox[0, :HDIM, there] = turned[:HDIM]
        dox[0, HDIM:, there] = extra(-inner0)
        dox[1, HDIM:, there] = turned[HDIM:]
        dox[1, :HDIM, there] = extra(-inner1)
        turned = q.astype(F32).T.astype(BF16)
        qx[0, :HDIM, there] = turned[:HDIM]
        qx[0, HDIM:, there] = extra(-lse_ref[0, 0:1, there])
        qx[1, HDIM:, there] = turned[HDIM:]
        qx[1, :HDIM, there] = extra(-lse_ref[0, 1:2, there])
        dk[there, :] = jnp.zeros((BK, 128), F32)
        dv[there, :] = jnp.zeros((BK, 128), F32)

    each_block(tab_ref, parts, width, prepare)

    def block(i, _):
        cols = pl.ds(pl.multiple_of(i * BQ, BQ), BQ)

        def step(blocks, j, carry):
            at = pl.ds(pl.multiple_of(j * BK, BK), blocks * BK)
            ok = allowed(kseg_ref, qseg_ref, i, j, blocks)
            new = []
            dvs = dv[at, :]
            dks = dk[at, :]
            for h in range(2):
                s = matmul(kx[h, at, :], qx[h, :, cols])
                s = jnp.where(ok, s, masked_score)
                p = jnp.exp(s)
                dp = matmul(vx[h, at, :], dox[h, :, cols])
                ds = (p * dp).astype(BF16)
                dvs = dvs + matmul(p.astype(BF16), dot[h, cols, :])
                dks = dks + matmul(ds, qt[h, cols, :])
                new.append(carry[h] + matmul(kt[h * HDIM : (h + 1) * HDIM, at], ds))
            dv[at, :] = dvs
            dk[at, :] = dks
            return tuple(new)

        init = tuple(jnp.zeros((HDIM, BQ), F32) for _ in range(2))
        res = sweep(tab_ref, i, step, init)
        for h in range(2):
            dq[h * HDIM : (h + 1) * HDIM, cols] = res[h] * (HDIM**-0.5)
        return 0

    lax.fori_loop(0, tokens // BQ, block, 0)

    def finish(part, here, there):
        out_refs[part][here, :PAIR] = dq[:, there].T.astype(BF16)
        out_refs[part][here, PAIR : 2 * PAIR] = dk[there, :].astype(BF16)
        out_refs[part][here, 2 * PAIR :] = dv[there, :].astype(BF16)

    each_block(tab_ref, parts, width, finish)


def lanes_of(first, step):
    return lambda g, t: (0, first + step * g)


def attend_specs(qkv_parts, chunk):
    parts = len(qkv_parts)
    width = qkv_parts[0].shape[0]
    tokens = parts * width
    every = qkv_parts[0].shape[1] // (3 * PAIR)
    first, pairs = chunk
    seg_specs = [
        pl.BlockSpec((tokens, 1), lambda g, t: (0, 0)),
        pl.BlockSpec((1, tokens), lambda g, t: (0, 0)),
    ]
    qkv_specs = [pl.BlockSpec((width, 3 * PAIR), lanes_of(first, 1))] * parts
    o_specs = [pl.BlockSpec((width, PAIR), lanes_of(first, 1))] * parts
    ot_spec = pl.BlockSpec((PAIR, tokens), lambda g, t: (first + g, 0))
    lse_spec = pl.BlockSpec((1, 2, tokens), lambda g, t: (first + g, 0, 0))
    return parts, width, tokens, every, pairs, seg_specs, qkv_specs, o_specs, ot_spec, lse_spec


def attend_forward(qkv_parts, seg, keep, tables, chunk, begun=()):
    parts, width, tokens, every, pairs, seg_specs, qkv_specs, o_specs, ot_spec, lse_spec = (
        attend_specs(qkv_parts, chunk)
    )
    kseg = jnp.where(keep == 1, seg, -1)[:, None]
    return pl.pallas_call(
        functools.partial(forward_kernel, parts),
        grid_spec=pltpu.PrefetchScalarGridSpec(
            num_scalar_prefetch=1,
            grid=(pairs,),
            in_specs=seg_specs + qkv_specs + [pl.BlockSpec(memory_space=pl.ANY)] * len(begun),
            out_specs=o_specs + [ot_spec, lse_spec],
            scratch_shapes=[
                pltpu.VMEM((2, tokens, 128), BF16),
                pltpu.VMEM((2, HDIM + 16, tokens), BF16),
                pltpu.VMEM((PAIR, tokens), BF16),
                pltpu.VMEM((2, tokens, BQ), F32),
            ],
        ),
        out_shape=[jax.ShapeDtypeStruct((width, every * PAIR), BF16)] * parts
        + [
            jax.ShapeDtypeStruct((every * PAIR, tokens), BF16),
            jax.ShapeDtypeStruct((every, 2, tokens), F32),
        ],
        compiler_params=pltpu.CompilerParams(vmem_limit_bytes=40 * 2**20),
        cost_estimate=pl.CostEstimate(
            flops=2**10, bytes_accessed=2**10, transcendentals=0
        ),
        input_output_aliases={3 + parts + n: n for n in range(len(begun))},
        name="attend_forward",
    )(tables, kseg, seg[None, :], *qkv_parts, *begun)


def attend_backward(qkv_parts, turned, grad_ctx, lse, seg, keep, tables, chunk, begun=()):
    parts, width, tokens, every, pairs, seg_specs, qkv_specs, o_specs, ot_spec, lse_spec = (
        attend_specs(qkv_parts, chunk)
    )
    kseg = jnp.where(keep == 1, seg, -1)[:, None]
    result = pl.BlockSpec((width, 3 * PAIR), lanes_of(chunk[0], 1))
    return pl.pallas_call(
        functools.partial(backward_kernel, parts),
        grid_spec=pltpu.PrefetchScalarGridSpec(
            num_scalar_prefetch=1,
            grid=(pairs,),
            in_specs=seg_specs
            + qkv_specs
            + o_specs
            + [ot_spec, lse_spec]
            + [pl.BlockSpec(memory_space=pl.ANY)] * len(begun),
            out_specs=[result] * parts,
            scratch_shapes=[
                pltpu.VMEM((2, tokens, 128), BF16),
                pltpu.VMEM((2, tokens, 128), BF16),
                pltpu.VMEM((PAIR, tokens), BF16),
                pltpu.VMEM((2, 128, tokens), BF16),
                pltpu.VMEM((2, 128, tokens), BF16),
                pltpu.VMEM((2, tokens, 128), BF16),
                pltpu.VMEM((2, tokens, 128), BF16),
                pltpu.VMEM((PAIR, tokens), F32),
                pltpu.VMEM((tokens, 128), F32),
                pltpu.VMEM((tokens, 128), F32),
            ],
        ),
        out_shape=[jax.ShapeDtypeStruct((width, every * 3 * PAIR), BF16)] * parts,
        input_output_aliases={5 + 2 * parts + n: n for n in range(len(begun))},
        compiler_params=pltpu.CompilerParams(vmem_limit_bytes=48 * 2**20),
        cost_estimate=pl.CostEstimate(
            flops=4000 * tokens * tokens * (pairs - 1),
            bytes_accessed=2**10,
            transcendentals=0,
        ),
        name="attend_backward",
    )(tables, kseg, seg[None, :], *qkv_parts, *grad_ctx, turned, lse, *begun)


def row_block(width):
    return FEED_ROWS if width % FEED_ROWS == 0 else width


def gelu_and_slope(u):
    root = 0.7978845608028654
    square = u * u
    t = jnp.tanh(u * (root + (root * 0.044715) * square))
    half = 0.5 * t + 0.5
    slope = half + (0.5 * u) * (1.0 - t * t) * (root + (root * 0.134145) * square)
    return u * half, slope


def feed_kernel(step, x_ref, up_ref, bias_ref, down_ref, *refs):
    x_all, hidden_all, slope_all, out_ref = refs[-4:]
    x = x_ref[...]
    x_all[...] = x
    units = up_ref.shape[1]
    total = None
    for first in range(0, units, step):
        at = slice(first, first + step)
        act, slope = gelu_and_slope(matmul(x, up_ref[:, at]) + bias_ref[:, at])
        act = act.astype(BF16)
        hidden_all[:, at] = act
        slope_all[:, at] = slope.astype(BF16)
        term = matmul(act, down_ref[at, :])
        total = term if total is None else total + term
    out_ref[...] = total.astype(BF16)


def feed_forward(part, parts, x, up, bias, down, begun):
    width, model = x.shape
    units = up.shape[1]
    rows = row_block(width)
    steps = width // rows
    own = lambda k: (k, 0)
    whole = lambda k: (part * steps + k, 0)
    fixed = lambda k: (0, 0)
    once = pl.Buffered(1)
    every = parts * width
    return pl.pallas_call(
        functools.partial(feed_kernel, min(units, FEED)),
        grid=(steps,),
        in_specs=[
            pl.BlockSpec((rows, model), own),
            pl.BlockSpec((model, units), fixed, pipeline_mode=once),
            pl.BlockSpec((1, units), fixed, pipeline_mode=once),
            pl.BlockSpec((units, model), fixed, pipeline_mode=once),
        ]
        + [pl.BlockSpec(memory_space=pl.ANY)] * len(begun),
        out_specs=[
            pl.BlockSpec((rows, model), whole),
            pl.BlockSpec((rows, units), whole),
            pl.BlockSpec((rows, units), whole),
            pl.BlockSpec((rows, model), own),
        ],
        out_shape=[
            jax.ShapeDtypeStruct((every, model), BF16),
            jax.ShapeDtypeStruct((every, units), BF16),
            jax.ShapeDtypeStruct((every, units), BF16),
            jax.ShapeDtypeStruct((width, model), BF16),
        ],
        input_output_aliases={4 + n: n for n in range(len(begun))},
        compiler_params=pltpu.CompilerParams(vmem_limit_bytes=48 * 2**20),
        cost_estimate=pl.CostEstimate(
            flops=6 * width * model * units, bytes_accessed=2**24, transcendentals=0
        ),
        name="feed_forward",
    )(x, up, bias[None, :], down, *begun)


def feed_back_kernel(step, g_ref, slope_ref, down_ref, up_ref, *refs):
    pre_all, sums_ref, out_ref = refs[-3:]
    g = g_ref[...]
    units = up_ref.shape[1]

    @pl.when(pl.program_id(0) == 0)
    def _():
        sums_ref[...] = jnp.zeros_like(sums_ref)

    total = None
    for first in range(0, units, step):
        at = slice(first, first + step)
        pre = contract_cols(g, down_ref[at, :]) * slope_ref[:, at].astype(F32)
        pre = pre.astype(BF16)
        pre_all[:, at] = pre
        sums_ref[:, at] += jnp.sum(pre.astype(F32), axis=0, keepdims=True)
        term = contract_cols(pre, up_ref[:, at])
        total = term if total is None else total + term
    out_ref[...] = total.astype(BF16)


def feed_back(part, parts, g, slope_all, up, down, begun):
    width, model = g.shape
    units = up.shape[1]
    rows = row_block(width)
    steps = width // rows
    own = lambda k: (k, 0)
    whole = lambda k: (part * steps + k, 0)
    fixed = lambda k: (0, 0)
    once = pl.Buffered(1)
    every = parts * width
    return pl.pallas_call(
        functools.partial(feed_back_kernel, min(units, FEED)),
        grid=(steps,),
        in_specs=[
            pl.BlockSpec((rows, model), own),
            pl.BlockSpec((rows, units), whole),
            pl.BlockSpec((units, model), fixed, pipeline_mode=once),
            pl.BlockSpec((model, units), fixed, pipeline_mode=once),
        ]
        + [pl.BlockSpec(memory_space=pl.ANY)] * len(begun),
        out_specs=[
            pl.BlockSpec((rows, units), whole),
            pl.BlockSpec((1, units), fixed),
            pl.BlockSpec((rows, model), own),
        ],
        out_shape=[
            jax.ShapeDtypeStruct((every, units), BF16),
            jax.ShapeDtypeStruct((1, units), F32),
            jax.ShapeDtypeStruct((width, model), BF16),
        ],
        input_output_aliases={4 + n: n for n in range(len(begun))},
        compiler_params=pltpu.CompilerParams(vmem_limit_bytes=48 * 2**20),
        cost_estimate=pl.CostEstimate(
            flops=2**10, bytes_accessed=2**10, transcendentals=0
        ),
        name="feed_back",
    )(g, slope_all, down, up, *begun)


def weight_grad_kernel(parts, *refs):
    a_refs, d_refs = refs[:parts], refs[parts : 2 * parts]
    out_ref, sums_ref = refs[2 * parts :]
    out_ref[...] = total([contract_rows(a[...], d[...]) for a, d in zip(a_refs, d_refs)]).astype(BF16)
    sums_ref[...] = total([jnp.sum(d[...].astype(F32), axis=0, keepdims=True) for d in d_refs])


def weight_grad(a_parts, d_parts, first, count):
    parts = len(a_parts)
    width, model = a_parts[0].shape
    columns = 3 * PAIR
    return pl.pallas_call(
        functools.partial(weight_grad_kernel, parts),
        grid=(count,),
        in_specs=[pl.BlockSpec((width, model), lambda k: (0, 0), pipeline_mode=pl.Buffered(1))] * parts
        + [pl.BlockSpec((width, columns), lambda k: (0, first + k))] * parts,
        out_specs=[
            pl.BlockSpec((model, columns), lambda k: (0, k)),
            pl.BlockSpec((1, columns), lambda k: (0, k)),
        ],
        out_shape=[
            jax.ShapeDtypeStruct((model, count * columns), BF16),
            jax.ShapeDtypeStruct((1, count * columns), F32),
        ],
        compiler_params=pltpu.CompilerParams(vmem_limit_bytes=40 * 2**20),
        cost_estimate=pl.CostEstimate(flops=2**10, bytes_accessed=2**10, transcendentals=0),
        name="weight_grad",
    )(*a_parts, *d_parts)


def input_grad_kernel(d_ref, w_ref, out_ref):
    out_ref[...] = contract_cols(d_ref[...], w_ref[...]).astype(BF16)


def input_grad(d, weight):
    width, columns = d.shape
    model = weight.shape[0]
    rows = row_block(width)
    return pl.pallas_call(
        input_grad_kernel,
        grid=(width // rows,),
        in_specs=[
            pl.BlockSpec((rows, columns), lambda k: (k, 0)),
            pl.BlockSpec((model, columns), lambda k: (0, 0), pipeline_mode=pl.Buffered(1)),
        ],
        out_specs=pl.BlockSpec((rows, model), lambda k: (k, 0)),
        out_shape=jax.ShapeDtypeStruct((width, model), BF16),
        compiler_params=pltpu.CompilerParams(vmem_limit_bytes=40 * 2**20),
        cost_estimate=pl.CostEstimate(flops=2**10, bytes_accessed=2**10, transcendentals=0),
        name="input_grad",
    )(d, weight)


def after(value, *others):
    return lax.optimization_barrier((value, *others))[0]


class Layout:
    def __init__(self, mesh):
        self.dp, self.n = mesh.shape["dp"], mesh.shape["mp"]
        self.pairs = self.dp // 2
        self.axes = ("dp", "mp")

    def device(self, pair, core, m):
        return (2 * pair + core) * self.n + m

    def at_rank(self, pair, group, rank):
        return self.device(pair, rank % 2, group * (self.n // 2) + rank // 2)

    def each(self):
        for pair in range(self.pairs):
            for group in range(2):
                for rank in range(self.n):
                    yield pair, group, rank

    def stays(self):
        core, m = lax.axis_index("dp") % 2, lax.axis_index("mp")
        return (m // (self.n // 2) == core) & (self.rank() == m)

    def send(self, value, back=False):
        moves = [(self.device(p, g, r), self.at_rank(p, g, r)) for p, g, r in self.each()]
        return lax.ppermute(
            value, self.axes, [(b, a) if back else (a, b) for a, b in moves if a != b]
        )

    def regroup(self, value):
        return jnp.where(self.stays(), value, self.send(value))

    def give_back(self, value):
        return jnp.where(self.stays(), value, self.send(value, True))

    def partner(self, value, bit, only=lambda p, g, r: True):
        def other(p, c):
            return (p, 1 - c) if bit < 0 else (p ^ (1 << bit), c)

        moves = [
            (self.device(*other(p, c), m), self.device(p, c, m))
            for p, c, m in self.each()
            if only(p, c, m)
        ]
        return lax.ppermute(value, self.axes, moves)

    def side(self, bit):
        dp = lax.axis_index("dp")
        return dp % 2 if bit < 0 else (dp // 2 >> bit) % 2

    def joined(self, mine, theirs, bit):
        high = self.side(bit) == 1
        return jnp.concatenate(
            [jnp.where(high, theirs, mine), jnp.where(high, mine, theirs)], 0
        )

    def regroup_first(self, weight, small, tokens):
        rows = weight.shape[0] // 4
        part = 2 * self.side(0) + self.side(1)
        quarter = lax.dynamic_slice_in_dim(weight, part * rows, rows, 0)
        got = self.send(quarter)
        small = self.regroup(after(small, got))
        tokens = self.regroup(after(tokens, got, small))
        for bit in (1, 0):
            got = self.joined(got, self.partner(got, bit, self.moving), bit)
        return jnp.where(self.stays(), weight, got), small, tokens

    def moving(self, pair, core, m):
        return self.at_rank(pair, core, m) != self.device(pair, core, m)

    def to_rank(self, value, ahead):
        moves = [
            (self.at_rank(p, g, r), self.at_rank(p, g, (r + ahead) % self.n))
            for p, g, r in self.each()
        ]
        return lax.ppermute(value, self.axes, moves)

    def rank(self):
        core = lax.axis_index("dp") % 2
        return (lax.axis_index("mp") % (self.n // 2)) * 2 + core

    def gather(self, mine):
        return [mine] + [self.to_rank(mine, self.n - k) for k in range(1, self.n)]

    def scatter_sum(self, shares):
        total = shares[0].astype(jnp.float32)
        for k in range(1, self.n):
            total = total + self.to_rank(shares[k].astype(jnp.bfloat16), k).astype(jnp.float32)
        return total

    def sum_all(self, value):
        devices = self.dp * self.n
        steps = [1 << k for k in range(devices.bit_length() - 1)]
        for step in steps:
            value = value + lax.ppermute(value, self.axes, [(i, i ^ step) for i in range(devices)])
        return value

    def halved(self, value, bit):
        half, high = value.shape[0] // 2, self.side(bit)
        sent = lax.dynamic_slice_in_dim(value, (1 - high) * half, half, 0)
        kept = lax.dynamic_slice_in_dim(value, high * half, half, 0)
        got = self.partner(sent, bit)
        return (kept.astype(jnp.float32) + got.astype(jnp.float32)).astype(jnp.bfloat16)

    def order(self, first):
        bits = list(range(self.pairs.bit_length() - 1))
        return bits[first:] + bits[:first]

    def halved_by(self, value, bits):
        for bit in bits:
            value = self.halved(value, bit)
        return value

    def joined_by(self, value, bits):
        for bit in bits[::-1]:
            value = self.joined(value, self.partner(value, bit), bit)
        return value


def for_kernel(shares, rank):
    width = shares[0].shape[0]
    if width % BQ == 0:
        return shares, rank * (width // BQ)
    return [jnp.roll(jnp.concatenate(shares, 0), rank * width, 0)], 0


def from_kernel(arrays, rank, shares):
    if len(arrays) == shares:
        return arrays
    width = arrays[0].shape[0] // shares
    return jnp.split(jnp.roll(arrays[0], -rank * width, 0), shares, 0)


def by_pairs(weight, pairs):
    return (
        weight.reshape(-1, 3, pairs, PAIR).transpose(0, 2, 1, 3).reshape(-1, 3 * pairs * PAIR)
    )


def total(terms):
    return functools.reduce(jnp.add, terms)


def body(
    layout,
    tokens,
    ln1_gain,
    ln1_bias,
    w_qkv,
    qv_bias,
    w_out,
    out_bias,
    ln2_gain,
    ln2_bias,
    ln3_gain,
    ln3_bias,
    w_up,
    up_bias,
    w_down,
    down_bias,
    ln4_gain,
    ln4_bias,
    row_grid,
    pad_mask,
    cotangent,
):
    f32, bf16 = jnp.float32, jnp.bfloat16
    model_dim = tokens.shape[1]
    group_rows = pad_mask.shape[0]
    width = w_qkv.shape[2]
    units = w_up.shape[1]
    shares = layout.n
    rank = layout.rank()

    small = jnp.concatenate(
        [
            qv_bias.reshape(-1),
            up_bias,
            pad_mask.astype(f32),
            row_grid[0].astype(f32),
        ]
    )
    pairs = width // PAIR
    chunks = 2 if pairs % 2 == 0 else 1
    w_qkv, small, tokens = layout.regroup_first(w_qkv, small, tokens)
    qv_bias = small[: 2 * width].reshape(2, width)
    up_bias = small[2 * width : 2 * width + units]
    keep = small[2 * width + units : 2 * width + units + group_rows].astype(jnp.int32)
    grid_row = small[2 * width + units + group_rows :].astype(jnp.int32)
    w_qkv = by_pairs(w_qkv, pairs)
    half = units // 2
    w_out_far = layout.send(after(w_out, tokens))
    w_up_far = layout.send(after(w_up, tokens))
    w_top_far = layout.send(after(w_down[:half], tokens))
    w_low_far = layout.send(after(w_down[half:], w_up_far))
    cotangent = layout.regroup(after(cotangent, w_top_far))

    resid_in = tokens.astype(f32)
    norm1_out, normed1, inv1 = norm_parts(resid_in, ln1_gain, ln1_bias)
    a1 = layout.gather(norm1_out.astype(bf16))
    zeros = jnp.zeros((width,), f32)
    qkv_bias = by_pairs(jnp.concatenate([qv_bias[0], zeros, qv_bias[1]]), pairs)
    qkv_scale = by_pairs(
        jnp.concatenate([zeros + HDIM ** (-0.5), zeros + 1.0, zeros + 1.0]), pairs
    )
    qkv = [((matmul(x, w_qkv) + qkv_bias) * qkv_scale).astype(bf16) for x in a1]
    qkv, turn = for_kernel(qkv, rank)
    seg, tables = row_tables(grid_row, group_rows, turn)
    begun = ()
    for pair in range(pairs):
        if pair and pair == pairs // 2:
            tables, w_out_far, w_up_far = lax.optimization_barrier((tables, w_out_far, w_up_far))
        begun = attend_forward(qkv, seg, keep, tables, (pair, 1), begun)
    *context, context_turned, log_total = begun
    *context, w_top_far = lax.optimization_barrier((*context, w_top_far))
    context = from_kernel(context, rank, shares)
    stays = layout.stays()
    w_out = jnp.where(stays, w_out, w_out_far)
    w_up = jnp.where(stays, w_up, w_up_far)
    w_down = jnp.where(stays, w_down, jnp.concatenate([w_top_far, w_low_far], 0))
    branch_z = layout.scatter_sum([matmul(x, w_out) for x in context]) + out_bias
    norm2_out, normed2, inv2 = norm_parts(branch_z, ln2_gain, ln2_bias)
    resid_mid = resid_in + norm2_out
    norm3_out, normed3, inv3 = norm_parts(resid_mid, ln3_gain, ln3_bias)
    a3 = layout.gather(norm3_out.astype(bf16))
    begun, shares_f = (), []
    for part, x in enumerate(a3):
        if part == shares - 1:
            x, cotangent = lax.optimization_barrier((x, cotangent))
        *begun, share = feed_forward(part, shares, x, w_up, up_bias, w_down, begun)
        shares_f.append(share)
    a3_all, hidden, slope = begun
    branch_f = layout.scatter_sum(shares_f) + down_bias
    norm4_out, normed4, inv4 = norm_parts(branch_f, ln4_gain, ln4_bias)
    layer_out = (resid_mid + norm4_out).astype(bf16)

    upstream = cotangent.astype(f32)
    grad_f = norm_back(upstream, normed4, inv4, ln4_gain).astype(bf16)
    grad_f_all = layout.gather(grad_f)
    g_w_down = contract_rows(hidden, jnp.concatenate(grad_f_all, 0)).astype(bf16)
    begun, shares_a3, g_up_bias = (), [], []
    for part, g in enumerate(grad_f_all):
        if part:
            g, g_w_down = lax.optimization_barrier((g, g_w_down))
        *begun, unit_sums, share = feed_back(part, shares, g, slope, w_up, w_down, begun)
        shares_a3.append(share)
        g_up_bias.append(unit_sums[0])
    [grad_pre] = begun
    g_w_down_far = layout.send(g_w_down, True)
    grad_a3 = layout.scatter_sum(shares_a3)
    g_up_bias = total(g_up_bias)
    g_w_up = contract_rows(a3_all, grad_pre).astype(bf16)
    g_w_up_far = layout.send(g_w_up, True)
    grad_mid = upstream + norm_back(grad_a3, normed3, inv3, ln3_gain)
    grad_z = norm_back(grad_mid, normed2, inv2, ln2_gain).astype(bf16)
    grad_z, g_w_down_far = lax.optimization_barrier((grad_z, g_w_down_far))
    grad_z_all = layout.gather(grad_z)
    grad_ctx = [contract_cols(g, w_out).astype(bf16) for g in grad_z_all]
    g_w_out = total([contract_rows(x, g) for x, g in zip(context, grad_z_all)]).astype(bf16)
    g_w_out_far = layout.send(g_w_out, True)
    grad_ctx, _ = for_kernel(grad_ctx, rank)
    grad_qkv = ()
    if pairs > 1:
        grad_qkv = attend_backward(
            qkv, context_turned, grad_ctx, log_total, seg, keep, tables, (0, 1), grad_qkv
        )
        g_w_up_far, g_w_out_far, *grad_qkv = lax.optimization_barrier(
            (g_w_up_far, g_w_out_far, *grad_qkv)
        )
    g_w_down = jnp.where(stays, g_w_down, g_w_down_far)
    g_w_up = jnp.where(stays, g_w_up, g_w_up_far)
    g_w_out = jnp.where(stays, g_w_out, g_w_out_far)
    tables, g_w_down, g_w_up, g_w_out = lax.optimization_barrier(
        (tables, g_w_down, g_w_up, g_w_out)
    )
    g_w_down = lax.psum(g_w_down, "dp")
    g_w_up = lax.psum(g_w_up, "dp")
    g_w_out = lax.psum(g_w_out, "dp")
    first = len(grad_qkv) and 1
    grad_qkv = attend_backward(
        qkv,
        context_turned,
        grad_ctx,
        log_total,
        seg,
        keep,
        tables,
        (first, pairs - first),
        grad_qkv,
    )
    layer_out = layout.give_back(after(layer_out, g_w_out_far))
    grad_qkv = from_kernel(grad_qkv, rank, shares)
    grad_a1 = [input_grad(g, w_qkv) for g in grad_qkv]
    grad_a1 = layout.scatter_sum(grad_a1)
    grad_input = grad_mid + norm_back(grad_a1, normed1, inv1, ln1_gain)
    grad_input = grad_input.astype(bf16)
    g_w_qkv, sums = [], []
    each = pairs // chunks
    for chunk in range(chunks):
        if chunk == chunks - 1:
            g_w_down, g_w_up, g_w_out, grad_input, *grad_qkv = lax.optimization_barrier(
                (g_w_down, g_w_up, g_w_out, grad_input, *grad_qkv)
            )
        g_part, part_sums = weight_grad(a1, grad_qkv, chunk * each, each)
        g_w_qkv.append(layout.halved(layout.give_back(g_part), -1))
        sums.append(part_sums)
    sums = jnp.concatenate(sums, 1)
    g_w_qkv = [layout.halved_by(g, layout.order(k)) for k, g in enumerate(g_w_qkv)]
    g_w_qkv = [layout.joined_by(g, [-1, *layout.order(k)]) for k, g in enumerate(g_w_qkv)]
    g_w_qkv = jnp.concatenate(g_w_qkv, 1).astype(f32)
    g_w_qkv = (
        g_w_qkv.reshape(model_dim, pairs, 3, PAIR)
        .transpose(0, 2, 1, 3)
        .reshape(model_dim, 3, width)
    )
    sums = sums.reshape(pairs, 3, PAIR).transpose(1, 0, 2).reshape(3, width)
    grad_input = layout.give_back(grad_input).astype(f32)

    norm_terms = jnp.stack(
        [
            jnp.sum(grad_a1 * normed1, 0),
            jnp.sum(grad_a1, 0),
            jnp.sum(grad_z.astype(f32), 0),
            jnp.sum(grad_mid * normed2, 0),
            jnp.sum(grad_mid, 0),
            jnp.sum(grad_a3 * normed3, 0),
            jnp.sum(grad_a3, 0),
            jnp.sum(grad_f.astype(f32), 0),
            jnp.sum(upstream * normed4, 0),
            jnp.sum(upstream, 0),
        ],
        0,
    )
    all_units = lax.dynamic_update_slice(jnp.zeros((units * shares,), f32), g_up_bias, (rank * units,))
    all_width = lax.dynamic_update_slice(
        jnp.zeros((2, width * shares), f32), jnp.stack([sums[0], sums[2]], 0), (0, rank * width)
    )
    small = layout.sum_all(
        jnp.concatenate([norm_terms.reshape(-1), all_width.reshape(-1), all_units])
    )
    norm_terms = small[: 10 * model_dim].reshape(10, model_dim)
    all_width = small[10 * model_dim : 12 * model_dim].reshape(2, width * shares)
    all_units = small[12 * model_dim :]
    m = lax.axis_index("mp")
    g_qv_bias = lax.dynamic_slice(all_width, (0, m * width), (2, width))
    g_up_bias = lax.dynamic_slice(all_units, (m * units,), (units,))
    return (
        layer_out,
        grad_input,
        norm_terms[0],
        norm_terms[1],
        g_w_qkv,
        g_qv_bias,
        g_w_out.astype(f32),
        norm_terms[2],
        norm_terms[3],
        norm_terms[4],
        norm_terms[5],
        norm_terms[6],
        g_w_up.astype(f32),
        g_up_bias,
        g_w_down.astype(f32),
        norm_terms[7],
        norm_terms[8],
        norm_terms[9],
    )


def solution(mesh):
    in_specs = (
        P(("dp", "mp"), None),
        P(),
        P(),
        P(None, None, "mp"),
        P(None, "mp"),
        P("mp", None),
        P(),
        P(),
        P(),
        P(),
        P(),
        P(None, "mp"),
        P("mp"),
        P("mp", None),
        P(),
        P(),
        P(),
        P("dp", None),
        P("dp"),
        P(("dp", "mp"), None),
    )
    out_specs = (
        P(("dp", "mp"), None),
        P(("dp", "mp"), None),
        P(),
        P(),
        P(None, None, "mp"),
        P(None, "mp"),
        P("mp", None),
        P(),
        P(),
        P(),
        P(),
        P(),
        P(None, "mp"),
        P("mp"),
        P("mp", None),
        P(),
        P(),
        P(),
    )
    return jax.shard_map(functools.partial(body, Layout(mesh)), mesh=mesh, in_specs=in_specs, out_specs=out_specs, check_vma=False)
```

```python
import functools

import jax
import jax.numpy as jnp
from jax import lax
from jax.experimental import pallas as pl
from jax.experimental.pallas import tpu as pltpu
from jax.sharding import PartitionSpec as P

HDIM = 64
TEXT = 64


epsilon = 1e-05
masked_score = -1e30


def norm_parts(values, ln_gain, ln_bias):
    centred = values - jnp.mean(values, -1, keepdims=True)
    inv_std = lax.rsqrt(jnp.mean(centred * centred, -1, keepdims=True) + epsilon)
    normed = centred * inv_std
    return (normed * ln_gain + ln_bias, normed, inv_std)


def norm_back(upstream, normed, inv_std, ln_gain):
    scaled = upstream * ln_gain
    return inv_std * (
        scaled
        - jnp.mean(scaled, -1, keepdims=True)
        - normed * jnp.mean(scaled * normed, -1, keepdims=True)
    )


def contract_rows(left, right):
    return lax.dot_general(
        left, right, (((0,), (0,)), ((), ())), preferred_element_type=jnp.float32
    )


def contract_cols(left, right):
    return lax.dot_general(
        left, right, (((1,), (1,)), ((), ())), preferred_element_type=jnp.float32
    )


BQ = 256
BK = 256
MOST = 4
FEED = 1024
FEED_ROWS = 640
PAIR = 2 * HDIM
F32 = jnp.float32
BF16 = jnp.bfloat16


def matmul(left, right):
    return jnp.dot(left, right, preferred_element_type=F32)


def row_tables(grid_row, tokens, turn):
    side = jnp.max(grid_row)
    length = TEXT + side * side
    rows = tokens // length
    used = rows * length
    position = jnp.arange(tokens, dtype=jnp.int32)
    seg = jnp.minimum(position // length, rows)
    blocks = tokens // BQ
    first = jnp.arange(blocks, dtype=jnp.int32) * BQ
    start = jnp.where(first < used, (first // length) * length, first)
    low = start // BK
    diag = first // BK
    turns = jnp.full((blocks,), turn, jnp.int32)
    return seg, jnp.stack([low, diag, turns]).astype(jnp.int32)


def allowed(kseg_ref, qseg_ref, i, j, blocks):
    qs = qseg_ref[:, pl.ds(pl.multiple_of(i * BQ, BQ), BQ)]
    ks = kseg_ref[pl.ds(pl.multiple_of(j * BK, BK), blocks * BK), :]
    ik = j * BK + lax.broadcasted_iota(jnp.int32, (blocks * BK, BQ), 0)
    iq = i * BQ + lax.broadcasted_iota(jnp.int32, (blocks * BK, BQ), 1)
    return ((ks == qs) & (ik <= iq)) | (ik == iq)


def sweep(tab_ref, i, step, carry):
    return several(tab_ref[0, i], tab_ref[1, i] + 1, step, carry)


def several(first, stop, step, carry, most=MOST):
    while most > 1:
        turns = (stop - first) // most

        def turn(n, carry, first=first, most=most):
            return step(most, first + most * n, carry)

        carry = lax.fori_loop(0, turns, turn, carry)
        first, most = first + most * turns, most // 2
    return lax.fori_loop(first, stop, functools.partial(step, 1), carry)


def each_block(tab_ref, parts, width, work):
    blocks = width // BQ
    count = blocks * parts
    for part in range(parts):

        def one(c, _, part=part):
            whole = lax.rem(tab_ref[2, 0] + part * blocks + c, count)
            work(
                part,
                pl.ds(pl.multiple_of(c * BQ, BQ), BQ),
                pl.ds(pl.multiple_of(whole * BQ, BQ), BQ),
            )
            return 0

        lax.fori_loop(0, blocks, one, 0)


def forward_kernel(parts, tab_ref, kseg_ref, qseg_ref, *refs):
    qkv_refs = refs[:parts]
    *o_refs, ot_ref, lse_ref, kx, vx, qx, scores = refs[-6 - parts :]
    tokens = qx.shape[1]
    width = tokens // parts
    lane = lax.broadcasted_iota(jnp.int32, (BK, 128), 1)
    zero = jnp.zeros((BK, 128), BF16)

    def prepare(part, here, there):
        k = qkv_refs[part][here, PAIR : 2 * PAIR]
        kx[0, there, :] = jnp.where(lane < HDIM, k, zero)
        kx[1, there, :] = jnp.where(lane < HDIM, zero, k)
        qx[:, there] = qkv_refs[part][here, :PAIR].astype(F32).T.astype(BF16)
        v = qkv_refs[part][here, 2 * PAIR :].astype(F32).T.astype(BF16)
        for h in range(2):
            vx[h, :HDIM, there] = v[h * HDIM : (h + 1) * HDIM]
            vx[h, HDIM:, there] = jnp.ones((16, BQ), BF16)

    each_block(tab_ref, parts, width, prepare)

    def block(i, _):
        cols = pl.ds(pl.multiple_of(i * BQ, BQ), BQ)
        qb = qx[:, cols]

        def score(blocks, j, tops):
            at = pl.ds(pl.multiple_of(j * BK, BK), blocks * BK)
            ok = allowed(kseg_ref, qseg_ref, i, j, blocks)
            out = []
            for h in range(2):
                s = matmul(kx[h, at, :], qb)
                s = jnp.where(ok, s, masked_score)
                scores[h, at, :] = s
                out.append(jnp.maximum(tops[h], jnp.max(s.reshape(blocks * BK // 8, 8, BQ), axis=0)))
            return tuple(out)

        tops = sweep(tab_ref, i, score, (jnp.full((8, BQ), masked_score, F32),) * 2)
        tops = [jnp.max(top, axis=0, keepdims=True) for top in tops]

        def weigh(blocks, j, accs):
            at = pl.ds(pl.multiple_of(j * BK, BK), blocks * BK)
            out = []
            for h in range(2):
                p = jnp.exp(scores[h, at, :] - tops[h]).astype(BF16)
                out.append(accs[h] + matmul(vx[h, :, at], p))
            return tuple(out)

        accs = sweep(tab_ref, i, weigh, (jnp.zeros((HDIM + 16, BQ), F32),) * 2)
        for h in range(2):
            total = accs[h][HDIM : HDIM + 1, :]
            ot_ref[h * HDIM : (h + 1) * HDIM, cols] = (accs[h][:HDIM, :] / total).astype(BF16)
            lse_ref[0, h : h + 1, cols] = tops[h] + jnp.log(total)
        return 0

    lax.fori_loop(0, tokens // BQ, block, 0)

    def finish(part, here, there):
        o_refs[part][here, :] = ot_ref[:, there].astype(F32).T.astype(BF16)

    each_block(tab_ref, parts, width, finish)


def three_parts(x):
    high = x.astype(BF16)
    rest = x - high.astype(F32)
    middle = rest.astype(BF16)
    return high, middle, (rest - middle.astype(F32)).astype(BF16)


def backward_kernel(parts, tab_ref, kseg_ref, qseg_ref, *refs):
    qkv_refs, do_refs = refs[:parts], refs[parts : 2 * parts]
    ot_ref, lse_ref = refs[2 * parts : 2 * parts + 2]
    *out_refs, kx, vx, kt, qx, dox, qt, dot, dq, dk, dv = refs[-10 - parts :]
    tokens = kt.shape[1]
    width = tokens // parts
    lane = lax.broadcasted_iota(jnp.int32, (BK, 128), 1)
    sub = lax.broadcasted_iota(jnp.int32, (HDIM, BK), 0)
    one0 = jnp.where((lane >= HDIM) & (lane < HDIM + 3), 1.0, 0.0).astype(BF16)
    one1 = jnp.where(lane < 3, 1.0, 0.0).astype(BF16)
    zero = jnp.zeros((BK, 128), BF16)

    def extra(x):
        high, middle, low = (e.astype(F32) for e in three_parts(x))
        rows = jnp.where(
            sub == 0, high, jnp.where(sub == 1, middle, jnp.where(sub == 2, low, 0.0))
        )
        return rows.astype(BF16)

    def prepare(part, here, there):
        k = qkv_refs[part][here, PAIR : 2 * PAIR]
        kt[:, there] = k.astype(F32).T.astype(BF16)
        kx[0, there, :] = jnp.where(lane < HDIM, k, one0)
        kx[1, there, :] = jnp.where(lane < HDIM, one1, k)
        v = qkv_refs[part][here, 2 * PAIR :]
        vx[0, there, :] = jnp.where(lane < HDIM, v, one0)
        vx[1, there, :] = jnp.where(lane < HDIM, one1, v)
        q = qkv_refs[part][here, :PAIR]
        qt[0, there, :] = jnp.where(lane < HDIM, q, zero)
        qt[1, there, :] = jnp.where(lane < HDIM, zero, q)
        do = do_refs[part][here, :]
        dot[0, there, :] = jnp.where(lane < HDIM, do, zero)
        dot[1, there, :] = jnp.where(lane < HDIM, zero, do)
        turned = do.astype(F32).T
        prod = turned * ot_ref[:, there].astype(F32)
        inner0 = jnp.sum(prod[:HDIM], axis=0, keepdims=True)
        inner1 = jnp.sum(prod[HDIM:], axis=0, keepdims=True)
        turned = turned.astype(BF16)
        dox[0, :HDIM, there] = turned[:HDIM]
        dox[0, HDIM:, there] = extra(-inner0)
        dox[1, HDIM:, there] = turned[HDIM:]
        dox[1, :HDIM, there] = extra(-inner1)
        turned = q.astype(F32).T.astype(BF16)
        qx[0, :HDIM, there] = turned[:HDIM]
        qx[0, HDIM:, there] = extra(-lse_ref[0, 0:1, there])
        qx[1, HDIM:, there] = turned[HDIM:]
        qx[1, :HDIM, there] = extra(-lse_ref[0, 1:2, there])
        dk[there, :] = jnp.zeros((BK, 128), F32)
        dv[there, :] = jnp.zeros((BK, 128), F32)

    each_block(tab_ref, parts, width, prepare)

    def block(i, _):
        cols = pl.ds(pl.multiple_of(i * BQ, BQ), BQ)

        def step(blocks, j, carry):
            at = pl.ds(pl.multiple_of(j * BK, BK), blocks * BK)
            ok = allowed(kseg_ref, qseg_ref, i, j, blocks)
            new = []
            dvs = dv[at, :]
            dks = dk[at, :]
            for h in range(2):
                s = matmul(kx[h, at, :], qx[h, :, cols])
                s = jnp.where(ok, s, masked_score)
                p = jnp.exp(s)
                dp = matmul(vx[h, at, :], dox[h, :, cols])
                ds = (p * dp).astype(BF16)
                dvs = dvs + matmul(p.astype(BF16), dot[h, cols, :])
                dks = dks + matmul(ds, qt[h, cols, :])
                new.append(carry[h] + matmul(kt[h * HDIM : (h + 1) * HDIM, at], ds))
            dv[at, :] = dvs
            dk[at, :] = dks
            return tuple(new)

        init = tuple(jnp.zeros((HDIM, BQ), F32) for _ in range(2))
        res = sweep(tab_ref, i, step, init)
        for h in range(2):
            dq[h * HDIM : (h + 1) * HDIM, cols] = res[h] * (HDIM**-0.5)
        return 0

    lax.fori_loop(0, tokens // BQ, block, 0)

    def finish(part, here, there):
        out_refs[part][here, :PAIR] = dq[:, there].T.astype(BF16)
        out_refs[part][here, PAIR : 2 * PAIR] = dk[there, :].astype(BF16)
        out_refs[part][here, 2 * PAIR :] = dv[there, :].astype(BF16)

    each_block(tab_ref, parts, width, finish)


def lanes_of(first, step):
    return lambda g, t: (0, first + step * g)


def attend_specs(qkv_parts, chunk):
    parts = len(qkv_parts)
    width = qkv_parts[0].shape[0]
    tokens = parts * width
    every = qkv_parts[0].shape[1] // (3 * PAIR)
    first, pairs = chunk
    seg_specs = [
        pl.BlockSpec((tokens, 1), lambda g, t: (0, 0)),
        pl.BlockSpec((1, tokens), lambda g, t: (0, 0)),
    ]
    qkv_specs = [pl.BlockSpec((width, 3 * PAIR), lanes_of(first, 1))] * parts
    o_specs = [pl.BlockSpec((width, PAIR), lanes_of(first, 1))] * parts
    ot_spec = pl.BlockSpec((PAIR, tokens), lambda g, t: (first + g, 0))
    lse_spec = pl.BlockSpec((1, 2, tokens), lambda g, t: (first + g, 0, 0))
    return parts, width, tokens, every, pairs, seg_specs, qkv_specs, o_specs, ot_spec, lse_spec


def attend_forward(qkv_parts, seg, keep, tables, chunk, begun=()):
    parts, width, tokens, every, pairs, seg_specs, qkv_specs, o_specs, ot_spec, lse_spec = (
        attend_specs(qkv_parts, chunk)
    )
    kseg = jnp.where(keep == 1, seg, -1)[:, None]
    return pl.pallas_call(
        functools.partial(forward_kernel, parts),
        grid_spec=pltpu.PrefetchScalarGridSpec(
            num_scalar_prefetch=1,
            grid=(pairs,),
            in_specs=seg_specs + qkv_specs + [pl.BlockSpec(memory_space=pl.ANY)] * len(begun),
            out_specs=o_specs + [ot_spec, lse_spec],
            scratch_shapes=[
                pltpu.VMEM((2, tokens, 128), BF16),
                pltpu.VMEM((2, HDIM + 16, tokens), BF16),
                pltpu.VMEM((PAIR, tokens), BF16),
                pltpu.VMEM((2, tokens, BQ), F32),
            ],
        ),
        out_shape=[jax.ShapeDtypeStruct((width, every * PAIR), BF16)] * parts
        + [
            jax.ShapeDtypeStruct((every * PAIR, tokens), BF16),
            jax.ShapeDtypeStruct((every, 2, tokens), F32),
        ],
        compiler_params=pltpu.CompilerParams(vmem_limit_bytes=40 * 2**20),
        cost_estimate=pl.CostEstimate(
            flops=2**10, bytes_accessed=2**10, transcendentals=0
        ),
        input_output_aliases={3 + parts + n: n for n in range(len(begun))},
        name="attend_forward",
    )(tables, kseg, seg[None, :], *qkv_parts, *begun)


def attend_backward(qkv_parts, turned, grad_ctx, lse, seg, keep, tables, chunk, begun=()):
    parts, width, tokens, every, pairs, seg_specs, qkv_specs, o_specs, ot_spec, lse_spec = (
        attend_specs(qkv_parts, chunk)
    )
    kseg = jnp.where(keep == 1, seg, -1)[:, None]
    result = pl.BlockSpec((width, 3 * PAIR), lanes_of(chunk[0], 1))
    return pl.pallas_call(
        functools.partial(backward_kernel, parts),
        grid_spec=pltpu.PrefetchScalarGridSpec(
            num_scalar_prefetch=1,
            grid=(pairs,),
            in_specs=seg_specs
            + qkv_specs
            + o_specs
            + [ot_spec, lse_spec]
            + [pl.BlockSpec(memory_space=pl.ANY)] * len(begun),
            out_specs=[result] * parts,
            scratch_shapes=[
                pltpu.VMEM((2, tokens, 128), BF16),
                pltpu.VMEM((2, tokens, 128), BF16),
                pltpu.VMEM((PAIR, tokens), BF16),
                pltpu.VMEM((2, 128, tokens), BF16),
                pltpu.VMEM((2, 128, tokens), BF16),
                pltpu.VMEM((2, tokens, 128), BF16),
                pltpu.VMEM((2, tokens, 128), BF16),
                pltpu.VMEM((PAIR, tokens), F32),
                pltpu.VMEM((tokens, 128), F32),
                pltpu.VMEM((tokens, 128), F32),
            ],
        ),
        out_shape=[jax.ShapeDtypeStruct((width, every * 3 * PAIR), BF16)] * parts,
        input_output_aliases={5 + 2 * parts + n: n for n in range(len(begun))},
        compiler_params=pltpu.CompilerParams(vmem_limit_bytes=48 * 2**20),
        cost_estimate=pl.CostEstimate(
            flops=2**10,
            bytes_accessed=2**10,
            transcendentals=0,
        ),
        name="attend_backward",
    )(tables, kseg, seg[None, :], *qkv_parts, *grad_ctx, turned, lse, *begun)


def row_block(width):
    return FEED_ROWS if width % FEED_ROWS == 0 else width


def gelu_and_slope(u):
    root = 0.7978845608028654
    square = u * u
    t = jnp.tanh(u * (root + (root * 0.044715) * square))
    half = 0.5 * t + 0.5
    slope = half + (0.5 * u) * (1.0 - t * t) * (root + (root * 0.134145) * square)
    return u * half, slope


def feed_kernel(step, x_ref, up_ref, bias_ref, down_ref, *refs):
    x_all, hidden_all, slope_all, out_ref = refs[-4:]
    x = x_ref[...]
    x_all[...] = x
    units = up_ref.shape[1]
    total = None
    for first in range(0, units, step):
        at = slice(first, first + step)
        act, slope = gelu_and_slope(matmul(x, up_ref[:, at]) + bias_ref[:, at])
        act = act.astype(BF16)
        hidden_all[:, at] = act
        slope_all[:, at] = slope.astype(BF16)
        term = matmul(act, down_ref[at, :])
        total = term if total is None else total + term
    out_ref[...] = total.astype(BF16)


def feed_forward(part, parts, x, up, bias, down, begun):
    width, model = x.shape
    units = up.shape[1]
    rows = row_block(width)
    steps = width // rows
    own = lambda k: (k, 0)
    whole = lambda k: (part * steps + k, 0)
    fixed = lambda k: (0, 0)
    once = pl.Buffered(1)
    every = parts * width
    return pl.pallas_call(
        functools.partial(feed_kernel, min(units, FEED)),
        grid=(steps,),
        in_specs=[
            pl.BlockSpec((rows, model), own),
            pl.BlockSpec((model, units), fixed, pipeline_mode=once),
            pl.BlockSpec((1, units), fixed, pipeline_mode=once),
            pl.BlockSpec((units, model), fixed, pipeline_mode=once),
        ]
        + [pl.BlockSpec(memory_space=pl.ANY)] * len(begun),
        out_specs=[
            pl.BlockSpec((rows, model), whole),
            pl.BlockSpec((rows, units), whole),
            pl.BlockSpec((rows, units), whole),
            pl.BlockSpec((rows, model), own),
        ],
        out_shape=[
            jax.ShapeDtypeStruct((every, model), BF16),
            jax.ShapeDtypeStruct((every, units), BF16),
            jax.ShapeDtypeStruct((every, units), BF16),
            jax.ShapeDtypeStruct((width, model), BF16),
        ],
        input_output_aliases={4 + n: n for n in range(len(begun))},
        compiler_params=pltpu.CompilerParams(vmem_limit_bytes=48 * 2**20),
        cost_estimate=pl.CostEstimate(
            flops=6 * width * model * units, bytes_accessed=2**24, transcendentals=0
        ),
        name="feed_forward",
    )(x, up, bias[None, :], down, *begun)


def feed_back_kernel(step, g_ref, slope_ref, down_ref, up_ref, *refs):
    pre_all, sums_ref, out_ref = refs[-3:]
    g = g_ref[...]
    units = up_ref.shape[1]

    @pl.when(pl.program_id(0) == 0)
    def _():
        sums_ref[...] = jnp.zeros_like(sums_ref)

    total = None
    for first in range(0, units, step):
        at = slice(first, first + step)
        pre = contract_cols(g, down_ref[at, :]) * slope_ref[:, at].astype(F32)
        pre = pre.astype(BF16)
        pre_all[:, at] = pre
        sums_ref[:, at] += jnp.sum(pre.astype(F32), axis=0, keepdims=True)
        term = contract_cols(pre, up_ref[:, at])
        total = term if total is None else total + term
    out_ref[...] = total.astype(BF16)


def feed_back(part, parts, g, slope_all, up, down, begun):
    width, model = g.shape
    units = up.shape[1]
    rows = row_block(width)
    steps = width // rows
    own = lambda k: (k, 0)
    whole = lambda k: (part * steps + k, 0)
    fixed = lambda k: (0, 0)
    once = pl.Buffered(1)
    every = parts * width
    return pl.pallas_call(
        functools.partial(feed_back_kernel, min(units, FEED)),
        grid=(steps,),
        in_specs=[
            pl.BlockSpec((rows, model), own),
            pl.BlockSpec((rows, units), whole),
            pl.BlockSpec((units, model), fixed, pipeline_mode=once),
            pl.BlockSpec((model, units), fixed, pipeline_mode=once),
        ]
        + [pl.BlockSpec(memory_space=pl.ANY)] * len(begun),
        out_specs=[
            pl.BlockSpec((rows, units), whole),
            pl.BlockSpec((1, units), fixed),
            pl.BlockSpec((rows, model), own),
        ],
        out_shape=[
            jax.ShapeDtypeStruct((every, units), BF16),
            jax.ShapeDtypeStruct((1, units), F32),
            jax.ShapeDtypeStruct((width, model), BF16),
        ],
        input_output_aliases={4 + n: n for n in range(len(begun))},
        compiler_params=pltpu.CompilerParams(vmem_limit_bytes=48 * 2**20),
        cost_estimate=pl.CostEstimate(
            flops=2**10, bytes_accessed=2**10, transcendentals=0
        ),
        name="feed_back",
    )(g, slope_all, down, up, *begun)


def weight_grad_kernel(parts, *refs):
    a_refs, d_refs = refs[:parts], refs[parts : 2 * parts]
    out_ref, sums_ref = refs[2 * parts :]
    out_ref[...] = total([contract_rows(a[...], d[...]) for a, d in zip(a_refs, d_refs)]).astype(BF16)
    sums_ref[...] = total([jnp.sum(d[...].astype(F32), axis=0, keepdims=True) for d in d_refs])


def weight_grad(a_parts, d_parts, first, count):
    parts = len(a_parts)
    width, model = a_parts[0].shape
    columns = 3 * PAIR
    return pl.pallas_call(
        functools.partial(weight_grad_kernel, parts),
        grid=(count,),
        in_specs=[pl.BlockSpec((width, model), lambda k: (0, 0), pipeline_mode=pl.Buffered(1))] * parts
        + [pl.BlockSpec((width, columns), lambda k: (0, first + k))] * parts,
        out_specs=[
            pl.BlockSpec((model, columns), lambda k: (0, k)),
            pl.BlockSpec((1, columns), lambda k: (0, k)),
        ],
        out_shape=[
            jax.ShapeDtypeStruct((model, count * columns), BF16),
            jax.ShapeDtypeStruct((1, count * columns), F32),
        ],
        compiler_params=pltpu.CompilerParams(vmem_limit_bytes=40 * 2**20),
        cost_estimate=pl.CostEstimate(flops=2**10, bytes_accessed=2**10, transcendentals=0),
        name="weight_grad",
    )(*a_parts, *d_parts)


def input_grad_kernel(d_ref, w_ref, out_ref):
    out_ref[...] = contract_cols(d_ref[...], w_ref[...]).astype(BF16)


def input_grad(d, weight):
    width, columns = d.shape
    model = weight.shape[0]
    rows = row_block(width)
    return pl.pallas_call(
        input_grad_kernel,
        grid=(width // rows,),
        in_specs=[
            pl.BlockSpec((rows, columns), lambda k: (k, 0)),
            pl.BlockSpec((model, columns), lambda k: (0, 0), pipeline_mode=pl.Buffered(1)),
        ],
        out_specs=pl.BlockSpec((rows, model), lambda k: (k, 0)),
        out_shape=jax.ShapeDtypeStruct((width, model), BF16),
        compiler_params=pltpu.CompilerParams(vmem_limit_bytes=40 * 2**20),
        cost_estimate=pl.CostEstimate(flops=2**10, bytes_accessed=2**10, transcendentals=0),
        name="input_grad",
    )(d, weight)


def spread_kernel(tab_ref, mine_ref, theirs_ref, out_ref):
    mine = pl.program_id(1) == tab_ref[0]

    def put(ref):
        for c in range(3):
            out_ref[c] = ref[:, c * PAIR : (c + 1) * PAIR].astype(F32)

    @pl.when(mine)
    def _():
        put(mine_ref)

    @pl.when(jnp.logical_not(mine))
    def _():
        put(theirs_ref)


def spread(mine, theirs, side, out_pairs, first, begun):
    half, columns = mine.shape
    count = columns // (3 * PAIR)
    block = pl.BlockSpec((half, 3 * PAIR), lambda k, s, t: (0, k))
    return pl.pallas_call(
        lambda tab, a, b, *refs: spread_kernel(tab, a, b, refs[-1]),
        grid_spec=pltpu.PrefetchScalarGridSpec(
            num_scalar_prefetch=1,
            grid=(count, 2),
            in_specs=[block, block] + [pl.BlockSpec(memory_space=pl.ANY)] * len(begun),
            out_specs=pl.BlockSpec((3, half, PAIR), lambda k, s, t: (0, s, first + k)),
        ),
        out_shape=jax.ShapeDtypeStruct((3, 2 * half, out_pairs * PAIR), F32),
        input_output_aliases={3 + n: n for n in range(len(begun))},
        compiler_params=pltpu.CompilerParams(vmem_limit_bytes=32 * 2**20),
        cost_estimate=pl.CostEstimate(flops=2**10, bytes_accessed=2**10, transcendentals=0),
        name="spread",
    )(jnp.reshape(side, (1,)).astype(jnp.int32), mine, theirs, *begun)


def after(value, *others):
    return lax.optimization_barrier((value, *others))[0]


class Layout:
    def __init__(self, mesh):
        self.dp, self.n = mesh.shape["dp"], mesh.shape["mp"]
        self.pairs = self.dp // 2
        self.axes = ("dp", "mp")

    def device(self, pair, core, m):
        return (2 * pair + core) * self.n + m

    def at_rank(self, pair, group, rank):
        return self.device(pair, rank % 2, group * (self.n // 2) + rank // 2)

    def each(self):
        for pair in range(self.pairs):
            for group in range(2):
                for rank in range(self.n):
                    yield pair, group, rank

    def stays(self):
        core, m = lax.axis_index("dp") % 2, lax.axis_index("mp")
        return (m // (self.n // 2) == core) & (self.rank() == m)

    def send(self, value, back=False):
        moves = [(self.device(p, g, r), self.at_rank(p, g, r)) for p, g, r in self.each()]
        return lax.ppermute(
            value, self.axes, [(b, a) if back else (a, b) for a, b in moves if a != b]
        )

    def regroup(self, value):
        return jnp.where(self.stays(), value, self.send(value))

    def give_back(self, value):
        return jnp.where(self.stays(), value, self.send(value, True))

    def partner(self, value, bit, only=lambda p, g, r: True):
        def other(p, c):
            return (p, 1 - c) if bit < 0 else (p ^ (1 << bit), c)

        moves = [
            (self.device(*other(p, c), m), self.device(p, c, m))
            for p, c, m in self.each()
            if only(p, c, m)
        ]
        return lax.ppermute(value, self.axes, moves)

    def side(self, bit):
        dp = lax.axis_index("dp")
        return dp % 2 if bit < 0 else (dp // 2 >> bit) % 2

    def joined(self, mine, theirs, bit):
        high = self.side(bit) == 1
        return jnp.concatenate(
            [jnp.where(high, theirs, mine), jnp.where(high, mine, theirs)], 0
        )

    def regroup_first(self, weight, small, tokens):
        rows = weight.shape[0] // 4
        part = 2 * self.side(0) + self.side(1)
        quarter = lax.dynamic_slice_in_dim(weight, part * rows, rows, 0)
        got = self.send(quarter)
        small = self.regroup(after(small, got))
        tokens = self.regroup(after(tokens, got, small))
        for bit in (1, 0):
            got = self.joined(got, self.partner(got, bit, self.moving), bit)
        return jnp.where(self.stays(), weight, got), small, tokens

    def moving(self, pair, core, m):
        return self.at_rank(pair, core, m) != self.device(pair, core, m)

    def to_rank(self, value, ahead):
        moves = [
            (self.at_rank(p, g, r), self.at_rank(p, g, (r + ahead) % self.n))
            for p, g, r in self.each()
        ]
        return lax.ppermute(value, self.axes, moves)

    def rank(self):
        core = lax.axis_index("dp") % 2
        return (lax.axis_index("mp") % (self.n // 2)) * 2 + core

    def gather(self, mine):
        return [mine] + [self.to_rank(mine, self.n - k) for k in range(1, self.n)]

    def scatter_sum(self, shares):
        total = shares[0].astype(jnp.float32)
        for k in range(1, self.n):
            total = total + self.to_rank(shares[k].astype(jnp.bfloat16), k).astype(jnp.float32)
        return total

    def sum_all(self, value):
        devices = self.dp * self.n
        steps = [1 << k for k in range(devices.bit_length() - 1)]
        for step in steps:
            value = value + lax.ppermute(value, self.axes, [(i, i ^ step) for i in range(devices)])
        return value

    def sum_dp(self, value, turn):
        order = [(i + turn) % self.dp for i in range(self.dp)]
        return lax.psum(value, "dp", axis_index_groups=[order])

    def halved(self, value, bit):
        half, high = value.shape[0] // 2, self.side(bit)
        sent = lax.dynamic_slice_in_dim(value, (1 - high) * half, half, 0)
        kept = lax.dynamic_slice_in_dim(value, high * half, half, 0)
        got = self.partner(sent, bit)
        return (kept.astype(jnp.float32) + got.astype(jnp.float32)).astype(jnp.bfloat16)

    def order(self, first):
        bits = list(range(self.pairs.bit_length() - 1))
        return bits[first:] + bits[:first]

    def halved_by(self, value, bits):
        for bit in bits:
            value = self.halved(value, bit)
        return value

    def joined_by(self, value, bits):
        for bit in bits[::-1]:
            value = self.joined(value, self.partner(value, bit), bit)
        return value


def for_kernel(shares, rank):
    width = shares[0].shape[0]
    if width % BQ == 0:
        return shares, rank * (width // BQ)
    return [jnp.roll(jnp.concatenate(shares, 0), rank * width, 0)], 0


def from_kernel(arrays, rank, shares):
    if len(arrays) == shares:
        return arrays
    width = arrays[0].shape[0] // shares
    return jnp.split(jnp.roll(arrays[0], -rank * width, 0), shares, 0)


def by_pairs(weight, pairs):
    return (
        weight.reshape(-1, 3, pairs, PAIR).transpose(0, 2, 1, 3).reshape(-1, 3 * pairs * PAIR)
    )


def total(terms):
    return functools.reduce(jnp.add, terms)


def body(
    layout,
    tokens,
    ln1_gain,
    ln1_bias,
    w_qkv,
    qv_bias,
    w_out,
    out_bias,
    ln2_gain,
    ln2_bias,
    ln3_gain,
    ln3_bias,
    w_up,
    up_bias,
    w_down,
    down_bias,
    ln4_gain,
    ln4_bias,
    row_grid,
    pad_mask,
    cotangent,
):
    f32, bf16 = jnp.float32, jnp.bfloat16
    model_dim = tokens.shape[1]
    group_rows = pad_mask.shape[0]
    width = w_qkv.shape[2]
    units = w_up.shape[1]
    shares = layout.n
    rank = layout.rank()

    small = jnp.concatenate(
        [
            qv_bias.reshape(-1),
            up_bias,
            pad_mask.astype(f32),
            row_grid[0].astype(f32),
        ]
    )
    pairs = width // PAIR
    chunks = 2 if pairs % 2 == 0 else 1
    w_qkv, small, tokens = layout.regroup_first(w_qkv, small, tokens)
    qv_bias = small[: 2 * width].reshape(2, width)
    up_bias = small[2 * width : 2 * width + units]
    keep = small[2 * width + units : 2 * width + units + group_rows].astype(jnp.int32)
    grid_row = small[2 * width + units + group_rows :].astype(jnp.int32)
    w_qkv = by_pairs(w_qkv, pairs)
    half = units // 2
    w_out_far = layout.send(after(w_out, tokens))
    w_up_far = layout.send(after(w_up, tokens))
    w_top_far = layout.send(after(w_down[:half], tokens))
    w_low_far = layout.send(after(w_down[half:], tokens))
    cotangent = layout.regroup(after(cotangent, w_low_far))

    resid_in = tokens.astype(f32)
    norm1_out, normed1, inv1 = norm_parts(resid_in, ln1_gain, ln1_bias)
    a1 = layout.gather(norm1_out.astype(bf16))
    zeros = jnp.zeros((width,), f32)
    qkv_bias = by_pairs(jnp.concatenate([qv_bias[0], zeros, qv_bias[1]]), pairs)
    qkv_scale = by_pairs(
        jnp.concatenate([zeros + HDIM ** (-0.5), zeros + 1.0, zeros + 1.0]), pairs
    )
    qkv = [((matmul(x, w_qkv) + qkv_bias) * qkv_scale).astype(bf16) for x in a1]
    qkv, turn = for_kernel(qkv, rank)
    seg, tables = row_tables(grid_row, group_rows, turn)
    begun = ()
    for pair in range(pairs):
        if pair and pair == pairs // 2:
            tables, w_up_far = lax.optimization_barrier((tables, w_up_far))
        begun = attend_forward(qkv, seg, keep, tables, (pair, 1), begun)
    *context, context_turned, log_total = begun
    *context, w_out_far, w_top_far, w_low_far = lax.optimization_barrier(
        (*context, w_out_far, w_top_far, w_low_far)
    )
    context = from_kernel(context, rank, shares)
    stays = layout.stays()
    w_out = jnp.where(stays, w_out, w_out_far)
    w_up = jnp.where(stays, w_up, w_up_far)
    w_down = jnp.where(stays, w_down, jnp.concatenate([w_top_far, w_low_far], 0))
    branch_z = layout.scatter_sum([matmul(x, w_out) for x in context]) + out_bias
    norm2_out, normed2, inv2 = norm_parts(branch_z, ln2_gain, ln2_bias)
    resid_mid = resid_in + norm2_out
    norm3_out, normed3, inv3 = norm_parts(resid_mid, ln3_gain, ln3_bias)
    a3 = layout.gather(norm3_out.astype(bf16))
    begun, shares_f = (), []
    for part, x in enumerate(a3):
        if part == shares - 1:
            x, cotangent = lax.optimization_barrier((x, cotangent))
        *begun, share = feed_forward(part, shares, x, w_up, up_bias, w_down, begun)
        shares_f.append(share)
    a3_all, hidden, slope = begun
    branch_f = layout.scatter_sum(shares_f) + down_bias
    norm4_out, normed4, inv4 = norm_parts(branch_f, ln4_gain, ln4_bias)
    layer_out = (resid_mid + norm4_out).astype(bf16)

    upstream = cotangent.astype(f32)
    grad_f = norm_back(upstream, normed4, inv4, ln4_gain).astype(bf16)
    grad_f_all = layout.gather(grad_f)
    g_w_down = contract_rows(hidden, jnp.concatenate(grad_f_all, 0)).astype(bf16)
    begun, shares_a3, g_up_bias = (), [], []
    for part, g in enumerate(grad_f_all):
        if part:
            g, g_w_down = lax.optimization_barrier((g, g_w_down))
        *begun, unit_sums, share = feed_back(part, shares, g, slope, w_up, w_down, begun)
        shares_a3.append(share)
        g_up_bias.append(unit_sums[0])
    [grad_pre] = begun
    g_w_down_far = layout.send(g_w_down, True)
    grad_a3 = layout.scatter_sum(shares_a3)
    g_up_bias = total(g_up_bias)
    g_w_up = contract_rows(a3_all, grad_pre).astype(bf16)
    g_w_up_far = layout.send(g_w_up, True)
    grad_mid = upstream + norm_back(grad_a3, normed3, inv3, ln3_gain)
    grad_z = norm_back(grad_mid, normed2, inv2, ln2_gain).astype(bf16)
    grad_z_all = layout.gather(grad_z)
    grad_ctx = [contract_cols(g, w_out).astype(bf16) for g in grad_z_all]
    g_w_out = total([contract_rows(x, g) for x, g in zip(context, grad_z_all)]).astype(bf16)
    g_w_out_far = layout.send(g_w_out, True)
    g_w_down_far, g_w_up, *grad_ctx = lax.optimization_barrier((g_w_down_far, g_w_up, *grad_ctx))
    grad_ctx, _ = for_kernel(grad_ctx, rank)
    g_w_down = jnp.where(stays, g_w_down, g_w_down_far)
    tables, g_w_down = lax.optimization_barrier((tables, g_w_down))
    g_w_down = layout.sum_dp(g_w_down, 1)
    calls = [(0, pairs // 2)] if pairs > 1 else []
    calls += [(k, 1) for k in range(pairs // 2, pairs)]
    grad_qkv = ()
    for call in calls:
        if call == calls[-1]:
            g_w_up_far, g_w_out_far, *grad_qkv = lax.optimization_barrier(
                (g_w_up_far, g_w_out_far, *grad_qkv)
            )
            g_w_up = jnp.where(stays, g_w_up, g_w_up_far)
            g_w_out = jnp.where(stays, g_w_out, g_w_out_far)
            tables, g_w_down, g_w_up, g_w_out = lax.optimization_barrier(
                (tables, g_w_down, g_w_up, g_w_out)
            )
            g_w_up = layout.sum_dp(g_w_up, 0)
            g_w_out = layout.sum_dp(g_w_out, 0)
        grad_qkv = attend_backward(
            qkv, context_turned, grad_ctx, log_total, seg, keep, tables, call, grad_qkv
        )
    layer_out = layout.give_back(after(layer_out, g_w_out_far))
    grad_qkv = from_kernel(grad_qkv, rank, shares)
    grad_a1 = [input_grad(g, w_qkv) for g in grad_qkv]
    grad_a1 = layout.scatter_sum(grad_a1)
    grad_input = grad_mid + norm_back(grad_a1, normed1, inv1, ln1_gain)
    grad_input = grad_input.astype(bf16)
    g_w_qkv, sums = [], []
    each = pairs // chunks
    for chunk in range(chunks):
        g_part, part_sums = weight_grad(a1, grad_qkv, chunk * each, each)
        g_w_qkv.append(layout.halved(layout.give_back(g_part), -1))
        sums.append(part_sums)
    sums = jnp.concatenate(sums, 1)
    g_w_qkv = [layout.halved_by(g, layout.order(k)) for k, g in enumerate(g_w_qkv)]
    g_w_qkv = [layout.joined_by(g, layout.order(k)) for k, g in enumerate(g_w_qkv)]
    begun = ()
    for chunk, mine in enumerate(g_w_qkv):
        theirs = layout.partner(mine, -1)
        begun = (spread(mine, theirs, layout.side(-1), pairs, chunk * each, begun),)
    g_w_qkv = begun[0].transpose(1, 0, 2)
    sums = sums.reshape(pairs, 3, PAIR).transpose(1, 0, 2).reshape(3, width)
    grad_input = layout.give_back(grad_input).astype(f32)

    norm_terms = jnp.stack(
        [
            jnp.sum(grad_a1 * normed1, 0),
            jnp.sum(grad_a1, 0),
            jnp.sum(grad_z.astype(f32), 0),
            jnp.sum(grad_mid * normed2, 0),
            jnp.sum(grad_mid, 0),
            jnp.sum(grad_a3 * normed3, 0),
            jnp.sum(grad_a3, 0),
            jnp.sum(grad_f.astype(f32), 0),
            jnp.sum(upstream * normed4, 0),
            jnp.sum(upstream, 0),
        ],
        0,
    )
    all_units = lax.dynamic_update_slice(jnp.zeros((units * shares,), f32), g_up_bias, (rank * units,))
    all_width = lax.dynamic_update_slice(
        jnp.zeros((2, width * shares), f32), jnp.stack([sums[0], sums[2]], 0), (0, rank * width)
    )
    small = layout.sum_all(
        jnp.concatenate([norm_terms.reshape(-1), all_width.reshape(-1), all_units])
    )
    norm_terms = small[: 10 * model_dim].reshape(10, model_dim)
    all_width = small[10 * model_dim : 12 * model_dim].reshape(2, width * shares)
    all_units = small[12 * model_dim :]
    m = lax.axis_index("mp")
    g_qv_bias = lax.dynamic_slice(all_width, (0, m * width), (2, width))
    g_up_bias = lax.dynamic_slice(all_units, (m * units,), (units,))
    return (
        layer_out,
        grad_input,
        norm_terms[0],
        norm_terms[1],
        g_w_qkv,
        g_qv_bias,
        g_w_out.astype(f32),
        norm_terms[2],
        norm_terms[3],
        norm_terms[4],
        norm_terms[5],
        norm_terms[6],
        g_w_up.astype(f32),
        g_up_bias,
        g_w_down.astype(f32),
        norm_terms[7],
        norm_terms[8],
        norm_terms[9],
    )


def solution(mesh):
    in_specs = (
        P(("dp", "mp"), None),
        P(),
        P(),
        P(None, None, "mp"),
        P(None, "mp"),
        P("mp", None),
        P(),
        P(),
        P(),
        P(),
        P(),
        P(None, "mp"),
        P("mp"),
        P("mp", None),
        P(),
        P(),
        P(),
        P("dp", None),
        P("dp"),
        P(("dp", "mp"), None),
    )
    out_specs = (
        P(("dp", "mp"), None),
        P(("dp", "mp"), None),
        P(),
        P(),
        P(None, None, "mp"),
        P(None, "mp"),
        P("mp", None),
        P(),
        P(),
        P(),
        P(),
        P(),
        P(None, "mp"),
        P("mp"),
        P("mp", None),
        P(),
        P(),
        P(),
    )
    return jax.shard_map(functools.partial(body, Layout(mesh)), mesh=mesh, in_specs=in_specs, out_specs=out_specs, check_vma=False)
```

```python
import functools

import jax
import jax.numpy as jnp
from jax import lax
from jax.experimental import pallas as pl
from jax.experimental.pallas import tpu as pltpu
from jax.sharding import PartitionSpec as P

HDIM = 64
TEXT = 64


epsilon = 1e-05
masked_score = -1e30


def norm_parts(values, ln_gain, ln_bias):
    centred = values - jnp.mean(values, -1, keepdims=True)
    inv_std = lax.rsqrt(jnp.mean(centred * centred, -1, keepdims=True) + epsilon)
    normed = centred * inv_std
    return (normed * ln_gain + ln_bias, normed, inv_std)


def norm_back(upstream, normed, inv_std, ln_gain):
    scaled = upstream * ln_gain
    return inv_std * (
        scaled
        - jnp.mean(scaled, -1, keepdims=True)
        - normed * jnp.mean(scaled * normed, -1, keepdims=True)
    )


def contract_rows(left, right):
    return lax.dot_general(
        left, right, (((0,), (0,)), ((), ())), preferred_element_type=jnp.float32
    )


def contract_cols(left, right):
    return lax.dot_general(
        left, right, (((1,), (1,)), ((), ())), preferred_element_type=jnp.float32
    )


BQ = 256
BK = 256
MOST = 4
FEED = 1024
FEED_ROWS = 640
PAIR = 2 * HDIM
F32 = jnp.float32
BF16 = jnp.bfloat16


def matmul(left, right):
    return jnp.dot(left, right, preferred_element_type=F32)


def row_tables(grid_row, tokens, turn):
    side = jnp.max(grid_row)
    length = TEXT + side * side
    rows = tokens // length
    used = rows * length
    position = jnp.arange(tokens, dtype=jnp.int32)
    seg = jnp.minimum(position // length, rows)
    blocks = tokens // BQ
    first = jnp.arange(blocks, dtype=jnp.int32) * BQ
    start = jnp.where(first < used, (first // length) * length, first)
    low = start // BK
    diag = first // BK
    turns = jnp.full((blocks,), turn, jnp.int32)
    return seg, jnp.stack([low, diag, turns]).astype(jnp.int32)


def allowed(kseg_ref, qseg_ref, i, j, blocks):
    qs = qseg_ref[:, pl.ds(pl.multiple_of(i * BQ, BQ), BQ)]
    ks = kseg_ref[pl.ds(pl.multiple_of(j * BK, BK), blocks * BK), :]
    ik = j * BK + lax.broadcasted_iota(jnp.int32, (blocks * BK, BQ), 0)
    iq = i * BQ + lax.broadcasted_iota(jnp.int32, (blocks * BK, BQ), 1)
    return ((ks == qs) & (ik <= iq)) | (ik == iq)


def sweep(tab_ref, i, step, carry):
    return several(tab_ref[0, i], tab_ref[1, i] + 1, step, carry)


def several(first, stop, step, carry, most=MOST):
    while most > 1:
        turns = (stop - first) // most

        def turn(n, carry, first=first, most=most):
            return step(most, first + most * n, carry)

        carry = lax.fori_loop(0, turns, turn, carry)
        first, most = first + most * turns, most // 2
    return lax.fori_loop(first, stop, functools.partial(step, 1), carry)


def each_block(tab_ref, parts, width, work):
    blocks = width // BQ
    count = blocks * parts
    for part in range(parts):

        def one(c, _, part=part):
            whole = lax.rem(tab_ref[2, 0] + part * blocks + c, count)
            work(
                part,
                pl.ds(pl.multiple_of(c * BQ, BQ), BQ),
                pl.ds(pl.multiple_of(whole * BQ, BQ), BQ),
            )
            return 0

        lax.fori_loop(0, blocks, one, 0)


def forward_kernel(parts, tab_ref, kseg_ref, qseg_ref, *refs):
    qkv_refs = refs[:parts]
    *o_refs, ot_ref, lse_ref, kx, vx, qx, scores = refs[-6 - parts :]
    tokens = qx.shape[1]
    width = tokens // parts
    lane = lax.broadcasted_iota(jnp.int32, (BK, 128), 1)
    zero = jnp.zeros((BK, 128), BF16)

    def prepare(part, here, there):
        k = qkv_refs[part][here, PAIR : 2 * PAIR]
        kx[0, there, :] = jnp.where(lane < HDIM, k, zero)
        kx[1, there, :] = jnp.where(lane < HDIM, zero, k)
        qx[:, there] = qkv_refs[part][here, :PAIR].astype(F32).T.astype(BF16)
        v = qkv_refs[part][here, 2 * PAIR :].astype(F32).T.astype(BF16)
        for h in range(2):
            vx[h, :HDIM, there] = v[h * HDIM : (h + 1) * HDIM]
            vx[h, HDIM:, there] = jnp.ones((16, BQ), BF16)

    each_block(tab_ref, parts, width, prepare)

    def block(i, _):
        cols = pl.ds(pl.multiple_of(i * BQ, BQ), BQ)
        qb = qx[:, cols]

        def score(blocks, j, tops):
            at = pl.ds(pl.multiple_of(j * BK, BK), blocks * BK)
            ok = allowed(kseg_ref, qseg_ref, i, j, blocks)
            out = []
            for h in range(2):
                s = matmul(kx[h, at, :], qb)
                s = jnp.where(ok, s, masked_score)
                scores[h, at, :] = s
                out.append(jnp.maximum(tops[h], jnp.max(s.reshape(blocks * BK // 8, 8, BQ), axis=0)))
            return tuple(out)

        tops = sweep(tab_ref, i, score, (jnp.full((8, BQ), masked_score, F32),) * 2)
        tops = [jnp.max(top, axis=0, keepdims=True) for top in tops]

        def weigh(blocks, j, accs):
            at = pl.ds(pl.multiple_of(j * BK, BK), blocks * BK)
            out = []
            for h in range(2):
                p = jnp.exp(scores[h, at, :] - tops[h]).astype(BF16)
                out.append(accs[h] + matmul(vx[h, :, at], p))
            return tuple(out)

        accs = sweep(tab_ref, i, weigh, (jnp.zeros((HDIM + 16, BQ), F32),) * 2)
        for h in range(2):
            total = accs[h][HDIM : HDIM + 1, :]
            ot_ref[h * HDIM : (h + 1) * HDIM, cols] = (accs[h][:HDIM, :] / total).astype(BF16)
            lse_ref[0, h : h + 1, cols] = tops[h] + jnp.log(total)
        return 0

    lax.fori_loop(0, tokens // BQ, block, 0)

    def finish(part, here, there):
        o_refs[part][here, :] = ot_ref[:, there].astype(F32).T.astype(BF16)

    each_block(tab_ref, parts, width, finish)


def three_parts(x):
    high = x.astype(BF16)
    rest = x - high.astype(F32)
    middle = rest.astype(BF16)
    return high, middle, (rest - middle.astype(F32)).astype(BF16)


def backward_kernel(parts, tab_ref, kseg_ref, qseg_ref, *refs):
    qkv_refs, do_refs = refs[:parts], refs[parts : 2 * parts]
    ot_ref, lse_ref = refs[2 * parts : 2 * parts + 2]
    *out_refs, kx, vx, kt, qx, dox, qt, dot, dq, dk, dv = refs[-10 - parts :]
    tokens = kt.shape[1]
    width = tokens // parts
    lane = lax.broadcasted_iota(jnp.int32, (BK, 128), 1)
    sub = lax.broadcasted_iota(jnp.int32, (HDIM, BK), 0)
    one0 = jnp.where((lane >= HDIM) & (lane < HDIM + 3), 1.0, 0.0).astype(BF16)
    one1 = jnp.where(lane < 3, 1.0, 0.0).astype(BF16)
    zero = jnp.zeros((BK, 128), BF16)

    def extra(x):
        high, middle, low = (e.astype(F32) for e in three_parts(x))
        rows = jnp.where(
            sub == 0, high, jnp.where(sub == 1, middle, jnp.where(sub == 2, low, 0.0))
        )
        return rows.astype(BF16)

    def prepare(part, here, there):
        k = qkv_refs[part][here, PAIR : 2 * PAIR]
        kt[:, there] = k.astype(F32).T.astype(BF16)
        kx[0, there, :] = jnp.where(lane < HDIM, k, one0)
        kx[1, there, :] = jnp.where(lane < HDIM, one1, k)
        v = qkv_refs[part][here, 2 * PAIR :]
        vx[0, there, :] = jnp.where(lane < HDIM, v, one0)
        vx[1, there, :] = jnp.where(lane < HDIM, one1, v)
        q = qkv_refs[part][here, :PAIR]
        qt[0, there, :] = jnp.where(lane < HDIM, q, zero)
        qt[1, there, :] = jnp.where(lane < HDIM, zero, q)
        do = do_refs[part][here, :]
        dot[0, there, :] = jnp.where(lane < HDIM, do, zero)
        dot[1, there, :] = jnp.where(lane < HDIM, zero, do)
        turned = do.astype(F32).T
        prod = turned * ot_ref[:, there].astype(F32)
        inner0 = jnp.sum(prod[:HDIM], axis=0, keepdims=True)
        inner1 = jnp.sum(prod[HDIM:], axis=0, keepdims=True)
        turned = turned.astype(BF16)
        dox[0, :HDIM, there] = turned[:HDIM]
        dox[0, HDIM:, there] = extra(-inner0)
        dox[1, HDIM:, there] = turned[HDIM:]
        dox[1, :HDIM, there] = extra(-inner1)
        turned = q.astype(F32).T.astype(BF16)
        qx[0, :HDIM, there] = turned[:HDIM]
        qx[0, HDIM:, there] = extra(-lse_ref[0, 0:1, there])
        qx[1, HDIM:, there] = turned[HDIM:]
        qx[1, :HDIM, there] = extra(-lse_ref[0, 1:2, there])
        dk[there, :] = jnp.zeros((BK, 128), F32)
        dv[there, :] = jnp.zeros((BK, 128), F32)

    each_block(tab_ref, parts, width, prepare)

    def block(i, _):
        cols = pl.ds(pl.multiple_of(i * BQ, BQ), BQ)

        def step(blocks, j, carry):
            at = pl.ds(pl.multiple_of(j * BK, BK), blocks * BK)
            ok = allowed(kseg_ref, qseg_ref, i, j, blocks)
            new = []
            dvs = dv[at, :]
            dks = dk[at, :]
            for h in range(2):
                s = matmul(kx[h, at, :], qx[h, :, cols])
                s = jnp.where(ok, s, masked_score)
                p = jnp.exp(s)
                dp = matmul(vx[h, at, :], dox[h, :, cols])
                ds = (p * dp).astype(BF16)
                dvs = dvs + matmul(p.astype(BF16), dot[h, cols, :])
                dks = dks + matmul(ds, qt[h, cols, :])
                new.append(carry[h] + matmul(kt[h * HDIM : (h + 1) * HDIM, at], ds))
            dv[at, :] = dvs
            dk[at, :] = dks
            return tuple(new)

        init = tuple(jnp.zeros((HDIM, BQ), F32) for _ in range(2))
        res = sweep(tab_ref, i, step, init)
        for h in range(2):
            dq[h * HDIM : (h + 1) * HDIM, cols] = res[h] * (HDIM**-0.5)
        return 0

    lax.fori_loop(0, tokens // BQ, block, 0)

    def finish(part, here, there):
        out_refs[part][here, :PAIR] = dq[:, there].T.astype(BF16)
        out_refs[part][here, PAIR : 2 * PAIR] = dk[there, :].astype(BF16)
        out_refs[part][here, 2 * PAIR :] = dv[there, :].astype(BF16)

    each_block(tab_ref, parts, width, finish)


def lanes_of(first, step):
    return lambda g, t: (0, first + step * g)


def attend_specs(qkv_parts, chunk):
    parts = len(qkv_parts)
    width = qkv_parts[0].shape[0]
    tokens = parts * width
    every = qkv_parts[0].shape[1] // (3 * PAIR)
    first, pairs = chunk
    seg_specs = [
        pl.BlockSpec((tokens, 1), lambda g, t: (0, 0)),
        pl.BlockSpec((1, tokens), lambda g, t: (0, 0)),
    ]
    qkv_specs = [pl.BlockSpec((width, 3 * PAIR), lanes_of(first, 1))] * parts
    o_specs = [pl.BlockSpec((width, PAIR), lanes_of(first, 1))] * parts
    ot_spec = pl.BlockSpec((PAIR, tokens), lambda g, t: (first + g, 0))
    lse_spec = pl.BlockSpec((1, 2, tokens), lambda g, t: (first + g, 0, 0))
    return parts, width, tokens, every, pairs, seg_specs, qkv_specs, o_specs, ot_spec, lse_spec


def attend_forward(qkv_parts, seg, keep, tables, chunk, begun=()):
    parts, width, tokens, every, pairs, seg_specs, qkv_specs, o_specs, ot_spec, lse_spec = (
        attend_specs(qkv_parts, chunk)
    )
    kseg = jnp.where(keep == 1, seg, -1)[:, None]
    return pl.pallas_call(
        functools.partial(forward_kernel, parts),
        grid_spec=pltpu.PrefetchScalarGridSpec(
            num_scalar_prefetch=1,
            grid=(pairs,),
            in_specs=seg_specs + qkv_specs + [pl.BlockSpec(memory_space=pl.ANY)] * len(begun),
            out_specs=o_specs + [ot_spec, lse_spec],
            scratch_shapes=[
                pltpu.VMEM((2, tokens, 128), BF16),
                pltpu.VMEM((2, HDIM + 16, tokens), BF16),
                pltpu.VMEM((PAIR, tokens), BF16),
                pltpu.VMEM((2, tokens, BQ), F32),
            ],
        ),
        out_shape=[jax.ShapeDtypeStruct((width, every * PAIR), BF16)] * parts
        + [
            jax.ShapeDtypeStruct((every * PAIR, tokens), BF16),
            jax.ShapeDtypeStruct((every, 2, tokens), F32),
        ],
        compiler_params=pltpu.CompilerParams(vmem_limit_bytes=40 * 2**20),
        cost_estimate=pl.CostEstimate(
            flops=2**10, bytes_accessed=2**10, transcendentals=0
        ),
        input_output_aliases={3 + parts + n: n for n in range(len(begun))},
        name="attend_forward",
    )(tables, kseg, seg[None, :], *qkv_parts, *begun)


def attend_backward(qkv_parts, turned, grad_ctx, lse, seg, keep, tables, chunk, begun=()):
    parts, width, tokens, every, pairs, seg_specs, qkv_specs, o_specs, ot_spec, lse_spec = (
        attend_specs(qkv_parts, chunk)
    )
    kseg = jnp.where(keep == 1, seg, -1)[:, None]
    result = pl.BlockSpec((width, 3 * PAIR), lanes_of(chunk[0], 1))
    return pl.pallas_call(
        functools.partial(backward_kernel, parts),
        grid_spec=pltpu.PrefetchScalarGridSpec(
            num_scalar_prefetch=1,
            grid=(pairs,),
            in_specs=seg_specs
            + qkv_specs
            + o_specs
            + [ot_spec, lse_spec]
            + [pl.BlockSpec(memory_space=pl.ANY)] * len(begun),
            out_specs=[result] * parts,
            scratch_shapes=[
                pltpu.VMEM((2, tokens, 128), BF16),
                pltpu.VMEM((2, tokens, 128), BF16),
                pltpu.VMEM((PAIR, tokens), BF16),
                pltpu.VMEM((2, 128, tokens), BF16),
                pltpu.VMEM((2, 128, tokens), BF16),
                pltpu.VMEM((2, tokens, 128), BF16),
                pltpu.VMEM((2, tokens, 128), BF16),
                pltpu.VMEM((PAIR, tokens), F32),
                pltpu.VMEM((tokens, 128), F32),
                pltpu.VMEM((tokens, 128), F32),
            ],
        ),
        out_shape=[jax.ShapeDtypeStruct((width, every * 3 * PAIR), BF16)] * parts,
        input_output_aliases={5 + 2 * parts + n: n for n in range(len(begun))},
        compiler_params=pltpu.CompilerParams(vmem_limit_bytes=48 * 2**20),
        cost_estimate=pl.CostEstimate(
            flops=2**10,
            bytes_accessed=2**10,
            transcendentals=0,
        ),
        name="attend_backward",
    )(tables, kseg, seg[None, :], *qkv_parts, *grad_ctx, turned, lse, *begun)


def row_block(width):
    return FEED_ROWS if width % FEED_ROWS == 0 else width


def gelu_and_slope(u):
    root = 0.7978845608028654
    square = u * u
    t = jnp.tanh(u * (root + (root * 0.044715) * square))
    half = 0.5 * t + 0.5
    slope = half + (0.5 * u) * (1.0 - t * t) * (root + (root * 0.134145) * square)
    return u * half, slope


def feed_kernel(step, x_ref, up_ref, bias_ref, down_ref, *refs):
    x_all, hidden_all, slope_all, out_ref = refs[-4:]
    x = x_ref[...]
    x_all[...] = x
    units = up_ref.shape[1]
    total = None
    for first in range(0, units, step):
        at = slice(first, first + step)
        act, slope = gelu_and_slope(matmul(x, up_ref[:, at]) + bias_ref[:, at])
        act = act.astype(BF16)
        hidden_all[:, at] = act
        slope_all[:, at] = slope.astype(BF16)
        term = matmul(act, down_ref[at, :])
        total = term if total is None else total + term
    out_ref[...] = total.astype(BF16)


def feed_forward(part, parts, x, up, bias, down, begun):
    width, model = x.shape
    units = up.shape[1]
    rows = row_block(width)
    steps = width // rows
    own = lambda k: (k, 0)
    whole = lambda k: (part * steps + k, 0)
    fixed = lambda k: (0, 0)
    once = pl.Buffered(1)
    every = parts * width
    return pl.pallas_call(
        functools.partial(feed_kernel, min(units, FEED)),
        grid=(steps,),
        in_specs=[
            pl.BlockSpec((rows, model), own),
            pl.BlockSpec((model, units), fixed, pipeline_mode=once),
            pl.BlockSpec((1, units), fixed, pipeline_mode=once),
            pl.BlockSpec((units, model), fixed, pipeline_mode=once),
        ]
        + [pl.BlockSpec(memory_space=pl.ANY)] * len(begun),
        out_specs=[
            pl.BlockSpec((rows, model), whole),
            pl.BlockSpec((rows, units), whole),
            pl.BlockSpec((rows, units), whole),
            pl.BlockSpec((rows, model), own),
        ],
        out_shape=[
            jax.ShapeDtypeStruct((every, model), BF16),
            jax.ShapeDtypeStruct((every, units), BF16),
            jax.ShapeDtypeStruct((every, units), BF16),
            jax.ShapeDtypeStruct((width, model), BF16),
        ],
        input_output_aliases={4 + n: n for n in range(len(begun))},
        compiler_params=pltpu.CompilerParams(vmem_limit_bytes=48 * 2**20),
        cost_estimate=pl.CostEstimate(
            flops=6 * width * model * units, bytes_accessed=2**24, transcendentals=0
        ),
        name="feed_forward",
    )(x, up, bias[None, :], down, *begun)


def feed_back_kernel(step, g_ref, slope_ref, down_ref, up_ref, *refs):
    pre_all, sums_ref, out_ref = refs[-3:]
    g = g_ref[...]
    units = up_ref.shape[1]

    @pl.when(pl.program_id(0) == 0)
    def _():
        sums_ref[...] = jnp.zeros_like(sums_ref)

    total = None
    for first in range(0, units, step):
        at = slice(first, first + step)
        pre = contract_cols(g, down_ref[at, :]) * slope_ref[:, at].astype(F32)
        pre = pre.astype(BF16)
        pre_all[:, at] = pre
        sums_ref[:, at] += jnp.sum(pre.astype(F32), axis=0, keepdims=True)
        term = contract_cols(pre, up_ref[:, at])
        total = term if total is None else total + term
    out_ref[...] = total.astype(BF16)


def feed_back(part, parts, g, slope_all, up, down, begun):
    width, model = g.shape
    units = up.shape[1]
    rows = row_block(width)
    steps = width // rows
    own = lambda k: (k, 0)
    whole = lambda k: (part * steps + k, 0)
    fixed = lambda k: (0, 0)
    once = pl.Buffered(1)
    every = parts * width
    return pl.pallas_call(
        functools.partial(feed_back_kernel, min(units, FEED)),
        grid=(steps,),
        in_specs=[
            pl.BlockSpec((rows, model), own),
            pl.BlockSpec((rows, units), whole),
            pl.BlockSpec((units, model), fixed, pipeline_mode=once),
            pl.BlockSpec((model, units), fixed, pipeline_mode=once),
        ]
        + [pl.BlockSpec(memory_space=pl.ANY)] * len(begun),
        out_specs=[
            pl.BlockSpec((rows, units), whole),
            pl.BlockSpec((1, units), fixed),
            pl.BlockSpec((rows, model), own),
        ],
        out_shape=[
            jax.ShapeDtypeStruct((every, units), BF16),
            jax.ShapeDtypeStruct((1, units), F32),
            jax.ShapeDtypeStruct((width, model), BF16),
        ],
        input_output_aliases={4 + n: n for n in range(len(begun))},
        compiler_params=pltpu.CompilerParams(vmem_limit_bytes=48 * 2**20),
        cost_estimate=pl.CostEstimate(
            flops=2**10, bytes_accessed=2**10, transcendentals=0
        ),
        name="feed_back",
    )(g, slope_all, down, up, *begun)


def weight_grad_kernel(parts, *refs):
    a_refs, d_refs = refs[:parts], refs[parts : 2 * parts]
    out_ref, sums_ref = refs[2 * parts :]
    out_ref[...] = total([contract_rows(a[...], d[...]) for a, d in zip(a_refs, d_refs)]).astype(BF16)
    sums_ref[...] = total([jnp.sum(d[...].astype(F32), axis=0, keepdims=True) for d in d_refs])


def weight_grad(a_parts, d_parts, first, count):
    parts = len(a_parts)
    width, model = a_parts[0].shape
    columns = 3 * PAIR
    return pl.pallas_call(
        functools.partial(weight_grad_kernel, parts),
        grid=(count,),
        in_specs=[pl.BlockSpec((width, model), lambda k: (0, 0), pipeline_mode=pl.Buffered(1))] * parts
        + [pl.BlockSpec((width, columns), lambda k: (0, first + k))] * parts,
        out_specs=[
            pl.BlockSpec((model, columns), lambda k: (0, k)),
            pl.BlockSpec((1, columns), lambda k: (0, k)),
        ],
        out_shape=[
            jax.ShapeDtypeStruct((model, count * columns), BF16),
            jax.ShapeDtypeStruct((1, count * columns), F32),
        ],
        compiler_params=pltpu.CompilerParams(vmem_limit_bytes=40 * 2**20),
        cost_estimate=pl.CostEstimate(flops=2**10, bytes_accessed=2**10, transcendentals=0),
        name="weight_grad",
    )(*a_parts, *d_parts)


def input_grad_kernel(d_ref, w_ref, out_ref):
    out_ref[...] = contract_cols(d_ref[...], w_ref[...]).astype(BF16)


def input_grad(d, weight):
    width, columns = d.shape
    model = weight.shape[0]
    rows = row_block(width)
    return pl.pallas_call(
        input_grad_kernel,
        grid=(width // rows,),
        in_specs=[
            pl.BlockSpec((rows, columns), lambda k: (k, 0)),
            pl.BlockSpec((model, columns), lambda k: (0, 0), pipeline_mode=pl.Buffered(1)),
        ],
        out_specs=pl.BlockSpec((rows, model), lambda k: (k, 0)),
        out_shape=jax.ShapeDtypeStruct((width, model), BF16),
        compiler_params=pltpu.CompilerParams(vmem_limit_bytes=40 * 2**20),
        cost_estimate=pl.CostEstimate(flops=2**10, bytes_accessed=2**10, transcendentals=0),
        name="input_grad",
    )(d, weight)


def spread_kernel(tab_ref, mine_ref, theirs_ref, out_ref):
    mine = pl.program_id(1) == tab_ref[0]

    def put(ref):
        for c in range(3):
            out_ref[c] = ref[:, c * PAIR : (c + 1) * PAIR].astype(F32)

    @pl.when(mine)
    def _():
        put(mine_ref)

    @pl.when(jnp.logical_not(mine))
    def _():
        put(theirs_ref)


def spread(mine, theirs, side, half, out_pairs, first, begun):
    columns = mine.shape[1]
    low = mine.shape[0] // half - 1
    count = columns // (3 * PAIR)
    upper = pl.BlockSpec((half, 3 * PAIR), lambda k, s, t: (0, k))
    lower = pl.BlockSpec((half, 3 * PAIR), lambda k, s, t: (low, k))
    return pl.pallas_call(
        lambda tab, a, b, *refs: spread_kernel(tab, a, b, refs[-1]),
        grid_spec=pltpu.PrefetchScalarGridSpec(
            num_scalar_prefetch=1,
            grid=(count, 2),
            in_specs=[upper, lower] + [pl.BlockSpec(memory_space=pl.ANY)] * len(begun),
            out_specs=pl.BlockSpec((3, half, PAIR), lambda k, s, t: (0, s, first + k)),
        ),
        out_shape=jax.ShapeDtypeStruct((3, 2 * half, out_pairs * PAIR), F32),
        input_output_aliases={3 + n: n for n in range(len(begun))},
        compiler_params=pltpu.CompilerParams(vmem_limit_bytes=32 * 2**20),
        cost_estimate=pl.CostEstimate(flops=2**10, bytes_accessed=2**10, transcendentals=0),
        name="spread",
    )(jnp.reshape(side, (1,)).astype(jnp.int32), mine, theirs, *begun)


def after(value, *others):
    return lax.optimization_barrier((value, *others))[0]


class Layout:
    def __init__(self, mesh):
        self.dp, self.n = mesh.shape["dp"], mesh.shape["mp"]
        self.pairs = self.dp // 2
        self.axes = ("dp", "mp")

    def device(self, pair, core, m):
        return (2 * pair + core) * self.n + m

    def at_rank(self, pair, group, rank):
        return self.device(pair, rank % 2, group * (self.n // 2) + rank // 2)

    def each(self):
        for pair in range(self.pairs):
            for group in range(2):
                for rank in range(self.n):
                    yield pair, group, rank

    def stays(self):
        core, m = lax.axis_index("dp") % 2, lax.axis_index("mp")
        return (m // (self.n // 2) == core) & (self.rank() == m)

    def send(self, value, back=False):
        moves = [(self.device(p, g, r), self.at_rank(p, g, r)) for p, g, r in self.each()]
        return lax.ppermute(
            value, self.axes, [(b, a) if back else (a, b) for a, b in moves if a != b]
        )

    def regroup(self, value):
        return jnp.where(self.stays(), value, self.send(value))

    def give_back(self, value):
        return jnp.where(self.stays(), value, self.send(value, True))

    def partner(self, value, bit, only=lambda p, g, r: True):
        def other(p, c):
            return (p, 1 - c) if bit < 0 else (p ^ (1 << bit), c)

        moves = [
            (self.device(*other(p, c), m), self.device(p, c, m))
            for p, c, m in self.each()
            if only(p, c, m)
        ]
        return lax.ppermute(value, self.axes, moves)

    def side(self, bit):
        dp = lax.axis_index("dp")
        return dp % 2 if bit < 0 else (dp // 2 >> bit) % 2

    def joined(self, mine, theirs, bit):
        high = self.side(bit) == 1
        return jnp.concatenate(
            [jnp.where(high, theirs, mine), jnp.where(high, mine, theirs)], 0
        )

    def regroup_first(self, weight, small, tokens):
        rows = weight.shape[0] // 4
        part = 2 * self.side(0) + self.side(1)
        quarter = lax.dynamic_slice_in_dim(weight, part * rows, rows, 0)
        got = self.send(quarter)
        small = self.regroup(after(small, got))
        tokens = self.regroup(after(tokens, got, small))
        for bit in (1, 0):
            got = self.joined(got, self.partner(got, bit, self.moving), bit)
        return jnp.where(self.stays(), weight, got), small, tokens

    def moving(self, pair, core, m):
        return self.at_rank(pair, core, m) != self.device(pair, core, m)

    def to_rank(self, value, ahead):
        moves = [
            (self.at_rank(p, g, r), self.at_rank(p, g, (r + ahead) % self.n))
            for p, g, r in self.each()
        ]
        return lax.ppermute(value, self.axes, moves)

    def rank(self):
        core = lax.axis_index("dp") % 2
        return (lax.axis_index("mp") % (self.n // 2)) * 2 + core

    def gather(self, mine):
        return [mine] + [self.to_rank(mine, self.n - k) for k in range(1, self.n)]

    def scatter_sum(self, shares):
        total = shares[0].astype(jnp.float32)
        for k in range(1, self.n):
            total = total + self.to_rank(shares[k].astype(jnp.bfloat16), k).astype(jnp.float32)
        return total

    def sum_all(self, value):
        devices = self.dp * self.n
        steps = [1 << k for k in range(devices.bit_length() - 1)]
        for step in steps:
            value = value + lax.ppermute(value, self.axes, [(i, i ^ step) for i in range(devices)])
        return value

    def sum_dp(self, value, turn):
        order = [(i + turn) % self.dp for i in range(self.dp)]
        return lax.psum(value, "dp", axis_index_groups=[order])

    def halved(self, value, bit):
        half, high = value.shape[0] // 2, self.side(bit)
        sent = lax.dynamic_slice_in_dim(value, (1 - high) * half, half, 0)
        kept = lax.dynamic_slice_in_dim(value, high * half, half, 0)
        got = self.partner(sent, bit)
        return (kept.astype(jnp.float32) + got.astype(jnp.float32)).astype(jnp.bfloat16)

    def order(self, first):
        bits = list(range(self.pairs.bit_length() - 1))
        return bits[first:] + bits[:first]

    def halved_by(self, value, bits):
        for bit in bits:
            value = self.halved(value, bit)
        return value

    def joined_by(self, value, bits):
        for bit in bits[::-1]:
            value = self.joined(value, self.partner(value, bit), bit)
        return value


def for_kernel(shares, rank):
    width = shares[0].shape[0]
    if width % BQ == 0:
        return shares, rank * (width // BQ)
    return [jnp.roll(jnp.concatenate(shares, 0), rank * width, 0)], 0


def from_kernel(arrays, rank, shares):
    if len(arrays) == shares:
        return arrays
    width = arrays[0].shape[0] // shares
    return jnp.split(jnp.roll(arrays[0], -rank * width, 0), shares, 0)


def by_pairs(weight, pairs):
    return (
        weight.reshape(-1, 3, pairs, PAIR).transpose(0, 2, 1, 3).reshape(-1, 3 * pairs * PAIR)
    )


def total(terms):
    return functools.reduce(jnp.add, terms)


def body(
    layout,
    tokens,
    ln1_gain,
    ln1_bias,
    w_qkv,
    qv_bias,
    w_out,
    out_bias,
    ln2_gain,
    ln2_bias,
    ln3_gain,
    ln3_bias,
    w_up,
    up_bias,
    w_down,
    down_bias,
    ln4_gain,
    ln4_bias,
    row_grid,
    pad_mask,
    cotangent,
):
    f32, bf16 = jnp.float32, jnp.bfloat16
    model_dim = tokens.shape[1]
    group_rows = pad_mask.shape[0]
    width = w_qkv.shape[2]
    units = w_up.shape[1]
    shares = layout.n
    rank = layout.rank()

    small = jnp.concatenate(
        [
            qv_bias.reshape(-1),
            up_bias,
            pad_mask.astype(f32),
            row_grid[0].astype(f32),
        ]
    )
    pairs = width // PAIR
    chunks = 2 if pairs % 2 == 0 else 1
    w_qkv, small, tokens = layout.regroup_first(w_qkv, small, tokens)
    qv_bias = small[: 2 * width].reshape(2, width)
    up_bias = small[2 * width : 2 * width + units]
    keep = small[2 * width + units : 2 * width + units + group_rows].astype(jnp.int32)
    grid_row = small[2 * width + units + group_rows :].astype(jnp.int32)
    w_qkv = by_pairs(w_qkv, pairs)
    half = units // 2
    w_out_far = layout.send(after(w_out, tokens))
    w_up_far = layout.send(after(w_up, tokens))
    w_top_far = layout.send(after(w_down[:half], tokens))
    w_low_far = layout.send(after(w_down[half:], tokens))
    cotangent = layout.regroup(after(cotangent, w_low_far))

    resid_in = tokens.astype(f32)
    norm1_out, normed1, inv1 = norm_parts(resid_in, ln1_gain, ln1_bias)
    a1 = layout.gather(norm1_out.astype(bf16))
    zeros = jnp.zeros((width,), f32)
    qkv_bias = by_pairs(jnp.concatenate([qv_bias[0], zeros, qv_bias[1]]), pairs)
    qkv_scale = by_pairs(
        jnp.concatenate([zeros + HDIM ** (-0.5), zeros + 1.0, zeros + 1.0]), pairs
    )
    qkv = [((matmul(x, w_qkv) + qkv_bias) * qkv_scale).astype(bf16) for x in a1]
    qkv, turn = for_kernel(qkv, rank)
    seg, tables = row_tables(grid_row, group_rows, turn)
    begun = ()
    for pair in range(pairs):
        if pair and pair == pairs // 2:
            tables, w_up_far = lax.optimization_barrier((tables, w_up_far))
        begun = attend_forward(qkv, seg, keep, tables, (pair, 1), begun)
    *context, context_turned, log_total = begun
    *context, w_out_far, w_top_far, w_low_far = lax.optimization_barrier(
        (*context, w_out_far, w_top_far, w_low_far)
    )
    context = from_kernel(context, rank, shares)
    stays = layout.stays()
    w_out = jnp.where(stays, w_out, w_out_far)
    w_up = jnp.where(stays, w_up, w_up_far)
    w_down = jnp.where(stays, w_down, jnp.concatenate([w_top_far, w_low_far], 0))
    branch_z = layout.scatter_sum([matmul(x, w_out) for x in context]) + out_bias
    norm2_out, normed2, inv2 = norm_parts(branch_z, ln2_gain, ln2_bias)
    resid_mid = resid_in + norm2_out
    norm3_out, normed3, inv3 = norm_parts(resid_mid, ln3_gain, ln3_bias)
    a3 = layout.gather(norm3_out.astype(bf16))
    begun, shares_f = (), []
    for part, x in enumerate(a3):
        if part == shares - 1:
            x, cotangent = lax.optimization_barrier((x, cotangent))
        *begun, share = feed_forward(part, shares, x, w_up, up_bias, w_down, begun)
        shares_f.append(share)
    a3_all, hidden, slope = begun
    branch_f = layout.scatter_sum(shares_f) + down_bias
    norm4_out, normed4, inv4 = norm_parts(branch_f, ln4_gain, ln4_bias)
    layer_out = (resid_mid + norm4_out).astype(bf16)

    upstream = cotangent.astype(f32)
    grad_f = norm_back(upstream, normed4, inv4, ln4_gain).astype(bf16)
    grad_f_all = layout.gather(grad_f)
    g_w_down = contract_rows(hidden, jnp.concatenate(grad_f_all, 0)).astype(bf16)
    begun, shares_a3, g_up_bias = (), [], []
    for part, g in enumerate(grad_f_all):
        if part:
            g, g_w_down = lax.optimization_barrier((g, g_w_down))
        *begun, unit_sums, share = feed_back(part, shares, g, slope, w_up, w_down, begun)
        shares_a3.append(share)
        g_up_bias.append(unit_sums[0])
    [grad_pre] = begun
    g_w_down_far = layout.send(g_w_down, True)
    grad_a3 = layout.scatter_sum(shares_a3)
    g_up_bias = total(g_up_bias)
    grad_mid = upstream + norm_back(grad_a3, normed3, inv3, ln3_gain)
    grad_z = norm_back(grad_mid, normed2, inv2, ln2_gain).astype(bf16)
    grad_z_all = layout.gather(grad_z)
    grad_ctx = [contract_cols(g, w_out).astype(bf16) for g in grad_z_all]
    g_w_out = total([contract_rows(x, g) for x, g in zip(context, grad_z_all)]).astype(bf16)
    g_w_out_far = layout.send(g_w_out, True)
    g_w_down_far, *grad_ctx = lax.optimization_barrier((g_w_down_far, *grad_ctx))
    grad_ctx, _ = for_kernel(grad_ctx, rank)
    g_w_down = jnp.where(stays, g_w_down, g_w_down_far)
    grad_pre, g_w_down = lax.optimization_barrier((grad_pre, g_w_down))
    g_w_down = layout.sum_dp(g_w_down, 1)
    g_w_up = contract_rows(a3_all, grad_pre).astype(bf16)
    g_w_up_far = layout.send(g_w_up, True)
    tables, g_w_up = lax.optimization_barrier((tables, g_w_up))
    calls = [(0, pairs // 2)] if pairs > 1 else []
    calls += [(k, 1) for k in range(pairs // 2, pairs)]
    grad_qkv = ()
    for call in calls:
        if call == calls[-1]:
            tables, g_w_down = lax.optimization_barrier((tables, g_w_down))
        grad_qkv = attend_backward(
            qkv, context_turned, grad_ctx, log_total, seg, keep, tables, call, grad_qkv
        )
    layer_out = layout.give_back(after(layer_out, g_w_out_far))
    grad_qkv = from_kernel(grad_qkv, rank, shares)
    grad_a1 = [input_grad(g, w_qkv) for g in grad_qkv]
    grad_a1 = layout.scatter_sum(grad_a1)
    grad_input = grad_mid + norm_back(grad_a1, normed1, inv1, ln1_gain)
    grad_input = grad_input.astype(bf16)
    g_w_qkv, sums = [], []
    each = pairs // chunks
    for chunk in range(chunks):
        g_part, part_sums = weight_grad(a1, grad_qkv, chunk * each, each)
        g_w_qkv.append(layout.give_back(g_part))
        sums.append(part_sums)
    sums = jnp.concatenate(sums, 1)
    g_w_up = layout.sum_dp(jnp.where(stays, g_w_up, g_w_up_far), 0)
    g_w_out = layout.sum_dp(jnp.where(stays, g_w_out, g_w_out_far), 0)
    begun = ()
    for chunk, part in enumerate(g_w_qkv):
        if chunk == 0:
            mine = theirs = layout.sum_dp(part, 0)
            side = jnp.zeros((), jnp.int32)
        else:
            part = layout.halved_by(part, [-1, *layout.order(0)])
            mine, side = layout.joined_by(part, layout.order(0)), layout.side(-1)
            theirs = layout.partner(mine, -1)
        begun = (spread(mine, theirs, side, model_dim // 2, pairs, chunk * each, begun),)
    g_w_qkv = begun[0].transpose(1, 0, 2)
    sums = sums.reshape(pairs, 3, PAIR).transpose(1, 0, 2).reshape(3, width)
    grad_input = layout.give_back(grad_input).astype(f32)

    norm_terms = jnp.stack(
        [
            jnp.sum(grad_a1 * normed1, 0),
            jnp.sum(grad_a1, 0),
            jnp.sum(grad_z.astype(f32), 0),
            jnp.sum(grad_mid * normed2, 0),
            jnp.sum(grad_mid, 0),
            jnp.sum(grad_a3 * normed3, 0),
            jnp.sum(grad_a3, 0),
            jnp.sum(grad_f.astype(f32), 0),
            jnp.sum(upstream * normed4, 0),
            jnp.sum(upstream, 0),
        ],
        0,
    )
    all_units = lax.dynamic_update_slice(jnp.zeros((units * shares,), f32), g_up_bias, (rank * units,))
    all_width = lax.dynamic_update_slice(
        jnp.zeros((2, width * shares), f32), jnp.stack([sums[0], sums[2]], 0), (0, rank * width)
    )
    small = layout.sum_all(
        jnp.concatenate([norm_terms.reshape(-1), all_width.reshape(-1), all_units])
    )
    norm_terms = small[: 10 * model_dim].reshape(10, model_dim)
    all_width = small[10 * model_dim : 12 * model_dim].reshape(2, width * shares)
    all_units = small[12 * model_dim :]
    m = lax.axis_index("mp")
    g_qv_bias = lax.dynamic_slice(all_width, (0, m * width), (2, width))
    g_up_bias = lax.dynamic_slice(all_units, (m * units,), (units,))
    return (
        layer_out,
        grad_input,
        norm_terms[0],
        norm_terms[1],
        g_w_qkv,
        g_qv_bias,
        g_w_out.astype(f32),
        norm_terms[2],
        norm_terms[3],
        norm_terms[4],
        norm_terms[5],
        norm_terms[6],
        g_w_up.astype(f32),
        g_up_bias,
        g_w_down.astype(f32),
        norm_terms[7],
        norm_terms[8],
        norm_terms[9],
    )


def solution(mesh):
    in_specs = (
        P(("dp", "mp"), None),
        P(),
        P(),
        P(None, None, "mp"),
        P(None, "mp"),
        P("mp", None),
        P(),
        P(),
        P(),
        P(),
        P(),
        P(None, "mp"),
        P("mp"),
        P("mp", None),
        P(),
        P(),
        P(),
        P("dp", None),
        P("dp"),
        P(("dp", "mp"), None),
    )
    out_specs = (
        P(("dp", "mp"), None),
        P(("dp", "mp"), None),
        P(),
        P(),
        P(None, None, "mp"),
        P(None, "mp"),
        P("mp", None),
        P(),
        P(),
        P(),
        P(),
        P(),
        P(None, "mp"),
        P("mp"),
        P("mp", None),
        P(),
        P(),
        P(),
    )
    return jax.shard_map(functools.partial(body, Layout(mesh)), mesh=mesh, in_specs=in_specs, out_specs=out_specs, check_vma=False)
```

```python
import functools

import jax
import jax.numpy as jnp
from jax import lax
from jax.experimental import pallas as pl
from jax.experimental.pallas import tpu as pltpu
from jax.sharding import PartitionSpec as P

HDIM = 64
TEXT = 64


epsilon = 1e-05
masked_score = -1e30


def norm_parts(values, ln_gain, ln_bias):
    centred = values - jnp.mean(values, -1, keepdims=True)
    inv_std = lax.rsqrt(jnp.mean(centred * centred, -1, keepdims=True) + epsilon)
    normed = centred * inv_std
    return (normed * ln_gain + ln_bias, normed, inv_std)


def norm_back(upstream, normed, inv_std, ln_gain):
    scaled = upstream * ln_gain
    return inv_std * (
        scaled
        - jnp.mean(scaled, -1, keepdims=True)
        - normed * jnp.mean(scaled * normed, -1, keepdims=True)
    )


def contract_rows(left, right):
    return lax.dot_general(
        left, right, (((0,), (0,)), ((), ())), preferred_element_type=jnp.float32
    )


def contract_cols(left, right):
    return lax.dot_general(
        left, right, (((1,), (1,)), ((), ())), preferred_element_type=jnp.float32
    )


BQ = 256
BK = 256
MOST = 4
FEED = 1024
FEED_ROWS = 640
PAIR = 2 * HDIM
F32 = jnp.float32
BF16 = jnp.bfloat16


def matmul(left, right):
    return jnp.dot(left, right, preferred_element_type=F32)


def row_tables(grid_row, tokens, turn):
    side = jnp.max(grid_row)
    length = TEXT + side * side
    rows = tokens // length
    used = rows * length
    position = jnp.arange(tokens, dtype=jnp.int32)
    seg = jnp.minimum(position // length, rows)
    blocks = tokens // BQ
    first = jnp.arange(blocks, dtype=jnp.int32) * BQ
    start = jnp.where(first < used, (first // length) * length, first)
    low = start // BK
    diag = first // BK
    turns = jnp.full((blocks,), turn, jnp.int32)
    return seg, jnp.stack([low, diag, turns]).astype(jnp.int32)


def allowed(kseg_ref, qseg_ref, i, j, blocks):
    qs = qseg_ref[:, pl.ds(pl.multiple_of(i * BQ, BQ), BQ)]
    ks = kseg_ref[pl.ds(pl.multiple_of(j * BK, BK), blocks * BK), :]
    ik = j * BK + lax.broadcasted_iota(jnp.int32, (blocks * BK, BQ), 0)
    iq = i * BQ + lax.broadcasted_iota(jnp.int32, (blocks * BK, BQ), 1)
    return ((ks == qs) & (ik <= iq)) | (ik == iq)


def sweep(tab_ref, i, step, carry):
    return several(tab_ref[0, i], tab_ref[1, i] + 1, step, carry)


def several(first, stop, step, carry, most=MOST):
    while most > 1:
        turns = (stop - first) // most

        def turn(n, carry, first=first, most=most):
            return step(most, first + most * n, carry)

        carry = lax.fori_loop(0, turns, turn, carry)
        first, most = first + most * turns, most // 2
    return lax.fori_loop(first, stop, functools.partial(step, 1), carry)


def each_block(tab_ref, parts, width, work):
    blocks = width // BQ
    count = blocks * parts
    for part in range(parts):

        def one(c, _, part=part):
            whole = lax.rem(tab_ref[2, 0] + part * blocks + c, count)
            work(
                part,
                pl.ds(pl.multiple_of(c * BQ, BQ), BQ),
                pl.ds(pl.multiple_of(whole * BQ, BQ), BQ),
            )
            return 0

        lax.fori_loop(0, blocks, one, 0)


def forward_kernel(parts, tab_ref, kseg_ref, qseg_ref, *refs):
    qkv_refs = refs[:parts]
    *o_refs, ot_ref, lse_ref, kx, vx, qx, scores = refs[-6 - parts :]
    tokens = qx.shape[1]
    width = tokens // parts
    lane = lax.broadcasted_iota(jnp.int32, (BK, 128), 1)
    zero = jnp.zeros((BK, 128), BF16)

    def prepare(part, here, there):
        k = qkv_refs[part][here, PAIR : 2 * PAIR]
        kx[0, there, :] = jnp.where(lane < HDIM, k, zero)
        kx[1, there, :] = jnp.where(lane < HDIM, zero, k)
        qx[:, there] = qkv_refs[part][here, :PAIR].astype(F32).T.astype(BF16)
        v = qkv_refs[part][here, 2 * PAIR :].astype(F32).T.astype(BF16)
        for h in range(2):
            vx[h, :HDIM, there] = v[h * HDIM : (h + 1) * HDIM]
            vx[h, HDIM:, there] = jnp.ones((16, BQ), BF16)

    each_block(tab_ref, parts, width, prepare)

    def block(i, _):
        cols = pl.ds(pl.multiple_of(i * BQ, BQ), BQ)
        qb = qx[:, cols]

        def score(blocks, j, tops):
            at = pl.ds(pl.multiple_of(j * BK, BK), blocks * BK)
            ok = allowed(kseg_ref, qseg_ref, i, j, blocks)
            out = []
            for h in range(2):
                s = matmul(kx[h, at, :], qb)
                s = jnp.where(ok, s, masked_score)
                scores[h, at, :] = s
                out.append(jnp.maximum(tops[h], jnp.max(s.reshape(blocks * BK // 8, 8, BQ), axis=0)))
            return tuple(out)

        tops = sweep(tab_ref, i, score, (jnp.full((8, BQ), masked_score, F32),) * 2)
        tops = [jnp.max(top, axis=0, keepdims=True) for top in tops]

        def weigh(blocks, j, accs):
            at = pl.ds(pl.multiple_of(j * BK, BK), blocks * BK)
            out = []
            for h in range(2):
                p = jnp.exp(scores[h, at, :] - tops[h]).astype(BF16)
                out.append(accs[h] + matmul(vx[h, :, at], p))
            return tuple(out)

        accs = sweep(tab_ref, i, weigh, (jnp.zeros((HDIM + 16, BQ), F32),) * 2)
        for h in range(2):
            total = accs[h][HDIM : HDIM + 1, :]
            ot_ref[h * HDIM : (h + 1) * HDIM, cols] = (accs[h][:HDIM, :] / total).astype(BF16)
            lse_ref[0, h : h + 1, cols] = tops[h] + jnp.log(total)
        return 0

    lax.fori_loop(0, tokens // BQ, block, 0)

    def finish(part, here, there):
        o_refs[part][here, :] = ot_ref[:, there].astype(F32).T.astype(BF16)

    each_block(tab_ref, parts, width, finish)


def three_parts(x):
    high = x.astype(BF16)
    rest = x - high.astype(F32)
    middle = rest.astype(BF16)
    return high, middle, (rest - middle.astype(F32)).astype(BF16)


def backward_kernel(parts, tab_ref, kseg_ref, qseg_ref, *refs):
    qkv_refs, do_refs = refs[:parts], refs[parts : 2 * parts]
    ot_ref, lse_ref = refs[2 * parts : 2 * parts + 2]
    *out_refs, kx, vx, kt, qx, dox, qt, dot, dq, dk, dv = refs[-10 - parts :]
    tokens = kt.shape[1]
    width = tokens // parts
    lane = lax.broadcasted_iota(jnp.int32, (BK, 128), 1)
    sub = lax.broadcasted_iota(jnp.int32, (HDIM, BK), 0)
    one0 = jnp.where((lane >= HDIM) & (lane < HDIM + 3), 1.0, 0.0).astype(BF16)
    one1 = jnp.where(lane < 3, 1.0, 0.0).astype(BF16)
    zero = jnp.zeros((BK, 128), BF16)

    def extra(x):
        high, middle, low = (e.astype(F32) for e in three_parts(x))
        rows = jnp.where(
            sub == 0, high, jnp.where(sub == 1, middle, jnp.where(sub == 2, low, 0.0))
        )
        return rows.astype(BF16)

    def prepare(part, here, there):
        k = qkv_refs[part][here, PAIR : 2 * PAIR]
        kt[:, there] = k.astype(F32).T.astype(BF16)
        kx[0, there, :] = jnp.where(lane < HDIM, k, one0)
        kx[1, there, :] = jnp.where(lane < HDIM, one1, k)
        v = qkv_refs[part][here, 2 * PAIR :]
        vx[0, there, :] = jnp.where(lane < HDIM, v, one0)
        vx[1, there, :] = jnp.where(lane < HDIM, one1, v)
        q = qkv_refs[part][here, :PAIR]
        qt[0, there, :] = jnp.where(lane < HDIM, q, zero)
        qt[1, there, :] = jnp.where(lane < HDIM, zero, q)
        do = do_refs[part][here, :]
        dot[0, there, :] = jnp.where(lane < HDIM, do, zero)
        dot[1, there, :] = jnp.where(lane < HDIM, zero, do)
        turned = do.astype(F32).T
        prod = turned * ot_ref[:, there].astype(F32)
        inner0 = jnp.sum(prod[:HDIM], axis=0, keepdims=True)
        inner1 = jnp.sum(prod[HDIM:], axis=0, keepdims=True)
        turned = turned.astype(BF16)
        dox[0, :HDIM, there] = turned[:HDIM]
        dox[0, HDIM:, there] = extra(-inner0)
        dox[1, HDIM:, there] = turned[HDIM:]
        dox[1, :HDIM, there] = extra(-inner1)
        turned = q.astype(F32).T.astype(BF16)
        qx[0, :HDIM, there] = turned[:HDIM]
        qx[0, HDIM:, there] = extra(-lse_ref[0, 0:1, there])
        qx[1, HDIM:, there] = turned[HDIM:]
        qx[1, :HDIM, there] = extra(-lse_ref[0, 1:2, there])
        dk[there, :] = jnp.zeros((BK, 128), F32)
        dv[there, :] = jnp.zeros((BK, 128), F32)

    each_block(tab_ref, parts, width, prepare)

    def block(i, _):
        cols = pl.ds(pl.multiple_of(i * BQ, BQ), BQ)

        def step(blocks, j, carry):
            at = pl.ds(pl.multiple_of(j * BK, BK), blocks * BK)
            ok = allowed(kseg_ref, qseg_ref, i, j, blocks)
            new = []
            dvs = dv[at, :]
            dks = dk[at, :]
            for h in range(2):
                s = matmul(kx[h, at, :], qx[h, :, cols])
                s = jnp.where(ok, s, masked_score)
                p = jnp.exp(s)
                dp = matmul(vx[h, at, :], dox[h, :, cols])
                ds = (p * dp).astype(BF16)
                dvs = dvs + matmul(p.astype(BF16), dot[h, cols, :])
                dks = dks + matmul(ds, qt[h, cols, :])
                new.append(carry[h] + matmul(kt[h * HDIM : (h + 1) * HDIM, at], ds))
            dv[at, :] = dvs
            dk[at, :] = dks
            return tuple(new)

        init = tuple(jnp.zeros((HDIM, BQ), F32) for _ in range(2))
        res = sweep(tab_ref, i, step, init)
        for h in range(2):
            dq[h * HDIM : (h + 1) * HDIM, cols] = res[h] * (HDIM**-0.5)
        return 0

    lax.fori_loop(0, tokens // BQ, block, 0)

    def finish(part, here, there):
        out_refs[part][here, :PAIR] = dq[:, there].T.astype(BF16)
        out_refs[part][here, PAIR : 2 * PAIR] = dk[there, :].astype(BF16)
        out_refs[part][here, 2 * PAIR :] = dv[there, :].astype(BF16)

    each_block(tab_ref, parts, width, finish)


def lanes_of(first, step):
    return lambda g, t: (0, first + step * g)


def attend_specs(qkv_parts, chunk):
    parts = len(qkv_parts)
    width = qkv_parts[0].shape[0]
    tokens = parts * width
    every = qkv_parts[0].shape[1] // (3 * PAIR)
    first, pairs = chunk
    seg_specs = [
        pl.BlockSpec((tokens, 1), lambda g, t: (0, 0)),
        pl.BlockSpec((1, tokens), lambda g, t: (0, 0)),
    ]
    qkv_specs = [pl.BlockSpec((width, 3 * PAIR), lanes_of(first, 1))] * parts
    o_specs = [pl.BlockSpec((width, PAIR), lanes_of(first, 1))] * parts
    ot_spec = pl.BlockSpec((PAIR, tokens), lambda g, t: (first + g, 0))
    lse_spec = pl.BlockSpec((1, 2, tokens), lambda g, t: (first + g, 0, 0))
    return parts, width, tokens, every, pairs, seg_specs, qkv_specs, o_specs, ot_spec, lse_spec


def attend_forward(qkv_parts, seg, keep, tables, chunk, begun=()):
    parts, width, tokens, every, pairs, seg_specs, qkv_specs, o_specs, ot_spec, lse_spec = (
        attend_specs(qkv_parts, chunk)
    )
    kseg = jnp.where(keep == 1, seg, -1)[:, None]
    return pl.pallas_call(
        functools.partial(forward_kernel, parts),
        grid_spec=pltpu.PrefetchScalarGridSpec(
            num_scalar_prefetch=1,
            grid=(pairs,),
            in_specs=seg_specs + qkv_specs + [pl.BlockSpec(memory_space=pl.ANY)] * len(begun),
            out_specs=o_specs + [ot_spec, lse_spec],
            scratch_shapes=[
                pltpu.VMEM((2, tokens, 128), BF16),
                pltpu.VMEM((2, HDIM + 16, tokens), BF16),
                pltpu.VMEM((PAIR, tokens), BF16),
                pltpu.VMEM((2, tokens, BQ), F32),
            ],
        ),
        out_shape=[jax.ShapeDtypeStruct((width, every * PAIR), BF16)] * parts
        + [
            jax.ShapeDtypeStruct((every * PAIR, tokens), BF16),
            jax.ShapeDtypeStruct((every, 2, tokens), F32),
        ],
        compiler_params=pltpu.CompilerParams(vmem_limit_bytes=40 * 2**20),
        cost_estimate=pl.CostEstimate(
            flops=2**10, bytes_accessed=2**10, transcendentals=0
        ),
        input_output_aliases={3 + parts + n: n for n in range(len(begun))},
        name="attend_forward",
    )(tables, kseg, seg[None, :], *qkv_parts, *begun)


def attend_backward(qkv_parts, turned, grad_ctx, lse, seg, keep, tables, chunk, place, begun=()):
    parts, width, tokens, every, pairs, seg_specs, qkv_specs, o_specs, ot_spec, lse_spec = (
        attend_specs(qkv_parts, chunk)
    )
    kseg = jnp.where(keep == 1, seg, -1)[:, None]
    result = pl.BlockSpec((width, 3 * PAIR), lanes_of(place[0], 1))
    return pl.pallas_call(
        functools.partial(backward_kernel, parts),
        grid_spec=pltpu.PrefetchScalarGridSpec(
            num_scalar_prefetch=1,
            grid=(pairs,),
            in_specs=seg_specs
            + qkv_specs
            + o_specs
            + [ot_spec, lse_spec]
            + [pl.BlockSpec(memory_space=pl.ANY)] * len(begun),
            out_specs=[result] * parts,
            scratch_shapes=[
                pltpu.VMEM((2, tokens, 128), BF16),
                pltpu.VMEM((2, tokens, 128), BF16),
                pltpu.VMEM((PAIR, tokens), BF16),
                pltpu.VMEM((2, 128, tokens), BF16),
                pltpu.VMEM((2, 128, tokens), BF16),
                pltpu.VMEM((2, tokens, 128), BF16),
                pltpu.VMEM((2, tokens, 128), BF16),
                pltpu.VMEM((PAIR, tokens), F32),
                pltpu.VMEM((tokens, 128), F32),
                pltpu.VMEM((tokens, 128), F32),
            ],
        ),
        out_shape=[jax.ShapeDtypeStruct((width, place[1] * 3 * PAIR), BF16)] * parts,
        input_output_aliases={5 + 2 * parts + n: n for n in range(len(begun))},
        compiler_params=pltpu.CompilerParams(vmem_limit_bytes=48 * 2**20),
        cost_estimate=pl.CostEstimate(
            flops=2**10,
            bytes_accessed=2**10,
            transcendentals=0,
        ),
        name="attend_backward",
    )(tables, kseg, seg[None, :], *qkv_parts, *grad_ctx, turned, lse, *begun)


def row_block(width):
    return FEED_ROWS if width % FEED_ROWS == 0 else width


def gelu_and_slope(u):
    root = 0.7978845608028654
    square = u * u
    t = jnp.tanh(u * (root + (root * 0.044715) * square))
    half = 0.5 * t + 0.5
    slope = half + (0.5 * u) * (1.0 - t * t) * (root + (root * 0.134145) * square)
    return u * half, slope


def feed_kernel(step, x_ref, up_ref, bias_ref, down_ref, *refs):
    x_all, hidden_all, slope_all, out_ref = refs[-4:]
    x = x_ref[...]
    x_all[...] = x
    units = up_ref.shape[1]
    total = None
    for first in range(0, units, step):
        at = slice(first, first + step)
        act, slope = gelu_and_slope(matmul(x, up_ref[:, at]) + bias_ref[:, at])
        act = act.astype(BF16)
        hidden_all[:, at] = act
        slope_all[:, at] = slope.astype(BF16)
        term = matmul(act, down_ref[at, :])
        total = term if total is None else total + term
    out_ref[...] = total.astype(BF16)


def feed_forward(part, parts, x, up, bias, down, begun):
    width, model = x.shape
    units = up.shape[1]
    rows = row_block(width)
    steps = width // rows
    own = lambda k: (k, 0)
    whole = lambda k: (part * steps + k, 0)
    fixed = lambda k: (0, 0)
    once = pl.Buffered(1)
    every = parts * width
    return pl.pallas_call(
        functools.partial(feed_kernel, min(units, FEED)),
        grid=(steps,),
        in_specs=[
            pl.BlockSpec((rows, model), own),
            pl.BlockSpec((model, units), fixed, pipeline_mode=once),
            pl.BlockSpec((1, units), fixed, pipeline_mode=once),
            pl.BlockSpec((units, model), fixed, pipeline_mode=once),
        ]
        + [pl.BlockSpec(memory_space=pl.ANY)] * len(begun),
        out_specs=[
            pl.BlockSpec((rows, model), whole),
            pl.BlockSpec((rows, units), whole),
            pl.BlockSpec((rows, units), whole),
            pl.BlockSpec((rows, model), own),
        ],
        out_shape=[
            jax.ShapeDtypeStruct((every, model), BF16),
            jax.ShapeDtypeStruct((every, units), BF16),
            jax.ShapeDtypeStruct((every, units), BF16),
            jax.ShapeDtypeStruct((width, model), BF16),
        ],
        input_output_aliases={4 + n: n for n in range(len(begun))},
        compiler_params=pltpu.CompilerParams(vmem_limit_bytes=48 * 2**20),
        cost_estimate=pl.CostEstimate(
            flops=6 * width * model * units, bytes_accessed=2**24, transcendentals=0
        ),
        name="feed_forward",
    )(x, up, bias[None, :], down, *begun)


def feed_back_kernel(step, g_ref, slope_ref, down_ref, up_ref, *refs):
    pre_all, sums_ref, out_ref = refs[-3:]
    g = g_ref[...]
    units = up_ref.shape[1]

    @pl.when(pl.program_id(0) == 0)
    def _():
        sums_ref[...] = jnp.zeros_like(sums_ref)

    total = None
    for first in range(0, units, step):
        at = slice(first, first + step)
        pre = contract_cols(g, down_ref[at, :]) * slope_ref[:, at].astype(F32)
        pre = pre.astype(BF16)
        pre_all[:, at] = pre
        sums_ref[:, at] += jnp.sum(pre.astype(F32), axis=0, keepdims=True)
        term = contract_cols(pre, up_ref[:, at])
        total = term if total is None else total + term
    out_ref[...] = total.astype(BF16)


def feed_back(part, parts, g, slope_all, up, down, begun):
    width, model = g.shape
    units = up.shape[1]
    rows = row_block(width)
    steps = width // rows
    own = lambda k: (k, 0)
    whole = lambda k: (part * steps + k, 0)
    fixed = lambda k: (0, 0)
    once = pl.Buffered(1)
    every = parts * width
    return pl.pallas_call(
        functools.partial(feed_back_kernel, min(units, FEED)),
        grid=(steps,),
        in_specs=[
            pl.BlockSpec((rows, model), own),
            pl.BlockSpec((rows, units), whole),
            pl.BlockSpec((units, model), fixed, pipeline_mode=once),
            pl.BlockSpec((model, units), fixed, pipeline_mode=once),
        ]
        + [pl.BlockSpec(memory_space=pl.ANY)] * len(begun),
        out_specs=[
            pl.BlockSpec((rows, units), whole),
            pl.BlockSpec((1, units), fixed),
            pl.BlockSpec((rows, model), own),
        ],
        out_shape=[
            jax.ShapeDtypeStruct((every, units), BF16),
            jax.ShapeDtypeStruct((1, units), F32),
            jax.ShapeDtypeStruct((width, model), BF16),
        ],
        input_output_aliases={4 + n: n for n in range(len(begun))},
        compiler_params=pltpu.CompilerParams(vmem_limit_bytes=48 * 2**20),
        cost_estimate=pl.CostEstimate(
            flops=2**10, bytes_accessed=2**10, transcendentals=0
        ),
        name="feed_back",
    )(g, slope_all, down, up, *begun)


def weight_grad_kernel(parts, *refs):
    a_refs, d_refs = refs[:parts], refs[parts : 2 * parts]
    out_ref, sums_ref = refs[2 * parts :]
    out_ref[...] = total([contract_rows(a[...], d[...]) for a, d in zip(a_refs, d_refs)]).astype(BF16)
    sums_ref[...] = total([jnp.sum(d[...].astype(F32), axis=0, keepdims=True) for d in d_refs])


def weight_grad(a_parts, d_parts, first, count):
    parts = len(a_parts)
    width, model = a_parts[0].shape
    columns = 3 * PAIR
    return pl.pallas_call(
        functools.partial(weight_grad_kernel, parts),
        grid=(count,),
        in_specs=[pl.BlockSpec((width, model), lambda k: (0, 0), pipeline_mode=pl.Buffered(1))] * parts
        + [pl.BlockSpec((width, columns), lambda k: (0, first + k))] * parts,
        out_specs=[
            pl.BlockSpec((model, columns), lambda k: (0, k)),
            pl.BlockSpec((1, columns), lambda k: (0, k)),
        ],
        out_shape=[
            jax.ShapeDtypeStruct((model, count * columns), BF16),
            jax.ShapeDtypeStruct((1, count * columns), F32),
        ],
        compiler_params=pltpu.CompilerParams(vmem_limit_bytes=40 * 2**20),
        cost_estimate=pl.CostEstimate(flops=2**10, bytes_accessed=2**10, transcendentals=0),
        name="weight_grad",
    )(*a_parts, *d_parts)


def input_grad_kernel(w_ref, *refs):
    *d_refs, out_ref = refs
    columns = d_refs[0].shape[1]
    terms = [
        contract_cols(d[...], w_ref[:, k * columns : (k + 1) * columns])
        for k, d in enumerate(d_refs)
    ]
    out_ref[...] = total(terms).astype(BF16)


def input_grad(chunks, weight):
    width, columns = chunks[0].shape
    model = weight.shape[0]
    rows = row_block(width)
    return pl.pallas_call(
        input_grad_kernel,
        grid=(width // rows,),
        in_specs=[
            pl.BlockSpec(weight.shape, lambda k: (0, 0), pipeline_mode=pl.Buffered(1)),
        ]
        + [pl.BlockSpec((rows, columns), lambda k: (k, 0))] * len(chunks),
        out_specs=pl.BlockSpec((rows, model), lambda k: (k, 0)),
        out_shape=jax.ShapeDtypeStruct((width, model), BF16),
        compiler_params=pltpu.CompilerParams(vmem_limit_bytes=40 * 2**20),
        cost_estimate=pl.CostEstimate(flops=2**10, bytes_accessed=2**10, transcendentals=0),
        name="input_grad",
    )(weight, *chunks)


def spread_kernel(tab_ref, mine_ref, theirs_ref, out_ref):
    mine = pl.program_id(1) == tab_ref[0]

    def put(ref):
        for c in range(3):
            out_ref[c] = ref[:, c * PAIR : (c + 1) * PAIR].astype(F32)

    @pl.when(mine)
    def _():
        put(mine_ref)

    @pl.when(jnp.logical_not(mine))
    def _():
        put(theirs_ref)


def spread(mine, theirs, side, out_pairs, first, begun):
    half, columns = mine.shape
    count = columns // (3 * PAIR)
    block = pl.BlockSpec((half, 3 * PAIR), lambda k, s, t: (0, k))
    return pl.pallas_call(
        lambda tab, a, b, *refs: spread_kernel(tab, a, b, refs[-1]),
        grid_spec=pltpu.PrefetchScalarGridSpec(
            num_scalar_prefetch=1,
            grid=(count, 2),
            in_specs=[block, block] + [pl.BlockSpec(memory_space=pl.ANY)] * len(begun),
            out_specs=pl.BlockSpec((3, half, PAIR), lambda k, s, t: (0, s, first + k)),
        ),
        out_shape=jax.ShapeDtypeStruct((3, 2 * half, out_pairs * PAIR), F32),
        input_output_aliases={3 + n: n for n in range(len(begun))},
        compiler_params=pltpu.CompilerParams(vmem_limit_bytes=32 * 2**20),
        cost_estimate=pl.CostEstimate(flops=2**10, bytes_accessed=2**10, transcendentals=0),
        name="spread",
    )(jnp.reshape(side, (1,)).astype(jnp.int32), mine, theirs, *begun)


def after(value, *others):
    return lax.optimization_barrier((value, *others))[0]


class Layout:
    def __init__(self, mesh):
        self.dp, self.n = mesh.shape["dp"], mesh.shape["mp"]
        self.pairs = self.dp // 2
        self.axes = ("dp", "mp")

    def device(self, pair, core, m):
        return (2 * pair + core) * self.n + m

    def at_rank(self, pair, group, rank):
        return self.device(pair, rank % 2, group * (self.n // 2) + rank // 2)

    def each(self):
        for pair in range(self.pairs):
            for group in range(2):
                for rank in range(self.n):
                    yield pair, group, rank

    def stays(self):
        core, m = lax.axis_index("dp") % 2, lax.axis_index("mp")
        return (m // (self.n // 2) == core) & (self.rank() == m)

    def send(self, value, back=False):
        moves = [(self.device(p, g, r), self.at_rank(p, g, r)) for p, g, r in self.each()]
        return lax.ppermute(
            value, self.axes, [(b, a) if back else (a, b) for a, b in moves if a != b]
        )

    def regroup(self, value):
        return jnp.where(self.stays(), value, self.send(value))

    def give_back(self, value):
        return jnp.where(self.stays(), value, self.send(value, True))

    def partner(self, value, bit, only=lambda p, g, r: True):
        def other(p, c):
            return (p, 1 - c) if bit < 0 else (p ^ (1 << bit), c)

        moves = [
            (self.device(*other(p, c), m), self.device(p, c, m))
            for p, c, m in self.each()
            if only(p, c, m)
        ]
        return lax.ppermute(value, self.axes, moves)

    def side(self, bit):
        dp = lax.axis_index("dp")
        return dp % 2 if bit < 0 else (dp // 2 >> bit) % 2

    def joined(self, mine, theirs, bit):
        high = self.side(bit) == 1
        return jnp.concatenate(
            [jnp.where(high, theirs, mine), jnp.where(high, mine, theirs)], 0
        )

    def regroup_first(self, weight, small, tokens):
        rows = weight.shape[0] // 4
        part = 2 * self.side(0) + self.side(1)
        quarter = lax.dynamic_slice_in_dim(weight, part * rows, rows, 0)
        got = self.send(quarter)
        small = self.regroup(after(small, got))
        tokens = self.regroup(after(tokens, got, small))
        for bit in (1, 0):
            got = self.joined(got, self.partner(got, bit, self.moving), bit)
        return jnp.where(self.stays(), weight, got), small, tokens

    def moving(self, pair, core, m):
        return self.at_rank(pair, core, m) != self.device(pair, core, m)

    def to_rank(self, value, ahead):
        moves = [
            (self.at_rank(p, g, r), self.at_rank(p, g, (r + ahead) % self.n))
            for p, g, r in self.each()
        ]
        return lax.ppermute(value, self.axes, moves)

    def rank(self):
        core = lax.axis_index("dp") % 2
        return (lax.axis_index("mp") % (self.n // 2)) * 2 + core

    def gather(self, mine):
        return [mine] + [self.to_rank(mine, self.n - k) for k in range(1, self.n)]

    def scatter_sum(self, shares):
        total = shares[0].astype(jnp.float32)
        for k in range(1, self.n):
            total = total + self.to_rank(shares[k].astype(jnp.bfloat16), k).astype(jnp.float32)
        return total

    def sum_all(self, value):
        devices = self.dp * self.n
        steps = [1 << k for k in range(devices.bit_length() - 1)]
        for step in steps:
            value = value + lax.ppermute(value, self.axes, [(i, i ^ step) for i in range(devices)])
        return value

    def sum_dp(self, value, turn):
        order = [(i + turn) % self.dp for i in range(self.dp)]
        return lax.psum(value, "dp", axis_index_groups=[order])

    def halved(self, value, bit):
        half, high = value.shape[0] // 2, self.side(bit)
        sent = lax.dynamic_slice_in_dim(value, (1 - high) * half, half, 0)
        kept = lax.dynamic_slice_in_dim(value, high * half, half, 0)
        got = self.partner(sent, bit)
        return (kept.astype(jnp.float32) + got.astype(jnp.float32)).astype(jnp.bfloat16)

    def order(self, first):
        bits = list(range(self.pairs.bit_length() - 1))
        return bits[first:] + bits[:first]

    def halved_by(self, value, bits):
        for bit in bits:
            value = self.halved(value, bit)
        return value

    def joined_by(self, value, bits):
        for bit in bits[::-1]:
            value = self.joined(value, self.partner(value, bit), bit)
        return value


def for_kernel(shares, rank):
    width = shares[0].shape[0]
    if width % BQ == 0:
        return shares, rank * (width // BQ)
    return [jnp.roll(jnp.concatenate(shares, 0), rank * width, 0)], 0


def from_kernel(arrays, rank, shares):
    if len(arrays) == shares:
        return arrays
    width = arrays[0].shape[0] // shares
    return jnp.split(jnp.roll(arrays[0], -rank * width, 0), shares, 0)


def by_pairs(weight, pairs):
    return (
        weight.reshape(-1, 3, pairs, PAIR).transpose(0, 2, 1, 3).reshape(-1, 3 * pairs * PAIR)
    )


def total(terms):
    return functools.reduce(jnp.add, terms)


def body(
    layout,
    tokens,
    ln1_gain,
    ln1_bias,
    w_qkv,
    qv_bias,
    w_out,
    out_bias,
    ln2_gain,
    ln2_bias,
    ln3_gain,
    ln3_bias,
    w_up,
    up_bias,
    w_down,
    down_bias,
    ln4_gain,
    ln4_bias,
    row_grid,
    pad_mask,
    cotangent,
):
    f32, bf16 = jnp.float32, jnp.bfloat16
    model_dim = tokens.shape[1]
    group_rows = pad_mask.shape[0]
    width = w_qkv.shape[2]
    units = w_up.shape[1]
    shares = layout.n
    rank = layout.rank()

    small = jnp.concatenate(
        [
            qv_bias.reshape(-1),
            up_bias,
            pad_mask.astype(f32),
            row_grid[0].astype(f32),
        ]
    )
    pairs = width // PAIR
    chunks = 2 if pairs % 2 == 0 else 1
    w_qkv, small, tokens = layout.regroup_first(w_qkv, small, tokens)
    qv_bias = small[: 2 * width].reshape(2, width)
    up_bias = small[2 * width : 2 * width + units]
    keep = small[2 * width + units : 2 * width + units + group_rows].astype(jnp.int32)
    grid_row = small[2 * width + units + group_rows :].astype(jnp.int32)
    w_qkv = by_pairs(w_qkv, pairs)
    half = units // 2
    w_out_far = layout.send(after(w_out, tokens))
    w_up_far = layout.send(after(w_up, tokens))
    w_top_far = layout.send(after(w_down[:half], tokens))
    w_low_far = layout.send(after(w_down[half:], tokens))
    cotangent = layout.regroup(after(cotangent, w_low_far))

    resid_in = tokens.astype(f32)
    norm1_out, normed1, inv1 = norm_parts(resid_in, ln1_gain, ln1_bias)
    a1 = layout.gather(norm1_out.astype(bf16))
    zeros = jnp.zeros((width,), f32)
    qkv_bias = by_pairs(jnp.concatenate([qv_bias[0], zeros, qv_bias[1]]), pairs)
    qkv_scale = by_pairs(
        jnp.concatenate([zeros + HDIM ** (-0.5), zeros + 1.0, zeros + 1.0]), pairs
    )
    qkv = [((matmul(x, w_qkv) + qkv_bias) * qkv_scale).astype(bf16) for x in a1]
    qkv, turn = for_kernel(qkv, rank)
    seg, tables = row_tables(grid_row, group_rows, turn)
    begun = ()
    for pair in range(pairs):
        if pair and pair == pairs // 2:
            tables, w_up_far = lax.optimization_barrier((tables, w_up_far))
        begun = attend_forward(qkv, seg, keep, tables, (pair, 1), begun)
    *context, context_turned, log_total = begun
    *context, w_out_far, w_top_far, w_low_far = lax.optimization_barrier(
        (*context, w_out_far, w_top_far, w_low_far)
    )
    context = from_kernel(context, rank, shares)
    stays = layout.stays()
    w_out = jnp.where(stays, w_out, w_out_far)
    w_up = jnp.where(stays, w_up, w_up_far)
    w_down = jnp.where(stays, w_down, jnp.concatenate([w_top_far, w_low_far], 0))
    branch_z = layout.scatter_sum([matmul(x, w_out) for x in context]) + out_bias
    norm2_out, normed2, inv2 = norm_parts(branch_z, ln2_gain, ln2_bias)
    resid_mid = resid_in + norm2_out
    norm3_out, normed3, inv3 = norm_parts(resid_mid, ln3_gain, ln3_bias)
    a3 = layout.gather(norm3_out.astype(bf16))
    begun, shares_f = (), []
    for part, x in enumerate(a3):
        if part == shares - 1:
            x, cotangent = lax.optimization_barrier((x, cotangent))
        *begun, share = feed_forward(part, shares, x, w_up, up_bias, w_down, begun)
        shares_f.append(share)
    a3_all, hidden, slope = begun
    branch_f = layout.scatter_sum(shares_f) + down_bias
    norm4_out, normed4, inv4 = norm_parts(branch_f, ln4_gain, ln4_bias)
    layer_out = (resid_mid + norm4_out).astype(bf16)

    upstream = cotangent.astype(f32)
    grad_f = norm_back(upstream, normed4, inv4, ln4_gain).astype(bf16)
    grad_f_all = layout.gather(grad_f)
    g_w_down = contract_rows(hidden, jnp.concatenate(grad_f_all, 0)).astype(bf16)
    begun, shares_a3, g_up_bias = (), [], []
    for part, g in enumerate(grad_f_all):
        if part:
            g, g_w_down = lax.optimization_barrier((g, g_w_down))
        *begun, unit_sums, share = feed_back(part, shares, g, slope, w_up, w_down, begun)
        shares_a3.append(share)
        g_up_bias.append(unit_sums[0])
    [grad_pre] = begun
    g_w_down_far = layout.send(g_w_down, True)
    grad_a3 = layout.scatter_sum(shares_a3)
    g_up_bias = total(g_up_bias)
    g_w_up = contract_rows(a3_all, grad_pre).astype(bf16)
    g_w_up_far = layout.send(g_w_up, True)
    grad_mid = upstream + norm_back(grad_a3, normed3, inv3, ln3_gain)
    grad_z = norm_back(grad_mid, normed2, inv2, ln2_gain).astype(bf16)
    grad_z_all = layout.gather(grad_z)
    grad_ctx = [contract_cols(g, w_out).astype(bf16) for g in grad_z_all]
    g_w_out = total([contract_rows(x, g) for x, g in zip(context, grad_z_all)]).astype(bf16)
    g_w_out_far = layout.send(g_w_out, True)
    g_w_down_far, g_w_up, *grad_ctx = lax.optimization_barrier((g_w_down_far, g_w_up, *grad_ctx))
    grad_ctx, _ = for_kernel(grad_ctx, rank)
    g_w_down = jnp.where(stays, g_w_down, g_w_down_far)
    tables, g_w_down = lax.optimization_barrier((tables, g_w_down))
    g_w_down = layout.sum_dp(g_w_down, 1)
    each = pairs // chunks
    calls = [(0, each)] + [(k, 1) for k in range(each, pairs)]
    done, g_w_qkv, sums, grad_qkv = [], [], [], ()
    for call in calls:
        if len(calls) > 1 and call == calls[-1]:
            g_w_up_far, g_w_out_far, *grad_qkv = lax.optimization_barrier(
                (g_w_up_far, g_w_out_far, *grad_qkv)
            )
            g_w_up = jnp.where(stays, g_w_up, g_w_up_far)
            g_w_out = jnp.where(stays, g_w_out, g_w_out_far)
            tables, g_w_down, g_w_up, g_w_out = lax.optimization_barrier(
                (tables, g_w_down, g_w_up, g_w_out)
            )
        grad_qkv = attend_backward(
            qkv,
            context_turned,
            grad_ctx,
            log_total,
            seg,
            keep,
            tables,
            call,
            (call[0] % each, each),
            grad_qkv,
        )
        if sum(call) % each == 0:
            shared = from_kernel(grad_qkv, rank, shares)
            g_part, part_sums = weight_grad(a1, shared, 0, each)
            tables, g_part = lax.optimization_barrier((tables, g_part))
            g_w_qkv.append(layout.halved(layout.give_back(g_part), -1))
            sums.append(part_sums)
            done.append(shared)
            grad_qkv = ()
    if len(calls) == 1:
        g_w_up = jnp.where(stays, g_w_up, g_w_up_far)
        g_w_out = jnp.where(stays, g_w_out, g_w_out_far)
    g_w_up = layout.sum_dp(g_w_up, 0)
    g_w_out = layout.sum_dp(g_w_out, 0)
    layer_out = layout.give_back(after(layer_out, g_w_qkv[0]))
    sums = jnp.concatenate(sums, 1)
    grad_a1 = [input_grad(d, w_qkv) for d in zip(*done)]
    grad_a1 = layout.scatter_sum(grad_a1)
    grad_input = grad_mid + norm_back(grad_a1, normed1, inv1, ln1_gain)
    grad_input = grad_input.astype(bf16)
    steps = [layout.order(k) for k in range(chunks)]
    g_w_qkv[0] = layout.halved(g_w_qkv[0], steps[0].pop(0))
    g_w_qkv = list(lax.optimization_barrier(tuple(g_w_qkv)))
    g_w_qkv = [layout.halved_by(g, s) for g, s in zip(g_w_qkv, steps)]
    g_w_qkv = [layout.joined_by(g, layout.order(k)) for k, g in enumerate(g_w_qkv)]
    begun = ()
    for chunk, mine in enumerate(g_w_qkv):
        theirs = layout.partner(mine, -1)
        begun = (spread(mine, theirs, layout.side(-1), pairs, chunk * each, begun),)
    g_w_qkv = begun[0].transpose(1, 0, 2)
    sums = sums.reshape(pairs, 3, PAIR).transpose(1, 0, 2).reshape(3, width)
    grad_input = layout.give_back(grad_input).astype(f32)

    norm_terms = jnp.stack(
        [
            jnp.sum(grad_a1 * normed1, 0),
            jnp.sum(grad_a1, 0),
            jnp.sum(grad_z.astype(f32), 0),
            jnp.sum(grad_mid * normed2, 0),
            jnp.sum(grad_mid, 0),
            jnp.sum(grad_a3 * normed3, 0),
            jnp.sum(grad_a3, 0),
            jnp.sum(grad_f.astype(f32), 0),
            jnp.sum(upstream * normed4, 0),
            jnp.sum(upstream, 0),
        ],
        0,
    )
    all_units = lax.dynamic_update_slice(jnp.zeros((units * shares,), f32), g_up_bias, (rank * units,))
    all_width = lax.dynamic_update_slice(
        jnp.zeros((2, width * shares), f32), jnp.stack([sums[0], sums[2]], 0), (0, rank * width)
    )
    small = layout.sum_all(
        jnp.concatenate([norm_terms.reshape(-1), all_width.reshape(-1), all_units])
    )
    norm_terms = small[: 10 * model_dim].reshape(10, model_dim)
    all_width = small[10 * model_dim : 12 * model_dim].reshape(2, width * shares)
    all_units = small[12 * model_dim :]
    m = lax.axis_index("mp")
    g_qv_bias = lax.dynamic_slice(all_width, (0, m * width), (2, width))
    g_up_bias = lax.dynamic_slice(all_units, (m * units,), (units,))
    return (
        layer_out,
        grad_input,
        norm_terms[0],
        norm_terms[1],
        g_w_qkv,
        g_qv_bias,
        g_w_out.astype(f32),
        norm_terms[2],
        norm_terms[3],
        norm_terms[4],
        norm_terms[5],
        norm_terms[6],
        g_w_up.astype(f32),
        g_up_bias,
        g_w_down.astype(f32),
        norm_terms[7],
        norm_terms[8],
        norm_terms[9],
    )


def solution(mesh):
    in_specs = (
        P(("dp", "mp"), None),
        P(),
        P(),
        P(None, None, "mp"),
        P(None, "mp"),
        P("mp", None),
        P(),
        P(),
        P(),
        P(),
        P(),
        P(None, "mp"),
        P("mp"),
        P("mp", None),
        P(),
        P(),
        P(),
        P("dp", None),
        P("dp"),
        P(("dp", "mp"), None),
    )
    out_specs = (
        P(("dp", "mp"), None),
        P(("dp", "mp"), None),
        P(),
        P(),
        P(None, None, "mp"),
        P(None, "mp"),
        P("mp", None),
        P(),
        P(),
        P(),
        P(),
        P(),
        P(None, "mp"),
        P("mp"),
        P("mp", None),
        P(),
        P(),
        P(),
    )
    return jax.shard_map(functools.partial(body, Layout(mesh)), mesh=mesh, in_specs=in_specs, out_specs=out_specs, check_vma=False)
```

```python
import functools

import jax
import jax.numpy as jnp
from jax import lax
from jax.experimental import pallas as pl
from jax.experimental.pallas import tpu as pltpu
from jax.sharding import PartitionSpec as P

HDIM = 64
TEXT = 64


epsilon = 1e-05
masked_score = -1e30


def norm_parts(values, ln_gain, ln_bias):
    centred = values - jnp.mean(values, -1, keepdims=True)
    inv_std = lax.rsqrt(jnp.mean(centred * centred, -1, keepdims=True) + epsilon)
    normed = centred * inv_std
    return (normed * ln_gain + ln_bias, normed, inv_std)


def norm_back(upstream, normed, inv_std, ln_gain):
    scaled = upstream * ln_gain
    return inv_std * (
        scaled
        - jnp.mean(scaled, -1, keepdims=True)
        - normed * jnp.mean(scaled * normed, -1, keepdims=True)
    )


def contract_rows(left, right):
    return lax.dot_general(
        left, right, (((0,), (0,)), ((), ())), preferred_element_type=jnp.float32
    )


def contract_cols(left, right):
    return lax.dot_general(
        left, right, (((1,), (1,)), ((), ())), preferred_element_type=jnp.float32
    )


BQ = 256
BK = 256
MOST = 4
FEED = 1024
FEED_ROWS = 640
PAIR = 2 * HDIM
F32 = jnp.float32
BF16 = jnp.bfloat16


def matmul(left, right):
    return jnp.dot(left, right, preferred_element_type=F32)


def row_tables(grid_row, tokens, turn):
    side = jnp.max(grid_row)
    length = TEXT + side * side
    rows = tokens // length
    used = rows * length
    position = jnp.arange(tokens, dtype=jnp.int32)
    seg = jnp.minimum(position // length, rows)
    blocks = tokens // BQ
    first = jnp.arange(blocks, dtype=jnp.int32) * BQ
    start = jnp.where(first < used, (first // length) * length, first)
    low = start // BK
    diag = first // BK
    turns = jnp.full((blocks,), turn, jnp.int32)
    return seg, jnp.stack([low, diag, turns]).astype(jnp.int32)


def allowed(kseg_ref, qseg_ref, i, j, blocks):
    qs = qseg_ref[:, pl.ds(pl.multiple_of(i * BQ, BQ), BQ)]
    ks = kseg_ref[pl.ds(pl.multiple_of(j * BK, BK), blocks * BK), :]
    ik = j * BK + lax.broadcasted_iota(jnp.int32, (blocks * BK, BQ), 0)
    iq = i * BQ + lax.broadcasted_iota(jnp.int32, (blocks * BK, BQ), 1)
    return ((ks == qs) & (ik <= iq)) | (ik == iq)


def sweep(tab_ref, i, step, carry):
    return several(tab_ref[0, i], tab_ref[1, i] + 1, step, carry)


def several(first, stop, step, carry, most=MOST):
    while most > 1:
        turns = (stop - first) // most

        def turn(n, carry, first=first, most=most):
            return step(most, first + most * n, carry)

        carry = lax.fori_loop(0, turns, turn, carry)
        first, most = first + most * turns, most // 2
    return lax.fori_loop(first, stop, functools.partial(step, 1), carry)


def each_block(tab_ref, parts, width, work):
    blocks = width // BQ
    count = blocks * parts
    for part in range(parts):

        def one(c, _, part=part):
            whole = lax.rem(tab_ref[2, 0] + part * blocks + c, count)
            work(
                part,
                pl.ds(pl.multiple_of(c * BQ, BQ), BQ),
                pl.ds(pl.multiple_of(whole * BQ, BQ), BQ),
            )
            return 0

        lax.fori_loop(0, blocks, one, 0)


def forward_kernel(parts, tab_ref, kseg_ref, qseg_ref, *refs):
    qkv_refs = refs[:parts]
    *o_refs, ot_ref, lse_ref, kx, vx, qx, scores = refs[-6 - parts :]
    tokens = qx.shape[1]
    width = tokens // parts
    lane = lax.broadcasted_iota(jnp.int32, (BK, 128), 1)
    zero = jnp.zeros((BK, 128), BF16)

    def prepare(part, here, there):
        k = qkv_refs[part][here, PAIR : 2 * PAIR]
        kx[0, there, :] = jnp.where(lane < HDIM, k, zero)
        kx[1, there, :] = jnp.where(lane < HDIM, zero, k)
        qx[:, there] = qkv_refs[part][here, :PAIR].astype(F32).T.astype(BF16)
        v = qkv_refs[part][here, 2 * PAIR :].astype(F32).T.astype(BF16)
        for h in range(2):
            vx[h, :HDIM, there] = v[h * HDIM : (h + 1) * HDIM]
            vx[h, HDIM:, there] = jnp.ones((16, BQ), BF16)

    each_block(tab_ref, parts, width, prepare)

    def block(i, _):
        cols = pl.ds(pl.multiple_of(i * BQ, BQ), BQ)
        qb = qx[:, cols]

        def score(blocks, j, tops):
            at = pl.ds(pl.multiple_of(j * BK, BK), blocks * BK)
            ok = allowed(kseg_ref, qseg_ref, i, j, blocks)
            out = []
            for h in range(2):
                s = matmul(kx[h, at, :], qb)
                s = jnp.where(ok, s, masked_score)
                scores[h, at, :] = s
                out.append(jnp.maximum(tops[h], jnp.max(s.reshape(blocks * BK // 8, 8, BQ), axis=0)))
            return tuple(out)

        tops = sweep(tab_ref, i, score, (jnp.full((8, BQ), masked_score, F32),) * 2)
        tops = [jnp.max(top, axis=0, keepdims=True) for top in tops]

        def weigh(blocks, j, accs):
            at = pl.ds(pl.multiple_of(j * BK, BK), blocks * BK)
            out = []
            for h in range(2):
                p = jnp.exp(scores[h, at, :] - tops[h]).astype(BF16)
                out.append(accs[h] + matmul(vx[h, :, at], p))
            return tuple(out)

        accs = sweep(tab_ref, i, weigh, (jnp.zeros((HDIM + 16, BQ), F32),) * 2)
        for h in range(2):
            total = accs[h][HDIM : HDIM + 1, :]
            ot_ref[h * HDIM : (h + 1) * HDIM, cols] = (accs[h][:HDIM, :] / total).astype(BF16)
            lse_ref[0, h : h + 1, cols] = tops[h] + jnp.log(total)
        return 0

    lax.fori_loop(0, tokens // BQ, block, 0)

    def finish(part, here, there):
        o_refs[part][here, :] = ot_ref[:, there].astype(F32).T.astype(BF16)

    each_block(tab_ref, parts, width, finish)


def three_parts(x):
    high = x.astype(BF16)
    rest = x - high.astype(F32)
    middle = rest.astype(BF16)
    return high, middle, (rest - middle.astype(F32)).astype(BF16)


def backward_kernel(parts, tab_ref, kseg_ref, qseg_ref, *refs):
    qkv_refs, do_refs = refs[:parts], refs[parts : 2 * parts]
    ot_ref, lse_ref = refs[2 * parts : 2 * parts + 2]
    *out_refs, kx, vx, kt, qx, dox, qt, dot, dq, dk, dv = refs[-10 - parts :]
    tokens = kt.shape[1]
    width = tokens // parts
    lane = lax.broadcasted_iota(jnp.int32, (BK, 128), 1)
    sub = lax.broadcasted_iota(jnp.int32, (HDIM, BK), 0)
    one0 = jnp.where((lane >= HDIM) & (lane < HDIM + 3), 1.0, 0.0).astype(BF16)
    one1 = jnp.where(lane < 3, 1.0, 0.0).astype(BF16)
    zero = jnp.zeros((BK, 128), BF16)

    def extra(x):
        high, middle, low = (e.astype(F32) for e in three_parts(x))
        rows = jnp.where(
            sub == 0, high, jnp.where(sub == 1, middle, jnp.where(sub == 2, low, 0.0))
        )
        return rows.astype(BF16)

    def prepare(part, here, there):
        k = qkv_refs[part][here, PAIR : 2 * PAIR]
        kt[:, there] = k.astype(F32).T.astype(BF16)
        kx[0, there, :] = jnp.where(lane < HDIM, k, one0)
        kx[1, there, :] = jnp.where(lane < HDIM, one1, k)
        v = qkv_refs[part][here, 2 * PAIR :]
        vx[0, there, :] = jnp.where(lane < HDIM, v, one0)
        vx[1, there, :] = jnp.where(lane < HDIM, one1, v)
        q = qkv_refs[part][here, :PAIR]
        qt[0, there, :] = jnp.where(lane < HDIM, q, zero)
        qt[1, there, :] = jnp.where(lane < HDIM, zero, q)
        do = do_refs[part][here, :]
        dot[0, there, :] = jnp.where(lane < HDIM, do, zero)
        dot[1, there, :] = jnp.where(lane < HDIM, zero, do)
        turned = do.astype(F32).T
        prod = turned * ot_ref[:, there].astype(F32)
        inner0 = jnp.sum(prod[:HDIM], axis=0, keepdims=True)
        inner1 = jnp.sum(prod[HDIM:], axis=0, keepdims=True)
        turned = turned.astype(BF16)
        dox[0, :HDIM, there] = turned[:HDIM]
        dox[0, HDIM:, there] = extra(-inner0)
        dox[1, HDIM:, there] = turned[HDIM:]
        dox[1, :HDIM, there] = extra(-inner1)
        turned = q.astype(F32).T.astype(BF16)
        qx[0, :HDIM, there] = turned[:HDIM]
        qx[0, HDIM:, there] = extra(-lse_ref[0, 0:1, there])
        qx[1, HDIM:, there] = turned[HDIM:]
        qx[1, :HDIM, there] = extra(-lse_ref[0, 1:2, there])
        dk[there, :] = jnp.zeros((BK, 128), F32)
        dv[there, :] = jnp.zeros((BK, 128), F32)

    each_block(tab_ref, parts, width, prepare)

    def block(i, _):
        cols = pl.ds(pl.multiple_of(i * BQ, BQ), BQ)

        def step(blocks, j, carry):
            at = pl.ds(pl.multiple_of(j * BK, BK), blocks * BK)
            ok = allowed(kseg_ref, qseg_ref, i, j, blocks)
            new = []
            dvs = dv[at, :]
            dks = dk[at, :]
            for h in range(2):
                s = matmul(kx[h, at, :], qx[h, :, cols])
                s = jnp.where(ok, s, masked_score)
                p = jnp.exp(s)
                dp = matmul(vx[h, at, :], dox[h, :, cols])
                ds = (p * dp).astype(BF16)
                dvs = dvs + matmul(p.astype(BF16), dot[h, cols, :])
                dks = dks + matmul(ds, qt[h, cols, :])
                new.append(carry[h] + matmul(kt[h * HDIM : (h + 1) * HDIM, at], ds))
            dv[at, :] = dvs
            dk[at, :] = dks
            return tuple(new)

        init = tuple(jnp.zeros((HDIM, BQ), F32) for _ in range(2))
        res = sweep(tab_ref, i, step, init)
        for h in range(2):
            dq[h * HDIM : (h + 1) * HDIM, cols] = res[h] * (HDIM**-0.5)
        return 0

    lax.fori_loop(0, tokens // BQ, block, 0)

    def finish(part, here, there):
        out_refs[part][here, :PAIR] = dq[:, there].T.astype(BF16)
        out_refs[part][here, PAIR : 2 * PAIR] = dk[there, :].astype(BF16)
        out_refs[part][here, 2 * PAIR :] = dv[there, :].astype(BF16)

    each_block(tab_ref, parts, width, finish)


def lanes_of(first, step):
    return lambda g, t: (0, first + step * g)


def attend_specs(qkv_parts, chunk):
    parts = len(qkv_parts)
    width = qkv_parts[0].shape[0]
    tokens = parts * width
    every = qkv_parts[0].shape[1] // (3 * PAIR)
    first, pairs = chunk
    seg_specs = [
        pl.BlockSpec((tokens, 1), lambda g, t: (0, 0)),
        pl.BlockSpec((1, tokens), lambda g, t: (0, 0)),
    ]
    qkv_specs = [pl.BlockSpec((width, 3 * PAIR), lanes_of(first, 1))] * parts
    o_specs = [pl.BlockSpec((width, PAIR), lanes_of(first, 1))] * parts
    ot_spec = pl.BlockSpec((PAIR, tokens), lambda g, t: (first + g, 0))
    lse_spec = pl.BlockSpec((1, 2, tokens), lambda g, t: (first + g, 0, 0))
    return parts, width, tokens, every, pairs, seg_specs, qkv_specs, o_specs, ot_spec, lse_spec


def attend_forward(qkv_parts, seg, keep, tables, chunk, begun=()):
    parts, width, tokens, every, pairs, seg_specs, qkv_specs, o_specs, ot_spec, lse_spec = (
        attend_specs(qkv_parts, chunk)
    )
    kseg = jnp.where(keep == 1, seg, -1)[:, None]
    return pl.pallas_call(
        functools.partial(forward_kernel, parts),
        grid_spec=pltpu.PrefetchScalarGridSpec(
            num_scalar_prefetch=1,
            grid=(pairs,),
            in_specs=seg_specs + qkv_specs + [pl.BlockSpec(memory_space=pl.ANY)] * len(begun),
            out_specs=o_specs + [ot_spec, lse_spec],
            scratch_shapes=[
                pltpu.VMEM((2, tokens, 128), BF16),
                pltpu.VMEM((2, HDIM + 16, tokens), BF16),
                pltpu.VMEM((PAIR, tokens), BF16),
                pltpu.VMEM((2, tokens, BQ), F32),
            ],
        ),
        out_shape=[jax.ShapeDtypeStruct((width, every * PAIR), BF16)] * parts
        + [
            jax.ShapeDtypeStruct((every * PAIR, tokens), BF16),
            jax.ShapeDtypeStruct((every, 2, tokens), F32),
        ],
        compiler_params=pltpu.CompilerParams(vmem_limit_bytes=40 * 2**20),
        cost_estimate=pl.CostEstimate(
            flops=2**10, bytes_accessed=2**10, transcendentals=0
        ),
        input_output_aliases={3 + parts + n: n for n in range(len(begun))},
        name="attend_forward",
    )(tables, kseg, seg[None, :], *qkv_parts, *begun)


def attend_backward(qkv_parts, turned, grad_ctx, lse, seg, keep, tables, chunk, place, begun=()):
    parts, width, tokens, every, pairs, seg_specs, qkv_specs, o_specs, ot_spec, lse_spec = (
        attend_specs(qkv_parts, chunk)
    )
    kseg = jnp.where(keep == 1, seg, -1)[:, None]
    result = pl.BlockSpec((width, 3 * PAIR), lanes_of(place[0], 1))
    return pl.pallas_call(
        functools.partial(backward_kernel, parts),
        grid_spec=pltpu.PrefetchScalarGridSpec(
            num_scalar_prefetch=1,
            grid=(pairs,),
            in_specs=seg_specs
            + qkv_specs
            + o_specs
            + [ot_spec, lse_spec]
            + [pl.BlockSpec(memory_space=pl.ANY)] * len(begun),
            out_specs=[result] * parts,
            scratch_shapes=[
                pltpu.VMEM((2, tokens, 128), BF16),
                pltpu.VMEM((2, tokens, 128), BF16),
                pltpu.VMEM((PAIR, tokens), BF16),
                pltpu.VMEM((2, 128, tokens), BF16),
                pltpu.VMEM((2, 128, tokens), BF16),
                pltpu.VMEM((2, tokens, 128), BF16),
                pltpu.VMEM((2, tokens, 128), BF16),
                pltpu.VMEM((PAIR, tokens), F32),
                pltpu.VMEM((tokens, 128), F32),
                pltpu.VMEM((tokens, 128), F32),
            ],
        ),
        out_shape=[jax.ShapeDtypeStruct((width, place[1] * 3 * PAIR), BF16)] * parts,
        input_output_aliases={5 + 2 * parts + n: n for n in range(len(begun))},
        compiler_params=pltpu.CompilerParams(vmem_limit_bytes=48 * 2**20),
        cost_estimate=pl.CostEstimate(
            flops=2**10,
            bytes_accessed=2**10,
            transcendentals=0,
        ),
        name="attend_backward",
    )(tables, kseg, seg[None, :], *qkv_parts, *grad_ctx, turned, lse, *begun)


def row_block(width):
    return FEED_ROWS if width % FEED_ROWS == 0 else width


def gelu_and_slope(u):
    root = 0.7978845608028654
    square = u * u
    t = jnp.tanh(u * (root + (root * 0.044715) * square))
    half = 0.5 * t + 0.5
    slope = half + (0.5 * u) * (1.0 - t * t) * (root + (root * 0.134145) * square)
    return u * half, slope


def feed_kernel(step, x_ref, up_ref, bias_ref, down_ref, *refs):
    x_all, hidden_all, slope_all, out_ref = refs[-4:]
    x = x_ref[...]
    x_all[...] = x
    units = up_ref.shape[1]
    total = None
    for first in range(0, units, step):
        at = slice(first, first + step)
        act, slope = gelu_and_slope(matmul(x, up_ref[:, at]) + bias_ref[:, at])
        act = act.astype(BF16)
        hidden_all[:, at] = act
        slope_all[:, at] = slope.astype(BF16)
        term = matmul(act, down_ref[at, :])
        total = term if total is None else total + term
    out_ref[...] = total.astype(BF16)


def feed_forward(part, parts, x, up, bias, down, begun):
    width, model = x.shape
    units = up.shape[1]
    rows = row_block(width)
    steps = width // rows
    own = lambda k: (k, 0)
    whole = lambda k: (part * steps + k, 0)
    fixed = lambda k: (0, 0)
    once = pl.Buffered(1)
    every = parts * width
    return pl.pallas_call(
        functools.partial(feed_kernel, min(units, FEED)),
        grid=(steps,),
        in_specs=[
            pl.BlockSpec((rows, model), own),
            pl.BlockSpec((model, units), fixed, pipeline_mode=once),
            pl.BlockSpec((1, units), fixed, pipeline_mode=once),
            pl.BlockSpec((units, model), fixed, pipeline_mode=once),
        ]
        + [pl.BlockSpec(memory_space=pl.ANY)] * len(begun),
        out_specs=[
            pl.BlockSpec((rows, model), whole),
            pl.BlockSpec((rows, units), whole),
            pl.BlockSpec((rows, units), whole),
            pl.BlockSpec((rows, model), own),
        ],
        out_shape=[
            jax.ShapeDtypeStruct((every, model), BF16),
            jax.ShapeDtypeStruct((every, units), BF16),
            jax.ShapeDtypeStruct((every, units), BF16),
            jax.ShapeDtypeStruct((width, model), BF16),
        ],
        input_output_aliases={4 + n: n for n in range(len(begun))},
        compiler_params=pltpu.CompilerParams(vmem_limit_bytes=48 * 2**20),
        cost_estimate=pl.CostEstimate(
            flops=6 * width * model * units, bytes_accessed=2**24, transcendentals=0
        ),
        name="feed_forward",
    )(x, up, bias[None, :], down, *begun)


def feed_back_kernel(step, g_ref, slope_ref, down_ref, up_ref, *refs):
    pre_all, sums_ref, out_ref = refs[-3:]
    g = g_ref[...]
    units = up_ref.shape[1]

    @pl.when(pl.program_id(0) == 0)
    def _():
        sums_ref[...] = jnp.zeros_like(sums_ref)

    total = None
    for first in range(0, units, step):
        at = slice(first, first + step)
        pre = contract_cols(g, down_ref[at, :]) * slope_ref[:, at].astype(F32)
        pre = pre.astype(BF16)
        pre_all[:, at] = pre
        sums_ref[:, at] += jnp.sum(pre.astype(F32), axis=0, keepdims=True)
        term = contract_cols(pre, up_ref[:, at])
        total = term if total is None else total + term
    out_ref[...] = total.astype(BF16)


def feed_back(part, parts, g, slope_all, up, down, begun):
    width, model = g.shape
    units = up.shape[1]
    rows = row_block(width)
    steps = width // rows
    own = lambda k: (k, 0)
    whole = lambda k: (part * steps + k, 0)
    fixed = lambda k: (0, 0)
    once = pl.Buffered(1)
    every = parts * width
    return pl.pallas_call(
        functools.partial(feed_back_kernel, min(units, FEED)),
        grid=(steps,),
        in_specs=[
            pl.BlockSpec((rows, model), own),
            pl.BlockSpec((rows, units), whole),
            pl.BlockSpec((units, model), fixed, pipeline_mode=once),
            pl.BlockSpec((model, units), fixed, pipeline_mode=once),
        ]
        + [pl.BlockSpec(memory_space=pl.ANY)] * len(begun),
        out_specs=[
            pl.BlockSpec((rows, units), whole),
            pl.BlockSpec((1, units), fixed),
            pl.BlockSpec((rows, model), own),
        ],
        out_shape=[
            jax.ShapeDtypeStruct((every, units), BF16),
            jax.ShapeDtypeStruct((1, units), F32),
            jax.ShapeDtypeStruct((width, model), BF16),
        ],
        input_output_aliases={4 + n: n for n in range(len(begun))},
        compiler_params=pltpu.CompilerParams(vmem_limit_bytes=48 * 2**20),
        cost_estimate=pl.CostEstimate(
            flops=2**10, bytes_accessed=2**10, transcendentals=0
        ),
        name="feed_back",
    )(g, slope_all, down, up, *begun)


def weight_grad_kernel(parts, *refs):
    a_refs, d_refs = refs[:parts], refs[parts : 2 * parts]
    out_ref, sums_ref = refs[2 * parts :]
    out_ref[...] = total([contract_rows(a[...], d[...]) for a, d in zip(a_refs, d_refs)]).astype(BF16)
    sums_ref[...] = total([jnp.sum(d[...].astype(F32), axis=0, keepdims=True) for d in d_refs])


def weight_grad(a_parts, d_parts, first, count):
    parts = len(a_parts)
    width, model = a_parts[0].shape
    columns = 3 * PAIR
    return pl.pallas_call(
        functools.partial(weight_grad_kernel, parts),
        grid=(count,),
        in_specs=[pl.BlockSpec((width, model), lambda k: (0, 0), pipeline_mode=pl.Buffered(1))] * parts
        + [pl.BlockSpec((width, columns), lambda k: (0, first + k))] * parts,
        out_specs=[
            pl.BlockSpec((model, columns), lambda k: (0, k)),
            pl.BlockSpec((1, columns), lambda k: (0, k)),
        ],
        out_shape=[
            jax.ShapeDtypeStruct((model, count * columns), BF16),
            jax.ShapeDtypeStruct((1, count * columns), F32),
        ],
        compiler_params=pltpu.CompilerParams(vmem_limit_bytes=40 * 2**20),
        cost_estimate=pl.CostEstimate(flops=2**10, bytes_accessed=2**10, transcendentals=0),
        name="weight_grad",
    )(*a_parts, *d_parts)


def input_grad_kernel(w_ref, *refs):
    *d_refs, out_ref = refs
    columns = d_refs[0].shape[1]
    terms = [
        contract_cols(d[...], w_ref[:, k * columns : (k + 1) * columns])
        for k, d in enumerate(d_refs)
    ]
    out_ref[...] = total(terms).astype(BF16)


def input_grad(chunks, weight):
    width, columns = chunks[0].shape
    model = weight.shape[0]
    rows = row_block(width)
    return pl.pallas_call(
        input_grad_kernel,
        grid=(width // rows,),
        in_specs=[
            pl.BlockSpec(weight.shape, lambda k: (0, 0), pipeline_mode=pl.Buffered(1)),
        ]
        + [pl.BlockSpec((rows, columns), lambda k: (k, 0))] * len(chunks),
        out_specs=pl.BlockSpec((rows, model), lambda k: (k, 0)),
        out_shape=jax.ShapeDtypeStruct((width, model), BF16),
        compiler_params=pltpu.CompilerParams(vmem_limit_bytes=40 * 2**20),
        cost_estimate=pl.CostEstimate(flops=2**10, bytes_accessed=2**10, transcendentals=0),
        name="input_grad",
    )(weight, *chunks)


def spread_kernel(tab_ref, mine_ref, theirs_ref, out_ref):
    mine = pl.program_id(1) == tab_ref[0]

    def put(ref):
        for c in range(3):
            out_ref[c] = ref[:, c * PAIR : (c + 1) * PAIR].astype(F32)

    @pl.when(mine)
    def _():
        put(mine_ref)

    @pl.when(jnp.logical_not(mine))
    def _():
        put(theirs_ref)


def spread(mine, theirs, side, out_pairs, first, begun):
    half, columns = mine.shape
    count = columns // (3 * PAIR)
    block = pl.BlockSpec((half, 3 * PAIR), lambda k, s, t: (0, k))
    return pl.pallas_call(
        lambda tab, a, b, *refs: spread_kernel(tab, a, b, refs[-1]),
        grid_spec=pltpu.PrefetchScalarGridSpec(
            num_scalar_prefetch=1,
            grid=(count, 2),
            in_specs=[block, block] + [pl.BlockSpec(memory_space=pl.ANY)] * len(begun),
            out_specs=pl.BlockSpec((3, half, PAIR), lambda k, s, t: (0, s, first + k)),
        ),
        out_shape=jax.ShapeDtypeStruct((3, 2 * half, out_pairs * PAIR), F32),
        input_output_aliases={3 + n: n for n in range(len(begun))},
        compiler_params=pltpu.CompilerParams(vmem_limit_bytes=32 * 2**20),
        cost_estimate=pl.CostEstimate(flops=2**10, bytes_accessed=2**10, transcendentals=0),
        name="spread",
    )(jnp.reshape(side, (1,)).astype(jnp.int32), mine, theirs, *begun)


def after(value, *others):
    return lax.optimization_barrier((value, *others))[0]


class Layout:
    def __init__(self, mesh):
        self.dp, self.n = mesh.shape["dp"], mesh.shape["mp"]
        self.pairs = self.dp // 2
        self.axes = ("dp", "mp")

    def device(self, pair, core, m):
        return (2 * pair + core) * self.n + m

    def at_rank(self, pair, group, rank):
        return self.device(pair, rank % 2, group * (self.n // 2) + rank // 2)

    def each(self):
        for pair in range(self.pairs):
            for group in range(2):
                for rank in range(self.n):
                    yield pair, group, rank

    def stays(self):
        core, m = lax.axis_index("dp") % 2, lax.axis_index("mp")
        return (m // (self.n // 2) == core) & (self.rank() == m)

    def send(self, value, back=False):
        moves = [(self.device(p, g, r), self.at_rank(p, g, r)) for p, g, r in self.each()]
        return lax.ppermute(
            value, self.axes, [(b, a) if back else (a, b) for a, b in moves if a != b]
        )

    def regroup(self, value):
        return jnp.where(self.stays(), value, self.send(value))

    def give_back(self, value):
        return jnp.where(self.stays(), value, self.send(value, True))

    def partner(self, value, bit, only=lambda p, g, r: True):
        def other(p, c):
            return (p, 1 - c) if bit < 0 else (p ^ (1 << bit), c)

        moves = [
            (self.device(*other(p, c), m), self.device(p, c, m))
            for p, c, m in self.each()
            if only(p, c, m)
        ]
        return lax.ppermute(value, self.axes, moves)

    def side(self, bit):
        dp = lax.axis_index("dp")
        return dp % 2 if bit < 0 else (dp // 2 >> bit) % 2

    def joined(self, mine, theirs, bit):
        high = self.side(bit) == 1
        return jnp.concatenate(
            [jnp.where(high, theirs, mine), jnp.where(high, mine, theirs)], 0
        )

    def regroup_first(self, weight, small, tokens):
        rows = weight.shape[0] // 4
        part = 2 * self.side(0) + self.side(1)
        quarter = lax.dynamic_slice_in_dim(weight, part * rows, rows, 0)
        got = self.send(quarter)
        small = self.regroup(after(small, got))
        tokens = self.regroup(after(tokens, got, small))
        for bit in (1, 0):
            got = self.joined(got, self.partner(got, bit, self.moving), bit)
        return jnp.where(self.stays(), weight, got), small, tokens

    def moving(self, pair, core, m):
        return self.at_rank(pair, core, m) != self.device(pair, core, m)

    def to_rank(self, value, ahead):
        moves = [
            (self.at_rank(p, g, r), self.at_rank(p, g, (r + ahead) % self.n))
            for p, g, r in self.each()
        ]
        return lax.ppermute(value, self.axes, moves)

    def rank(self):
        core = lax.axis_index("dp") % 2
        return (lax.axis_index("mp") % (self.n // 2)) * 2 + core

    def gather(self, mine):
        return [mine] + [self.to_rank(mine, self.n - k) for k in range(1, self.n)]

    def scatter_sum(self, shares):
        total = shares[0].astype(jnp.float32)
        for k in range(1, self.n):
            total = total + self.to_rank(shares[k].astype(jnp.bfloat16), k).astype(jnp.float32)
        return total

    def sum_all(self, value):
        devices = self.dp * self.n
        steps = [1 << k for k in range(devices.bit_length() - 1)]
        for step in steps:
            value = value + lax.ppermute(value, self.axes, [(i, i ^ step) for i in range(devices)])
        return value

    def sum_dp(self, value, turn):
        order = [(i + turn) % self.dp for i in range(self.dp)]
        return lax.psum(value, "dp", axis_index_groups=[order])

    def halved(self, value, bit):
        half, high = value.shape[0] // 2, self.side(bit)
        sent = lax.dynamic_slice_in_dim(value, (1 - high) * half, half, 0)
        kept = lax.dynamic_slice_in_dim(value, high * half, half, 0)
        got = self.partner(sent, bit)
        return (kept.astype(jnp.float32) + got.astype(jnp.float32)).astype(jnp.bfloat16)

    def order(self, first):
        bits = list(range(self.pairs.bit_length() - 1))
        return bits[first:] + bits[:first]

    def halved_by(self, value, bits):
        for bit in bits:
            value = self.halved(value, bit)
        return value

    def joined_by(self, value, bits):
        for bit in bits[::-1]:
            value = self.joined(value, self.partner(value, bit), bit)
        return value


def for_kernel(shares, rank):
    width = shares[0].shape[0]
    if width % BQ == 0:
        return shares, rank * (width // BQ)
    return [jnp.roll(jnp.concatenate(shares, 0), rank * width, 0)], 0


def from_kernel(arrays, rank, shares):
    if len(arrays) == shares:
        return arrays
    width = arrays[0].shape[0] // shares
    return jnp.split(jnp.roll(arrays[0], -rank * width, 0), shares, 0)


def by_pairs(weight, pairs):
    return (
        weight.reshape(-1, 3, pairs, PAIR).transpose(0, 2, 1, 3).reshape(-1, 3 * pairs * PAIR)
    )


def total(terms):
    return functools.reduce(jnp.add, terms)


def body(
    layout,
    tokens,
    ln1_gain,
    ln1_bias,
    w_qkv,
    qv_bias,
    w_out,
    out_bias,
    ln2_gain,
    ln2_bias,
    ln3_gain,
    ln3_bias,
    w_up,
    up_bias,
    w_down,
    down_bias,
    ln4_gain,
    ln4_bias,
    row_grid,
    pad_mask,
    cotangent,
):
    f32, bf16 = jnp.float32, jnp.bfloat16
    model_dim = tokens.shape[1]
    group_rows = pad_mask.shape[0]
    width = w_qkv.shape[2]
    units = w_up.shape[1]
    shares = layout.n
    rank = layout.rank()

    small = jnp.concatenate(
        [
            qv_bias.reshape(-1),
            up_bias,
            pad_mask.astype(f32),
            row_grid[0].astype(f32),
        ]
    )
    pairs = width // PAIR
    chunks = 2 if pairs % 2 == 0 else 1
    w_qkv, small, tokens = layout.regroup_first(w_qkv, small, tokens)
    qv_bias = small[: 2 * width].reshape(2, width)
    up_bias = small[2 * width : 2 * width + units]
    keep = small[2 * width + units : 2 * width + units + group_rows].astype(jnp.int32)
    grid_row = small[2 * width + units + group_rows :].astype(jnp.int32)
    w_qkv = by_pairs(w_qkv, pairs)
    half = units // 2
    w_out_far = layout.send(after(w_out, tokens))
    w_up_far = layout.send(after(w_up, tokens))
    w_top_far = layout.send(after(w_down[:half], tokens))
    w_low_far = layout.send(after(w_down[half:], tokens))
    cotangent = layout.regroup(after(cotangent, w_low_far))

    resid_in = tokens.astype(f32)
    norm1_out, normed1, inv1 = norm_parts(resid_in, ln1_gain, ln1_bias)
    a1 = layout.gather(norm1_out.astype(bf16))
    zeros = jnp.zeros((width,), f32)
    qkv_bias = by_pairs(jnp.concatenate([qv_bias[0], zeros, qv_bias[1]]), pairs)
    qkv_scale = by_pairs(
        jnp.concatenate([zeros + HDIM ** (-0.5), zeros + 1.0, zeros + 1.0]), pairs
    )
    qkv = [((matmul(x, w_qkv) + qkv_bias) * qkv_scale).astype(bf16) for x in a1]
    qkv, turn = for_kernel(qkv, rank)
    seg, tables = row_tables(grid_row, group_rows, turn)
    begun = ()
    for pair in range(pairs):
        if pair and pair == pairs // 2:
            tables, w_up_far = lax.optimization_barrier((tables, w_up_far))
        begun = attend_forward(qkv, seg, keep, tables, (pair, 1), begun)
    *context, context_turned, log_total = begun
    *context, w_out_far, w_top_far, w_low_far = lax.optimization_barrier(
        (*context, w_out_far, w_top_far, w_low_far)
    )
    context = from_kernel(context, rank, shares)
    stays = layout.stays()
    w_out = jnp.where(stays, w_out, w_out_far)
    w_up = jnp.where(stays, w_up, w_up_far)
    w_down = jnp.where(stays, w_down, jnp.concatenate([w_top_far, w_low_far], 0))
    branch_z = layout.scatter_sum([matmul(x, w_out) for x in context]) + out_bias
    norm2_out, normed2, inv2 = norm_parts(branch_z, ln2_gain, ln2_bias)
    resid_mid = resid_in + norm2_out
    norm3_out, normed3, inv3 = norm_parts(resid_mid, ln3_gain, ln3_bias)
    a3 = layout.gather(norm3_out.astype(bf16))
    begun, shares_f = (), []
    for part, x in enumerate(a3):
        if part == shares - 1:
            x, cotangent = lax.optimization_barrier((x, cotangent))
        *begun, share = feed_forward(part, shares, x, w_up, up_bias, w_down, begun)
        shares_f.append(share)
    a3_all, hidden, slope = begun
    branch_f = layout.scatter_sum(shares_f) + down_bias
    norm4_out, normed4, inv4 = norm_parts(branch_f, ln4_gain, ln4_bias)
    layer_out = (resid_mid + norm4_out).astype(bf16)

    upstream = cotangent.astype(f32)
    grad_f = norm_back(upstream, normed4, inv4, ln4_gain).astype(bf16)
    grad_f_all = layout.gather(grad_f)
    g_w_down = contract_rows(hidden, jnp.concatenate(grad_f_all, 0)).astype(bf16)
    begun, shares_a3, g_up_bias = (), [], []
    for part, g in enumerate(grad_f_all):
        if part:
            g, g_w_down = lax.optimization_barrier((g, g_w_down))
        *begun, unit_sums, share = feed_back(part, shares, g, slope, w_up, w_down, begun)
        shares_a3.append(share)
        g_up_bias.append(unit_sums[0])
    [grad_pre] = begun
    g_w_down_far = layout.send(g_w_down, True)
    grad_a3 = layout.scatter_sum(shares_a3)
    g_up_bias = total(g_up_bias)
    g_w_up = contract_rows(a3_all, grad_pre).astype(bf16)
    g_w_up_far = layout.send(g_w_up, True)
    grad_mid = upstream + norm_back(grad_a3, normed3, inv3, ln3_gain)
    grad_z = norm_back(grad_mid, normed2, inv2, ln2_gain).astype(bf16)
    grad_z_all = layout.gather(grad_z)
    grad_ctx = [contract_cols(g, w_out).astype(bf16) for g in grad_z_all]
    g_w_out = total([contract_rows(x, g) for x, g in zip(context, grad_z_all)]).astype(bf16)
    g_w_out_far = layout.send(g_w_out, True)
    g_w_down_far, g_w_up, *grad_ctx = lax.optimization_barrier((g_w_down_far, g_w_up, *grad_ctx))
    grad_ctx, _ = for_kernel(grad_ctx, rank)
    g_w_down = jnp.where(stays, g_w_down, g_w_down_far)
    tables, g_w_down = lax.optimization_barrier((tables, g_w_down))
    g_w_down = layout.sum_dp(g_w_down, 1)
    each = pairs // chunks
    calls = [(0, each)] + [(k, 1) for k in range(each, pairs)]
    done, g_w_qkv, sums, grad_qkv = [], [], [], ()
    for call in calls:
        if len(calls) > 1 and call == calls[-1]:
            g_w_up_far, g_w_out_far, *grad_qkv = lax.optimization_barrier(
                (g_w_up_far, g_w_out_far, *grad_qkv)
            )
            g_w_up = jnp.where(stays, g_w_up, g_w_up_far)
            g_w_out = jnp.where(stays, g_w_out, g_w_out_far)
            tables, g_w_down, g_w_up, g_w_out = lax.optimization_barrier(
                (tables, g_w_down, g_w_up, g_w_out)
            )
        grad_qkv = attend_backward(
            qkv,
            context_turned,
            grad_ctx,
            log_total,
            seg,
            keep,
            tables,
            call,
            (call[0] % each, each),
            grad_qkv,
        )
        if sum(call) % each == 0:
            shared = from_kernel(grad_qkv, rank, shares)
            g_part, part_sums = weight_grad(a1, shared, 0, each)
            tables, g_part = lax.optimization_barrier((tables, g_part))
            g_w_qkv.append(layout.halved(layout.give_back(g_part), -1))
            sums.append(part_sums)
            done.append(shared)
            grad_qkv = ()
    if len(calls) == 1:
        g_w_up = jnp.where(stays, g_w_up, g_w_up_far)
        g_w_out = jnp.where(stays, g_w_out, g_w_out_far)
    g_w_up = layout.sum_dp(g_w_up, 0)
    bits = [-1, *layout.order(2 % len(layout.order(0)))]
    g_w_out = layout.halved_by(g_w_out, bits)
    layer_out = layout.give_back(after(layer_out, g_w_qkv[0]))
    sums = jnp.concatenate(sums, 1)
    grad_a1 = [input_grad(d, w_qkv) for d in zip(*done)]
    grad_a1 = layout.scatter_sum(grad_a1)
    grad_input = grad_mid + norm_back(grad_a1, normed1, inv1, ln1_gain)
    grad_input = grad_input.astype(bf16)
    steps = [layout.order(k) for k in range(chunks)]
    g_w_qkv[0] = layout.halved(g_w_qkv[0], steps[0].pop(0))
    g_w_out, *g_w_qkv = lax.optimization_barrier((g_w_out, *g_w_qkv))
    g_w_out = layout.joined_by(g_w_out, bits)
    g_w_qkv = [layout.halved_by(g, s) for g, s in zip(g_w_qkv, steps)]
    g_w_qkv = [layout.joined_by(g, layout.order(k)) for k, g in enumerate(g_w_qkv)]
    begun = ()
    for chunk, mine in enumerate(g_w_qkv):
        theirs = layout.partner(mine, -1)
        begun = (spread(mine, theirs, layout.side(-1), pairs, chunk * each, begun),)
    g_w_qkv = begun[0].transpose(1, 0, 2)
    sums = sums.reshape(pairs, 3, PAIR).transpose(1, 0, 2).reshape(3, width)
    grad_input = layout.give_back(grad_input).astype(f32)

    norm_terms = jnp.stack(
        [
            jnp.sum(grad_a1 * normed1, 0),
            jnp.sum(grad_a1, 0),
            jnp.sum(grad_z.astype(f32), 0),
            jnp.sum(grad_mid * normed2, 0),
            jnp.sum(grad_mid, 0),
            jnp.sum(grad_a3 * normed3, 0),
            jnp.sum(grad_a3, 0),
            jnp.sum(grad_f.astype(f32), 0),
            jnp.sum(upstream * normed4, 0),
            jnp.sum(upstream, 0),
        ],
        0,
    )
    all_units = lax.dynamic_update_slice(jnp.zeros((units * shares,), f32), g_up_bias, (rank * units,))
    all_width = lax.dynamic_update_slice(
        jnp.zeros((2, width * shares), f32), jnp.stack([sums[0], sums[2]], 0), (0, rank * width)
    )
    small = layout.sum_all(
        jnp.concatenate([norm_terms.reshape(-1), all_width.reshape(-1), all_units])
    )
    norm_terms = small[: 10 * model_dim].reshape(10, model_dim)
    all_width = small[10 * model_dim : 12 * model_dim].reshape(2, width * shares)
    all_units = small[12 * model_dim :]
    m = lax.axis_index("mp")
    g_qv_bias = lax.dynamic_slice(all_width, (0, m * width), (2, width))
    g_up_bias = lax.dynamic_slice(all_units, (m * units,), (units,))
    return (
        layer_out,
        grad_input,
        norm_terms[0],
        norm_terms[1],
        g_w_qkv,
        g_qv_bias,
        g_w_out.astype(f32),
        norm_terms[2],
        norm_terms[3],
        norm_terms[4],
        norm_terms[5],
        norm_terms[6],
        g_w_up.astype(f32),
        g_up_bias,
        g_w_down.astype(f32),
        norm_terms[7],
        norm_terms[8],
        norm_terms[9],
    )


def solution(mesh):
    in_specs = (
        P(("dp", "mp"), None),
        P(),
        P(),
        P(None, None, "mp"),
        P(None, "mp"),
        P("mp", None),
        P(),
        P(),
        P(),
        P(),
        P(),
        P(None, "mp"),
        P("mp"),
        P("mp", None),
        P(),
        P(),
        P(),
        P("dp", None),
        P("dp"),
        P(("dp", "mp"), None),
    )
    out_specs = (
        P(("dp", "mp"), None),
        P(("dp", "mp"), None),
        P(),
        P(),
        P(None, None, "mp"),
        P(None, "mp"),
        P("mp", None),
        P(),
        P(),
        P(),
        P(),
        P(),
        P(None, "mp"),
        P("mp"),
        P("mp", None),
        P(),
        P(),
        P(),
    )
    return jax.shard_map(functools.partial(body, Layout(mesh)), mesh=mesh, in_specs=in_specs, out_specs=out_specs, check_vma=False)
```

```python
import functools

import jax
import jax.numpy as jnp
from jax import lax
from jax.experimental import pallas as pl
from jax.experimental.pallas import tpu as pltpu
from jax.sharding import PartitionSpec as P

HDIM = 64
TEXT = 64


epsilon = 1e-05
masked_score = -1e30


def norm_parts(values, ln_gain, ln_bias):
    centred = values - jnp.mean(values, -1, keepdims=True)
    inv_std = lax.rsqrt(jnp.mean(centred * centred, -1, keepdims=True) + epsilon)
    normed = centred * inv_std
    return (normed * ln_gain + ln_bias, normed, inv_std)


def norm_back(upstream, normed, inv_std, ln_gain):
    scaled = upstream * ln_gain
    return inv_std * (
        scaled
        - jnp.mean(scaled, -1, keepdims=True)
        - normed * jnp.mean(scaled * normed, -1, keepdims=True)
    )


def contract_rows(left, right):
    return lax.dot_general(
        left, right, (((0,), (0,)), ((), ())), preferred_element_type=jnp.float32
    )


def contract_cols(left, right):
    return lax.dot_general(
        left, right, (((1,), (1,)), ((), ())), preferred_element_type=jnp.float32
    )


BQ = 256
BK = 256
MOST = 4
FEED = 1024
FEED_ROWS = 640
PAIR = 2 * HDIM
F32 = jnp.float32
BF16 = jnp.bfloat16


def matmul(left, right):
    return jnp.dot(left, right, preferred_element_type=F32)


def row_tables(grid_row, tokens, turn):
    side = jnp.max(grid_row)
    length = TEXT + side * side
    rows = tokens // length
    used = rows * length
    position = jnp.arange(tokens, dtype=jnp.int32)
    seg = jnp.minimum(position // length, rows)
    blocks = tokens // BQ
    first = jnp.arange(blocks, dtype=jnp.int32) * BQ
    start = jnp.where(first < used, (first // length) * length, first)
    low = start // BK
    diag = first // BK
    turns = jnp.full((blocks,), turn, jnp.int32)
    return seg, jnp.stack([low, diag, turns]).astype(jnp.int32)


def allowed(kseg_ref, qseg_ref, i, j, blocks):
    qs = qseg_ref[:, pl.ds(pl.multiple_of(i * BQ, BQ), BQ)]
    ks = kseg_ref[pl.ds(pl.multiple_of(j * BK, BK), blocks * BK), :]
    ik = j * BK + lax.broadcasted_iota(jnp.int32, (blocks * BK, BQ), 0)
    iq = i * BQ + lax.broadcasted_iota(jnp.int32, (blocks * BK, BQ), 1)
    return ((ks == qs) & (ik <= iq)) | (ik == iq)


def sweep(tab_ref, i, step, carry):
    return several(tab_ref[0, i], tab_ref[1, i] + 1, step, carry)


def several(first, stop, step, carry, most=MOST):
    while most > 1:
        turns = (stop - first) // most

        def turn(n, carry, first=first, most=most):
            return step(most, first + most * n, carry)

        carry = lax.fori_loop(0, turns, turn, carry)
        first, most = first + most * turns, most // 2
    return lax.fori_loop(first, stop, functools.partial(step, 1), carry)


def each_block(tab_ref, parts, width, work):
    blocks = width // BQ
    count = blocks * parts
    for part in range(parts):

        def one(c, _, part=part):
            whole = lax.rem(tab_ref[2, 0] + part * blocks + c, count)
            work(
                part,
                pl.ds(pl.multiple_of(c * BQ, BQ), BQ),
                pl.ds(pl.multiple_of(whole * BQ, BQ), BQ),
            )
            return 0

        lax.fori_loop(0, blocks, one, 0)


def forward_kernel(parts, tab_ref, kseg_ref, qseg_ref, *refs):
    qkv_refs = refs[:parts]
    *o_refs, ot_ref, lse_ref, kx, vx, qx, scores = refs[-6 - parts :]
    tokens = qx.shape[1]
    width = tokens // parts
    lane = lax.broadcasted_iota(jnp.int32, (BK, 128), 1)
    zero = jnp.zeros((BK, 128), BF16)

    def prepare(part, here, there):
        k = qkv_refs[part][here, PAIR : 2 * PAIR]
        kx[0, there, :] = jnp.where(lane < HDIM, k, zero)
        kx[1, there, :] = jnp.where(lane < HDIM, zero, k)
        qx[:, there] = qkv_refs[part][here, :PAIR].astype(F32).T.astype(BF16)
        v = qkv_refs[part][here, 2 * PAIR :].astype(F32).T.astype(BF16)
        for h in range(2):
            vx[h, :HDIM, there] = v[h * HDIM : (h + 1) * HDIM]
            vx[h, HDIM:, there] = jnp.ones((16, BQ), BF16)

    each_block(tab_ref, parts, width, prepare)

    def block(i, _):
        cols = pl.ds(pl.multiple_of(i * BQ, BQ), BQ)
        qb = qx[:, cols]

        def score(blocks, j, tops):
            at = pl.ds(pl.multiple_of(j * BK, BK), blocks * BK)
            ok = allowed(kseg_ref, qseg_ref, i, j, blocks)
            out = []
            for h in range(2):
                s = matmul(kx[h, at, :], qb)
                s = jnp.where(ok, s, masked_score)
                scores[h, at, :] = s
                out.append(jnp.maximum(tops[h], jnp.max(s.reshape(blocks * BK // 8, 8, BQ), axis=0)))
            return tuple(out)

        tops = sweep(tab_ref, i, score, (jnp.full((8, BQ), masked_score, F32),) * 2)
        tops = [jnp.max(top, axis=0, keepdims=True) for top in tops]

        def weigh(blocks, j, accs):
            at = pl.ds(pl.multiple_of(j * BK, BK), blocks * BK)
            out = []
            for h in range(2):
                p = jnp.exp(scores[h, at, :] - tops[h]).astype(BF16)
                out.append(accs[h] + matmul(vx[h, :, at], p))
            return tuple(out)

        accs = sweep(tab_ref, i, weigh, (jnp.zeros((HDIM + 16, BQ), F32),) * 2)
        for h in range(2):
            total = accs[h][HDIM : HDIM + 1, :]
            ot_ref[h * HDIM : (h + 1) * HDIM, cols] = (accs[h][:HDIM, :] / total).astype(BF16)
            lse_ref[0, h : h + 1, cols] = tops[h] + jnp.log(total)
        return 0

    lax.fori_loop(0, tokens // BQ, block, 0)

    def finish(part, here, there):
        o_refs[part][here, :] = ot_ref[:, there].astype(F32).T.astype(BF16)

    each_block(tab_ref, parts, width, finish)


def three_parts(x):
    high = x.astype(BF16)
    rest = x - high.astype(F32)
    middle = rest.astype(BF16)
    return high, middle, (rest - middle.astype(F32)).astype(BF16)


def backward_kernel(parts, tab_ref, kseg_ref, qseg_ref, *refs):
    qkv_refs, do_refs = refs[:parts], refs[parts : 2 * parts]
    ot_ref, lse_ref = refs[2 * parts : 2 * parts + 2]
    *out_refs, kx, vx, kt, qx, dox, qt, dot, dq, dk, dv = refs[-10 - parts :]
    tokens = kt.shape[1]
    width = tokens // parts
    lane = lax.broadcasted_iota(jnp.int32, (BK, 128), 1)
    sub = lax.broadcasted_iota(jnp.int32, (HDIM, BK), 0)
    one0 = jnp.where((lane >= HDIM) & (lane < HDIM + 3), 1.0, 0.0).astype(BF16)
    one1 = jnp.where(lane < 3, 1.0, 0.0).astype(BF16)
    zero = jnp.zeros((BK, 128), BF16)

    def extra(x):
        high, middle, low = (e.astype(F32) for e in three_parts(x))
        rows = jnp.where(
            sub == 0, high, jnp.where(sub == 1, middle, jnp.where(sub == 2, low, 0.0))
        )
        return rows.astype(BF16)

    def prepare(part, here, there):
        k = qkv_refs[part][here, PAIR : 2 * PAIR]
        kt[:, there] = k.astype(F32).T.astype(BF16)
        kx[0, there, :] = jnp.where(lane < HDIM, k, one0)
        kx[1, there, :] = jnp.where(lane < HDIM, one1, k)
        v = qkv_refs[part][here, 2 * PAIR :]
        vx[0, there, :] = jnp.where(lane < HDIM, v, one0)
        vx[1, there, :] = jnp.where(lane < HDIM, one1, v)
        q = qkv_refs[part][here, :PAIR]
        qt[0, there, :] = jnp.where(lane < HDIM, q, zero)
        qt[1, there, :] = jnp.where(lane < HDIM, zero, q)
        do = do_refs[part][here, :]
        dot[0, there, :] = jnp.where(lane < HDIM, do, zero)
        dot[1, there, :] = jnp.where(lane < HDIM, zero, do)
        turned = do.astype(F32).T
        prod = turned * ot_ref[:, there].astype(F32)
        inner0 = jnp.sum(prod[:HDIM], axis=0, keepdims=True)
        inner1 = jnp.sum(prod[HDIM:], axis=0, keepdims=True)
        turned = turned.astype(BF16)
        dox[0, :HDIM, there] = turned[:HDIM]
        dox[0, HDIM:, there] = extra(-inner0)
        dox[1, HDIM:, there] = turned[HDIM:]
        dox[1, :HDIM, there] = extra(-inner1)
        turned = q.astype(F32).T.astype(BF16)
        qx[0, :HDIM, there] = turned[:HDIM]
        qx[0, HDIM:, there] = extra(-lse_ref[0, 0:1, there])
        qx[1, HDIM:, there] = turned[HDIM:]
        qx[1, :HDIM, there] = extra(-lse_ref[0, 1:2, there])
        dk[there, :] = jnp.zeros((BK, 128), F32)
        dv[there, :] = jnp.zeros((BK, 128), F32)

    each_block(tab_ref, parts, width, prepare)

    def block(i, _):
        cols = pl.ds(pl.multiple_of(i * BQ, BQ), BQ)

        def step(blocks, j, carry):
            at = pl.ds(pl.multiple_of(j * BK, BK), blocks * BK)
            ok = allowed(kseg_ref, qseg_ref, i, j, blocks)
            new = []
            dvs = dv[at, :]
            dks = dk[at, :]
            for h in range(2):
                s = matmul(kx[h, at, :], qx[h, :, cols])
                s = jnp.where(ok, s, masked_score)
                p = jnp.exp(s)
                dp = matmul(vx[h, at, :], dox[h, :, cols])
                ds = (p * dp).astype(BF16)
                dvs = dvs + matmul(p.astype(BF16), dot[h, cols, :])
                dks = dks + matmul(ds, qt[h, cols, :])
                new.append(carry[h] + matmul(kt[h * HDIM : (h + 1) * HDIM, at], ds))
            dv[at, :] = dvs
            dk[at, :] = dks
            return tuple(new)

        init = tuple(jnp.zeros((HDIM, BQ), F32) for _ in range(2))
        res = sweep(tab_ref, i, step, init)
        for h in range(2):
            dq[h * HDIM : (h + 1) * HDIM, cols] = res[h] * (HDIM**-0.5)
        return 0

    lax.fori_loop(0, tokens // BQ, block, 0)

    def finish(part, here, there):
        out_refs[part][here, :PAIR] = dq[:, there].T.astype(BF16)
        out_refs[part][here, PAIR : 2 * PAIR] = dk[there, :].astype(BF16)
        out_refs[part][here, 2 * PAIR :] = dv[there, :].astype(BF16)

    each_block(tab_ref, parts, width, finish)


def lanes_of(first, step):
    return lambda g, t: (0, first + step * g)


def attend_specs(qkv_parts, chunk):
    parts = len(qkv_parts)
    width = qkv_parts[0].shape[0]
    tokens = parts * width
    every = qkv_parts[0].shape[1] // (3 * PAIR)
    first, pairs = chunk
    seg_specs = [
        pl.BlockSpec((tokens, 1), lambda g, t: (0, 0)),
        pl.BlockSpec((1, tokens), lambda g, t: (0, 0)),
    ]
    qkv_specs = [pl.BlockSpec((width, 3 * PAIR), lanes_of(first, 1))] * parts
    o_specs = [pl.BlockSpec((width, PAIR), lanes_of(first, 1))] * parts
    ot_spec = pl.BlockSpec((PAIR, tokens), lambda g, t: (first + g, 0))
    lse_spec = pl.BlockSpec((1, 2, tokens), lambda g, t: (first + g, 0, 0))
    return parts, width, tokens, every, pairs, seg_specs, qkv_specs, o_specs, ot_spec, lse_spec


def attend_forward(qkv_parts, seg, keep, tables, chunk, begun=()):
    parts, width, tokens, every, pairs, seg_specs, qkv_specs, o_specs, ot_spec, lse_spec = (
        attend_specs(qkv_parts, chunk)
    )
    kseg = jnp.where(keep == 1, seg, -1)[:, None]
    return pl.pallas_call(
        functools.partial(forward_kernel, parts),
        grid_spec=pltpu.PrefetchScalarGridSpec(
            num_scalar_prefetch=1,
            grid=(pairs,),
            in_specs=seg_specs + qkv_specs + [pl.BlockSpec(memory_space=pl.ANY)] * len(begun),
            out_specs=o_specs + [ot_spec, lse_spec],
            scratch_shapes=[
                pltpu.VMEM((2, tokens, 128), BF16),
                pltpu.VMEM((2, HDIM + 16, tokens), BF16),
                pltpu.VMEM((PAIR, tokens), BF16),
                pltpu.VMEM((2, tokens, BQ), F32),
            ],
        ),
        out_shape=[jax.ShapeDtypeStruct((width, every * PAIR), BF16)] * parts
        + [
            jax.ShapeDtypeStruct((every * PAIR, tokens), BF16),
            jax.ShapeDtypeStruct((every, 2, tokens), F32),
        ],
        compiler_params=pltpu.CompilerParams(vmem_limit_bytes=40 * 2**20),
        cost_estimate=pl.CostEstimate(
            flops=2**10, bytes_accessed=2**10, transcendentals=0
        ),
        input_output_aliases={3 + parts + n: n for n in range(len(begun))},
        name="attend_forward",
    )(tables, kseg, seg[None, :], *qkv_parts, *begun)


def attend_backward(qkv_parts, turned, grad_ctx, lse, seg, keep, tables, chunk, place, begun=()):
    parts, width, tokens, every, pairs, seg_specs, qkv_specs, o_specs, ot_spec, lse_spec = (
        attend_specs(qkv_parts, chunk)
    )
    kseg = jnp.where(keep == 1, seg, -1)[:, None]
    result = pl.BlockSpec((width, 3 * PAIR), lanes_of(place[0], 1))
    return pl.pallas_call(
        functools.partial(backward_kernel, parts),
        grid_spec=pltpu.PrefetchScalarGridSpec(
            num_scalar_prefetch=1,
            grid=(pairs,),
            in_specs=seg_specs
            + qkv_specs
            + o_specs
            + [ot_spec, lse_spec]
            + [pl.BlockSpec(memory_space=pl.ANY)] * len(begun),
            out_specs=[result] * parts,
            scratch_shapes=[
                pltpu.VMEM((2, tokens, 128), BF16),
                pltpu.VMEM((2, tokens, 128), BF16),
                pltpu.VMEM((PAIR, tokens), BF16),
                pltpu.VMEM((2, 128, tokens), BF16),
                pltpu.VMEM((2, 128, tokens), BF16),
                pltpu.VMEM((2, tokens, 128), BF16),
                pltpu.VMEM((2, tokens, 128), BF16),
                pltpu.VMEM((PAIR, tokens), F32),
                pltpu.VMEM((tokens, 128), F32),
                pltpu.VMEM((tokens, 128), F32),
            ],
        ),
        out_shape=[jax.ShapeDtypeStruct((width, place[1] * 3 * PAIR), BF16)] * parts,
        input_output_aliases={5 + 2 * parts + n: n for n in range(len(begun))},
        compiler_params=pltpu.CompilerParams(vmem_limit_bytes=48 * 2**20),
        cost_estimate=pl.CostEstimate(
            flops=2**10,
            bytes_accessed=2**10,
            transcendentals=0,
        ),
        name="attend_backward",
    )(tables, kseg, seg[None, :], *qkv_parts, *grad_ctx, turned, lse, *begun)


def row_block(width):
    return FEED_ROWS if width % FEED_ROWS == 0 else width


def gelu_and_slope(u):
    root = 0.7978845608028654
    square = u * u
    t = jnp.tanh(u * (root + (root * 0.044715) * square))
    half = 0.5 * t + 0.5
    slope = half + (0.5 * u) * (1.0 - t * t) * (root + (root * 0.134145) * square)
    return u * half, slope


def feed_kernel(step, x_ref, up_ref, bias_ref, down_ref, *refs):
    x_all, hidden_all, slope_all, out_ref = refs[-4:]
    x = x_ref[...]
    x_all[...] = x
    units = up_ref.shape[1]
    total = None
    for first in range(0, units, step):
        at = slice(first, first + step)
        act, slope = gelu_and_slope(matmul(x, up_ref[:, at]) + bias_ref[:, at])
        act = act.astype(BF16)
        hidden_all[:, at] = act
        slope_all[:, at] = slope.astype(BF16)
        term = matmul(act, down_ref[at, :])
        total = term if total is None else total + term
    out_ref[...] = total.astype(BF16)


def feed_forward(part, parts, x, up, bias, down, begun):
    width, model = x.shape
    units = up.shape[1]
    rows = row_block(width)
    steps = width // rows
    own = lambda k: (k, 0)
    whole = lambda k: (part * steps + k, 0)
    fixed = lambda k: (0, 0)
    once = pl.Buffered(1)
    every = parts * width
    return pl.pallas_call(
        functools.partial(feed_kernel, min(units, FEED)),
        grid=(steps,),
        in_specs=[
            pl.BlockSpec((rows, model), own),
            pl.BlockSpec((model, units), fixed, pipeline_mode=once),
            pl.BlockSpec((1, units), fixed, pipeline_mode=once),
            pl.BlockSpec((units, model), fixed, pipeline_mode=once),
        ]
        + [pl.BlockSpec(memory_space=pl.ANY)] * len(begun),
        out_specs=[
            pl.BlockSpec((rows, model), whole),
            pl.BlockSpec((rows, units), whole),
            pl.BlockSpec((rows, units), whole),
            pl.BlockSpec((rows, model), own),
        ],
        out_shape=[
            jax.ShapeDtypeStruct((every, model), BF16),
            jax.ShapeDtypeStruct((every, units), BF16),
            jax.ShapeDtypeStruct((every, units), BF16),
            jax.ShapeDtypeStruct((width, model), BF16),
        ],
        input_output_aliases={4 + n: n for n in range(len(begun))},
        compiler_params=pltpu.CompilerParams(vmem_limit_bytes=48 * 2**20),
        cost_estimate=pl.CostEstimate(
            flops=6 * width * model * units, bytes_accessed=2**24, transcendentals=0
        ),
        name="feed_forward",
    )(x, up, bias[None, :], down, *begun)


def feed_back_kernel(step, g_ref, slope_ref, down_ref, up_ref, *refs):
    pre_all, sums_ref, out_ref = refs[-3:]
    g = g_ref[...]
    units = up_ref.shape[1]

    @pl.when(pl.program_id(0) == 0)
    def _():
        sums_ref[...] = jnp.zeros_like(sums_ref)

    total = None
    for first in range(0, units, step):
        at = slice(first, first + step)
        pre = contract_cols(g, down_ref[at, :]) * slope_ref[:, at].astype(F32)
        pre = pre.astype(BF16)
        pre_all[:, at] = pre
        sums_ref[:, at] += jnp.sum(pre.astype(F32), axis=0, keepdims=True)
        term = contract_cols(pre, up_ref[:, at])
        total = term if total is None else total + term
    out_ref[...] = total.astype(BF16)


def feed_back(part, parts, g, slope_all, up, down, begun):
    width, model = g.shape
    units = up.shape[1]
    rows = row_block(width)
    steps = width // rows
    own = lambda k: (k, 0)
    whole = lambda k: (part * steps + k, 0)
    fixed = lambda k: (0, 0)
    once = pl.Buffered(1)
    every = parts * width
    return pl.pallas_call(
        functools.partial(feed_back_kernel, min(units, FEED)),
        grid=(steps,),
        in_specs=[
            pl.BlockSpec((rows, model), own),
            pl.BlockSpec((rows, units), whole),
            pl.BlockSpec((units, model), fixed, pipeline_mode=once),
            pl.BlockSpec((model, units), fixed, pipeline_mode=once),
        ]
        + [pl.BlockSpec(memory_space=pl.ANY)] * len(begun),
        out_specs=[
            pl.BlockSpec((rows, units), whole),
            pl.BlockSpec((1, units), fixed),
            pl.BlockSpec((rows, model), own),
        ],
        out_shape=[
            jax.ShapeDtypeStruct((every, units), BF16),
            jax.ShapeDtypeStruct((1, units), F32),
            jax.ShapeDtypeStruct((width, model), BF16),
        ],
        input_output_aliases={4 + n: n for n in range(len(begun))},
        compiler_params=pltpu.CompilerParams(vmem_limit_bytes=48 * 2**20),
        cost_estimate=pl.CostEstimate(
            flops=2**10, bytes_accessed=2**10, transcendentals=0
        ),
        name="feed_back",
    )(g, slope_all, down, up, *begun)


def weight_grad_kernel(parts, *refs):
    a_refs, d_refs = refs[:parts], refs[parts : 2 * parts]
    out_ref, sums_ref = refs[2 * parts :]
    out_ref[...] = total([contract_rows(a[...], d[...]) for a, d in zip(a_refs, d_refs)]).astype(BF16)
    sums_ref[...] = total([jnp.sum(d[...].astype(F32), axis=0, keepdims=True) for d in d_refs])


def weight_grad(a_parts, d_parts, first, count):
    parts = len(a_parts)
    width, model = a_parts[0].shape
    columns = 3 * PAIR
    return pl.pallas_call(
        functools.partial(weight_grad_kernel, parts),
        grid=(count,),
        in_specs=[pl.BlockSpec((width, model), lambda k: (0, 0), pipeline_mode=pl.Buffered(1))] * parts
        + [pl.BlockSpec((width, columns), lambda k: (0, first + k))] * parts,
        out_specs=[
            pl.BlockSpec((model, columns), lambda k: (0, k)),
            pl.BlockSpec((1, columns), lambda k: (0, k)),
        ],
        out_shape=[
            jax.ShapeDtypeStruct((model, count * columns), BF16),
            jax.ShapeDtypeStruct((1, count * columns), F32),
        ],
        compiler_params=pltpu.CompilerParams(vmem_limit_bytes=40 * 2**20),
        cost_estimate=pl.CostEstimate(flops=2**10, bytes_accessed=2**10, transcendentals=0),
        name="weight_grad",
    )(*a_parts, *d_parts)


def input_grad_kernel(w_ref, *refs):
    *d_refs, out_ref = refs
    columns = d_refs[0].shape[1]
    terms = [
        contract_cols(d[...], w_ref[:, k * columns : (k + 1) * columns])
        for k, d in enumerate(d_refs)
    ]
    out_ref[...] = total(terms).astype(BF16)


def input_grad(chunks, weight):
    width, columns = chunks[0].shape
    model = weight.shape[0]
    rows = row_block(width)
    return pl.pallas_call(
        input_grad_kernel,
        grid=(width // rows,),
        in_specs=[
            pl.BlockSpec(weight.shape, lambda k: (0, 0), pipeline_mode=pl.Buffered(1)),
        ]
        + [pl.BlockSpec((rows, columns), lambda k: (k, 0))] * len(chunks),
        out_specs=pl.BlockSpec((rows, model), lambda k: (k, 0)),
        out_shape=jax.ShapeDtypeStruct((width, model), BF16),
        compiler_params=pltpu.CompilerParams(vmem_limit_bytes=40 * 2**20),
        cost_estimate=pl.CostEstimate(flops=2**10, bytes_accessed=2**10, transcendentals=0),
        name="input_grad",
    )(weight, *chunks)


def spread_kernel(tab_ref, mine_ref, theirs_ref, out_ref):
    mine = pl.program_id(1) == tab_ref[0]

    def put(ref):
        for c in range(3):
            out_ref[c] = ref[:, c * PAIR : (c + 1) * PAIR].astype(F32)

    @pl.when(mine)
    def _():
        put(mine_ref)

    @pl.when(jnp.logical_not(mine))
    def _():
        put(theirs_ref)


def spread(mine, theirs, side, out_pairs, first, begun):
    half, columns = mine.shape
    count = columns // (3 * PAIR)
    block = pl.BlockSpec((half, 3 * PAIR), lambda k, s, t: (0, k))
    return pl.pallas_call(
        lambda tab, a, b, *refs: spread_kernel(tab, a, b, refs[-1]),
        grid_spec=pltpu.PrefetchScalarGridSpec(
            num_scalar_prefetch=1,
            grid=(count, 2),
            in_specs=[block, block] + [pl.BlockSpec(memory_space=pl.ANY)] * len(begun),
            out_specs=pl.BlockSpec((3, half, PAIR), lambda k, s, t: (0, s, first + k)),
        ),
        out_shape=jax.ShapeDtypeStruct((3, 2 * half, out_pairs * PAIR), F32),
        input_output_aliases={3 + n: n for n in range(len(begun))},
        compiler_params=pltpu.CompilerParams(vmem_limit_bytes=32 * 2**20),
        cost_estimate=pl.CostEstimate(flops=2**10, bytes_accessed=2**10, transcendentals=0),
        name="spread",
    )(jnp.reshape(side, (1,)).astype(jnp.int32), mine, theirs, *begun)


def after(value, *others):
    return lax.optimization_barrier((value, *others))[0]


class Layout:
    def __init__(self, mesh):
        self.dp, self.n = mesh.shape["dp"], mesh.shape["mp"]
        self.pairs = self.dp // 2
        self.axes = ("dp", "mp")

    def device(self, pair, core, m):
        return (2 * pair + core) * self.n + m

    def at_rank(self, pair, group, rank):
        return self.device(pair, rank % 2, group * (self.n // 2) + rank // 2)

    def each(self):
        for pair in range(self.pairs):
            for group in range(2):
                for rank in range(self.n):
                    yield pair, group, rank

    def stays(self):
        core, m = lax.axis_index("dp") % 2, lax.axis_index("mp")
        return (m // (self.n // 2) == core) & (self.rank() == m)

    def send(self, value, back=False):
        moves = [(self.device(p, g, r), self.at_rank(p, g, r)) for p, g, r in self.each()]
        return lax.ppermute(
            value, self.axes, [(b, a) if back else (a, b) for a, b in moves if a != b]
        )

    def regroup(self, value):
        return jnp.where(self.stays(), value, self.send(value))

    def give_back(self, value):
        return jnp.where(self.stays(), value, self.send(value, True))

    def partner(self, value, bit, only=lambda p, g, r: True):
        def other(p, c):
            return (p, 1 - c) if bit < 0 else (p ^ (1 << bit), c)

        moves = [
            (self.device(*other(p, c), m), self.device(p, c, m))
            for p, c, m in self.each()
            if only(p, c, m)
        ]
        return lax.ppermute(value, self.axes, moves)

    def side(self, bit):
        dp = lax.axis_index("dp")
        return dp % 2 if bit < 0 else (dp // 2 >> bit) % 2

    def joined(self, mine, theirs, bit):
        high = self.side(bit) == 1
        return jnp.concatenate(
            [jnp.where(high, theirs, mine), jnp.where(high, mine, theirs)], 0
        )

    def regroup_first(self, weight, small, tokens):
        rows = weight.shape[0] // 4
        part = 2 * self.side(0) + self.side(1)
        quarter = lax.dynamic_slice_in_dim(weight, part * rows, rows, 0)
        got = self.send(quarter)
        small = self.regroup(after(small, got))
        tokens = self.regroup(after(tokens, got, small))
        for bit in (1, 0):
            got = self.joined(got, self.partner(got, bit, self.moving), bit)
        return jnp.where(self.stays(), weight, got), small, tokens

    def moving(self, pair, core, m):
        return self.at_rank(pair, core, m) != self.device(pair, core, m)

    def to_rank(self, value, ahead):
        moves = [
            (self.at_rank(p, g, r), self.at_rank(p, g, (r + ahead) % self.n))
            for p, g, r in self.each()
        ]
        return lax.ppermute(value, self.axes, moves)

    def rank(self):
        core = lax.axis_index("dp") % 2
        return (lax.axis_index("mp") % (self.n // 2)) * 2 + core

    def gather(self, mine):
        return [mine] + [self.to_rank(mine, self.n - k) for k in range(1, self.n)]

    def scatter_sum(self, shares):
        total = shares[0].astype(jnp.float32)
        for k in range(1, self.n):
            total = total + self.to_rank(shares[k].astype(jnp.bfloat16), k).astype(jnp.float32)
        return total

    def sum_all(self, value):
        devices = self.dp * self.n
        steps = [1 << k for k in range(devices.bit_length() - 1)]
        for step in steps:
            value = value + lax.ppermute(value, self.axes, [(i, i ^ step) for i in range(devices)])
        return value

    def sum_dp(self, value, turn):
        order = [(i + turn) % self.dp for i in range(self.dp)]
        return lax.psum(value, "dp", axis_index_groups=[order])

    def halved(self, value, bit):
        half, high = value.shape[0] // 2, self.side(bit)
        sent = lax.dynamic_slice_in_dim(value, (1 - high) * half, half, 0)
        kept = lax.dynamic_slice_in_dim(value, high * half, half, 0)
        got = self.partner(sent, bit)
        return (kept.astype(jnp.float32) + got.astype(jnp.float32)).astype(jnp.bfloat16)

    def order(self, first):
        bits = list(range(self.pairs.bit_length() - 1))
        return bits[first:] + bits[:first]

    def halved_by(self, value, bits):
        for bit in bits:
            value = self.halved(value, bit)
        return value

    def joined_by(self, value, bits):
        for bit in bits[::-1]:
            value = self.joined(value, self.partner(value, bit), bit)
        return value


def for_kernel(shares, rank):
    width = shares[0].shape[0]
    if width % BQ == 0:
        return shares, rank * (width // BQ)
    return [jnp.roll(jnp.concatenate(shares, 0), rank * width, 0)], 0


def from_kernel(arrays, rank, shares):
    if len(arrays) == shares:
        return arrays
    width = arrays[0].shape[0] // shares
    return jnp.split(jnp.roll(arrays[0], -rank * width, 0), shares, 0)


def by_pairs(weight, pairs):
    return (
        weight.reshape(-1, 3, pairs, PAIR).transpose(0, 2, 1, 3).reshape(-1, 3 * pairs * PAIR)
    )


def total(terms):
    return functools.reduce(jnp.add, terms)


def body(
    layout,
    tokens,
    ln1_gain,
    ln1_bias,
    w_qkv,
    qv_bias,
    w_out,
    out_bias,
    ln2_gain,
    ln2_bias,
    ln3_gain,
    ln3_bias,
    w_up,
    up_bias,
    w_down,
    down_bias,
    ln4_gain,
    ln4_bias,
    row_grid,
    pad_mask,
    cotangent,
):
    f32, bf16 = jnp.float32, jnp.bfloat16
    model_dim = tokens.shape[1]
    group_rows = pad_mask.shape[0]
    width = w_qkv.shape[2]
    units = w_up.shape[1]
    shares = layout.n
    rank = layout.rank()

    small = jnp.concatenate(
        [
            qv_bias.reshape(-1),
            up_bias,
            pad_mask.astype(f32),
            row_grid[0].astype(f32),
        ]
    )
    pairs = width // PAIR
    chunks = 2 if pairs % 2 == 0 else 1
    w_qkv, small, tokens = layout.regroup_first(w_qkv, small, tokens)
    qv_bias = small[: 2 * width].reshape(2, width)
    up_bias = small[2 * width : 2 * width + units]
    keep = small[2 * width + units : 2 * width + units + group_rows].astype(jnp.int32)
    grid_row = small[2 * width + units + group_rows :].astype(jnp.int32)
    w_qkv = by_pairs(w_qkv, pairs)
    half = units // 2
    w_out_far = layout.send(after(w_out, tokens))
    w_up_far = layout.send(after(w_up, tokens))
    w_top_far = layout.send(after(w_down[:half], tokens))
    w_low_far = layout.send(after(w_down[half:], tokens))
    cotangent = layout.regroup(after(cotangent, w_low_far))

    resid_in = tokens.astype(f32)
    norm1_out, normed1, inv1 = norm_parts(resid_in, ln1_gain, ln1_bias)
    a1 = layout.gather(norm1_out.astype(bf16))
    zeros = jnp.zeros((width,), f32)
    qkv_bias = by_pairs(jnp.concatenate([qv_bias[0], zeros, qv_bias[1]]), pairs)
    qkv_scale = by_pairs(
        jnp.concatenate([zeros + HDIM ** (-0.5), zeros + 1.0, zeros + 1.0]), pairs
    )
    qkv = [((matmul(x, w_qkv) + qkv_bias) * qkv_scale).astype(bf16) for x in a1]
    qkv, turn = for_kernel(qkv, rank)
    seg, tables = row_tables(grid_row, group_rows, turn)
    begun = ()
    for pair in range(pairs):
        if pair and pair == pairs // 2:
            tables, w_up_far = lax.optimization_barrier((tables, w_up_far))
        begun = attend_forward(qkv, seg, keep, tables, (pair, 1), begun)
    *context, context_turned, log_total = begun
    *context, w_out_far, w_top_far, w_low_far = lax.optimization_barrier(
        (*context, w_out_far, w_top_far, w_low_far)
    )
    context = from_kernel(context, rank, shares)
    stays = layout.stays()
    w_out = jnp.where(stays, w_out, w_out_far)
    w_up = jnp.where(stays, w_up, w_up_far)
    w_down = jnp.where(stays, w_down, jnp.concatenate([w_top_far, w_low_far], 0))
    branch_z = layout.scatter_sum([matmul(x, w_out) for x in context]) + out_bias
    norm2_out, normed2, inv2 = norm_parts(branch_z, ln2_gain, ln2_bias)
    resid_mid = resid_in + norm2_out
    norm3_out, normed3, inv3 = norm_parts(resid_mid, ln3_gain, ln3_bias)
    a3 = layout.gather(norm3_out.astype(bf16))
    begun, shares_f = (), []
    for part, x in enumerate(a3):
        if part == shares - 1:
            x, cotangent = lax.optimization_barrier((x, cotangent))
        *begun, share = feed_forward(part, shares, x, w_up, up_bias, w_down, begun)
        shares_f.append(share)
    a3_all, hidden, slope = begun
    branch_f = layout.scatter_sum(shares_f) + down_bias
    norm4_out, normed4, inv4 = norm_parts(branch_f, ln4_gain, ln4_bias)
    layer_out = (resid_mid + norm4_out).astype(bf16)

    upstream = cotangent.astype(f32)
    grad_f = norm_back(upstream, normed4, inv4, ln4_gain).astype(bf16)
    grad_f_all = layout.gather(grad_f)
    g_w_down = contract_rows(hidden, jnp.concatenate(grad_f_all, 0)).astype(bf16)
    begun, shares_a3, g_up_bias = (), [], []
    for part, g in enumerate(grad_f_all):
        if part:
            g, g_w_down = lax.optimization_barrier((g, g_w_down))
        *begun, unit_sums, share = feed_back(part, shares, g, slope, w_up, w_down, begun)
        shares_a3.append(share)
        g_up_bias.append(unit_sums[0])
    [grad_pre] = begun
    g_w_down_far = layout.send(g_w_down, True)
    grad_a3 = layout.scatter_sum(shares_a3)
    g_up_bias = total(g_up_bias)
    g_w_up = contract_rows(a3_all, grad_pre).astype(bf16)
    g_w_up_far = layout.send(g_w_up, True)
    grad_mid = upstream + norm_back(grad_a3, normed3, inv3, ln3_gain)
    grad_z = norm_back(grad_mid, normed2, inv2, ln2_gain).astype(bf16)
    grad_z_all = layout.gather(grad_z)
    grad_ctx = [contract_cols(g, w_out).astype(bf16) for g in grad_z_all]
    g_w_out = total([contract_rows(x, g) for x, g in zip(context, grad_z_all)]).astype(bf16)
    g_w_out_far = layout.send(g_w_out, True)
    g_w_down_far, g_w_up, *grad_ctx = lax.optimization_barrier((g_w_down_far, g_w_up, *grad_ctx))
    grad_ctx, _ = for_kernel(grad_ctx, rank)
    g_w_down = jnp.where(stays, g_w_down, g_w_down_far)
    tables, g_w_down = lax.optimization_barrier((tables, g_w_down))
    g_w_down = layout.sum_dp(g_w_down, 1)
    each = pairs // chunks
    calls = [(0, each)] + [(k, 1) for k in range(each, pairs)]
    done, g_w_qkv, sums, grad_qkv = [], [], [], ()
    for call in calls:
        if len(calls) > 1 and call == calls[-1]:
            g_w_up_far, g_w_out_far, *grad_qkv = lax.optimization_barrier(
                (g_w_up_far, g_w_out_far, *grad_qkv)
            )
            g_w_up = jnp.where(stays, g_w_up, g_w_up_far)
            g_w_out = jnp.where(stays, g_w_out, g_w_out_far)
            tables, g_w_down, g_w_up, g_w_out = lax.optimization_barrier(
                (tables, g_w_down, g_w_up, g_w_out)
            )
        grad_qkv = attend_backward(
            qkv,
            context_turned,
            grad_ctx,
            log_total,
            seg,
            keep,
            tables,
            call,
            (call[0] % each, each),
            grad_qkv,
        )
        if sum(call) % each == 0:
            shared = from_kernel(grad_qkv, rank, shares)
            g_part, part_sums = weight_grad(a1, shared, 0, each)
            tables, g_part = lax.optimization_barrier((tables, g_part))
            g_w_qkv.append(layout.halved(layout.give_back(g_part), -1))
            sums.append(part_sums)
            done.append(shared)
            grad_qkv = ()
    if len(calls) == 1:
        g_w_up = jnp.where(stays, g_w_up, g_w_up_far)
        g_w_out = jnp.where(stays, g_w_out, g_w_out_far)
    g_w_up = layout.sum_dp(g_w_up, 0)
    bits = [-1, *layout.order(2 % len(layout.order(0)))]
    g_w_out = layout.halved_by(g_w_out, bits)
    layer_out = layout.give_back(after(layer_out, g_w_qkv[0]))
    sums = jnp.concatenate(sums, 1)
    grad_a1 = [input_grad(d, w_qkv) for d in zip(*done)]
    grad_a1 = layout.scatter_sum(grad_a1)
    grad_input = grad_mid + norm_back(grad_a1, normed1, inv1, ln1_gain)
    grad_input = grad_input.astype(bf16)
    steps = [layout.order(k) for k in range(chunks)]
    g_w_qkv[0] = layout.halved(g_w_qkv[0], steps[0].pop(0))
    g_w_out, *g_w_qkv = lax.optimization_barrier((g_w_out, *g_w_qkv))
    g_w_out = layout.joined_by(g_w_out, bits)
    g_w_qkv = [layout.halved_by(g, s) for g, s in zip(g_w_qkv, steps)]
    g_w_qkv = [layout.joined_by(g, layout.order(k)) for k, g in enumerate(g_w_qkv)]
    g_w_up, *g_w_qkv = lax.optimization_barrier((g_w_up, *g_w_qkv))
    begun = ()
    for chunk, mine in enumerate(g_w_qkv):
        theirs = layout.partner(mine, -1)
        begun = (spread(mine, theirs, layout.side(-1), pairs, chunk * each, begun),)
    g_w_qkv = begun[0].transpose(1, 0, 2)
    sums = sums.reshape(pairs, 3, PAIR).transpose(1, 0, 2).reshape(3, width)
    grad_input = layout.give_back(grad_input).astype(f32)

    norm_terms = jnp.stack(
        [
            jnp.sum(grad_a1 * normed1, 0),
            jnp.sum(grad_a1, 0),
            jnp.sum(grad_z.astype(f32), 0),
            jnp.sum(grad_mid * normed2, 0),
            jnp.sum(grad_mid, 0),
            jnp.sum(grad_a3 * normed3, 0),
            jnp.sum(grad_a3, 0),
            jnp.sum(grad_f.astype(f32), 0),
            jnp.sum(upstream * normed4, 0),
            jnp.sum(upstream, 0),
        ],
        0,
    )
    all_units = lax.dynamic_update_slice(jnp.zeros((units * shares,), f32), g_up_bias, (rank * units,))
    all_width = lax.dynamic_update_slice(
        jnp.zeros((2, width * shares), f32), jnp.stack([sums[0], sums[2]], 0), (0, rank * width)
    )
    small = layout.sum_all(
        jnp.concatenate([norm_terms.reshape(-1), all_width.reshape(-1), all_units])
    )
    norm_terms = small[: 10 * model_dim].reshape(10, model_dim)
    all_width = small[10 * model_dim : 12 * model_dim].reshape(2, width * shares)
    all_units = small[12 * model_dim :]
    m = lax.axis_index("mp")
    g_qv_bias = lax.dynamic_slice(all_width, (0, m * width), (2, width))
    g_up_bias = lax.dynamic_slice(all_units, (m * units,), (units,))
    return (
        layer_out,
        grad_input,
        norm_terms[0],
        norm_terms[1],
        g_w_qkv,
        g_qv_bias,
        g_w_out.astype(f32),
        norm_terms[2],
        norm_terms[3],
        norm_terms[4],
        norm_terms[5],
        norm_terms[6],
        g_w_up.astype(f32),
        g_up_bias,
        g_w_down.astype(f32),
        norm_terms[7],
        norm_terms[8],
        norm_terms[9],
    )


def solution(mesh):
    in_specs = (
        P(("dp", "mp"), None),
        P(),
        P(),
        P(None, None, "mp"),
        P(None, "mp"),
        P("mp", None),
        P(),
        P(),
        P(),
        P(),
        P(),
        P(None, "mp"),
        P("mp"),
        P("mp", None),
        P(),
        P(),
        P(),
        P("dp", None),
        P("dp"),
        P(("dp", "mp"), None),
    )
    out_specs = (
        P(("dp", "mp"), None),
        P(("dp", "mp"), None),
        P(),
        P(),
        P(None, None, "mp"),
        P(None, "mp"),
        P("mp", None),
        P(),
        P(),
        P(),
        P(),
        P(),
        P(None, "mp"),
        P("mp"),
        P("mp", None),
        P(),
        P(),
        P(),
    )
    return jax.shard_map(functools.partial(body, Layout(mesh)), mesh=mesh, in_specs=in_specs, out_specs=out_specs, check_vma=False)
```
